32 devices in a mesh: dp: 4 (over y, x), seq: 8 (over z, core).
Axes of the slice: x: 2, y: 2, z: 4, core: 2. Of those that a mesh axis runs over, the one named last changes fastest.
Arguments:
- latents: bfloat16 [4, 1024, 1536], P('dp', 'seq'), may hold values from -6 to 6
- context: bfloat16 [4, 128, 768], P('dp'), may hold values from -6 to 6
- clip_starts: int32 [4, 4], P('dp'), may hold values from 0 to 1023, as said below
- buckets: int32 [4], replicated, may hold values from 0 to 4
- owners: int32 [32], replicated, may hold values from 0 to 31, each once
- cotangent: bfloat16 [4, 1024, 1536], P('dp', 'seq'), may hold values from -6 to 6
- sheet: float32 [1536, 29192], P(('dp', 'seq')), may hold values from -2 to 2, as said below
- first: float32 [1536, 29192], P(('dp', 'seq')), may hold values from -0.00059735496 to 0.00059735496
- second: float32 [1536, 29192], P(('dp', 'seq')), may hold values from 2.2302057e-08 to 8.920823e-08
Outputs:
- output: bfloat16 [4, 1024, 1536], P('dp', 'seq')
- latent_grad: float32 [4, 1024, 1536], P('dp', 'seq')
- grad_norm: float32 [], replicated
- sheet_grad: float32 [1536, 29192], P(('dp', 'seq'))
- gain_grad: float32 [1536, 8], P(('dp', 'seq'))
- first_new: float32 [1536, 29192], P(('dp', 'seq'))
- second_new: float32 [1536, 29192], P(('dp', 'seq'))
- sheet_new: float32 [1536, 29192], P(('dp', 'seq'))
- sheet_copy: bfloat16 [1536, 29192], P(('dp', 'seq'))
The draws below stay inside these ranges and needn't reach their ends.
Inputs may be any that keep to these rules, and one draw needn't show every extreme that they name: `clip_starts`: in each row the starts rise; the first is 0, the second lies in 1 to 64, the last two lie in the last 64 frames. `sheet`: columns from 29184 on are positive.
All inputs are finite; a program needn't handle non-finite values.
Results may differ from the reference program's by a relative error of at most 0.02.
Values may be sent and summed in bfloat16 or wider, within the bound.
A program may use at most 960 MiB of HBM per device.

```python
import math
import jax
import jax.numpy as jnp
import numpy as np
from jax import lax

D = 1536
FF = 6144
HEAD = 64
CTXW = 768
CTX = 128
NB = 5
STEP = 10
FRAMES_DEV = 128
ROWS = 4
BLOCKS = 32
LENGTH = 1024
SHEET = 29192


def column_spread_drawn(length):
    column = jnp.arange(SHEET, dtype=jnp.int32)
    base_std = D ** (-0.5)
    spread = jnp.full((SHEET,), base_std, jnp.float32)
    spread = jnp.where((column >= 3 * D) & (column < 4 * D), base_std * math.sqrt(length) / 4.0, spread)
    spread = jnp.where((column >= 5 * D) & (column < 6 * D), base_std * math.sqrt(CTX), spread)
    spread = jnp.where((column >= 6 * D + 2 * FF) & (column < 6 * D + 3 * FF), FF ** (-0.5), spread)
    spread = jnp.where((column >= 6 * D + 3 * FF) & (column < 6 * D + 3 * FF + 2 * CTXW), CTXW ** (-0.5), spread)
    spread = jnp.where(column >= 6 * D + 3 * FF + 2 * CTXW, 0.3, spread)
    return spread


def draw_sheet(key, part):
    key = jax.random.fold_in(key, 11)
    noise_key, gain_key = jax.random.split(key)
    row_frac = jnp.arange(D, dtype=jnp.float32) / D
    base_draw = jax.random.truncated_normal(noise_key, -4.0, 4.0, (D, SHEET), jnp.float32)
    rising = jnp.sqrt(0.5 + row_frac)
    jitter = 1.0 + 0.15 * jax.random.uniform(gain_key, (D, SHEET), jnp.float32, -1.0, 1.0)
    column = jnp.arange(SHEET, dtype=jnp.int32)
    gain_values = rising[:, None] * jitter
    matrix_values = base_draw * column_spread_drawn(LENGTH)[None, :]
    return jnp.where(column[None, :] >= 6 * D + 3 * FF + 2 * CTXW, gain_values, matrix_values)


def draw_clip_starts(key, part):
    key = jax.random.fold_in(key, 5)
    head_key, tail_key, last_key, pick_key = jax.random.split(key, 4)
    head_len = jax.random.randint(head_key, (ROWS,), 1, FRAMES_DEV // 2 + 1)
    tail_len = jax.random.randint(tail_key, (ROWS,), 1, FRAMES_DEV // 4 + 1)
    last_len = jax.random.randint(last_key, (ROWS,), 1, FRAMES_DEV // 4 + 1)
    chosen = jax.random.randint(pick_key, (), 0, ROWS)
    last_len = jnp.where(jnp.arange(ROWS, dtype=jnp.int32) == chosen, 1, last_len)
    zeros_col = jnp.zeros((ROWS,), jnp.int32)
    return jnp.stack([zeros_col, head_len, LENGTH - tail_len - last_len, LENGTH - last_len], axis=1).astype(jnp.int32)


def plant(result, rng, low, top_value):
    place = [jax.random.randint(jax.random.fold_in(rng, axis), (), 0, length) for axis, length in enumerate(result.shape)]
    main_axis = result.shape.index(max(result.shape))
    neighbour = place[:main_axis] + [(place[main_axis] + 1) % result.shape[main_axis]] + place[main_axis + 1:]
    return result.at[tuple(place)].set(low).at[tuple(neighbour)].set(top_value)


def level_of(key, extent, pieces, low, top_value):
    def one(dim, parts):
        draws = jax.random.uniform(jax.random.fold_in(jax.random.fold_in(key, 6), dim), (parts,), jnp.float32, low / len(pieces), top_value / len(pieces))
        return jnp.repeat(jnp.exp(draws), extent[dim] // parts).reshape((-1,) + (1,) * (len(extent) - dim - 1))

    level = one(*pieces[0])
    for cut in pieces[1:]:
        level = level * one(*cut)
    return level


def rank_table(amount, lean):
    portions = [(1 << 20) // math.isqrt(standing ** lean) + 1 for standing in range(1, amount + 1)]
    width = 1 + sum(portions) // (1 << 30)
    return np.cumsum(np.array([max(1, weight // width) for weight in portions]))


def skewed_ids(rng, dims, amount, skew):
    table = rank_table(amount, skew)
    ticket = jax.random.randint(jax.random.fold_in(rng, 1), dims, 0, int(table[amount - 1]))
    rank = jnp.searchsorted(jnp.asarray(table, jnp.int32), ticket, side="right")
    return jax.random.permutation(jax.random.fold_in(rng, 2), amount)[rank].astype(jnp.int32)


def gaussian(stream_key, extent, deviation, limit, cuts=(), kind=jnp.bfloat16):
    gain = level_of(stream_key, extent, cuts, -0.22, 0.18) if cuts else 1.0
    values = jax.random.normal(stream_key, extent, jnp.float32) * deviation * gain
    return jnp.minimum(jnp.maximum(values, -limit), limit).astype(kind)


def setup_inputs(seed: int = 0) -> dict:
    keys = jax.random.split(jax.random.key(seed), 10)
    return {
        "latents": gaussian(keys[0], (ROWS, LENGTH, D), 1.0, 6.0, ((0, 4), (1, 8))),
        "context": gaussian(keys[1], (ROWS, CTX, CTXW), 1.0, 6.0, ((0, 4),)),
        "clip_starts": draw_clip_starts(jax.random.fold_in(keys[9], 71), 0),
        "buckets": plant(skewed_ids(keys[3], (ROWS,), NB, 2), jax.random.fold_in(keys[3], 3), 0, NB - 1).astype(jnp.int32),
        "owners": jax.random.permutation(keys[4], BLOCKS).astype(jnp.int32),
        "cotangent": gaussian(keys[5], (ROWS, LENGTH, D), 1.0, 6.0, ((0, 4), (1, 8))),
        "sheet": draw_sheet(jax.random.fold_in(keys[9], 71), 0),
        "first": gaussian(keys[7], (D, SHEET), (1.0 / (D * SHEET) ** 0.5), 0.00059735496, ((0, 32),), jnp.float32),
        "second": jnp.clip(jnp.exp(math.log(8.920822835989384e-08) - 1.3862944 * jax.random.uniform(keys[8], (D, SHEET), jnp.float32) ** level_of(keys[8], (D, SHEET), ((0, 32),), -0.2, 0.2)), 2.230205708997346e-08, 8.920822835989384e-08),
    }


HIGHEST = lax.Precision.HIGHEST
EPS_NORM = 1e-05
EPS_ADAM = 1e-08
MASKED_SCORE = -1e+30
BETA_ONE = 0.5
BETA_TWO = 0.5
WEIGHT_DECAY = 0.01

@jax.custom_vjp
def low(v):
    return lax.optimization_barrier(v.astype(jnp.bfloat16)).astype(jnp.float32)

@jax.custom_vjp
def low_back(v):
    return v

def low_keep(v):
    return (low(v), None)

def low_pass(kept, grad):
    return (grad,)

def back_keep(v):
    return (v, None)

def back_low(kept, grad):
    return (low(grad),)
low.defvjp(low_keep, low_pass)
low_back.defvjp(back_keep, back_low)

def column_spread(length):
    column = jnp.arange(SHEET, dtype=jnp.int32)
    base_std = D ** (-0.5)
    spread = jnp.full((SHEET,), base_std, jnp.float32)
    spread = jnp.where((column >= 3 * D) & (column < 4 * D), base_std * math.sqrt(length) / 4.0, spread)
    spread = jnp.where((column >= 5 * D) & (column < 6 * D), base_std * math.sqrt(CTX), spread)
    spread = jnp.where((column >= 6 * D + 2 * FF) & (column < 6 * D + 3 * FF), FF ** (-0.5), spread)
    spread = jnp.where((column >= 6 * D + 3 * FF) & (column < 6 * D + 3 * FF + 2 * CTXW), CTXW ** (-0.5), spread)
    spread = jnp.where(column >= 6 * D + 3 * FF + 2 * CTXW, 0.3, spread)
    return spread

def layer_norm(values):
    average = lax.optimization_barrier(jnp.mean(values, axis=-1, keepdims=True))
    centered = values - average
    variance = lax.optimization_barrier(jnp.mean(centered * centered, axis=-1, keepdims=True))
    return centered * lax.rsqrt(variance + EPS_NORM)

def softmax_rows(scores):
    row_max = lax.optimization_barrier(jnp.max(scores, axis=-1, keepdims=True))
    exponent = jnp.exp(scores - row_max)
    return exponent / lax.optimization_barrier(jnp.sum(exponent, axis=-1, keepdims=True))

def rope_tables(positions):
    half_dim = HEAD // 2
    frequency = jnp.exp(-math.log(10000.0) * jnp.arange(half_dim, dtype=jnp.float32) / half_dim)
    angles = positions.astype(jnp.float32)[:, None] * frequency[None, :]
    return (jnp.cos(angles)[:, None, :], jnp.sin(angles)[:, None, :])

def rotate(values, cosine, sine_table):
    half_dim = values.shape[-1] // 2
    first_half = values[..., :half_dim]
    second_half = values[..., half_dim:]
    return jnp.concatenate([first_half * cosine - second_half * sine_table, second_half * cosine + first_half * sine_table], axis=-1)

def segment_ids(starts, positions):
    return lax.optimization_barrier(jnp.sum((starts[None, :] <= positions[:, None]).astype(jnp.int32), axis=1)) - 1

def self_attention(queries, key_rows, value_rows, segments):
    block_rows = math.gcd(LENGTH, 512)
    head_count = D // HEAD
    score_scale = HEAD ** (-0.5)

    def one_block(block_items):
        query_block, segment_block = block_items
        scores = low_back(jnp.einsum('qhd,khd->hqk', query_block, key_rows, precision=HIGHEST) * score_scale)
        scores = jnp.where((segment_block[:, None] == segments[None, :])[None], scores, MASKED_SCORE)
        attn_probs = low(softmax_rows(scores))
        return jnp.einsum('hqk,khd->qhd', attn_probs, value_rows, precision=HIGHEST)
    attended = lax.map(jax.checkpoint(one_block), (queries.reshape(LENGTH // block_rows, block_rows, head_count, HEAD), segments.reshape(LENGTH // block_rows, block_rows)))
    return attended.reshape(LENGTH, D)

def row_forward(weights, row_latents, row_text, row_starts, row_pick):
    positions = jnp.arange(LENGTH, dtype=jnp.int32)
    segments = segment_ids(row_starts, positions)
    cosine, sine_table = rope_tables(positions)
    head_count = D // HEAD
    score_scale = HEAD ** (-0.5)
    gain_col = 6 * D + 3 * FF + 2 * CTXW
    gains = weights[:, gain_col:gain_col + 3]
    time_gain = jnp.dot(weights[:, gain_col + 3:], row_pick, precision=HIGHEST)
    h_one = low(layer_norm(row_latents) * gains[:, 0] * time_gain)
    joint_qkv = low_back(jnp.dot(h_one, weights[:, :3 * D], precision=HIGHEST))
    queries = low(rotate(joint_qkv[:, :D].reshape(LENGTH, head_count, HEAD), cosine, sine_table))
    key_rows = low(rotate(joint_qkv[:, D:2 * D].reshape(LENGTH, head_count, HEAD), cosine, sine_table))
    value_rows = low(joint_qkv[:, 2 * D:].reshape(LENGTH, head_count, HEAD))
    attn_out = low(low_back(self_attention(queries, key_rows, value_rows, segments)))
    x_one = row_latents + low_back(jnp.dot(attn_out, weights[:, 3 * D:4 * D], precision=HIGHEST))
    h_two = low(layer_norm(x_one) * gains[:, 1])
    cross_q = low(low_back(jnp.dot(h_two, weights[:, 4 * D:5 * D], precision=HIGHEST))).reshape(LENGTH, head_count, HEAD)
    text_keys = low(jnp.dot(row_text, weights[:, gain_col - 2 * CTXW:gain_col - CTXW].T, precision=HIGHEST)).reshape(CTX, head_count, HEAD)
    text_values = low(jnp.dot(row_text, weights[:, gain_col - CTXW:gain_col].T, precision=HIGHEST)).reshape(CTX, head_count, HEAD)
    cross_scores = low_back(jnp.einsum('qhd,khd->hqk', cross_q, text_keys, precision=HIGHEST) * score_scale)
    cross_probs = low(softmax_rows(cross_scores))
    cross_out = low(low_back(jnp.einsum('hqk,khd->qhd', cross_probs, text_values, precision=HIGHEST).reshape(LENGTH, D)))
    x_two = x_one + low_back(jnp.dot(cross_out, weights[:, 5 * D:6 * D], precision=HIGHEST))
    h_three = low(layer_norm(x_two) * gains[:, 2])
    gate_up = low_back(jnp.dot(h_three, weights[:, 6 * D:6 * D + 2 * FF], precision=HIGHEST))
    hidden = low(jax.nn.silu(gate_up[:, :FF]) * gate_up[:, FF:])
    return x_two + low_back(jnp.dot(hidden, weights[:, 6 * D + 2 * FF:6 * D + 3 * FF].T, precision=HIGHEST))

def reference(latents, context, clip_starts, buckets, owners, cotangent, sheet, first, second):
    group_ids = jnp.arange(BLOCKS, dtype=jnp.int32)
    inverse = lax.optimization_barrier(jnp.sum(jnp.where(owners[None, :] == group_ids[:, None], group_ids[None, :], 0), axis=1)).astype(jnp.int32)
    logical = sheet.reshape(BLOCKS, D // BLOCKS, SHEET)[inverse].reshape(D, SHEET)
    bucket_ids = jnp.arange(NB, dtype=jnp.int32)
    picks = (buckets[:, None] == bucket_ids[None, :]).astype(jnp.float32)
    counts = lax.optimization_barrier(jnp.sum(picks, axis=0))
    row_weight = ROWS / (NB * lax.optimization_barrier(jnp.sum(picks * counts[None, :], axis=1)))
    checked_row = jax.checkpoint(row_forward)
    text_all = context.astype(jnp.float32)

    def forward(master, latent_rows):
        weights = low(master)

        def row_step(carried, row_items):
            row_latents, row_text, row_starts, row_pick = row_items
            return (carried, checked_row(weights, row_latents, row_text, row_starts, row_pick))
        final_carry, outputs_all = lax.scan(row_step, jnp.zeros((), jnp.float32), (latent_rows, text_all, clip_starts, picks))
        return outputs_all
    outputs_all, pullback = jax.vjp(forward, logical, latents.astype(jnp.float32))
    grad_output = cotangent.astype(jnp.float32) * row_weight[:, None, None]
    grad_logical, latent_grad = pullback(grad_output)
    grad_sheet = grad_logical.reshape(BLOCKS, D // BLOCKS, SHEET)[owners].reshape(D, SHEET)
    grad_norm = jnp.sqrt(jnp.sum(grad_sheet * grad_sheet))
    clipped = grad_sheet / jnp.maximum(grad_norm, 1.0)
    gain_grad = clipped[:, 6 * D + 3 * FF + 2 * CTXW:]
    first_new = BETA_ONE * first + (1.0 - BETA_ONE) * clipped
    second_new = BETA_TWO * second + (1.0 - BETA_TWO) * clipped * clipped
    mean_hat = first_new / (1.0 - BETA_ONE ** STEP)
    square_hat = second_new / (1.0 - BETA_TWO ** STEP)
    rates = column_spread(LENGTH)[None, :]
    sheet_new = sheet - rates * (mean_hat / (jnp.sqrt(square_hat) + EPS_ADAM) + WEIGHT_DECAY * sheet)
    return (outputs_all.astype(jnp.bfloat16), latent_grad, grad_norm, clipped, gain_grad, first_new, second_new, sheet_new, sheet_new.astype(jnp.bfloat16))
```

```python
import math

import jax
import jax.numpy as jnp
from jax import lax
from jax.sharding import Mesh
from jax.sharding import PartitionSpec as P

D = 1536
FF = 6144
HEAD = 64
CTXW = 768
CTX = 128
NB = 5
STEP = 10
SHEET = 29192


HIGHEST = lax.Precision.HIGHEST
EPS_NORM = 1e-05
EPS_ADAM = 1e-08
MASKED_SCORE = -1e30
BETA_ONE = 0.5
BETA_TWO = 0.5
WEIGHT_DECAY = 0.01


def reorder(values, ordering):
    leading = values.shape[:-1]
    groups = ordering.shape[0]
    blocks = values.reshape(leading + (groups, values.shape[-1] // groups))
    return jnp.take(blocks, ordering, axis=-2).reshape(values.shape)


def norm_parts(values):
    average = jnp.mean(values, axis=-1, keepdims=True)
    centered = values - average
    variance = jnp.mean(centered * centered, axis=-1, keepdims=True)
    inverse_std = lax.rsqrt(variance + EPS_NORM)
    return (centered * inverse_std, inverse_std)


def norm_back(grad_normed, normed, inverse_std):
    return inverse_std * (
        grad_normed
        - jnp.mean(grad_normed, axis=-1, keepdims=True)
        - normed * jnp.mean(grad_normed * normed, axis=-1, keepdims=True)
    )


def softmax_rows(scores):
    row_max = jnp.max(scores, axis=-1, keepdims=True)
    exponent = jnp.exp(scores - row_max)
    return exponent / jnp.sum(exponent, axis=-1, keepdims=True)


def rope_tables(positions, head_dim):
    half_dim = head_dim // 2
    frequency = jnp.exp(-math.log(10000.0) * jnp.arange(half_dim, dtype=jnp.float32) / half_dim)
    angles = positions.astype(jnp.float32)[:, None] * frequency[None, :]
    return (jnp.cos(angles)[:, None, :], jnp.sin(angles)[:, None, :])


def rotate(values, cosine, sine_table):
    half_dim = values.shape[-1] // 2
    first_half = values[..., :half_dim]
    second_half = values[..., half_dim:]
    return jnp.concatenate(
        [
            first_half * cosine - second_half * sine_table,
            second_half * cosine + first_half * sine_table,
        ],
        axis=-1,
    )


def unrotate(grads, cosine, sine_table):
    half_dim = grads.shape[-1] // 2
    first_half = grads[..., :half_dim]
    second_half = grads[..., half_dim:]
    return jnp.concatenate(
        [
            first_half * cosine + second_half * sine_table,
            second_half * cosine - first_half * sine_table,
        ],
        axis=-1,
    )


def segment_ids(starts, positions):
    return jnp.sum((starts[None, :] <= positions[:, None]).astype(jnp.int32), axis=1) - 1


def column_spread(length):
    column = jnp.arange(SHEET, dtype=jnp.int32)
    base_std = D ** (-0.5)
    spread = jnp.full((SHEET,), base_std, jnp.float32)
    spread = jnp.where(
        (column >= 3 * D) & (column < 4 * D), base_std * math.sqrt(length) / 4.0, spread
    )
    spread = jnp.where((column >= 5 * D) & (column < 6 * D), base_std * math.sqrt(CTX), spread)
    spread = jnp.where((column >= 6 * D + 2 * FF) & (column < 6 * D + 3 * FF), FF ** (-0.5), spread)
    spread = jnp.where(
        (column >= 6 * D + 3 * FF) & (column < 6 * D + 3 * FF + 2 * CTXW), CTXW ** (-0.5), spread
    )
    spread = jnp.where(column >= 6 * D + 3 * FF + 2 * CTXW, 0.3, spread)
    return spread


def inner_rows(left, right):
    return lax.dot_general(
        left, right, (((0,), (0,)), ((), ())), preferred_element_type=jnp.float32
    )


def inner_rows_high(left, right):
    return lax.dot_general(
        left, right, (((0,), (0,)), ((), ())), precision=HIGHEST, preferred_element_type=jnp.float32
    )


def gather_plan(latents, context, clip_starts, buckets, owners, cotangent, sheet, first, second):
    frames = latents.shape[1]
    seq_count = lax.axis_size("seq")
    length = frames * seq_count
    head_count = D // HEAD
    score_scale = HEAD ** (-0.5)
    group_ids = jnp.arange(owners.shape[0], dtype=jnp.int32)
    inverse = jnp.sum(
        jnp.where(owners[None, :] == group_ids[:, None], group_ids[None, :], 0), axis=1
    )
    gathered = lax.all_gather(sheet.astype(jnp.bfloat16), ("dp", "seq"), axis=0, tiled=True)
    tail_col = 6 * D + 3 * FF
    gain_col = tail_col + 2 * CTXW
    gain_rows = reorder(gathered[:, gain_col:].astype(jnp.float32).T, inverse)
    row_index = lax.axis_index("dp")
    bucket_ids = jnp.arange(NB, dtype=jnp.int32)
    bucket_pick = (bucket_ids == buckets[row_index]).astype(jnp.float32)
    counts = jnp.sum((buckets[:, None] == bucket_ids[None, :]).astype(jnp.float32), axis=0)
    row_weight = buckets.shape[0] / (NB * jnp.sum(bucket_pick * counts))
    gain_one = gain_rows[0]
    gain_two = gain_rows[1]
    gain_three = gain_rows[2]
    time_gain = jnp.sum(gain_rows[3:] * bucket_pick[:, None], axis=0)
    tokens = latents[0].astype(jnp.float32)
    positions = lax.axis_index("seq") * frames + jnp.arange(frames, dtype=jnp.int32)
    all_positions = jnp.arange(length, dtype=jnp.int32)
    starts = clip_starts[0]
    same_clip = (
        segment_ids(starts, positions)[:, None] == segment_ids(starts, all_positions)[None, :]
    )[None]
    cosine, sine_table = rope_tables(positions, HEAD)
    normed_one, inverse_one = norm_parts(tokens)
    scaled_one = gain_one * time_gain
    h_one_st = reorder((normed_one * scaled_one).astype(jnp.bfloat16), owners)
    joint_qkv = jnp.dot(h_one_st, gathered[:, : 3 * D], preferred_element_type=jnp.float32)
    queries = rotate(joint_qkv[:, :D].reshape(frames, head_count, HEAD), cosine, sine_table).astype(
        jnp.bfloat16
    )
    key_local = rotate(
        joint_qkv[:, D : 2 * D].reshape(frames, head_count, HEAD), cosine, sine_table
    ).astype(jnp.bfloat16)
    value_local = joint_qkv[:, 2 * D :].reshape(frames, head_count, HEAD).astype(jnp.bfloat16)
    key_all, value_all = (
        lax.all_gather(key_local, "seq", axis=0, tiled=True),
        lax.all_gather(value_local, "seq", axis=0, tiled=True),
    )
    scores = (
        jnp.einsum("qhd,khd->hqk", queries, key_all, preferred_element_type=jnp.float32)
        * score_scale
    )
    attn_probs = softmax_rows(jnp.where(same_clip, scores, MASKED_SCORE))
    probs_low = attn_probs.astype(jnp.bfloat16)
    attn_out = (
        jnp.einsum("hqk,khd->qhd", probs_low, value_all, preferred_element_type=jnp.float32)
        .reshape(frames, D)
        .astype(jnp.bfloat16)
    )
    attn_st = reorder(attn_out, owners)
    x_one = tokens + jnp.dot(
        attn_st, gathered[:, 3 * D : 4 * D], preferred_element_type=jnp.float32
    )
    normed_two, inverse_two = norm_parts(x_one)
    h_two_st = reorder((normed_two * gain_two).astype(jnp.bfloat16), owners)
    cross_q = (
        jnp.dot(h_two_st, gathered[:, 4 * D : 5 * D], preferred_element_type=jnp.float32)
        .astype(jnp.bfloat16)
        .reshape(frames, head_count, HEAD)
    )
    text_tokens = context[0]
    text_kv = jnp.einsum(
        "tc,dec->etd",
        text_tokens,
        gathered[:, tail_col:gain_col].reshape(D, 2, CTXW),
        preferred_element_type=jnp.float32,
    )
    text_kv = reorder(text_kv, inverse).astype(jnp.bfloat16).reshape(2, CTX, head_count, HEAD)
    text_keys = text_kv[0]
    text_values = text_kv[1]
    cross_scores = (
        jnp.einsum("qhd,khd->hqk", cross_q, text_keys, preferred_element_type=jnp.float32)
        * score_scale
    )
    cross_probs = softmax_rows(cross_scores)
    cross_low = cross_probs.astype(jnp.bfloat16)
    cross_out = (
        jnp.einsum("hqk,khd->qhd", cross_low, text_values, preferred_element_type=jnp.float32)
        .reshape(frames, D)
        .astype(jnp.bfloat16)
    )
    cross_st = reorder(cross_out, owners)
    x_two = x_one + jnp.dot(
        cross_st, gathered[:, 5 * D : 6 * D], preferred_element_type=jnp.float32
    )
    normed_three, inverse_three = norm_parts(x_two)
    h_three_st = reorder((normed_three * gain_three).astype(jnp.bfloat16), owners)
    grad_out = cotangent[0].astype(jnp.float32) * row_weight
    grad_ff_st = reorder(grad_out.astype(jnp.bfloat16), owners)
    gate_weight = gathered[:, 6 * D : 6 * D + 2 * FF]
    down_weight = gathered[:, 6 * D + 2 * FF : 6 * D + 3 * FF]
    units = down_weight.shape[1]
    gate_up = jnp.dot(h_three_st, gate_weight, preferred_element_type=jnp.float32)
    gate_pre = gate_up[:, :units]
    up_part = gate_up[:, units:]
    sigmoid_gate = jax.nn.sigmoid(gate_pre)
    silu_gate = gate_pre * sigmoid_gate
    hidden = (silu_gate * up_part).astype(jnp.bfloat16)
    ff_out = reorder(
        jnp.einsum("nf,df->nd", hidden, down_weight, preferred_element_type=jnp.float32), inverse
    )
    result = x_two + ff_out
    grad_hidden = jnp.dot(grad_ff_st, down_weight, preferred_element_type=jnp.float32)
    grad_gate = grad_hidden * up_part * (sigmoid_gate * (1.0 + gate_pre * (1.0 - sigmoid_gate)))
    grad_up = grad_hidden * silu_gate
    grad_gu = jnp.concatenate([grad_gate, grad_up], axis=1).astype(jnp.bfloat16)
    grad_h_three = reorder(
        jnp.einsum("nf,df->nd", grad_gu, gate_weight, preferred_element_type=jnp.float32), inverse
    )
    grad_gain_three = jnp.sum(grad_h_three * normed_three, axis=0)
    grad_x_two = grad_out + norm_back(grad_h_three * gain_three, normed_three, inverse_three)
    grad_cross = grad_x_two.astype(jnp.bfloat16)
    grad_cross_out = (
        reorder(
            jnp.einsum(
                "nd,ed->ne",
                grad_cross,
                gathered[:, 5 * D : 6 * D],
                preferred_element_type=jnp.float32,
            ),
            inverse,
        )
        .astype(jnp.bfloat16)
        .reshape(frames, head_count, HEAD)
    )
    grad_cross_probs = jnp.einsum(
        "qhd,khd->hqk", grad_cross_out, text_values, preferred_element_type=jnp.float32
    )
    grad_cross_scores = (
        cross_probs
        * (grad_cross_probs - jnp.sum(cross_probs * grad_cross_probs, axis=-1, keepdims=True))
    ).astype(jnp.bfloat16)
    grad_cross_q = (
        (
            jnp.einsum(
                "hqk,khd->qhd", grad_cross_scores, text_keys, preferred_element_type=jnp.float32
            )
            * score_scale
        )
        .reshape(frames, D)
        .astype(jnp.bfloat16)
    )
    grad_text_keys = (
        jnp.einsum("hqk,qhd->khd", grad_cross_scores, cross_q, preferred_element_type=jnp.float32)
        * score_scale
    )
    grad_text_values = jnp.einsum(
        "hqk,qhd->khd", cross_low, grad_cross_out, preferred_element_type=jnp.float32
    )
    grad_text = reorder(
        jnp.stack([grad_text_keys.reshape(CTX, D), grad_text_values.reshape(CTX, D)]), owners
    )
    grad_h_two = reorder(
        jnp.einsum(
            "ne,de->nd",
            grad_cross_q,
            gathered[:, 4 * D : 5 * D],
            preferred_element_type=jnp.float32,
        ),
        inverse,
    )
    grad_gain_two = jnp.sum(grad_h_two * normed_two, axis=0)
    grad_x_one = grad_x_two + norm_back(grad_h_two * gain_two, normed_two, inverse_two)
    grad_attn = grad_x_one.astype(jnp.bfloat16)
    grad_attn_out = (
        reorder(
            jnp.einsum(
                "nd,ed->ne",
                grad_attn,
                gathered[:, 3 * D : 4 * D],
                preferred_element_type=jnp.float32,
            ),
            inverse,
        )
        .astype(jnp.bfloat16)
        .reshape(frames, head_count, HEAD)
    )
    key_back, value_back = (key_all, value_all)

    def head_grads(head_items):
        head_probs, head_grad_out, head_values = head_items
        grad_probs = jnp.einsum(
            "qd,kd->qk", head_grad_out, head_values, preferred_element_type=jnp.float32
        )
        return (
            head_probs * (grad_probs - jnp.sum(head_probs * grad_probs, axis=-1, keepdims=True))
        ).astype(jnp.bfloat16)

    grad_scores_low = lax.map(
        head_grads, (attn_probs, jnp.swapaxes(grad_attn_out, 0, 1), jnp.swapaxes(value_back, 0, 1))
    )
    grad_queries = (
        jnp.einsum("hqk,khd->qhd", grad_scores_low, key_back, preferred_element_type=jnp.float32)
        * score_scale
    )
    grad_keys = (
        jnp.einsum("hqk,qhd->khd", grad_scores_low, queries, preferred_element_type=jnp.float32)
        * score_scale
    )
    grad_values = jnp.einsum(
        "hqk,qhd->khd", probs_low, grad_attn_out, preferred_element_type=jnp.float32
    )
    key_sums = lax.psum_scatter(
        jnp.concatenate(
            [
                grad_keys.reshape(frames * lax.axis_size("seq"), D),
                grad_values.reshape(frames * lax.axis_size("seq"), D),
            ],
            axis=1,
        ).astype(jnp.bfloat16),
        "seq",
        scatter_dimension=0,
        tiled=True,
    ).astype(jnp.float32)
    grad_q_raw = unrotate(grad_queries, cosine, sine_table).reshape(frames, D)
    grad_k_raw = unrotate(
        key_sums[:, :D].reshape(frames, head_count, HEAD), cosine, sine_table
    ).reshape(frames, D)
    grad_qkv = jnp.concatenate([grad_q_raw, grad_k_raw, key_sums[:, D:]], axis=1).astype(
        jnp.bfloat16
    )
    grad_h_one = reorder(
        jnp.einsum("ne,de->nd", grad_qkv, gathered[:, : 3 * D], preferred_element_type=jnp.float32),
        inverse,
    )
    grad_gain_one = jnp.sum(grad_h_one * normed_one * time_gain, axis=0)
    grad_time = jnp.sum(grad_h_one * normed_one * gain_one, axis=0)
    latent_grad = grad_x_one + norm_back(grad_h_one * scaled_one, normed_one, inverse_one)
    gain_grads = jnp.concatenate(
        [
            jnp.stack([grad_gain_one, grad_gain_two, grad_gain_three]),
            bucket_pick[:, None] * grad_time[None, :],
        ],
        axis=0,
    )
    gain_grads = reorder(gain_grads, owners).T
    text_float = text_tokens.astype(jnp.float32)
    pieces = [
        inner_rows(h_one_st, grad_qkv),
        inner_rows(attn_st, grad_attn),
        inner_rows(h_two_st, grad_cross_q),
        inner_rows(cross_st, grad_cross),
    ]
    pieces = pieces + [inner_rows(h_three_st, grad_gu), inner_rows(grad_ff_st, hidden)]
    pieces = pieces + [
        inner_rows_high(grad_text[0], text_float),
        inner_rows_high(grad_text[1], text_float),
        gain_grads,
    ]
    other_shard = lax.psum_scatter(
        jnp.concatenate(pieces, axis=1), ("dp", "seq"), scatter_dimension=0, tiled=True
    )
    total_squares = lax.psum(jnp.sum(other_shard * other_shard), ("dp", "seq"))
    grad_norm = jnp.sqrt(total_squares)
    clipped = other_shard / jnp.maximum(grad_norm, 1.0)
    gain_grad = clipped[:, 6 * D + 3 * FF + 2 * CTXW :]
    first_new = BETA_ONE * first + (1.0 - BETA_ONE) * clipped
    second_new = BETA_TWO * second + (1.0 - BETA_TWO) * clipped * clipped
    mean_hat = first_new / (1.0 - BETA_ONE**STEP)
    square_hat = second_new / (1.0 - BETA_TWO**STEP)
    rates = column_spread(length)[None, :]
    sheet_new = sheet - rates * (
        mean_hat / (jnp.sqrt(square_hat) + EPS_ADAM) + WEIGHT_DECAY * sheet
    )
    return (
        result.astype(jnp.bfloat16)[None],
        latent_grad[None],
        grad_norm,
        clipped,
        gain_grad,
        first_new,
        second_new,
        sheet_new,
        sheet_new.astype(jnp.bfloat16),
    )


PLANE = ("dp", "core")


def norm_columns(values):
    average = jnp.mean(values, axis=0, keepdims=True)
    centered = values - average
    variance = jnp.mean(centered * centered, axis=0, keepdims=True)
    inverse_std = lax.rsqrt(variance + EPS_NORM)
    return (centered * inverse_std, inverse_std)


def norm_columns_back(grad_normed, normed, inverse_std):
    return inverse_std * (
        grad_normed
        - jnp.mean(grad_normed, axis=0, keepdims=True)
        - normed * jnp.mean(grad_normed * normed, axis=0, keepdims=True)
    )


def rotate_columns(values, cosine, sine_table):
    half_dim = HEAD // 2
    first_half = values[:, :half_dim]
    second_half = values[:, half_dim:]
    return jnp.concatenate(
        [
            first_half * cosine - second_half * sine_table,
            second_half * cosine + first_half * sine_table,
        ],
        axis=1,
    )


def contract_rows(left, right):
    return lax.dot_general(
        left, right, (((0,), (0,)), ((), ())), preferred_element_type=jnp.float32
    )


def contract_last(left, right):
    return lax.dot_general(
        left, right, (((1,), (1,)), ((), ())), preferred_element_type=jnp.float32
    )


def matmul(left, right):
    return jnp.dot(left, right, preferred_element_type=jnp.float32)


def plane_gather(shard):
    return lax.all_gather(shard, PLANE, axis=1, tiled=True)


def plane_gather_rows(shard):
    return lax.all_gather(shard, PLANE, axis=0, tiled=True)


def plane_scatter_frames(partial):
    return lax.psum_scatter(partial, PLANE, scatter_dimension=1, tiled=True)


def plane_scatter_rows(partial):
    return lax.psum_scatter(partial, PLANE, scatter_dimension=0, tiled=True)


def to_frames(rows):
    return lax.all_to_all(rows, PLANE, split_axis=1, concat_axis=0, tiled=True)


def to_rows(frames):
    return lax.all_to_all(frames, PLANE, split_axis=0, concat_axis=1, tiled=True)


def row_to_plane(local):
    groups = lax.axis_size("dp")
    frames, width = local.shape
    pieces = lax.all_to_all(local, "dp", split_axis=0, concat_axis=0, tiled=True)
    return lax.all_to_all(pieces, "z", split_axis=0, concat_axis=0, tiled=True)


def plane_to_row(local):
    pieces = lax.all_to_all(local, "z", split_axis=0, concat_axis=0, tiled=True)
    return lax.all_to_all(pieces, "dp", split_axis=0, concat_axis=0, tiled=True)


def split_columns(block, members):
    rows, columns = block.shape
    return block.reshape(rows, members, columns // members)


def gather_columns(block, order):
    rows, members, width = block.shape
    mine = lax.all_to_all(jnp.swapaxes(block, 0, 1), PLANE, split_axis=0, concat_axis=0, tiled=True)
    blocks = lax.all_gather(mine, "z", axis=0, tiled=True)
    return jnp.take(blocks, order, axis=0).reshape(-1, width)


def scatter_columns(grad, order, planes):
    blocks = grad.astype(jnp.bfloat16).reshape(order.shape[0], -1, grad.shape[-1])
    blocks = jnp.take(blocks, order, axis=0)
    mine = lax.psum_scatter(blocks, "z", scatter_dimension=0, tiled=True)
    return jnp.swapaxes(lax.all_to_all(mine, PLANE, split_axis=0, concat_axis=0, tiled=True), 0, 1)


def plane_plan(latents, context, clip_starts, buckets, owners, cotangent, sheet, first, second):
    groups = lax.axis_size("dp")
    planes = lax.axis_size("z")
    cores = lax.axis_size("core")
    members = groups * cores
    frames = latents.shape[1]
    length = frames * members
    rows = sheet.shape[0]
    blocks = owners.shape[0]
    head_count = D // HEAD // members
    span = D // members
    units = FF // members
    score_scale = HEAD ** (-0.5)
    tail_col = 6 * D + 3 * FF
    gain_col = tail_col + 2 * CTXW
    plane = lax.axis_index("z")

    group_ids = jnp.arange(blocks, dtype=jnp.int32)
    inverse = jnp.sum(
        jnp.where(owners[None, :] == group_ids[:, None], group_ids[None, :], 0), axis=1
    )
    slot = group_ids.reshape(groups, planes, cores).swapaxes(0, 1).reshape(-1)
    slot_of = jnp.sum(
        jnp.where(slot[None, :] == group_ids[:, None], group_ids[None, :], 0), axis=1
    )
    to_logical = jnp.take(slot_of, inverse)
    to_slots = jnp.take(owners, slot)

    low_sheet = sheet.astype(jnp.bfloat16)

    def columns_of(start, width):
        return split_columns(low_sheet[:, start : start + width], members)

    gains = lax.all_gather(low_sheet[:, gain_col:], ("z", "dp", "core"), axis=0, tiled=True)
    gains = jnp.take(gains.reshape(blocks, rows, 8), to_logical, axis=0).reshape(D, 8)
    gains = gains.astype(jnp.float32)
    weight_one = gather_columns(
        jnp.concatenate([columns_of(k * D, D) for k in range(4)], axis=2), to_logical
    )
    weight_two = gather_columns(
        jnp.concatenate(
            [
                columns_of(4 * D, D),
                columns_of(5 * D, D),
                columns_of(tail_col, CTXW),
                columns_of(tail_col + CTXW, CTXW),
            ],
            axis=2,
        ),
        to_logical,
    )
    weight_gu = gather_columns(
        jnp.concatenate([columns_of(6 * D, FF), columns_of(6 * D + FF, FF)], axis=2), to_logical
    )
    weight_down = gather_columns(columns_of(6 * D + 2 * FF, FF), to_logical)
    weight_qkv = weight_one[:, : 3 * span]
    weight_ao = weight_one[:, 3 * span :]
    weight_cq = weight_two[:, :span]
    weight_co = weight_two[:, span : 2 * span]
    weight_text = weight_two[:, 2 * span :]

    bucket_ids = jnp.arange(NB, dtype=jnp.int32)
    bucket_pick = (bucket_ids == buckets[plane]).astype(jnp.float32)
    counts = jnp.sum((buckets[:, None] == bucket_ids[None, :]).astype(jnp.float32), axis=0)
    row_weight = buckets.shape[0] / (NB * jnp.sum(bucket_pick * counts))
    gain_one = gains[:, 0:1]
    gain_two = gains[:, 1:2]
    gain_three = gains[:, 2:3]
    time_gain = jnp.sum(gains[:, 3:] * bucket_pick[None, :], axis=1, keepdims=True)

    both = row_to_plane(jnp.concatenate([latents[0], cotangent[0]], axis=1))
    tokens = both[:, :D].astype(jnp.float32).T
    grad_out = both[:, D:].astype(jnp.float32).T * row_weight

    rest = frames // planes
    place = jnp.arange(length, dtype=jnp.int32).reshape(planes, cores, groups, rest)
    positions = place.transpose(2, 1, 0, 3).reshape(-1)
    starts = lax.all_gather(clip_starts, "dp", axis=0, tiled=True)[plane]
    segments = segment_ids(starts, positions)
    same_clip = segments[:, None] == segments[None, :]
    frequency = jnp.exp(
        -math.log(10000.0) * jnp.arange(HEAD // 2, dtype=jnp.float32) / (HEAD // 2)
    )
    angles = frequency[:, None] * positions.astype(jnp.float32)[None, :]
    cosine = jnp.cos(angles)[None]
    sine_table = jnp.sin(angles)[None]

    grad_ff = plane_gather(grad_out.astype(jnp.bfloat16))
    normed_one, inverse_one = norm_columns(tokens)
    scaled_one = gain_one * time_gain
    h_one = plane_gather((normed_one * scaled_one).astype(jnp.bfloat16))

    joint = contract_rows(weight_qkv, h_one).reshape(3, head_count, HEAD, length)
    queries = rotate_columns(joint[0], cosine, sine_table).astype(jnp.bfloat16)
    keys = rotate_columns(joint[1], cosine, sine_table).astype(jnp.bfloat16)
    values = joint[2].astype(jnp.bfloat16)
    scores = (
        jnp.einsum("hdq,hdk->hqk", queries, keys, preferred_element_type=jnp.float32) * score_scale
    )
    attn_probs = softmax_rows(jnp.where(same_clip[None], scores, MASKED_SCORE))
    probs_low = attn_probs.astype(jnp.bfloat16)
    attn_out = jnp.einsum("hqk,hdk->hdq", probs_low, values, preferred_element_type=jnp.float32)
    attn_out = plane_gather_rows(attn_out.reshape(span, length).astype(jnp.bfloat16))
    x_one = tokens + to_frames(contract_rows(weight_ao, attn_out).astype(jnp.bfloat16)).astype(
        jnp.float32
    )

    text_part = lax.dynamic_index_in_dim(
        lax.all_gather(context, "dp", axis=0, tiled=True), plane, 0, keepdims=False
    )
    member = lax.axis_index("dp") * cores + lax.axis_index("core")
    text_width = CTXW // members
    text_mine = lax.dynamic_slice_in_dim(text_part, member * text_width, text_width, axis=1)
    text_kv = jnp.stack(
        [
            contract_last(weight_text[:, :text_width], text_mine),
            contract_last(weight_text[:, text_width:], text_mine),
        ],
        axis=1,
    ).reshape(D, 2 * CTX)
    text_kv = plane_scatter_rows(text_kv.astype(jnp.bfloat16)).reshape(head_count, HEAD, 2, CTX)
    text_keys = text_kv[:, :, 0]
    text_values = text_kv[:, :, 1]
    normed_two, inverse_two = norm_columns(x_one)
    h_two = plane_gather((normed_two * gain_two).astype(jnp.bfloat16))
    cross_q = contract_rows(weight_cq, h_two).astype(jnp.bfloat16).reshape(head_count, HEAD, length)
    cross_scores = (
        jnp.einsum("hdq,hdk->hqk", cross_q, text_keys, preferred_element_type=jnp.float32)
        * score_scale
    )
    cross_probs = softmax_rows(cross_scores)
    cross_low = cross_probs.astype(jnp.bfloat16)
    cross_out = jnp.einsum(
        "hqk,hdk->hdq", cross_low, text_values, preferred_element_type=jnp.float32
    )
    cross_out = plane_gather_rows(cross_out.reshape(span, length).astype(jnp.bfloat16))
    x_two = x_one + to_frames(contract_rows(weight_co, cross_out).astype(jnp.bfloat16)).astype(
        jnp.float32
    )

    normed_three, inverse_three = norm_columns(x_two)
    h_three = plane_gather((normed_three * gain_three).astype(jnp.bfloat16))
    gate_up = contract_rows(weight_gu, h_three)
    gate_pre = gate_up[:units]
    up_part = gate_up[units:]
    sigmoid_gate = jax.nn.sigmoid(gate_pre)
    silu_gate = gate_pre * sigmoid_gate
    hidden = (silu_gate * up_part).astype(jnp.bfloat16)
    ff_out = plane_scatter_frames(matmul(weight_down, hidden).astype(jnp.bfloat16))
    result = x_two + ff_out.astype(jnp.float32)
    output = plane_to_row(result.astype(jnp.bfloat16).T)

    grad_hidden = contract_rows(weight_down, grad_ff)
    grad_gate = grad_hidden * up_part * (sigmoid_gate * (1.0 + gate_pre * (1.0 - sigmoid_gate)))
    grad_up = grad_hidden * silu_gate
    grad_gu = jnp.concatenate([grad_gate, grad_up], axis=0).astype(jnp.bfloat16)
    grad_weight_gu = contract_last(h_three, grad_gu)
    grad_weight_down = contract_last(grad_ff, hidden)
    sums_gu = scatter_columns(grad_weight_gu, to_slots, planes)
    sums_down = scatter_columns(grad_weight_down, to_slots, planes)
    grad_h_three = plane_scatter_frames(matmul(weight_gu, grad_gu).astype(jnp.bfloat16)).astype(
        jnp.float32
    )
    grad_gain_three = jnp.sum(grad_h_three * normed_three, axis=1)
    grad_x_two = grad_out + norm_columns_back(
        grad_h_three * gain_three, normed_three, inverse_three
    )
    grad_cross = to_rows(grad_x_two.astype(jnp.bfloat16))
    grad_weight_co = contract_last(cross_out, grad_cross)
    grad_cross_out = plane_scatter_rows(
        matmul(weight_co, grad_cross).astype(jnp.bfloat16)
    ).reshape(head_count, HEAD, length)
    grad_cross_probs = jnp.einsum(
        "hdq,hdk->hqk", grad_cross_out, text_values, preferred_element_type=jnp.float32
    )
    grad_cross_scores = (
        cross_probs
        * (grad_cross_probs - jnp.sum(cross_probs * grad_cross_probs, axis=-1, keepdims=True))
    ).astype(jnp.bfloat16)
    grad_cross_q = (
        jnp.einsum("hqk,hdk->hdq", grad_cross_scores, text_keys, preferred_element_type=jnp.float32)
        * score_scale
    )
    grad_cross_q = grad_cross_q.reshape(span, length).astype(jnp.bfloat16)
    grad_text_keys = (
        jnp.einsum("hqk,hdq->hdk", grad_cross_scores, cross_q, preferred_element_type=jnp.float32)
        * score_scale
    )
    grad_text_values = jnp.einsum(
        "hqk,hdq->hdk", cross_low, grad_cross_out, preferred_element_type=jnp.float32
    )
    grad_text = jnp.concatenate(
        [grad_text_keys.reshape(span, CTX), grad_text_values.reshape(span, CTX)], axis=1
    )
    grad_text = plane_gather_rows(grad_text.astype(jnp.bfloat16))
    grad_weight_cq = contract_last(h_two, grad_cross_q)
    grad_weight_text = [
        matmul(grad_text[:, :CTX], text_mine),
        matmul(grad_text[:, CTX:], text_mine),
    ]
    sums_two = scatter_columns(
        jnp.concatenate([grad_weight_cq, grad_weight_co] + grad_weight_text, axis=1),
        to_slots,
        planes,
    )
    grad_h_two = plane_scatter_frames(
        matmul(weight_cq, grad_cross_q).astype(jnp.bfloat16)
    ).astype(jnp.float32)
    grad_gain_two = jnp.sum(grad_h_two * normed_two, axis=1)
    grad_x_one = grad_x_two + norm_columns_back(grad_h_two * gain_two, normed_two, inverse_two)
    grad_attn = to_rows(grad_x_one.astype(jnp.bfloat16))
    grad_weight_ao = contract_last(attn_out, grad_attn)
    grad_attn_out = plane_scatter_rows(matmul(weight_ao, grad_attn).astype(jnp.bfloat16)).reshape(
        head_count, HEAD, length
    )
    grad_probs = jnp.einsum(
        "hdq,hdk->hqk", grad_attn_out, values, preferred_element_type=jnp.float32
    )
    grad_scores = (
        attn_probs * (grad_probs - jnp.sum(attn_probs * grad_probs, axis=-1, keepdims=True))
    ).astype(jnp.bfloat16)
    grad_queries = (
        jnp.einsum("hqk,hdk->hdq", grad_scores, keys, preferred_element_type=jnp.float32)
        * score_scale
    )
    grad_keys = (
        jnp.einsum("hqk,hdq->hdk", grad_scores, queries, preferred_element_type=jnp.float32)
        * score_scale
    )
    grad_values = jnp.einsum(
        "hqk,hdq->hdk", probs_low, grad_attn_out, preferred_element_type=jnp.float32
    )
    grad_qkv = jnp.stack(
        [
            rotate_columns(grad_queries, cosine, -sine_table),
            rotate_columns(grad_keys, cosine, -sine_table),
            grad_values,
        ]
    )
    grad_qkv = grad_qkv.reshape(3 * span, length).astype(jnp.bfloat16)
    grad_weight_qkv = contract_last(h_one, grad_qkv)
    sums_one = scatter_columns(
        jnp.concatenate([grad_weight_qkv, grad_weight_ao], axis=1), to_slots, planes
    )
    grad_h_one = plane_scatter_frames(matmul(weight_qkv, grad_qkv).astype(jnp.bfloat16)).astype(
        jnp.float32
    )
    grad_gain_one = jnp.sum(grad_h_one * normed_one * time_gain, axis=1)
    grad_time = jnp.sum(grad_h_one * normed_one * gain_one, axis=1)
    latent_grad = grad_x_one + norm_columns_back(grad_h_one * scaled_one, normed_one, inverse_one)
    latent_grad = plane_to_row(latent_grad.astype(jnp.bfloat16).T).astype(jnp.float32)
    gain_grads = jnp.concatenate(
        [
            jnp.stack([grad_gain_one, grad_gain_two, grad_gain_three], axis=1),
            grad_time[:, None] * bucket_pick[None, :],
        ],
        axis=1,
    )
    gain_grads = jnp.take(gain_grads.reshape(blocks, rows, 8), to_slots, axis=0)
    gain_sums = lax.psum_scatter(
        gain_grads.reshape(D, 8), ("z", "dp", "core"), scatter_dimension=0, tiled=True
    )

    def joined(part):
        return part.reshape(rows, -1)

    grad_sheet = jnp.concatenate(
        [joined(sums_one[:, :, k * span : (k + 1) * span]) for k in range(4)]
        + [joined(sums_two[:, :, :span]), joined(sums_two[:, :, span : 2 * span])]
        + [joined(sums_gu[:, :, :units]), joined(sums_gu[:, :, units:]), joined(sums_down)]
        + [
            joined(sums_two[:, :, 2 * span : 2 * span + text_width]),
            joined(sums_two[:, :, 2 * span + text_width :]),
        ],
        axis=1,
    ).astype(jnp.float32)
    grad_sheet = jnp.concatenate([grad_sheet, gain_sums], axis=1)
    total_squares = lax.psum(jnp.sum(grad_sheet * grad_sheet), ("dp", "z", "core"))
    return (output[None], latent_grad[None]) + update(
        grad_sheet, total_squares, sheet, first, second, length
    )


def update(grad_sheet, total_squares, sheet, first, second, length):
    grad_norm = jnp.sqrt(total_squares)
    clipped = grad_sheet / jnp.maximum(grad_norm, 1.0)
    gain_grad = clipped[:, 6 * D + 3 * FF + 2 * CTXW :]
    first_new = BETA_ONE * first + (1.0 - BETA_ONE) * clipped
    second_new = BETA_TWO * second + (1.0 - BETA_TWO) * clipped * clipped
    mean_hat = first_new / (1.0 - BETA_ONE**STEP)
    square_hat = second_new / (1.0 - BETA_TWO**STEP)
    rates = column_spread(length)[None, :]
    sheet_new = sheet - rates * (
        mean_hat / (jnp.sqrt(square_hat) + EPS_ADAM) + WEIGHT_DECAY * sheet
    )
    return (
        grad_norm,
        clipped,
        gain_grad,
        first_new,
        second_new,
        sheet_new,
        sheet_new.astype(jnp.bfloat16),
    )


def solution(mesh):
    groups, seq_count = mesh.shape["dp"], mesh.shape["seq"]
    by_plane = seq_count == 2 * groups and (D // HEAD) % seq_count == 0
    if by_plane:
        mesh = Mesh(mesh.devices.reshape(groups, seq_count // 2, 2), ("dp", "z", "core"))
    seq = ("z", "core") if by_plane else "seq"
    both = ("dp", "z", "core") if by_plane else ("dp", "seq")
    in_specs = (
        P("dp", seq, None),
        P("dp", None, None),
        P("dp", None),
        P(),
        P(),
        P("dp", seq, None),
        P(both, None),
        P(both, None),
        P(both, None),
    )
    out_specs = (
        P("dp", seq, None),
        P("dp", seq, None),
        P(),
        P(both, None),
        P(both, None),
        P(both, None),
        P(both, None),
        P(both, None),
        P(both, None),
    )
    return jax.shard_map(
        plane_plan if by_plane else gather_plan,
        mesh=mesh,
        in_specs=in_specs,
        out_specs=out_specs,
        check_vma=False,
    )
```

```python
import functools
import math

import jax
import jax.numpy as jnp
from jax import lax
from jax.experimental import pallas as pl
from jax.experimental.pallas import tpu as pltpu
from jax.sharding import Mesh
from jax.sharding import PartitionSpec as P

D = 1536
FF = 6144
HEAD = 64
CTXW = 768
CTX = 128
NB = 5
STEP = 10
SHEET = 29192


HIGHEST = lax.Precision.HIGHEST
EPS_NORM = 1e-05
EPS_ADAM = 1e-08
MASKED_SCORE = -1e30
BETA_ONE = 0.5
BETA_TWO = 0.5
WEIGHT_DECAY = 0.01


def reorder(values, ordering):
    leading = values.shape[:-1]
    groups = ordering.shape[0]
    blocks = values.reshape(leading + (groups, values.shape[-1] // groups))
    return jnp.take(blocks, ordering, axis=-2).reshape(values.shape)


def norm_parts(values):
    average = jnp.mean(values, axis=-1, keepdims=True)
    centered = values - average
    variance = jnp.mean(centered * centered, axis=-1, keepdims=True)
    inverse_std = lax.rsqrt(variance + EPS_NORM)
    return (centered * inverse_std, inverse_std)


def norm_back(grad_normed, normed, inverse_std):
    return inverse_std * (
        grad_normed
        - jnp.mean(grad_normed, axis=-1, keepdims=True)
        - normed * jnp.mean(grad_normed * normed, axis=-1, keepdims=True)
    )


def softmax_rows(scores):
    row_max = jnp.max(scores, axis=-1, keepdims=True)
    exponent = jnp.exp(scores - row_max)
    return exponent / jnp.sum(exponent, axis=-1, keepdims=True)


def rope_tables(positions, head_dim):
    half_dim = head_dim // 2
    frequency = jnp.exp(-math.log(10000.0) * jnp.arange(half_dim, dtype=jnp.float32) / half_dim)
    angles = positions.astype(jnp.float32)[:, None] * frequency[None, :]
    return (jnp.cos(angles)[:, None, :], jnp.sin(angles)[:, None, :])


def rotate(values, cosine, sine_table):
    half_dim = values.shape[-1] // 2
    first_half = values[..., :half_dim]
    second_half = values[..., half_dim:]
    return jnp.concatenate(
        [
            first_half * cosine - second_half * sine_table,
            second_half * cosine + first_half * sine_table,
        ],
        axis=-1,
    )


def unrotate(grads, cosine, sine_table):
    half_dim = grads.shape[-1] // 2
    first_half = grads[..., :half_dim]
    second_half = grads[..., half_dim:]
    return jnp.concatenate(
        [
            first_half * cosine + second_half * sine_table,
            second_half * cosine - first_half * sine_table,
        ],
        axis=-1,
    )


def segment_ids(starts, positions):
    return jnp.sum((starts[None, :] <= positions[:, None]).astype(jnp.int32), axis=1) - 1


def column_spread(length):
    column = jnp.arange(SHEET, dtype=jnp.int32)
    base_std = D ** (-0.5)
    spread = jnp.full((SHEET,), base_std, jnp.float32)
    spread = jnp.where(
        (column >= 3 * D) & (column < 4 * D), base_std * math.sqrt(length) / 4.0, spread
    )
    spread = jnp.where((column >= 5 * D) & (column < 6 * D), base_std * math.sqrt(CTX), spread)
    spread = jnp.where((column >= 6 * D + 2 * FF) & (column < 6 * D + 3 * FF), FF ** (-0.5), spread)
    spread = jnp.where(
        (column >= 6 * D + 3 * FF) & (column < 6 * D + 3 * FF + 2 * CTXW), CTXW ** (-0.5), spread
    )
    spread = jnp.where(column >= 6 * D + 3 * FF + 2 * CTXW, 0.3, spread)
    return spread


def inner_rows(left, right):
    return lax.dot_general(
        left, right, (((0,), (0,)), ((), ())), preferred_element_type=jnp.float32
    )


def inner_rows_high(left, right):
    return lax.dot_general(
        left, right, (((0,), (0,)), ((), ())), precision=HIGHEST, preferred_element_type=jnp.float32
    )


def gather_plan(latents, context, clip_starts, buckets, owners, cotangent, sheet, first, second):
    frames = latents.shape[1]
    seq_count = lax.axis_size("seq")
    length = frames * seq_count
    head_count = D // HEAD
    score_scale = HEAD ** (-0.5)
    group_ids = jnp.arange(owners.shape[0], dtype=jnp.int32)
    inverse = jnp.sum(
        jnp.where(owners[None, :] == group_ids[:, None], group_ids[None, :], 0), axis=1
    )
    gathered = lax.all_gather(sheet.astype(jnp.bfloat16), ("dp", "seq"), axis=0, tiled=True)
    tail_col = 6 * D + 3 * FF
    gain_col = tail_col + 2 * CTXW
    gain_rows = reorder(gathered[:, gain_col:].astype(jnp.float32).T, inverse)
    row_index = lax.axis_index("dp")
    bucket_ids = jnp.arange(NB, dtype=jnp.int32)
    bucket_pick = (bucket_ids == buckets[row_index]).astype(jnp.float32)
    counts = jnp.sum((buckets[:, None] == bucket_ids[None, :]).astype(jnp.float32), axis=0)
    row_weight = buckets.shape[0] / (NB * jnp.sum(bucket_pick * counts))
    gain_one = gain_rows[0]
    gain_two = gain_rows[1]
    gain_three = gain_rows[2]
    time_gain = jnp.sum(gain_rows[3:] * bucket_pick[:, None], axis=0)
    tokens = latents[0].astype(jnp.float32)
    positions = lax.axis_index("seq") * frames + jnp.arange(frames, dtype=jnp.int32)
    all_positions = jnp.arange(length, dtype=jnp.int32)
    starts = clip_starts[0]
    same_clip = (
        segment_ids(starts, positions)[:, None] == segment_ids(starts, all_positions)[None, :]
    )[None]
    cosine, sine_table = rope_tables(positions, HEAD)
    normed_one, inverse_one = norm_parts(tokens)
    scaled_one = gain_one * time_gain
    h_one_st = reorder((normed_one * scaled_one).astype(jnp.bfloat16), owners)
    joint_qkv = jnp.dot(h_one_st, gathered[:, : 3 * D], preferred_element_type=jnp.float32)
    queries = rotate(joint_qkv[:, :D].reshape(frames, head_count, HEAD), cosine, sine_table).astype(
        jnp.bfloat16
    )
    key_local = rotate(
        joint_qkv[:, D : 2 * D].reshape(frames, head_count, HEAD), cosine, sine_table
    ).astype(jnp.bfloat16)
    value_local = joint_qkv[:, 2 * D :].reshape(frames, head_count, HEAD).astype(jnp.bfloat16)
    key_all, value_all = (
        lax.all_gather(key_local, "seq", axis=0, tiled=True),
        lax.all_gather(value_local, "seq", axis=0, tiled=True),
    )
    scores = (
        jnp.einsum("qhd,khd->hqk", queries, key_all, preferred_element_type=jnp.float32)
        * score_scale
    )
    attn_probs = softmax_rows(jnp.where(same_clip, scores, MASKED_SCORE))
    probs_low = attn_probs.astype(jnp.bfloat16)
    attn_out = (
        jnp.einsum("hqk,khd->qhd", probs_low, value_all, preferred_element_type=jnp.float32)
        .reshape(frames, D)
        .astype(jnp.bfloat16)
    )
    attn_st = reorder(attn_out, owners)
    x_one = tokens + jnp.dot(
        attn_st, gathered[:, 3 * D : 4 * D], preferred_element_type=jnp.float32
    )
    normed_two, inverse_two = norm_parts(x_one)
    h_two_st = reorder((normed_two * gain_two).astype(jnp.bfloat16), owners)
    cross_q = (
        jnp.dot(h_two_st, gathered[:, 4 * D : 5 * D], preferred_element_type=jnp.float32)
        .astype(jnp.bfloat16)
        .reshape(frames, head_count, HEAD)
    )
    text_tokens = context[0]
    text_kv = jnp.einsum(
        "tc,dec->etd",
        text_tokens,
        gathered[:, tail_col:gain_col].reshape(D, 2, CTXW),
        preferred_element_type=jnp.float32,
    )
    text_kv = reorder(text_kv, inverse).astype(jnp.bfloat16).reshape(2, CTX, head_count, HEAD)
    text_keys = text_kv[0]
    text_values = text_kv[1]
    cross_scores = (
        jnp.einsum("qhd,khd->hqk", cross_q, text_keys, preferred_element_type=jnp.float32)
        * score_scale
    )
    cross_probs = softmax_rows(cross_scores)
    cross_low = cross_probs.astype(jnp.bfloat16)
    cross_out = (
        jnp.einsum("hqk,khd->qhd", cross_low, text_values, preferred_element_type=jnp.float32)
        .reshape(frames, D)
        .astype(jnp.bfloat16)
    )
    cross_st = reorder(cross_out, owners)
    x_two = x_one + jnp.dot(
        cross_st, gathered[:, 5 * D : 6 * D], preferred_element_type=jnp.float32
    )
    normed_three, inverse_three = norm_parts(x_two)
    h_three_st = reorder((normed_three * gain_three).astype(jnp.bfloat16), owners)
    grad_out = cotangent[0].astype(jnp.float32) * row_weight
    grad_ff_st = reorder(grad_out.astype(jnp.bfloat16), owners)
    gate_weight = gathered[:, 6 * D : 6 * D + 2 * FF]
    down_weight = gathered[:, 6 * D + 2 * FF : 6 * D + 3 * FF]
    units = down_weight.shape[1]
    gate_up = jnp.dot(h_three_st, gate_weight, preferred_element_type=jnp.float32)
    gate_pre = gate_up[:, :units]
    up_part = gate_up[:, units:]
    sigmoid_gate = jax.nn.sigmoid(gate_pre)
    silu_gate = gate_pre * sigmoid_gate
    hidden = (silu_gate * up_part).astype(jnp.bfloat16)
    ff_out = reorder(
        jnp.einsum("nf,df->nd", hidden, down_weight, preferred_element_type=jnp.float32), inverse
    )
    result = x_two + ff_out
    grad_hidden = jnp.dot(grad_ff_st, down_weight, preferred_element_type=jnp.float32)
    grad_gate = grad_hidden * up_part * (sigmoid_gate * (1.0 + gate_pre * (1.0 - sigmoid_gate)))
    grad_up = grad_hidden * silu_gate
    grad_gu = jnp.concatenate([grad_gate, grad_up], axis=1).astype(jnp.bfloat16)
    grad_h_three = reorder(
        jnp.einsum("nf,df->nd", grad_gu, gate_weight, preferred_element_type=jnp.float32), inverse
    )
    grad_gain_three = jnp.sum(grad_h_three * normed_three, axis=0)
    grad_x_two = grad_out + norm_back(grad_h_three * gain_three, normed_three, inverse_three)
    grad_cross = grad_x_two.astype(jnp.bfloat16)
    grad_cross_out = (
        reorder(
            jnp.einsum(
                "nd,ed->ne",
                grad_cross,
                gathered[:, 5 * D : 6 * D],
                preferred_element_type=jnp.float32,
            ),
            inverse,
        )
        .astype(jnp.bfloat16)
        .reshape(frames, head_count, HEAD)
    )
    grad_cross_probs = jnp.einsum(
        "qhd,khd->hqk", grad_cross_out, text_values, preferred_element_type=jnp.float32
    )
    grad_cross_scores = (
        cross_probs
        * (grad_cross_probs - jnp.sum(cross_probs * grad_cross_probs, axis=-1, keepdims=True))
    ).astype(jnp.bfloat16)
    grad_cross_q = (
        (
            jnp.einsum(
                "hqk,khd->qhd", grad_cross_scores, text_keys, preferred_element_type=jnp.float32
            )
            * score_scale
        )
        .reshape(frames, D)
        .astype(jnp.bfloat16)
    )
    grad_text_keys = (
        jnp.einsum("hqk,qhd->khd", grad_cross_scores, cross_q, preferred_element_type=jnp.float32)
        * score_scale
    )
    grad_text_values = jnp.einsum(
        "hqk,qhd->khd", cross_low, grad_cross_out, preferred_element_type=jnp.float32
    )
    grad_text = reorder(
        jnp.stack([grad_text_keys.reshape(CTX, D), grad_text_values.reshape(CTX, D)]), owners
    )
    grad_h_two = reorder(
        jnp.einsum(
            "ne,de->nd",
            grad_cross_q,
            gathered[:, 4 * D : 5 * D],
            preferred_element_type=jnp.float32,
        ),
        inverse,
    )
    grad_gain_two = jnp.sum(grad_h_two * normed_two, axis=0)
    grad_x_one = grad_x_two + norm_back(grad_h_two * gain_two, normed_two, inverse_two)
    grad_attn = grad_x_one.astype(jnp.bfloat16)
    grad_attn_out = (
        reorder(
            jnp.einsum(
                "nd,ed->ne",
                grad_attn,
                gathered[:, 3 * D : 4 * D],
                preferred_element_type=jnp.float32,
            ),
            inverse,
        )
        .astype(jnp.bfloat16)
        .reshape(frames, head_count, HEAD)
    )
    key_back, value_back = (key_all, value_all)

    def head_grads(head_items):
        head_probs, head_grad_out, head_values = head_items
        grad_probs = jnp.einsum(
            "qd,kd->qk", head_grad_out, head_values, preferred_element_type=jnp.float32
        )
        return (
            head_probs * (grad_probs - jnp.sum(head_probs * grad_probs, axis=-1, keepdims=True))
        ).astype(jnp.bfloat16)

    grad_scores_low = lax.map(
        head_grads, (attn_probs, jnp.swapaxes(grad_attn_out, 0, 1), jnp.swapaxes(value_back, 0, 1))
    )
    grad_queries = (
        jnp.einsum("hqk,khd->qhd", grad_scores_low, key_back, preferred_element_type=jnp.float32)
        * score_scale
    )
    grad_keys = (
        jnp.einsum("hqk,qhd->khd", grad_scores_low, queries, preferred_element_type=jnp.float32)
        * score_scale
    )
    grad_values = jnp.einsum(
        "hqk,qhd->khd", probs_low, grad_attn_out, preferred_element_type=jnp.float32
    )
    key_sums = lax.psum_scatter(
        jnp.concatenate(
            [
                grad_keys.reshape(frames * lax.axis_size("seq"), D),
                grad_values.reshape(frames * lax.axis_size("seq"), D),
            ],
            axis=1,
        ).astype(jnp.bfloat16),
        "seq",
        scatter_dimension=0,
        tiled=True,
    ).astype(jnp.float32)
    grad_q_raw = unrotate(grad_queries, cosine, sine_table).reshape(frames, D)
    grad_k_raw = unrotate(
        key_sums[:, :D].reshape(frames, head_count, HEAD), cosine, sine_table
    ).reshape(frames, D)
    grad_qkv = jnp.concatenate([grad_q_raw, grad_k_raw, key_sums[:, D:]], axis=1).astype(
        jnp.bfloat16
    )
    grad_h_one = reorder(
        jnp.einsum("ne,de->nd", grad_qkv, gathered[:, : 3 * D], preferred_element_type=jnp.float32),
        inverse,
    )
    grad_gain_one = jnp.sum(grad_h_one * normed_one * time_gain, axis=0)
    grad_time = jnp.sum(grad_h_one * normed_one * gain_one, axis=0)
    latent_grad = grad_x_one + norm_back(grad_h_one * scaled_one, normed_one, inverse_one)
    gain_grads = jnp.concatenate(
        [
            jnp.stack([grad_gain_one, grad_gain_two, grad_gain_three]),
            bucket_pick[:, None] * grad_time[None, :],
        ],
        axis=0,
    )
    gain_grads = reorder(gain_grads, owners).T
    text_float = text_tokens.astype(jnp.float32)
    pieces = [
        inner_rows(h_one_st, grad_qkv),
        inner_rows(attn_st, grad_attn),
        inner_rows(h_two_st, grad_cross_q),
        inner_rows(cross_st, grad_cross),
    ]
    pieces = pieces + [inner_rows(h_three_st, grad_gu), inner_rows(grad_ff_st, hidden)]
    pieces = pieces + [
        inner_rows_high(grad_text[0], text_float),
        inner_rows_high(grad_text[1], text_float),
        gain_grads,
    ]
    other_shard = lax.psum_scatter(
        jnp.concatenate(pieces, axis=1), ("dp", "seq"), scatter_dimension=0, tiled=True
    )
    total_squares = lax.psum(jnp.sum(other_shard * other_shard), ("dp", "seq"))
    grad_norm = jnp.sqrt(total_squares)
    clipped = other_shard / jnp.maximum(grad_norm, 1.0)
    gain_grad = clipped[:, 6 * D + 3 * FF + 2 * CTXW :]
    first_new = BETA_ONE * first + (1.0 - BETA_ONE) * clipped
    second_new = BETA_TWO * second + (1.0 - BETA_TWO) * clipped * clipped
    mean_hat = first_new / (1.0 - BETA_ONE**STEP)
    square_hat = second_new / (1.0 - BETA_TWO**STEP)
    rates = column_spread(length)[None, :]
    sheet_new = sheet - rates * (
        mean_hat / (jnp.sqrt(square_hat) + EPS_ADAM) + WEIGHT_DECAY * sheet
    )
    return (
        result.astype(jnp.bfloat16)[None],
        latent_grad[None],
        grad_norm,
        clipped,
        gain_grad,
        first_new,
        second_new,
        sheet_new,
        sheet_new.astype(jnp.bfloat16),
    )


PLANE = ("dp", "core")


def norm_columns(values):
    average = jnp.mean(values, axis=0, keepdims=True)
    centered = values - average
    variance = jnp.mean(centered * centered, axis=0, keepdims=True)
    inverse_std = lax.rsqrt(variance + EPS_NORM)
    return (centered * inverse_std, inverse_std)


def norm_columns_back(grad_normed, normed, inverse_std):
    return inverse_std * (
        grad_normed
        - jnp.mean(grad_normed, axis=0, keepdims=True)
        - normed * jnp.mean(grad_normed * normed, axis=0, keepdims=True)
    )


def rotate_columns(values, cosine, sine_table):
    half_dim = HEAD // 2
    first_half = values[:, :half_dim]
    second_half = values[:, half_dim:]
    return jnp.concatenate(
        [
            first_half * cosine - second_half * sine_table,
            second_half * cosine + first_half * sine_table,
        ],
        axis=1,
    )


def contract_rows(left, right):
    return lax.dot_general(
        left, right, (((0,), (0,)), ((), ())), preferred_element_type=jnp.float32
    )


def contract_last(left, right):
    return lax.dot_general(
        left, right, (((1,), (1,)), ((), ())), preferred_element_type=jnp.float32
    )


def matmul(left, right):
    return jnp.dot(left, right, preferred_element_type=jnp.float32)


MESH_ID = pl.DeviceIdType.MESH
IDENTITIES = {}


def identity_of(name, *arrays):
    key = (name,) + tuple((array.shape, str(array.dtype)) for array in arrays)
    return IDENTITIES.setdefault(key, len(IDENTITIES))


IN_HBM = pl.BlockSpec(memory_space=pl.ANY)
IN_VMEM = pl.BlockSpec(memory_space=pltpu.VMEM)
BRIEF = pl.CostEstimate(flops=0, bytes_accessed=1024, transcendentals=0)


def greet(peers):
    barrier = pltpu.get_barrier_semaphore()
    for peer in peers:
        pl.semaphore_signal(barrier, inc=1, device_id=peer, device_id_type=MESH_ID)
    pl.semaphore_wait(barrier, len(peers))


def near():
    group, core = lax.axis_index("dp"), lax.axis_index("core")
    across = group + 1 - 2 * lax.rem(group, 2)
    along = lax.rem(group + 2, 4)
    return group, core, across, along


def member_rows(width):
    def place(ref, member, start, count):
        first_row = pl.multiple_of(member * width + start, 16)
        return ref.at[pl.ds(first_row, count), :]

    return place


def member_lanes(width):
    def place(ref, member, start, count):
        return ref.at[pl.ds(start, count), pl.ds(pl.multiple_of(member * width, 128), width)]

    return place


def mover(send_sem, recv_sem, first=0):
    def copy(k, source, target, peer):
        return pltpu.make_async_remote_copy(
            src_ref=source,
            dst_ref=target,
            send_sem=send_sem.at[first + k],
            recv_sem=recv_sem.at[first + k],
            device_id=peer,
            device_id_type=MESH_ID,
        )

    return copy


def member_at(member):
    return {"dp": lax.div(member, 2), "core": lax.rem(member, 2)}


def plane_peers():
    group, core, _, _ = near()
    member = group * 2 + core
    return [lax.rem(member + step, 8) for step in range(1, 8)]


def gather_steps(place, x_ref, o_ref, local_sem, copy):
    group, core, across, along = near()
    beyond = across + along - group
    other = 1 - core
    sibling, by_x, by_y = {"core": other}, {"dp": across}, {"dp": along}
    half = x_ref.shape[0] // 2

    def part(owner, owner_core, piece):
        return place(o_ref, owner * 2 + owner_core, piece * half, half)

    sent = []

    def send(k, source, target, peer):
        moving = copy(k, source, target, peer)
        moving.start()
        sent.append(moving)

    def own(k, piece, peer):
        send(k, x_ref.at[pl.ds(piece * half, half), :], part(group, core, piece), peer)

    def relay(k, owner, piece, peer):
        send(k, part(owner, core, piece), part(owner, core, piece), peer)

    def arrived(k, owner, owner_core, piece):
        landed = part(owner, owner_core, piece)
        copy(k, landed, landed, sibling).wait_recv()

    local = pltpu.make_async_copy(
        x_ref, place(o_ref, group * 2 + core, 0, 2 * half), local_sem
    )
    local.start()
    own(0, 0, by_x)
    own(1, 1, by_y)
    own(2, 1, by_x)
    own(3, 0, by_y)
    own(4, 0, sibling)
    own(5, 1, sibling)

    def finish():
        arrived(0, across, core, 0)
        relay(6, across, 0, by_y)
        relay(7, across, 0, sibling)
        arrived(1, along, core, 1)
        relay(8, along, 1, by_x)
        relay(9, along, 1, sibling)
        arrived(2, across, core, 1)
        relay(10, across, 1, sibling)
        arrived(3, along, core, 0)
        relay(11, along, 0, sibling)
        arrived(6, beyond, core, 0)
        relay(12, beyond, 0, sibling)
        arrived(8, beyond, core, 1)
        relay(13, beyond, 1, sibling)
        arrived(4, group, other, 0)
        arrived(5, group, other, 1)
        arrived(7, across, other, 0)
        arrived(9, along, other, 1)
        arrived(10, across, other, 1)
        arrived(11, along, other, 0)
        arrived(12, beyond, other, 0)
        arrived(13, beyond, other, 1)
        local.wait()
        for moving in sent:
            moving.wait_send()

    return finish


def exchange_steps(source, target, x_ref, o_ref, local_sem, copy):
    group, core, _, _ = near()
    member = group * 2 + core
    local = pltpu.make_async_copy(source(x_ref, member), target(o_ref, member), local_sem)
    local.start()
    sent = []
    for k, peer in enumerate(plane_peers()):
        sent.append(copy(k, source(x_ref, peer), target(o_ref, member), member_at(peer)))
        sent[-1].start()

    def finish():
        for k in range(7):
            sender = lax.rem(member + 7 - k, 8)
            landed = target(o_ref, sender)
            copy(k, landed, landed, member_at(sender)).wait_recv()
        local.wait()
        for moving in sent:
            moving.wait_send()

    return finish


def gather_kernel(place, x_ref, *refs):
    o_ref, local_sem, send_sem, recv_sem = refs[-4:]
    _, core, across, along = near()
    greet([{"dp": across}, {"dp": along}, {"core": 1 - core}])
    gather_steps(place, x_ref, o_ref, local_sem, mover(send_sem, recv_sem))()


def plane_gather_call(shard, shape, place, kind, after):
    return pl.pallas_call(
        functools.partial(gather_kernel, place),
        out_shape=jax.ShapeDtypeStruct(shape, shard.dtype),
        in_specs=[IN_HBM] * (1 + len(after)),
        out_specs=IN_HBM,
        scratch_shapes=[
            pltpu.SemaphoreType.DMA,
            pltpu.SemaphoreType.DMA((14,)),
            pltpu.SemaphoreType.DMA((14,)),
        ],
        compiler_params=pltpu.CompilerParams(
            collective_id=identity_of(kind, shard, *after), has_side_effects=True
        ),
        cost_estimate=BRIEF,
        name="plane_gather",
    )(shard, *after)


def plane_gather(shard, after=()):
    rows, width = shard.shape
    return plane_gather_call(shard, (rows, 8 * width), member_lanes(width), "gather lanes", after)


def plane_gather_rows(shard, after=()):
    rows, width = shard.shape
    return plane_gather_call(shard, (8 * rows, width), member_rows(rows), "gather rows", after)


def scatter_kernel(place, p_ref, *refs):
    o_ref, pair, total, from_x, from_y, relay, send_sem, recv_sem = refs[-8:]
    group, core, across, along = near()
    beyond = across + along - group
    other = 1 - core
    sibling, by_x, by_y = {"core": other}, {"dp": across}, {"dp": along}
    rows = o_ref.shape[0]
    half = rows // 2
    low, high = pl.ds(0, half), pl.ds(half, half)

    copy = mover(send_sem, recv_sem)
    sent = []

    def send(k, source, target, peer):
        moving = copy(k, source, target, peer)
        moving.start()
        sent.append(moving)

    def arrived(k, target):
        copy(k, target, target, sibling).wait_recv()

    def wide(ref):
        return ref[...].astype(jnp.float32)

    def both_cores(k, owner):
        arrived(k, pair.at[k])
        summed = wide(place(p_ref, owner * 2 + core, 0, rows)) + wide(pair.at[k])
        total[k] = summed.astype(total.dtype)

    greet([by_x, by_y, sibling])
    for k, owner in enumerate((beyond, across, along, group)):
        send(k, place(p_ref, owner * 2 + other, 0, rows), pair.at[k], sibling)
    both_cores(0, beyond)
    send(4, total.at[0, low], relay.at[0], by_x)
    send(5, total.at[0, high], relay.at[1], by_y)
    both_cores(1, across)
    send(6, total.at[1, low], from_x.at[low], by_x)
    both_cores(2, along)
    send(7, total.at[2, high], from_y.at[high], by_y)
    both_cores(3, group)
    arrived(5, relay.at[1])
    total[1, high] = (wide(total.at[1, high]) + wide(relay.at[1])).astype(total.dtype)
    send(8, total.at[1, high], from_x.at[high], by_x)
    arrived(4, relay.at[0])
    total[2, low] = (wide(total.at[2, low]) + wide(relay.at[0])).astype(total.dtype)
    send(9, total.at[2, low], from_y.at[low], by_y)
    arrived(6, from_x.at[low])
    arrived(7, from_y.at[high])
    arrived(8, from_x.at[high])
    arrived(9, from_y.at[low])
    o_ref[...] = (wide(total.at[3]) + wide(from_x) + wide(from_y)).astype(o_ref.dtype)
    for moving in sent:
        moving.wait_send()


def plane_scatter_call(partial, shape, place, dtype, kind, after):
    rows, width = shape
    slot = pltpu.VMEM((rows, width), jnp.bfloat16)
    return pl.pallas_call(
        functools.partial(scatter_kernel, place),
        out_shape=jax.ShapeDtypeStruct(shape, dtype),
        in_specs=[IN_VMEM] + [IN_HBM] * len(after),
        out_specs=IN_VMEM,
        scratch_shapes=[
            pltpu.VMEM((4, rows, width), jnp.bfloat16),
            pltpu.VMEM((4, rows, width), jnp.bfloat16),
            slot,
            slot,
            pltpu.VMEM((2, rows // 2, width), jnp.bfloat16),
            pltpu.SemaphoreType.DMA((10,)),
            pltpu.SemaphoreType.DMA((10,)),
        ],
        compiler_params=pltpu.CompilerParams(
            collective_id=identity_of(kind, partial, *after),
            has_side_effects=True,
            vmem_limit_bytes=24 * 2**20,
        ),
        cost_estimate=BRIEF,
        name="plane_scatter",
    )(partial, *after)


def plane_scatter_frames(partial, after=()):
    rows, width = partial.shape[0], partial.shape[1] // 8
    place = member_lanes(width)
    return plane_scatter_call(partial, (rows, width), place, jnp.float32, "scatter lanes", after)


def plane_scatter_rows(partial, after=()):
    rows, width = partial.shape[0] // 8, partial.shape[1]
    place = member_rows(rows)
    return plane_scatter_call(partial, (rows, width), place, jnp.bfloat16, "scatter rows", after)


def exchange_kernel(source, target, x_ref, *refs):
    o_ref, local_sem, send_sem, recv_sem = refs[-4:]
    greet([member_at(peer) for peer in plane_peers()])
    exchange_steps(source, target, x_ref, o_ref, local_sem, mover(send_sem, recv_sem))()


def exchange(array, shape, source, target, kind, after=()):
    return pl.pallas_call(
        functools.partial(exchange_kernel, source, target),
        out_shape=jax.ShapeDtypeStruct(shape, array.dtype),
        in_specs=[IN_HBM] * (1 + len(after)),
        out_specs=IN_HBM,
        scratch_shapes=[
            pltpu.SemaphoreType.DMA,
            pltpu.SemaphoreType.DMA((7,)),
            pltpu.SemaphoreType.DMA((7,)),
        ],
        compiler_params=pltpu.CompilerParams(
            collective_id=identity_of(kind, array, *after), has_side_effects=True
        ),
        cost_estimate=BRIEF,
        name="plane_exchange",
    )(array, *after)


def whole_rows(rows):
    place = member_rows(rows)
    return lambda ref, member: place(ref, member, 0, rows)


def whole_lanes(rows, width):
    place = member_lanes(width)
    return lambda ref, member: place(ref, member, 0, rows)


def to_frames(part):
    rows, width = part.shape[0], part.shape[1] // 8
    return exchange(part, (8 * rows, width), whole_lanes(rows, width), whole_rows(rows), "to frames")


def to_rows(part):
    rows, width = part.shape[0] // 8, part.shape[1]
    return exchange(part, (rows, 8 * width), whole_rows(rows), whole_lanes(rows, width), "to rows")


def block(ref, member):
    return ref.at[member]


def exchange_blocks(blocks, after=()):
    return exchange(blocks, blocks.shape, block, block, "blocks", after)


def lanes(ref, start, width):
    return ref.at[:, pl.ds(pl.multiple_of(start, 128), width)]


def sheet_part(start, width):
    return lambda ref, member: lanes(ref, start + member * width, width)


def block_part(start, width):
    return lambda ref, member: lanes(ref.at[member], start, width)


def feed_kernel(count, *refs):
    gu_ref, down_ref = refs[:2]
    o_ref, local_sem, send_sem, recv_sem = refs[-4:]
    width = down_ref.shape[-1]
    greet([member_at(peer) for peer in plane_peers()])
    finish = []
    for k, (ref, start) in enumerate(((gu_ref, 0), (gu_ref, width), (down_ref, 0))):
        source, target = block_part(start, width), sheet_part(8 * k * width, width)
        copy = mover(send_sem, recv_sem, 7 * k)
        finish.append(exchange_steps(source, target, ref, o_ref, local_sem.at[k], copy))
    for end in finish:
        end()


def feed(gu, down, after=()):
    return pl.pallas_call(
        functools.partial(feed_kernel, len(after)),
        out_shape=jax.ShapeDtypeStruct((gu.shape[1], 24 * down.shape[-1]), gu.dtype),
        in_specs=[IN_HBM] * (2 + len(after)),
        out_specs=IN_HBM,
        scratch_shapes=[
            pltpu.SemaphoreType.DMA((3,)),
            pltpu.SemaphoreType.DMA((21,)),
            pltpu.SemaphoreType.DMA((21,)),
        ],
        compiler_params=pltpu.CompilerParams(
            collective_id=identity_of("feed", gu, down, *after), has_side_effects=True
        ),
        cost_estimate=BRIEF,
        name="feed",
    )(gu, down, *after)


def opening_kernel(
    x_ref,
    small_ref,
    text_ref,
    w_ref,
    v_ref,
    t_ref,
    all_ref,
    mine_ref,
    wo_ref,
    vo_ref,
    held,
    local_sem,
    send_sem,
    recv_sem,
):
    group, core, _, _ = near()
    member = group * 2 + core
    plane = lax.axis_index("z")
    step = x_ref.shape[0] // 4
    text_rows = mine_ref.shape[0]
    teacher = jnp.logical_and(group == plane, core == 0)

    def frames(ref, j):
        return ref.at[pl.ds(pl.multiple_of(j * step, 16), step), :]

    peers = plane_peers()
    line = [lax.rem(plane + k, 4) for k in range(1, 4)]
    greet([member_at(peer) for peer in peers] + [{"z": there} for there in line])

    near_copy = mover(send_sem, recv_sem)
    line_copy = mover(send_sem, recv_sem, 7)
    small_local = pltpu.make_async_copy(small_ref, all_ref.at[plane, member], local_sem.at[0])
    small_local.start()
    first = [
        near_copy(k, small_ref, all_ref.at[plane, member], member_at(peer))
        for k, peer in enumerate(peers)
    ]
    for moving in first:
        moving.start()

    others = [lax.rem(group + k, 4) for k in range(1, 4)]
    keep = pltpu.make_async_copy(frames(x_ref, group), frames(held, group), local_sem.at[1])
    keep.start()

    def spread(owner, landing):
        return pltpu.make_async_remote_copy(
            src_ref=frames(x_ref, owner),
            dst_ref=frames(held, landing),
            send_sem=send_sem.at[10 + owner],
            recv_sem=recv_sem.at[10 + landing],
            device_id={"dp": owner},
            device_id_type=MESH_ID,
        )

    for owner in others:
        spread(owner, group).start()

    def rise(row):
        return pltpu.make_async_remote_copy(
            src_ref=frames(held, row),
            dst_ref=frames(t_ref, plane),
            send_sem=send_sem.at[28 + row],
            recv_sem=recv_sem.at[28 + plane],
            device_id={"z": row},
            device_id_type=MESH_ID,
        )

    stay = pltpu.make_async_copy(frames(held, plane), frames(t_ref, plane), local_sem.at[4])

    def pass_on(row):
        pl.when(row == plane)(stay.start)
        pl.when(row != plane)(rise(row).start)

    first_done = exchange_steps(
        block, block, w_ref, wo_ref, local_sem.at[2], mover(send_sem, recv_sem, 14)
    )
    second_done = exchange_steps(
        block, block, v_ref, vo_ref, local_sem.at[5], mover(send_sem, recv_sem, 32)
    )

    def text_copy(k, peer):
        return pltpu.make_async_remote_copy(
            src_ref=text_ref.at[pl.ds(pl.multiple_of(peer * text_rows, 16), text_rows), :],
            dst_ref=mine_ref,
            send_sem=send_sem.at[21 + k],
            recv_sem=recv_sem.at[21],
            device_id=member_at(peer),
            device_id_type=MESH_ID,
        )

    own_text = text_ref.at[pl.ds(pl.multiple_of(member * text_rows, 16), text_rows), :]
    text_local = pltpu.make_async_copy(own_text, mine_ref, local_sem.at[3])

    @pl.when(teacher)
    def _():
        text_local.start()
        for k, peer in enumerate(peers):
            text_copy(k, peer).start()

    keep.wait()
    pass_on(group)
    for owner in others:
        spread(owner, owner).wait_recv()
        pass_on(owner)

    for k in range(7):
        landed = all_ref.at[plane, lax.rem(member + 7 - k, 8)]
        near_copy(k, landed, landed, member_at(peers[k])).wait_recv()
    small_local.wait()
    second = [
        line_copy(k, all_ref.at[plane], all_ref.at[plane], {"z": there})
        for k, there in enumerate(line)
    ]
    for moving in second:
        moving.start()
    for k in range(3):
        landed = all_ref.at[lax.rem(plane + 3 - k, 4)]
        line_copy(k, landed, landed, {"z": line[k]}).wait_recv()

    for there in line:
        landed = frames(t_ref, there)
        pltpu.make_async_remote_copy(
            src_ref=landed,
            dst_ref=landed,
            send_sem=send_sem.at[28 + there],
            recv_sem=recv_sem.at[28 + there],
            device_id={"z": there},
            device_id_type=MESH_ID,
        ).wait_recv()
    stay.wait()
    first_done()
    second_done()

    @pl.when(teacher)
    def _():
        text_local.wait()
        for k, peer in enumerate(peers):
            text_copy(k, peer).wait_send()

    @pl.when(jnp.logical_not(teacher))
    def _():
        text_copy(0, peers[0]).wait_recv()

    for moving in first + second:
        moving.wait_send()
    for owner in others:
        spread(owner, group).wait_send()
    for there in line:
        rise(there).wait_send()


def opening(local, small, text, first, second):
    return pl.pallas_call(
        opening_kernel,
        out_shape=(
            jax.ShapeDtypeStruct(local.shape, local.dtype),
            jax.ShapeDtypeStruct((4, 8) + small.shape, small.dtype),
            jax.ShapeDtypeStruct((text.shape[0] // 8, text.shape[1]), text.dtype),
            jax.ShapeDtypeStruct(first.shape, first.dtype),
            jax.ShapeDtypeStruct(second.shape, second.dtype),
        ),
        in_specs=[IN_HBM] * 5,
        out_specs=(IN_HBM,) * 5,
        scratch_shapes=[
            pltpu.VMEM(local.shape, local.dtype),
            pltpu.SemaphoreType.DMA((6,)),
            pltpu.SemaphoreType.DMA((39,)),
            pltpu.SemaphoreType.DMA((39,)),
        ],
        compiler_params=pltpu.CompilerParams(
            collective_id=identity_of("opening", local), has_side_effects=True
        ),
        cost_estimate=BRIEF,
        name="opening",
    )(local, small, text, first, second)


def first_gather_kernel(x_ref, y_ref, sheet_ref, ox_ref, oy_ref, w_ref, local_sem, send_sem, recv_sem):
    place = member_lanes(x_ref.shape[1])
    width = FF // 8
    greet([member_at(peer) for peer in plane_peers()])
    finish = [
        gather_steps(place, x_ref, ox_ref, local_sem.at[0], mover(send_sem, recv_sem)),
        gather_steps(place, y_ref, oy_ref, local_sem.at[1], mover(send_sem, recv_sem, 14)),
    ]
    for k in range(3):
        source, target = sheet_part(6 * D + k * FF, width), block_part(k * width, width)
        copy = mover(send_sem, recv_sem, 28 + 7 * k)
        finish.append(exchange_steps(source, target, sheet_ref, w_ref, local_sem.at[2 + k], copy))
    for end in finish:
        end()


def first_gather(shard, other, sheet):
    rows, width = shard.shape
    whole = jax.ShapeDtypeStruct((rows, 8 * width), shard.dtype)
    return pl.pallas_call(
        first_gather_kernel,
        out_shape=(
            whole,
            whole,
            jax.ShapeDtypeStruct((8, sheet.shape[0], 3 * FF // 8), sheet.dtype),
        ),
        in_specs=[IN_HBM] * 3,
        out_specs=(IN_HBM,) * 3,
        scratch_shapes=[
            pltpu.SemaphoreType.DMA((5,)),
            pltpu.SemaphoreType.DMA((49,)),
            pltpu.SemaphoreType.DMA((49,)),
        ],
        compiler_params=pltpu.CompilerParams(
            collective_id=identity_of("first gather", shard, sheet), has_side_effects=True
        ),
        cost_estimate=BRIEF,
        name="first_gather",
    )(shard, other, sheet)


def closing_kernel(
    x_ref, w_ref, g_ref, _, t_ref, o_ref, s_ref, held, tall, local_sem, send_sem, recv_sem
):
    group, core, _, _ = near()
    member = group * 2 + core
    plane = lax.axis_index("z")
    step = x_ref.shape[0] // 4
    line = [lax.rem(plane + k, 4) for k in range(1, 4)]
    back = [lax.rem(plane + 3 - k, 4) for k in range(3)]
    groups = [lax.rem(group + k, 4) for k in range(1, 4)]
    peers = plane_peers()
    greet([member_at(peer) for peer in peers] + [{"z": there} for there in line])

    def frames(ref, j):
        return ref.at[pl.ds(pl.multiple_of(j * step, 16), step), :]

    copy = mover(send_sem, recv_sem)
    gain_line = mover(send_sem, recv_sem, 14)
    gain_plane = mover(send_sem, recv_sem, 17)
    gain_local = pltpu.make_async_copy(g_ref, tall.at[plane], local_sem.at[3])
    gain_local.start()
    sent = [gain_line(k, g_ref, tall.at[plane], {"z": there}) for k, there in enumerate(line)]
    local = pltpu.make_async_copy(frames(x_ref, plane), frames(held, plane), local_sem.at[0])
    local.start()
    sent += [
        copy(k, frames(x_ref, there), frames(held, plane), {"z": there})
        for k, there in enumerate(line)
    ]
    for moving in sent:
        moving.start()
    weights_done = exchange_steps(
        block, block, w_ref, o_ref, local_sem.at[1], mover(send_sem, recv_sem, 7)
    )

    gain_local.wait()
    for k, origin in enumerate(back):
        gain_line(k, tall.at[origin], tall.at[origin], {"z": origin}).wait_recv()
    tall[4] = tall[0] + tall[1] + tall[2] + tall[3]
    gain_keep = pltpu.make_async_copy(tall.at[4], s_ref.at[member], local_sem.at[4])
    gain_keep.start()
    given = [
        gain_plane(k, tall.at[4], s_ref.at[member], member_at(peer)) for k, peer in enumerate(peers)
    ]
    for moving in given:
        moving.start()

    def onward(owner):
        return pltpu.make_async_remote_copy(
            src_ref=frames(held, owner),
            dst_ref=frames(t_ref, group),
            send_sem=send_sem.at[3 + owner],
            recv_sem=recv_sem.at[3 + group],
            device_id={"dp": owner},
            device_id_type=MESH_ID,
        )

    keep = pltpu.make_async_copy(frames(held, group), frames(t_ref, group), local_sem.at[2])

    def pass_on(owner):
        pl.when(owner == group)(keep.start)
        pl.when(owner != group)(onward(owner).start)

    local.wait()
    pass_on(plane)
    for k, origin in enumerate(back):
        landed = frames(held, origin)
        copy(k, landed, landed, {"z": origin}).wait_recv()
        pass_on(origin)
    for origin in groups:
        landed = frames(t_ref, origin)
        pltpu.make_async_remote_copy(
            src_ref=landed,
            dst_ref=landed,
            send_sem=send_sem.at[3 + origin],
            recv_sem=recv_sem.at[3 + origin],
            device_id={"dp": origin},
            device_id_type=MESH_ID,
        ).wait_recv()
    keep.wait()
    weights_done()
    gain_keep.wait()
    for k in range(7):
        landed = s_ref.at[lax.rem(member + 7 - k, 8)]
        gain_plane(k, landed, landed, member_at(peers[k])).wait_recv()
    for moving in sent + given:
        moving.wait_send()
    for origin in groups:
        onward(origin).wait_send()


def closing(local, weights, gains, after):
    return pl.pallas_call(
        closing_kernel,
        out_shape=(
            jax.ShapeDtypeStruct(local.shape, local.dtype),
            jax.ShapeDtypeStruct(weights.shape, weights.dtype),
            jax.ShapeDtypeStruct((8,) + gains.shape, gains.dtype),
        ),
        in_specs=[IN_HBM] * 4,
        out_specs=(IN_HBM,) * 3,
        scratch_shapes=[
            pltpu.VMEM(local.shape, local.dtype),
            pltpu.VMEM((5,) + gains.shape, gains.dtype),
            pltpu.SemaphoreType.DMA((5,)),
            pltpu.SemaphoreType.DMA((24,)),
            pltpu.SemaphoreType.DMA((24,)),
        ],
        compiler_params=pltpu.CompilerParams(
            collective_id=identity_of("closing", local), has_side_effects=True
        ),
        cost_estimate=BRIEF,
        name="closing",
    )(local, weights, gains, after)


def everywhere_kernel(x_ref, o_ref, local_sem, send_sem, recv_sem):
    group, core, _, _ = near()
    member = group * 2 + core
    plane = lax.axis_index("z")
    peers = [lax.rem(member + step, 8) for step in range(1, 8)]
    places = [{"dp": lax.div(peer, 2), "core": lax.rem(peer, 2)} for peer in peers]
    places = places + [{"z": lax.rem(plane + step, 4)} for step in range(1, 4)]
    greet(places)

    def copy(k, source, target):
        return pltpu.make_async_remote_copy(
            src_ref=source,
            dst_ref=target,
            send_sem=send_sem.at[k],
            recv_sem=recv_sem.at[k],
            device_id=places[k],
            device_id_type=MESH_ID,
        )

    local = pltpu.make_async_copy(x_ref, o_ref.at[plane, member], local_sem)
    local.start()
    copies = [copy(k, x_ref, o_ref.at[plane, member]) for k in range(7)]
    for moving in copies:
        moving.start()
    for k in range(7):
        landed = o_ref.at[plane, lax.rem(member + 7 - k, 8)]
        copy(k, landed, landed).wait_recv()
    local.wait()
    between = [copy(7 + k, o_ref.at[plane], o_ref.at[plane]) for k in range(3)]
    for moving in between:
        moving.start()
    for k in range(3):
        landed = o_ref.at[lax.rem(plane + 3 - k, 4)]
        copy(7 + k, landed, landed).wait_recv()
    for moving in copies + between:
        moving.wait_send()


def gather_everywhere(block):
    return pl.pallas_call(
        everywhere_kernel,
        out_shape=jax.ShapeDtypeStruct((4, 8) + block.shape, block.dtype),
        in_specs=[IN_VMEM],
        out_specs=IN_VMEM,
        scratch_shapes=[
            pltpu.SemaphoreType.DMA,
            pltpu.SemaphoreType.DMA((10,)),
            pltpu.SemaphoreType.DMA((10,)),
        ],
        compiler_params=pltpu.CompilerParams(
            collective_id=identity_of("everywhere", block), has_side_effects=True
        ),
        cost_estimate=BRIEF,
        name="gather_everywhere",
    )(block)


def split_columns(block, members):
    rows, columns = block.shape
    return block.reshape(rows, members, columns // members)


def pick_blocks(blocks, order):
    return blocks.at[order].get(mode="promise_in_bounds")


def gather_line(mine, order):
    blocks = lax.all_gather(mine, "z", axis=0, tiled=True)
    return pick_blocks(blocks, order).reshape(-1, mine.shape[-1])


def grad_blocks(grad, order):
    blocks = grad.astype(jnp.bfloat16).reshape(order.shape[0], -1, grad.shape[-1])
    return pick_blocks(blocks, order)


def scatter_line(blocks):
    return lax.psum_scatter(blocks, "z", scatter_dimension=0, tiled=True)


def plane_plan(latents, context, clip_starts, buckets, owners, cotangent, sheet, first, second):
    groups = lax.axis_size("dp")
    planes = lax.axis_size("z")
    cores = lax.axis_size("core")
    members = groups * cores
    frames = latents.shape[1]
    length = frames * members
    rows = sheet.shape[0]
    blocks = owners.shape[0]
    head_count = D // HEAD // members
    span = D // members
    units = FF // members
    score_scale = HEAD ** (-0.5)
    tail_col = 6 * D + 3 * FF
    gain_col = tail_col + 2 * CTXW
    plane = lax.axis_index("z")

    group_ids = jnp.arange(blocks, dtype=jnp.int32)
    inverse = jnp.sum(
        jnp.where(owners[None, :] == group_ids[:, None], group_ids[None, :], 0), axis=1
    )
    slot = group_ids.reshape(groups, planes, cores).swapaxes(0, 1).reshape(-1)
    slot_of = jnp.sum(
        jnp.where(slot[None, :] == group_ids[:, None], group_ids[None, :], 0), axis=1
    )
    to_logical = jnp.take(slot_of, inverse)
    to_slots = jnp.take(owners, slot)

    low_sheet = sheet.astype(jnp.bfloat16)

    def columns_of(start, width):
        return split_columns(low_sheet[:, start : start + width], members)

    def member_blocks(*pieces):
        return jnp.swapaxes(jnp.concatenate(pieces, axis=2), 0, 1)

    blocks_qkv = member_blocks(*[columns_of(k * D, D) for k in range(3)])
    blocks_two = member_blocks(
        columns_of(3 * D, D),
        columns_of(4 * D, D),
        columns_of(5 * D, D),
        columns_of(tail_col, CTXW),
        columns_of(tail_col + CTXW, CTXW),
    )
    small = jnp.concatenate(
        [
            jnp.pad(low_sheet[:, gain_col:].astype(jnp.float32).T, ((0, 0), (0, 64 - rows))),
            jnp.pad(clip_starts.astype(jnp.float32), ((0, 7), (0, 64 - clip_starts.shape[1]))),
        ],
        axis=1,
    )
    both, small, text_mine, mine_qkv, mine_two = opening(
        jnp.concatenate([latents[0], cotangent[0]], axis=1),
        small,
        context[0].T,
        blocks_qkv,
        blocks_two,
    )
    weight_qkv = gather_line(mine_qkv, to_logical)
    weight_two = gather_line(mine_two, to_logical)
    weight_ao = weight_two[:, :span]
    weight_cq = weight_two[:, span : 2 * span]
    weight_co = weight_two[:, 2 * span : 3 * span]
    weight_text = weight_two[:, 3 * span :]
    gains = pick_blocks(small[..., :rows].reshape(blocks, 8, rows), to_logical)
    gains = gains.swapaxes(1, 2).reshape(D, 8)
    starts = lax.dynamic_index_in_dim(
        small[0, :, 0, 64 : 64 + clip_starts.shape[1]], plane * cores, 0, False
    )
    starts = starts.astype(jnp.int32)

    bucket_ids = jnp.arange(NB, dtype=jnp.int32)
    bucket_pick = (bucket_ids == buckets[plane]).astype(jnp.float32)
    counts = jnp.sum((buckets[:, None] == bucket_ids[None, :]).astype(jnp.float32), axis=0)
    row_weight = buckets.shape[0] / (NB * jnp.sum(bucket_pick * counts))
    gain_one = gains[:, 0:1]
    gain_two = gains[:, 1:2]
    gain_three = gains[:, 2:3]
    time_gain = jnp.sum(gains[:, 3:] * bucket_pick[None, :], axis=1, keepdims=True)

    tokens = both[:, :D].astype(jnp.float32).T
    grad_out = both[:, D:].astype(jnp.float32).T * row_weight

    rest = frames // planes
    place = jnp.arange(length, dtype=jnp.int32).reshape(planes, cores, groups, rest)
    positions = place.transpose(2, 1, 0, 3).reshape(-1)
    segments = segment_ids(starts, positions)
    same_clip = segments[:, None] == segments[None, :]
    frequency = jnp.exp(
        -math.log(10000.0) * jnp.arange(HEAD // 2, dtype=jnp.float32) / (HEAD // 2)
    )
    angles = frequency[:, None] * positions.astype(jnp.float32)[None, :]
    cosine = jnp.cos(angles)[None]
    sine_table = jnp.sin(angles)[None]

    normed_one, inverse_one = norm_columns(tokens)
    scaled_one = gain_one * time_gain
    h_one, grad_ff, mine_feed = first_gather(
        (normed_one * scaled_one).astype(jnp.bfloat16), grad_out.astype(jnp.bfloat16), low_sheet
    )
    weight_feed = gather_line(mine_feed, to_logical)
    weight_gu = weight_feed[:, : 2 * units]
    weight_down = weight_feed[:, 2 * units :]

    joint = contract_rows(weight_qkv, h_one).reshape(3, head_count, HEAD, length)
    queries = rotate_columns(joint[0], cosine, sine_table).astype(jnp.bfloat16)
    keys = rotate_columns(joint[1], cosine, sine_table).astype(jnp.bfloat16)
    values = joint[2].astype(jnp.bfloat16)
    scores = (
        jnp.einsum("hdq,hdk->hqk", queries, keys, preferred_element_type=jnp.float32) * score_scale
    )
    attn_probs = softmax_rows(jnp.where(same_clip[None], scores, MASKED_SCORE))
    probs_low = attn_probs.astype(jnp.bfloat16)
    attn_out = jnp.einsum("hqk,hdk->hdq", probs_low, values, preferred_element_type=jnp.float32)
    attn_out = plane_gather_rows(attn_out.reshape(span, length).astype(jnp.bfloat16))
    x_one = tokens + to_frames(contract_rows(weight_ao, attn_out).astype(jnp.bfloat16)).astype(
        jnp.float32
    )

    text_width = CTXW // members
    text_kv = jnp.stack(
        [
            matmul(weight_text[:, :text_width], text_mine),
            matmul(weight_text[:, text_width:], text_mine),
        ],
        axis=1,
    ).reshape(D, 2 * CTX)
    text_kv = plane_scatter_rows(text_kv.astype(jnp.bfloat16)).reshape(head_count, HEAD, 2, CTX)
    text_keys = text_kv[:, :, 0]
    text_values = text_kv[:, :, 1]
    normed_two, inverse_two = norm_columns(x_one)
    h_two = plane_gather((normed_two * gain_two).astype(jnp.bfloat16))
    cross_q = contract_rows(weight_cq, h_two).astype(jnp.bfloat16).reshape(head_count, HEAD, length)
    cross_scores = (
        jnp.einsum("hdq,hdk->hqk", cross_q, text_keys, preferred_element_type=jnp.float32)
        * score_scale
    )
    cross_probs = softmax_rows(cross_scores)
    cross_low = cross_probs.astype(jnp.bfloat16)
    cross_out = jnp.einsum(
        "hqk,hdk->hdq", cross_low, text_values, preferred_element_type=jnp.float32
    )
    cross_out = plane_gather_rows(cross_out.reshape(span, length).astype(jnp.bfloat16))
    x_two = x_one + to_frames(contract_rows(weight_co, cross_out).astype(jnp.bfloat16)).astype(
        jnp.float32
    )

    normed_three, inverse_three = norm_columns(x_two)
    h_three = plane_gather((normed_three * gain_three).astype(jnp.bfloat16))
    gate_up = contract_rows(weight_gu, h_three)
    gate_pre = gate_up[:units]
    up_part = gate_up[units:]
    sigmoid_gate = jax.nn.sigmoid(gate_pre)
    silu_gate = gate_pre * sigmoid_gate
    hidden = (silu_gate * up_part).astype(jnp.bfloat16)
    ff_out = plane_scatter_frames(matmul(weight_down, hidden).astype(jnp.bfloat16))
    result = x_two + ff_out

    grad_hidden = contract_rows(weight_down, grad_ff)
    grad_gate = grad_hidden * up_part * (sigmoid_gate * (1.0 + gate_pre * (1.0 - sigmoid_gate)))
    grad_up = grad_hidden * silu_gate
    grad_gu = jnp.concatenate([grad_gate, grad_up], axis=0).astype(jnp.bfloat16)
    grad_blocks_gu = grad_blocks(contract_last(h_three, grad_gu), to_slots)
    grad_blocks_down = grad_blocks(contract_last(grad_ff, hidden), to_slots)
    grad_h_three = plane_scatter_frames(
        matmul(weight_gu, grad_gu).astype(jnp.bfloat16), [grad_blocks_gu, grad_blocks_down]
    )
    sums_gu = scatter_line(grad_blocks_gu)
    sums_down = scatter_line(grad_blocks_down)
    grad_gain_three = jnp.sum(grad_h_three * normed_three, axis=1)
    grad_x_two = grad_out + norm_columns_back(
        grad_h_three * gain_three, normed_three, inverse_three
    )
    grad_cross = to_rows(grad_x_two.astype(jnp.bfloat16))
    grad_weight_co = contract_last(cross_out, grad_cross)
    grad_cross_out = plane_scatter_rows(
        matmul(weight_co, grad_cross).astype(jnp.bfloat16)
    ).reshape(head_count, HEAD, length)
    grad_cross_probs = jnp.einsum(
        "hdq,hdk->hqk", grad_cross_out, text_values, preferred_element_type=jnp.float32
    )
    grad_cross_scores = (
        cross_probs
        * (grad_cross_probs - jnp.sum(cross_probs * grad_cross_probs, axis=-1, keepdims=True))
    ).astype(jnp.bfloat16)
    grad_cross_q = (
        jnp.einsum("hqk,hdk->hdq", grad_cross_scores, text_keys, preferred_element_type=jnp.float32)
        * score_scale
    )
    grad_cross_q = grad_cross_q.reshape(span, length).astype(jnp.bfloat16)
    grad_text_keys = (
        jnp.einsum("hqk,hdq->hdk", grad_cross_scores, cross_q, preferred_element_type=jnp.float32)
        * score_scale
    )
    grad_text_values = jnp.einsum(
        "hqk,hdq->hdk", cross_low, grad_cross_out, preferred_element_type=jnp.float32
    )
    grad_text = jnp.concatenate(
        [grad_text_keys.reshape(span, CTX), grad_text_values.reshape(span, CTX)], axis=1
    )
    grad_text = plane_gather_rows(grad_text.astype(jnp.bfloat16))
    grad_weight_cq = contract_last(h_two, grad_cross_q)
    grad_weight_text = [
        contract_last(grad_text[:, :CTX], text_mine),
        contract_last(grad_text[:, CTX:], text_mine),
    ]
    grad_h_two = plane_scatter_frames(
        matmul(weight_cq, grad_cross_q).astype(jnp.bfloat16), [sums_gu]
    )
    grad_gain_two = jnp.sum(grad_h_two * normed_two, axis=1)
    grad_x_one = grad_x_two + norm_columns_back(grad_h_two * gain_two, normed_two, inverse_two)
    grad_attn = to_rows(grad_x_one.astype(jnp.bfloat16))
    grad_weight_ao = contract_last(attn_out, grad_attn)
    grad_blocks_two = grad_blocks(
        jnp.concatenate(
            [grad_weight_ao, grad_weight_cq, grad_weight_co] + grad_weight_text, axis=1
        ),
        to_slots,
    )
    sums_two = scatter_line(grad_blocks_two)
    grad_attn_out = plane_scatter_rows(
        matmul(weight_ao, grad_attn).astype(jnp.bfloat16), [sums_down, grad_blocks_two]
    ).reshape(head_count, HEAD, length)
    grad_probs = jnp.einsum(
        "hdq,hdk->hqk", grad_attn_out, values, preferred_element_type=jnp.float32
    )
    grad_scores = (
        attn_probs * (grad_probs - jnp.sum(attn_probs * grad_probs, axis=-1, keepdims=True))
    ).astype(jnp.bfloat16)
    grad_queries = (
        jnp.einsum("hqk,hdk->hdq", grad_scores, keys, preferred_element_type=jnp.float32)
        * score_scale
    )
    grad_keys = (
        jnp.einsum("hqk,hdq->hdk", grad_scores, queries, preferred_element_type=jnp.float32)
        * score_scale
    )
    grad_values = jnp.einsum(
        "hqk,hdq->hdk", probs_low, grad_attn_out, preferred_element_type=jnp.float32
    )
    grad_qkv = jnp.stack(
        [
            rotate_columns(grad_queries, cosine, -sine_table),
            rotate_columns(grad_keys, cosine, -sine_table),
            grad_values,
        ]
    )
    grad_qkv = grad_qkv.reshape(3 * span, length).astype(jnp.bfloat16)
    grad_weight_qkv = contract_last(h_one, grad_qkv)
    grad_blocks_qkv = grad_blocks(grad_weight_qkv, to_slots)
    sums_one = scatter_line(grad_blocks_qkv)
    sums_feed = feed(sums_gu, sums_down, [grad_blocks_qkv])
    grad_h_one = plane_scatter_frames(
        matmul(weight_qkv, grad_qkv).astype(jnp.bfloat16), [sums_two, grad_blocks_qkv]
    )
    grad_gain_one = jnp.sum(grad_h_one * normed_one * time_gain, axis=1)
    grad_time = jnp.sum(grad_h_one * normed_one * gain_one, axis=1)
    latent_grad = grad_x_one + norm_columns_back(grad_h_one * scaled_one, normed_one, inverse_one)
    gain_grads = jnp.concatenate(
        [
            jnp.stack([grad_gain_one, grad_gain_two, grad_gain_three]),
            bucket_pick[:, None] * grad_time[None, :],
        ],
        axis=0,
    )
    sums_two = exchange_blocks(sums_two, [sums_feed])
    out_pair, sums_one, gain_sums = closing(
        jnp.concatenate([result.T, latent_grad.T], axis=1).astype(jnp.bfloat16),
        sums_one,
        gain_grads,
        sums_two,
    )
    output = out_pair[:, :D]
    latent_grad = out_pair[:, D:].astype(jnp.float32)
    place = lax.axis_index("dp") * (planes * cores) + plane * cores + lax.axis_index("core")
    gain_sums = lax.dynamic_index_in_dim(
        jnp.sum(gain_sums, axis=0).reshape(8, blocks, rows), owners[place], 1, False
    ).T
    sums_one, sums_two = jnp.swapaxes(sums_one, 0, 1), jnp.swapaxes(sums_two, 0, 1)

    def joined(part):
        return part.reshape(rows, -1)

    grad_sheet = jnp.concatenate(
        [joined(sums_one[:, :, k * span : (k + 1) * span]) for k in range(3)]
        + [joined(sums_two[:, :, k * span : (k + 1) * span]) for k in range(3)]
        + [sums_feed]
        + [
            joined(sums_two[:, :, 3 * span : 3 * span + text_width]),
            joined(sums_two[:, :, 3 * span + text_width :]),
        ]
        + [gain_sums.astype(jnp.bfloat16)],
        axis=1,
    ).astype(jnp.float32)
    squares = jnp.pad(jnp.sum(grad_sheet * grad_sheet).reshape(1, 1), ((0, 7), (0, 127)))
    total_squares = jnp.sum(gather_everywhere(squares))
    return (output[None], latent_grad[None]) + update(
        grad_sheet, total_squares, sheet, first, second, length
    )


def update(grad_sheet, total_squares, sheet, first, second, length):
    grad_norm = jnp.sqrt(total_squares)
    clipped = grad_sheet / jnp.maximum(grad_norm, 1.0)
    gain_grad = clipped[:, 6 * D + 3 * FF + 2 * CTXW :]
    first_new = BETA_ONE * first + (1.0 - BETA_ONE) * clipped
    second_new = BETA_TWO * second + (1.0 - BETA_TWO) * clipped * clipped
    mean_hat = first_new / (1.0 - BETA_ONE**STEP)
    square_hat = second_new / (1.0 - BETA_TWO**STEP)
    rates = column_spread(length)[None, :]
    sheet_new = sheet - rates * (
        mean_hat / (jnp.sqrt(square_hat) + EPS_ADAM) + WEIGHT_DECAY * sheet
    )
    return (
        grad_norm,
        clipped,
        gain_grad,
        first_new,
        second_new,
        sheet_new,
        sheet_new.astype(jnp.bfloat16),
    )


def solution(mesh):
    groups, seq_count = mesh.shape["dp"], mesh.shape["seq"]
    by_plane = groups == 4 and seq_count == 8
    if by_plane:
        mesh = Mesh(mesh.devices.reshape(groups, seq_count // 2, 2), ("dp", "z", "core"))
    seq = ("z", "core") if by_plane else "seq"
    both = ("dp", "z", "core") if by_plane else ("dp", "seq")
    in_specs = (
        P("dp", seq, None),
        P("dp", None, None),
        P("dp", None),
        P(),
        P(),
        P("dp", seq, None),
        P(both, None),
        P(both, None),
        P(both, None),
    )
    out_specs = (
        P("dp", seq, None),
        P("dp", seq, None),
        P(),
        P(both, None),
        P(both, None),
        P(both, None),
        P(both, None),
        P(both, None),
        P(both, None),
    )
    return jax.shard_map(
        plane_plan if by_plane else gather_plan,
        mesh=mesh,
        in_specs=in_specs,
        out_specs=out_specs,
        check_vma=False,
    )
```

```python
import functools
import math

import jax
import jax.numpy as jnp
from jax import lax
from jax.experimental import pallas as pl
from jax.experimental.pallas import tpu as pltpu
from jax.sharding import Mesh
from jax.sharding import PartitionSpec as P

D = 1536
FF = 6144
HEAD = 64
CTXW = 768
CTX = 128
NB = 5
STEP = 10
SHEET = 29192


HIGHEST = lax.Precision.HIGHEST
EPS_NORM = 1e-05
EPS_ADAM = 1e-08
MASKED_SCORE = -1e30
BETA_ONE = 0.5
BETA_TWO = 0.5
WEIGHT_DECAY = 0.01


def reorder(values, ordering):
    leading = values.shape[:-1]
    groups = ordering.shape[0]
    blocks = values.reshape(leading + (groups, values.shape[-1] // groups))
    return jnp.take(blocks, ordering, axis=-2).reshape(values.shape)


def norm_parts(values):
    average = jnp.mean(values, axis=-1, keepdims=True)
    centered = values - average
    variance = jnp.mean(centered * centered, axis=-1, keepdims=True)
    inverse_std = lax.rsqrt(variance + EPS_NORM)
    return (centered * inverse_std, inverse_std)


def norm_back(grad_normed, normed, inverse_std):
    return inverse_std * (
        grad_normed
        - jnp.mean(grad_normed, axis=-1, keepdims=True)
        - normed * jnp.mean(grad_normed * normed, axis=-1, keepdims=True)
    )


def softmax_rows(scores):
    row_max = jnp.max(scores, axis=-1, keepdims=True)
    exponent = jnp.exp(scores - row_max)
    return exponent / jnp.sum(exponent, axis=-1, keepdims=True)


def rope_tables(positions, head_dim):
    half_dim = head_dim // 2
    frequency = jnp.exp(-math.log(10000.0) * jnp.arange(half_dim, dtype=jnp.float32) / half_dim)
    angles = positions.astype(jnp.float32)[:, None] * frequency[None, :]
    return (jnp.cos(angles)[:, None, :], jnp.sin(angles)[:, None, :])


def rotate(values, cosine, sine_table):
    half_dim = values.shape[-1] // 2
    first_half = values[..., :half_dim]
    second_half = values[..., half_dim:]
    return jnp.concatenate(
        [
            first_half * cosine - second_half * sine_table,
            second_half * cosine + first_half * sine_table,
        ],
        axis=-1,
    )


def unrotate(grads, cosine, sine_table):
    half_dim = grads.shape[-1] // 2
    first_half = grads[..., :half_dim]
    second_half = grads[..., half_dim:]
    return jnp.concatenate(
        [
            first_half * cosine + second_half * sine_table,
            second_half * cosine - first_half * sine_table,
        ],
        axis=-1,
    )


def segment_ids(starts, positions):
    return jnp.sum((starts[None, :] <= positions[:, None]).astype(jnp.int32), axis=1) - 1


def column_spread(length):
    column = jnp.arange(SHEET, dtype=jnp.int32)
    base_std = D ** (-0.5)
    spread = jnp.full((SHEET,), base_std, jnp.float32)
    spread = jnp.where(
        (column >= 3 * D) & (column < 4 * D), base_std * math.sqrt(length) / 4.0, spread
    )
    spread = jnp.where((column >= 5 * D) & (column < 6 * D), base_std * math.sqrt(CTX), spread)
    spread = jnp.where((column >= 6 * D + 2 * FF) & (column < 6 * D + 3 * FF), FF ** (-0.5), spread)
    spread = jnp.where(
        (column >= 6 * D + 3 * FF) & (column < 6 * D + 3 * FF + 2 * CTXW), CTXW ** (-0.5), spread
    )
    spread = jnp.where(column >= 6 * D + 3 * FF + 2 * CTXW, 0.3, spread)
    return spread


def inner_rows(left, right):
    return lax.dot_general(
        left, right, (((0,), (0,)), ((), ())), preferred_element_type=jnp.float32
    )


def inner_rows_high(left, right):
    return lax.dot_general(
        left, right, (((0,), (0,)), ((), ())), precision=HIGHEST, preferred_element_type=jnp.float32
    )


def gather_plan(latents, context, clip_starts, buckets, owners, cotangent, sheet, first, second):
    frames = latents.shape[1]
    seq_count = lax.axis_size("seq")
    length = frames * seq_count
    head_count = D // HEAD
    score_scale = HEAD ** (-0.5)
    group_ids = jnp.arange(owners.shape[0], dtype=jnp.int32)
    inverse = jnp.sum(
        jnp.where(owners[None, :] == group_ids[:, None], group_ids[None, :], 0), axis=1
    )
    gathered = lax.all_gather(sheet.astype(jnp.bfloat16), ("dp", "seq"), axis=0, tiled=True)
    tail_col = 6 * D + 3 * FF
    gain_col = tail_col + 2 * CTXW
    gain_rows = reorder(gathered[:, gain_col:].astype(jnp.float32).T, inverse)
    row_index = lax.axis_index("dp")
    bucket_ids = jnp.arange(NB, dtype=jnp.int32)
    bucket_pick = (bucket_ids == buckets[row_index]).astype(jnp.float32)
    counts = jnp.sum((buckets[:, None] == bucket_ids[None, :]).astype(jnp.float32), axis=0)
    row_weight = buckets.shape[0] / (NB * jnp.sum(bucket_pick * counts))
    gain_one = gain_rows[0]
    gain_two = gain_rows[1]
    gain_three = gain_rows[2]
    time_gain = jnp.sum(gain_rows[3:] * bucket_pick[:, None], axis=0)
    tokens = latents[0].astype(jnp.float32)
    positions = lax.axis_index("seq") * frames + jnp.arange(frames, dtype=jnp.int32)
    all_positions = jnp.arange(length, dtype=jnp.int32)
    starts = clip_starts[0]
    same_clip = (
        segment_ids(starts, positions)[:, None] == segment_ids(starts, all_positions)[None, :]
    )[None]
    cosine, sine_table = rope_tables(positions, HEAD)
    normed_one, inverse_one = norm_parts(tokens)
    scaled_one = gain_one * time_gain
    h_one_st = reorder((normed_one * scaled_one).astype(jnp.bfloat16), owners)
    joint_qkv = jnp.dot(h_one_st, gathered[:, : 3 * D], preferred_element_type=jnp.float32)
    queries = rotate(joint_qkv[:, :D].reshape(frames, head_count, HEAD), cosine, sine_table).astype(
        jnp.bfloat16
    )
    key_local = rotate(
        joint_qkv[:, D : 2 * D].reshape(frames, head_count, HEAD), cosine, sine_table
    ).astype(jnp.bfloat16)
    value_local = joint_qkv[:, 2 * D :].reshape(frames, head_count, HEAD).astype(jnp.bfloat16)
    key_all, value_all = (
        lax.all_gather(key_local, "seq", axis=0, tiled=True),
        lax.all_gather(value_local, "seq", axis=0, tiled=True),
    )
    scores = (
        jnp.einsum("qhd,khd->hqk", queries, key_all, preferred_element_type=jnp.float32)
        * score_scale
    )
    attn_probs = softmax_rows(jnp.where(same_clip, scores, MASKED_SCORE))
    probs_low = attn_probs.astype(jnp.bfloat16)
    attn_out = (
        jnp.einsum("hqk,khd->qhd", probs_low, value_all, preferred_element_type=jnp.float32)
        .reshape(frames, D)
        .astype(jnp.bfloat16)
    )
    attn_st = reorder(attn_out, owners)
    x_one = tokens + jnp.dot(
        attn_st, gathered[:, 3 * D : 4 * D], preferred_element_type=jnp.float32
    )
    normed_two, inverse_two = norm_parts(x_one)
    h_two_st = reorder((normed_two * gain_two).astype(jnp.bfloat16), owners)
    cross_q = (
        jnp.dot(h_two_st, gathered[:, 4 * D : 5 * D], preferred_element_type=jnp.float32)
        .astype(jnp.bfloat16)
        .reshape(frames, head_count, HEAD)
    )
    text_tokens = context[0]
    text_kv = jnp.einsum(
        "tc,dec->etd",
        text_tokens,
        gathered[:, tail_col:gain_col].reshape(D, 2, CTXW),
        preferred_element_type=jnp.float32,
    )
    text_kv = reorder(text_kv, inverse).astype(jnp.bfloat16).reshape(2, CTX, head_count, HEAD)
    text_keys = text_kv[0]
    text_values = text_kv[1]
    cross_scores = (
        jnp.einsum("qhd,khd->hqk", cross_q, text_keys, preferred_element_type=jnp.float32)
        * score_scale
    )
    cross_probs = softmax_rows(cross_scores)
    cross_low = cross_probs.astype(jnp.bfloat16)
    cross_out = (
        jnp.einsum("hqk,khd->qhd", cross_low, text_values, preferred_element_type=jnp.float32)
        .reshape(frames, D)
        .astype(jnp.bfloat16)
    )
    cross_st = reorder(cross_out, owners)
    x_two = x_one + jnp.dot(
        cross_st, gathered[:, 5 * D : 6 * D], preferred_element_type=jnp.float32
    )
    normed_three, inverse_three = norm_parts(x_two)
    h_three_st = reorder((normed_three * gain_three).astype(jnp.bfloat16), owners)
    grad_out = cotangent[0].astype(jnp.float32) * row_weight
    grad_ff_st = reorder(grad_out.astype(jnp.bfloat16), owners)
    gate_weight = gathered[:, 6 * D : 6 * D + 2 * FF]
    down_weight = gathered[:, 6 * D + 2 * FF : 6 * D + 3 * FF]
    units = down_weight.shape[1]
    gate_up = jnp.dot(h_three_st, gate_weight, preferred_element_type=jnp.float32)
    gate_pre = gate_up[:, :units]
    up_part = gate_up[:, units:]
    sigmoid_gate = jax.nn.sigmoid(gate_pre)
    silu_gate = gate_pre * sigmoid_gate
    hidden = (silu_gate * up_part).astype(jnp.bfloat16)
    ff_out = reorder(
        jnp.einsum("nf,df->nd", hidden, down_weight, preferred_element_type=jnp.float32), inverse
    )
    result = x_two + ff_out
    grad_hidden = jnp.dot(grad_ff_st, down_weight, preferred_element_type=jnp.float32)
    grad_gate = grad_hidden * up_part * (sigmoid_gate * (1.0 + gate_pre * (1.0 - sigmoid_gate)))
    grad_up = grad_hidden * silu_gate
    grad_gu = jnp.concatenate([grad_gate, grad_up], axis=1).astype(jnp.bfloat16)
    grad_h_three = reorder(
        jnp.einsum("nf,df->nd", grad_gu, gate_weight, preferred_element_type=jnp.float32), inverse
    )
    grad_gain_three = jnp.sum(grad_h_three * normed_three, axis=0)
    grad_x_two = grad_out + norm_back(grad_h_three * gain_three, normed_three, inverse_three)
    grad_cross = grad_x_two.astype(jnp.bfloat16)
    grad_cross_out = (
        reorder(
            jnp.einsum(
                "nd,ed->ne",
                grad_cross,
                gathered[:, 5 * D : 6 * D],
                preferred_element_type=jnp.float32,
            ),
            inverse,
        )
        .astype(jnp.bfloat16)
        .reshape(frames, head_count, HEAD)
    )
    grad_cross_probs = jnp.einsum(
        "qhd,khd->hqk", grad_cross_out, text_values, preferred_element_type=jnp.float32
    )
    grad_cross_scores = (
        cross_probs
        * (grad_cross_probs - jnp.sum(cross_probs * grad_cross_probs, axis=-1, keepdims=True))
    ).astype(jnp.bfloat16)
    grad_cross_q = (
        (
            jnp.einsum(
                "hqk,khd->qhd", grad_cross_scores, text_keys, preferred_element_type=jnp.float32
            )
            * score_scale
        )
        .reshape(frames, D)
        .astype(jnp.bfloat16)
    )
    grad_text_keys = (
        jnp.einsum("hqk,qhd->khd", grad_cross_scores, cross_q, preferred_element_type=jnp.float32)
        * score_scale
    )
    grad_text_values = jnp.einsum(
        "hqk,qhd->khd", cross_low, grad_cross_out, preferred_element_type=jnp.float32
    )
    grad_text = reorder(
        jnp.stack([grad_text_keys.reshape(CTX, D), grad_text_values.reshape(CTX, D)]), owners
    )
    grad_h_two = reorder(
        jnp.einsum(
            "ne,de->nd",
            grad_cross_q,
            gathered[:, 4 * D : 5 * D],
            preferred_element_type=jnp.float32,
        ),
        inverse,
    )
    grad_gain_two = jnp.sum(grad_h_two * normed_two, axis=0)
    grad_x_one = grad_x_two + norm_back(grad_h_two * gain_two, normed_two, inverse_two)
    grad_attn = grad_x_one.astype(jnp.bfloat16)
    grad_attn_out = (
        reorder(
            jnp.einsum(
                "nd,ed->ne",
                grad_attn,
                gathered[:, 3 * D : 4 * D],
                preferred_element_type=jnp.float32,
            ),
            inverse,
        )
        .astype(jnp.bfloat16)
        .reshape(frames, head_count, HEAD)
    )
    key_back, value_back = (key_all, value_all)

    def head_grads(head_items):
        head_probs, head_grad_out, head_values = head_items
        grad_probs = jnp.einsum(
            "qd,kd->qk", head_grad_out, head_values, preferred_element_type=jnp.float32
        )
        return (
            head_probs * (grad_probs - jnp.sum(head_probs * grad_probs, axis=-1, keepdims=True))
        ).astype(jnp.bfloat16)

    grad_scores_low = lax.map(
        head_grads, (attn_probs, jnp.swapaxes(grad_attn_out, 0, 1), jnp.swapaxes(value_back, 0, 1))
    )
    grad_queries = (
        jnp.einsum("hqk,khd->qhd", grad_scores_low, key_back, preferred_element_type=jnp.float32)
        * score_scale
    )
    grad_keys = (
        jnp.einsum("hqk,qhd->khd", grad_scores_low, queries, preferred_element_type=jnp.float32)
        * score_scale
    )
    grad_values = jnp.einsum(
        "hqk,qhd->khd", probs_low, grad_attn_out, preferred_element_type=jnp.float32
    )
    key_sums = lax.psum_scatter(
        jnp.concatenate(
            [
                grad_keys.reshape(frames * lax.axis_size("seq"), D),
                grad_values.reshape(frames * lax.axis_size("seq"), D),
            ],
            axis=1,
        ).astype(jnp.bfloat16),
        "seq",
        scatter_dimension=0,
        tiled=True,
    ).astype(jnp.float32)
    grad_q_raw = unrotate(grad_queries, cosine, sine_table).reshape(frames, D)
    grad_k_raw = unrotate(
        key_sums[:, :D].reshape(frames, head_count, HEAD), cosine, sine_table
    ).reshape(frames, D)
    grad_qkv = jnp.concatenate([grad_q_raw, grad_k_raw, key_sums[:, D:]], axis=1).astype(
        jnp.bfloat16
    )
    grad_h_one = reorder(
        jnp.einsum("ne,de->nd", grad_qkv, gathered[:, : 3 * D], preferred_element_type=jnp.float32),
        inverse,
    )
    grad_gain_one = jnp.sum(grad_h_one * normed_one * time_gain, axis=0)
    grad_time = jnp.sum(grad_h_one * normed_one * gain_one, axis=0)
    latent_grad = grad_x_one + norm_back(grad_h_one * scaled_one, normed_one, inverse_one)
    gain_grads = jnp.concatenate(
        [
            jnp.stack([grad_gain_one, grad_gain_two, grad_gain_three]),
            bucket_pick[:, None] * grad_time[None, :],
        ],
        axis=0,
    )
    gain_grads = reorder(gain_grads, owners).T
    text_float = text_tokens.astype(jnp.float32)
    pieces = [
        inner_rows(h_one_st, grad_qkv),
        inner_rows(attn_st, grad_attn),
        inner_rows(h_two_st, grad_cross_q),
        inner_rows(cross_st, grad_cross),
    ]
    pieces = pieces + [inner_rows(h_three_st, grad_gu), inner_rows(grad_ff_st, hidden)]
    pieces = pieces + [
        inner_rows_high(grad_text[0], text_float),
        inner_rows_high(grad_text[1], text_float),
        gain_grads,
    ]
    other_shard = lax.psum_scatter(
        jnp.concatenate(pieces, axis=1), ("dp", "seq"), scatter_dimension=0, tiled=True
    )
    total_squares = lax.psum(jnp.sum(other_shard * other_shard), ("dp", "seq"))
    grad_norm = jnp.sqrt(total_squares)
    clipped = other_shard / jnp.maximum(grad_norm, 1.0)
    gain_grad = clipped[:, 6 * D + 3 * FF + 2 * CTXW :]
    first_new = BETA_ONE * first + (1.0 - BETA_ONE) * clipped
    second_new = BETA_TWO * second + (1.0 - BETA_TWO) * clipped * clipped
    mean_hat = first_new / (1.0 - BETA_ONE**STEP)
    square_hat = second_new / (1.0 - BETA_TWO**STEP)
    rates = column_spread(length)[None, :]
    sheet_new = sheet - rates * (
        mean_hat / (jnp.sqrt(square_hat) + EPS_ADAM) + WEIGHT_DECAY * sheet
    )
    return (
        result.astype(jnp.bfloat16)[None],
        latent_grad[None],
        grad_norm,
        clipped,
        gain_grad,
        first_new,
        second_new,
        sheet_new,
        sheet_new.astype(jnp.bfloat16),
    )


PLANE = ("dp", "core")


def norm_columns(values):
    average = jnp.mean(values, axis=0, keepdims=True)
    centered = values - average
    variance = jnp.mean(centered * centered, axis=0, keepdims=True)
    inverse_std = lax.rsqrt(variance + EPS_NORM)
    return (centered * inverse_std, inverse_std)


def norm_columns_back(grad_normed, normed, inverse_std):
    return inverse_std * (
        grad_normed
        - jnp.mean(grad_normed, axis=0, keepdims=True)
        - normed * jnp.mean(grad_normed * normed, axis=0, keepdims=True)
    )


def rotate_columns(values, cosine, sine_table):
    half_dim = HEAD // 2
    first_half = values[:, :half_dim]
    second_half = values[:, half_dim:]
    return jnp.concatenate(
        [
            first_half * cosine - second_half * sine_table,
            second_half * cosine + first_half * sine_table,
        ],
        axis=1,
    )


def contract_rows(left, right):
    return lax.dot_general(
        left, right, (((0,), (0,)), ((), ())), preferred_element_type=jnp.float32
    )


def contract_last(left, right):
    return lax.dot_general(
        left, right, (((1,), (1,)), ((), ())), preferred_element_type=jnp.float32
    )


def matmul(left, right):
    return jnp.dot(left, right, preferred_element_type=jnp.float32)


MESH_ID = pl.DeviceIdType.MESH
IDENTITIES = {}


def identity_of(name, *arrays):
    key = (name,) + tuple((array.shape, str(array.dtype)) for array in arrays)
    return IDENTITIES.setdefault(key, len(IDENTITIES))


IN_HBM = pl.BlockSpec(memory_space=pltpu.HBM)
IN_SMEM = pl.BlockSpec(memory_space=pltpu.SMEM)
IN_VMEM = pl.BlockSpec(memory_space=pltpu.VMEM)
BRIEF = pl.CostEstimate(flops=0, bytes_accessed=1024, transcendentals=0)


def reorder_blocks(source, target, order):
    rows = source.shape[1]

    @pl.loop(0, source.shape[0])
    def _(b):
        target[pl.ds(pl.multiple_of(b * rows, 16), rows), :] = source[order(b)]


def wide(ref):
    return ref[...].astype(jnp.float32)


def greet(peers):
    barrier = pltpu.get_barrier_semaphore()
    for peer in peers:
        pl.semaphore_signal(barrier, inc=1, device_id=peer, device_id_type=MESH_ID)
    pl.semaphore_wait(barrier, len(peers))


def near():
    group, core = lax.axis_index("dp"), lax.axis_index("core")
    across = group + 1 - 2 * lax.rem(group, 2)
    along = lax.rem(group + 2, 4)
    return group, core, across, along


def member_rows(width):
    def place(ref, member, start, count):
        first_row = pl.multiple_of(member * width + start, 16)
        return ref.at[pl.ds(first_row, count), :]

    return place


def member_lanes(width):
    def place(ref, member, start, count):
        return ref.at[pl.ds(start, count), pl.ds(pl.multiple_of(member * width, 128), width)]

    return place


def mover(send_sem, recv_sem, first=0):
    def copy(k, source, target, peer):
        return pltpu.make_async_remote_copy(
            src_ref=source,
            dst_ref=target,
            send_sem=send_sem.at[first + k],
            recv_sem=recv_sem.at[first + k],
            device_id=peer,
            device_id_type=MESH_ID,
        )

    return copy


def member_at(member):
    return {"dp": lax.div(member, 2), "core": lax.rem(member, 2)}


def plane_peers():
    group, core, _, _ = near()
    member = group * 2 + core
    return [lax.rem(member + step, 8) for step in range(1, 8)]


def gather_steps(place, x_ref, o_ref, local_sem, copy, arrived_whole=lambda member: None):
    group, core, across, along = near()
    beyond = across + along - group
    other = 1 - core
    sibling, by_x, by_y = {"core": other}, {"dp": across}, {"dp": along}
    half = x_ref.shape[0] // 2

    def part(owner, owner_core, piece):
        return place(o_ref, owner * 2 + owner_core, piece * half, half)

    sent = []

    def send(k, source, target, peer):
        moving = copy(k, source, target, peer)
        moving.start()
        sent.append(moving)

    def own(k, piece, peer):
        send(k, x_ref.at[pl.ds(piece * half, half), :], part(group, core, piece), peer)

    def relay(k, owner, piece, peer):
        send(k, part(owner, core, piece), part(owner, core, piece), peer)

    def arrived(k, owner, owner_core, piece):
        landed = part(owner, owner_core, piece)
        copy(k, landed, landed, sibling).wait_recv()

    local = pltpu.make_async_copy(
        x_ref, place(o_ref, group * 2 + core, 0, 2 * half), local_sem
    )
    local.start()
    own(0, 0, by_x)
    own(1, 1, by_y)
    own(2, 1, by_x)
    own(3, 0, by_y)
    own(4, 0, sibling)
    own(5, 1, sibling)

    def finish():
        local.wait()
        arrived_whole(group * 2 + core)
        arrived(4, group, other, 0)
        arrived(5, group, other, 1)
        arrived_whole(group * 2 + other)
        arrived(0, across, core, 0)
        relay(6, across, 0, by_y)
        relay(7, across, 0, sibling)
        arrived(1, along, core, 1)
        relay(8, along, 1, by_x)
        relay(9, along, 1, sibling)
        arrived(2, across, core, 1)
        relay(10, across, 1, sibling)
        arrived_whole(across * 2 + core)
        arrived(3, along, core, 0)
        relay(11, along, 0, sibling)
        arrived_whole(along * 2 + core)
        arrived(7, across, other, 0)
        arrived(10, across, other, 1)
        arrived_whole(across * 2 + other)
        arrived(6, beyond, core, 0)
        relay(12, beyond, 0, sibling)
        arrived(8, beyond, core, 1)
        relay(13, beyond, 1, sibling)
        arrived_whole(beyond * 2 + core)
        arrived(9, along, other, 1)
        arrived(11, along, other, 0)
        arrived_whole(along * 2 + other)
        arrived(12, beyond, other, 0)
        arrived(13, beyond, other, 1)
        arrived_whole(beyond * 2 + other)
        for moving in sent:
            moving.wait_send()

    return finish


def exchange_steps(source, target, x_ref, o_ref, local_sem, copy):
    group, core, _, _ = near()
    member = group * 2 + core
    local = pltpu.make_async_copy(source(x_ref, member), target(o_ref, member), local_sem)
    local.start()
    sent = []
    for k, peer in enumerate(plane_peers()):
        sent.append(copy(k, source(x_ref, peer), target(o_ref, member), member_at(peer)))
        sent[-1].start()

    def finish():
        for k in range(7):
            sender = lax.rem(member + 7 - k, 8)
            landed = target(o_ref, sender)
            copy(k, landed, landed, member_at(sender)).wait_recv()
        local.wait()
        for moving in sent:
            moving.wait_send()

    return finish


def gather_kernel(place, x_ref, *refs):
    o_ref, local_sem, send_sem, recv_sem = refs[-4:]
    _, core, across, along = near()
    greet([{"dp": across}, {"dp": along}, {"core": 1 - core}])
    gather_steps(place, x_ref, o_ref, local_sem, mover(send_sem, recv_sem))()


def plane_gather_call(shard, shape, place, kind, after):
    return pl.pallas_call(
        functools.partial(gather_kernel, place),
        out_shape=jax.ShapeDtypeStruct(shape, shard.dtype),
        in_specs=[IN_HBM] * (1 + len(after)),
        out_specs=IN_HBM,
        scratch_shapes=[
            pltpu.SemaphoreType.DMA,
            pltpu.SemaphoreType.DMA((14,)),
            pltpu.SemaphoreType.DMA((14,)),
        ],
        compiler_params=pltpu.CompilerParams(
            collective_id=identity_of(kind, shard, *after), has_side_effects=True
        ),
        cost_estimate=BRIEF,
        name="plane_gather",
    )(shard, *after)


def plane_gather(shard, after=()):
    rows, width = shard.shape
    return plane_gather_call(shard, (rows, 8 * width), member_lanes(width), "gather lanes", after)


def plane_gather_rows(shard, after=()):
    rows, width = shard.shape
    return plane_gather_call(shard, (8 * rows, width), member_rows(rows), "gather rows", after)


def scatter_steps(place, p_ref, bufs, copy):
    pair, total, from_x, from_y, relay = bufs
    group, core, across, along = near()
    beyond = across + along - group
    other = 1 - core
    sibling, by_x, by_y = {"core": other}, {"dp": across}, {"dp": along}
    rows = total.shape[1]
    half = rows // 2
    low, high = pl.ds(0, half), pl.ds(half, half)
    sent = []

    def send(k, source, target, peer):
        moving = copy(k, source, target, peer)
        moving.start()
        sent.append(moving)

    def arrived(k, target):
        copy(k, target, target, sibling).wait_recv()

    def both_cores(k, owner):
        arrived(k, pair.at[k])
        summed = wide(place(p_ref, owner * 2 + core, 0, rows)) + wide(pair.at[k])
        total[k] = summed.astype(total.dtype)

    def cores():
        for k, owner in enumerate((beyond, across, along, group)):
            send(k, place(p_ref, owner * 2 + other, 0, rows), pair.at[k], sibling)

    def chips():
        both_cores(0, beyond)
        send(4, total.at[0, low], relay.at[0], by_x)
        send(5, total.at[0, high], relay.at[1], by_y)
        both_cores(1, across)
        send(6, total.at[1, low], from_x.at[low], by_x)
        both_cores(2, along)
        send(7, total.at[2, high], from_y.at[high], by_y)
        both_cores(3, group)

    def relays():
        arrived(5, relay.at[1])
        total[1, high] = (wide(total.at[1, high]) + wide(relay.at[1])).astype(total.dtype)
        send(8, total.at[1, high], from_x.at[high], by_x)
        arrived(4, relay.at[0])
        total[2, low] = (wide(total.at[2, low]) + wide(relay.at[0])).astype(total.dtype)
        send(9, total.at[2, low], from_y.at[low], by_y)

    def finish():
        arrived(6, from_x.at[low])
        arrived(7, from_y.at[high])
        arrived(8, from_x.at[high])
        arrived(9, from_y.at[low])
        summed = wide(total.at[3]) + wide(from_x) + wide(from_y)
        for moving in sent:
            moving.wait_send()
        return summed

    return cores, chips, relays, finish


def scatter_bufs(rows, width):
    slot = pltpu.VMEM((rows, width), jnp.bfloat16)
    four = pltpu.VMEM((4, rows, width), jnp.bfloat16)
    return [four, four, slot, slot, pltpu.VMEM((2, rows // 2, width), jnp.bfloat16)]


def scatter_kernel(place, p_ref, *refs):
    o_ref, *bufs, send_sem, recv_sem = refs[-8:]
    _, core, across, along = near()
    greet([{"dp": across}, {"dp": along}, {"core": 1 - core}])
    cores, chips, relays, finish = scatter_steps(place, p_ref, bufs, mover(send_sem, recv_sem))
    cores()
    chips()
    relays()
    o_ref[...] = finish().astype(o_ref.dtype)


def plane_scatter_call(partial, shape, place, dtype, kind, after):
    rows, width = shape
    return pl.pallas_call(
        functools.partial(scatter_kernel, place),
        out_shape=jax.ShapeDtypeStruct(shape, dtype),
        in_specs=[IN_VMEM] + [IN_HBM] * len(after),
        out_specs=IN_VMEM,
        scratch_shapes=scatter_bufs(rows, width)
        + [
            pltpu.SemaphoreType.DMA((10,)),
            pltpu.SemaphoreType.DMA((10,)),
        ],
        compiler_params=pltpu.CompilerParams(
            collective_id=identity_of(kind, partial, *after),
            has_side_effects=True,
            vmem_limit_bytes=24 * 2**20,
        ),
        cost_estimate=BRIEF,
        name="plane_scatter",
    )(partial, *after)


def plane_scatter_frames(partial, after=()):
    rows, width = partial.shape[0], partial.shape[1] // 8
    place = member_lanes(width)
    return plane_scatter_call(partial, (rows, width), place, jnp.float32, "scatter lanes", after)


def plane_scatter_rows(partial, after=()):
    rows, width = partial.shape[0] // 8, partial.shape[1]
    place = member_rows(rows)
    return plane_scatter_call(partial, (rows, width), place, jnp.bfloat16, "scatter rows", after)


def project_kernel(kind, order_ref, s_ref, w_ref, base_ref, gain_ref, side_ref, *refs):
    full_ref, x_ref, n_ref, i_ref, h_ref, side_out, *refs = refs
    full, total, part, landed, shard, by_block, base, gain, residual, normed, *refs = refs
    heads, weight, *bufs, local_sem, send_sem, recv_sem = refs
    rows, length = s_ref.shape
    width = base_ref.shape[1]
    fetches = [
        pltpu.make_async_copy(ref, held, local_sem.at[8 + k])
        for k, (ref, held) in enumerate(
            [(s_ref, heads), (w_ref, weight), (base_ref, base), (gain_ref, gain)]
            + ([(side_ref, bufs[-1])] if kind == "sum" else [])
        )
    ]
    for fetch in fetches:
        fetch.start()
    greet([member_at(peer) for peer in plane_peers()])
    side = mover(send_sem, recv_sem, 35)
    if kind == "sum":
        cores, chips, relays, finish = scatter_steps(
            member_rows(side_out.shape[0]), bufs[-1], bufs[:-1], side
        )
        fetches[4].wait()
        cores()
    fetches[0].wait()
    fetches[1].wait()
    total[...] = jnp.zeros_like(total)

    def add(member):
        first = pl.multiple_of(member * rows, 16)

        @pl.loop(0, length // 256)
        def _(i):
            at = pl.ds(pl.multiple_of(i * 256, 256), 256)
            total[:, at] += jnp.dot(
                weight[member], full[pl.ds(first, rows), at], preferred_element_type=jnp.float32
            )

    gathered = gather_steps(
        member_rows(rows), heads, full, local_sem.at[0], mover(send_sem, recv_sem), add
    )
    if kind == "sum":
        chips()
    else:
        side_done = gather_steps(
            member_lanes(width), side_ref, side_out, local_sem.at[7], side
        )
    gathered()
    kept = pltpu.make_async_copy(full, full_ref, local_sem.at[0])
    kept.start()
    part[...] = total[...].astype(part.dtype)
    exchanged = exchange_steps(
        whole_lanes(rows, width),
        whole_rows(rows),
        part,
        landed,
        local_sem.at[3],
        mover(send_sem, recv_sem, 14),
    )
    if kind == "sum":
        relays()
    exchanged()
    fetches[2].wait()
    fetches[3].wait()
    residual[...] = base[...] + wide(landed)
    standard, inverse_std = norm_columns(residual[...])
    normed[...] = standard
    i_ref[...] = inverse_std
    scaled = (standard * gain[...]).astype(shard.dtype)
    if kind == "gather":
        by_block[...] = scaled.reshape(by_block.shape)
        reorder_blocks(by_block, shard, lambda b: order_ref[0, b])
    else:
        shard[...] = scaled
    gathered = gather_steps(
        member_lanes(width), shard, h_ref, local_sem.at[4], mover(send_sem, recv_sem, 21)
    )
    x_copy = pltpu.make_async_copy(residual, x_ref, local_sem.at[5])
    x_copy.start()
    n_copy = pltpu.make_async_copy(normed, n_ref, local_sem.at[6])
    n_copy.start()
    if kind == "sum":
        side_out[...] = finish().astype(side_out.dtype)
    else:
        side_done()
    gathered()
    kept.wait()
    x_copy.wait()
    n_copy.wait()


def project(kind, orders, heads, weight, base, gain, side):
    rows, length = heads.shape
    features, width = base.shape
    by_member = weight.reshape(8, rows, rows).swapaxes(1, 2)
    whole = jax.ShapeDtypeStruct((features, length), jnp.bfloat16)
    frames = jax.ShapeDtypeStruct(base.shape, jnp.float32)
    if kind == "sum":
        side_out = jax.ShapeDtypeStruct((side.shape[0] // 8, side.shape[1]), side.dtype)
        bufs, at = scatter_bufs(*side_out.shape), IN_VMEM
        bufs.append(pltpu.VMEM(side.shape, side.dtype))
    else:
        side_out, bufs, at = whole, [], IN_HBM
    low, high = pltpu.VMEM(base.shape, jnp.bfloat16), pltpu.VMEM(base.shape, jnp.float32)
    return pl.pallas_call(
        functools.partial(project_kernel, kind),
        out_shape=(whole, frames, frames, jax.ShapeDtypeStruct((1, width), jnp.float32), whole)
        + (side_out,),
        in_specs=[IN_SMEM] + [IN_HBM] * 5,
        out_specs=(IN_HBM, IN_HBM, IN_HBM, IN_VMEM, IN_HBM, at),
        scratch_shapes=[
            pltpu.VMEM((features, length), jnp.bfloat16),
            pltpu.VMEM((rows, length), jnp.float32),
            pltpu.VMEM((rows, length), jnp.bfloat16),
            low,
            low,
            pltpu.VMEM((orders.shape[1], features // orders.shape[1], width), jnp.bfloat16),
            high,
            pltpu.VMEM(gain.shape, jnp.float32),
            high,
            high,
            pltpu.VMEM(heads.shape, heads.dtype),
            pltpu.VMEM(by_member.shape, by_member.dtype),
        ]
        + bufs
        + [
            pltpu.SemaphoreType.DMA((13,)),
            pltpu.SemaphoreType.DMA((49,)),
            pltpu.SemaphoreType.DMA((49,)),
        ],
        compiler_params=pltpu.CompilerParams(
            collective_id=identity_of("project " + kind, heads),
            has_side_effects=True,
            vmem_limit_bytes=32 * 2**20,
        ),
        cost_estimate=BRIEF,
        name="project_" + kind,
    )(orders, heads, by_member, base, gain, side)


def back_kernel(plan, *refs):
    by_rows, send_rows, text, in_slots, after = plan
    refs = list(refs)

    def take(count):
        taken = refs[:count]
        del refs[:count]
        return taken

    order_ref = take(1)[0]
    sources = take(3 if by_rows else 7)
    text_ref = take(1)[0] if text else None
    take(after)
    o_ref, own_out = take(2)
    sum_ref = None if by_rows else take(1)[0]
    rows_ref = take(1)[0] if send_rows else None
    text_out = take(1)[0] if text else None
    held = take(len(sources))
    w_ref, g_ref, act, *norms = held
    results = take(0 if by_rows else 2)
    mine, theirs, pair, from_x, from_y, relay, shard, slots, own_ref = take(9)
    local_sem, send_sem, recv_sem = refs
    fetches = [
        pltpu.make_async_copy(ref, here, local_sem.at[4 + k])
        for k, (ref, here) in enumerate(zip(sources, held))
    ]
    for fetch in fetches:
        fetch.start()

    group, core, across, along = near()
    beyond = across + along - group
    sibling, by_x, by_y = {"core": 1 - core}, {"dp": across}, {"dp": along}
    rows, width = mine.shape[1:]
    half = rows // 2
    low, high = pl.ds(0, half), pl.ds(half, half)
    copy = mover(send_sem, recv_sem)
    sent = []

    def send(k, source, target, peer):
        moving = copy(k, source, target, peer)
        moving.start()
        sent.append(moving)

    def arrived(k, target):
        copy(k, target, target, sibling).wait_recv()

    def split(k, at_rows, at_lanes, first, second):
        mine[k, at_rows, at_lanes] = jnp.where(core == 0, first, second).astype(mine.dtype)
        theirs[k, at_rows, at_lanes] = jnp.where(core == 0, second, first).astype(mine.dtype)

    def work_out(k, owner):
        if by_rows:

            @pl.loop(0, width // 256)
            def _(i):
                at = pl.ds(pl.multiple_of(i * 256, 256), 256)
                both = jnp.dot(
                    w_ref[pl.ds(pl.multiple_of(owner * 2 * rows, 16), 2 * rows), :],
                    g_ref[:, at],
                    preferred_element_type=jnp.float32,
                )
                split(k, slice(None), at, both[:rows], both[rows:])

        else:

            @pl.loop(0, rows // 256)
            def _(i):
                at = pl.ds(pl.multiple_of(i * 256, 256), 256)
                both = jnp.dot(
                    w_ref[at, :],
                    g_ref[:, pl.ds(pl.multiple_of(owner * 2 * width, 256), 2 * width)],
                    preferred_element_type=jnp.float32,
                )
                split(k, at, slice(None), both[:, :width], both[:, width:])

        send(k, theirs.at[k], pair.at[k], sibling)

    def both_cores(k):
        arrived(k, pair.at[k])
        mine[k] = (wide(mine.at[k]) + wide(pair.at[k])).astype(mine.dtype)

    def weight_grads(first, last):
        rows_of = act if in_slots else slots
        tile, count = rows_of.shape[0] // 6, g_ref.shape[0]

        @pl.loop(first, last)
        def _(i):
            at = pl.ds(pl.multiple_of(i * tile, tile), tile)
            for j in range(0, count, 256):
                of = slice(j, min(j + 256, count))
                own_ref[at, of] = contract_last(rows_of[at, :], g_ref[of, :]).astype(
                    own_ref.dtype
                )

    if send_rows or text:
        greet([member_at(peer) for peer in plane_peers()])
    else:
        greet([by_x, by_y, sibling])
    fetches[0].wait()
    fetches[1].wait()
    for k, owner in enumerate((beyond, across, along, group)):
        work_out(k, owner)
        if k == 1:
            both_cores(0)
            send(4, mine.at[0, low], relay.at[0], by_x)
            send(5, mine.at[0, high], relay.at[1], by_y)
        if k == 2:
            both_cores(1)
            send(6, mine.at[1, low], from_x.at[low], by_x)
        if k == 3:
            both_cores(2)
            send(7, mine.at[2, high], from_y.at[high], by_y)
    if text:
        text_done = gather_steps(
            member_rows(text_ref.shape[0]),
            text_ref,
            text_out,
            local_sem.at[1],
            mover(send_sem, recv_sem, 17),
        )
    fetches[2].wait()
    if not in_slots:
        reorder_blocks(act, slots, lambda b: order_ref[0, b])
    weight_grads(0, 2)
    arrived(5, relay.at[1])
    mine[1, high] = (wide(mine.at[1, high]) + wide(relay.at[1])).astype(mine.dtype)
    send(8, mine.at[1, high], from_x.at[high], by_x)
    arrived(4, relay.at[0])
    mine[2, low] = (wide(mine.at[2, low]) + wide(relay.at[0])).astype(mine.dtype)
    send(9, mine.at[2, low], from_y.at[low], by_y)
    both_cores(3)
    weight_grads(2, 6)
    own_copy = pltpu.make_async_copy(own_ref, own_out, local_sem.at[2])
    own_copy.start()
    arrived(6, from_x.at[low])
    arrived(7, from_y.at[high])
    arrived(8, from_x.at[high])
    arrived(9, from_y.at[low])
    summed = wide(mine.at[3]) + wide(from_x) + wide(from_y)
    if by_rows:
        shard[...] = summed.astype(shard.dtype)
        result_copy = pltpu.make_async_copy(shard, o_ref, local_sem.at[3])
        result_copy.start()
    else:
        for fetch in fetches[3:]:
            fetch.wait()
        normed, inverse_std, gain, base = norms
        result, by_block = results
        if in_slots:
            by_block[...] = summed.reshape(by_block.shape)
            reorder_blocks(by_block, result, lambda b: order_ref[1, b])
            summed = result[...]
        result[...] = base[...] + norm_columns_back(
            summed * gain[...], normed[...], inverse_std[...]
        )
        result_copy = pltpu.make_async_copy(result, o_ref, local_sem.at[3])
        result_copy.start()
        if send_rows:
            shard[...] = result[...].astype(shard.dtype)
            rows_done = exchange_steps(
                whole_rows(rows // 8),
                whole_lanes(rows // 8, width),
                shard,
                rows_ref,
                local_sem.at[0],
                mover(send_sem, recv_sem, 10),
            )
        sum_ref[...] = lax.dot_general(
            jnp.ones((8, width), jnp.float32),
            summed * normed[...],
            (((1,), (1,)), ((), ())),
            precision=HIGHEST,
            preferred_element_type=jnp.float32,
        )
        if send_rows:
            rows_done()
    result_copy.wait()
    own_copy.wait()
    if text:
        text_done()
    for moving in sent:
        moving.wait_send()


def back(orders, weight, grad, act, norm=None, send_rows=False, text=None, in_slots=False, after=()):
    by_rows = norm is None
    features, length = weight.shape[0], grad.shape[1]
    shape = (features // 8, length) if by_rows else (features, length // 8)
    small = jnp.bfloat16
    own = jax.ShapeDtypeStruct((features, grad.shape[0]), small)
    outs = [jax.ShapeDtypeStruct(shape, small if by_rows else jnp.float32), own]
    specs = [IN_HBM, IN_HBM]
    if not by_rows:
        outs.append(jax.ShapeDtypeStruct((8, features), jnp.float32))
        specs.append(IN_VMEM)
    if send_rows:
        outs.append(jax.ShapeDtypeStruct((features // 8, length), small))
        specs.append(IN_HBM)
    count = orders.shape[1]
    if not in_slots:
        act = act.reshape(count, features // count, length)
    sources = [weight, grad, act] + list(norm or ())
    operands = [orders] + sources
    if text is not None:
        operands.append(text)
        outs.append(jax.ShapeDtypeStruct((8 * text.shape[0], text.shape[1]), text.dtype))
        specs.append(IN_HBM)
    operands += list(after)
    plan = (by_rows, send_rows, text is not None, in_slots, len(after))
    rows, width = shape
    four, slot = pltpu.VMEM((4, rows, width), small), pltpu.VMEM((rows, width), small)
    return pl.pallas_call(
        functools.partial(back_kernel, plan),
        out_shape=tuple(outs),
        in_specs=[IN_SMEM] + [IN_HBM] * (len(operands) - 1),
        out_specs=tuple(specs),
        scratch_shapes=[pltpu.VMEM(array.shape, array.dtype) for array in sources]
        + (
            []
            if by_rows
            else [
                pltpu.VMEM(shape, jnp.float32),
                pltpu.VMEM((count, rows // count, width), jnp.float32),
            ]
        )
        + [four, four, four, slot, slot, pltpu.VMEM((2, rows // 2, width), small), slot]
        + [
            pltpu.VMEM((16, 128) if in_slots else (features, length), small),
            pltpu.VMEM(own.shape, small),
            pltpu.SemaphoreType.DMA((11,)),
            pltpu.SemaphoreType.DMA((31,)),
            pltpu.SemaphoreType.DMA((31,)),
        ],
        compiler_params=pltpu.CompilerParams(
            collective_id=identity_of("back" + str(plan), *operands),
            has_side_effects=True,
            vmem_limit_bytes=44 * 2**20,
        ),
        cost_estimate=BRIEF,
        name="back",
    )(*operands)


def exchange_kernel(source, target, x_ref, *refs):
    o_ref, local_sem, send_sem, recv_sem = refs[-4:]
    greet([member_at(peer) for peer in plane_peers()])
    exchange_steps(source, target, x_ref, o_ref, local_sem, mover(send_sem, recv_sem))()


def exchange(array, shape, source, target, kind, after=()):
    return pl.pallas_call(
        functools.partial(exchange_kernel, source, target),
        out_shape=jax.ShapeDtypeStruct(shape, array.dtype),
        in_specs=[IN_HBM] * (1 + len(after)),
        out_specs=IN_HBM,
        scratch_shapes=[
            pltpu.SemaphoreType.DMA,
            pltpu.SemaphoreType.DMA((7,)),
            pltpu.SemaphoreType.DMA((7,)),
        ],
        compiler_params=pltpu.CompilerParams(
            collective_id=identity_of(kind, array, *after), has_side_effects=True
        ),
        cost_estimate=BRIEF,
        name="plane_exchange",
    )(array, *after)


def whole_rows(rows):
    place = member_rows(rows)
    return lambda ref, member: place(ref, member, 0, rows)


def whole_lanes(rows, width):
    place = member_lanes(width)
    return lambda ref, member: place(ref, member, 0, rows)


def to_frames(part):
    rows, width = part.shape[0], part.shape[1] // 8
    return exchange(part, (8 * rows, width), whole_lanes(rows, width), whole_rows(rows), "to frames")


def to_rows(part):
    rows, width = part.shape[0] // 8, part.shape[1]
    return exchange(part, (rows, 8 * width), whole_rows(rows), whole_lanes(rows, width), "to rows")


def block(ref, member):
    return ref.at[member]


def exchange_blocks(blocks, after=()):
    return exchange(blocks, blocks.shape, block, block, "blocks", after)


def lanes(ref, start, width):
    return ref.at[:, pl.ds(pl.multiple_of(start, 128), width)]


def sheet_part(start, width):
    return lambda ref, member: lanes(ref, start + member * width, width)


def block_part(start, width):
    return lambda ref, member: lanes(ref.at[member], start, width)


def feed_kernel(gu_ref, down_ref, p_ref, *refs):
    o_ref, y_ref, part, summed, *bufs, local_sem, send_sem, recv_sem = refs[-12:]
    width = down_ref.shape[-1]
    fetch = pltpu.make_async_copy(p_ref, part, local_sem.at[3])
    fetch.start()
    greet([member_at(peer) for peer in plane_peers()])
    cores, chips, relays, ended = scatter_steps(
        member_lanes(y_ref.shape[1]), part, bufs, mover(send_sem, recv_sem, 21)
    )
    fetch.wait()
    cores()
    chips()
    finish = []
    for k, (ref, start) in enumerate(((gu_ref, 0), (gu_ref, width), (down_ref, 0))):
        source, target = block_part(start, width), sheet_part(8 * k * width, width)
        copy = mover(send_sem, recv_sem, 7 * k)
        finish.append(exchange_steps(source, target, ref, o_ref, local_sem.at[k], copy))
    relays()
    summed[...] = ended()
    kept = pltpu.make_async_copy(summed, y_ref, local_sem.at[4])
    kept.start()
    for end in finish:
        end()
    kept.wait()


def feed(gu, down, partial, after=()):
    rows, width = partial.shape[0], partial.shape[1] // 8
    return pl.pallas_call(
        feed_kernel,
        out_shape=(
            jax.ShapeDtypeStruct((gu.shape[1], 24 * down.shape[-1]), gu.dtype),
            jax.ShapeDtypeStruct((rows, width), jnp.float32),
        ),
        in_specs=[IN_HBM] * (3 + len(after)),
        out_specs=(IN_HBM, IN_HBM),
        scratch_shapes=[
            pltpu.VMEM(partial.shape, partial.dtype),
            pltpu.VMEM((rows, width), jnp.float32),
        ]
        + scatter_bufs(rows, width)
        + [
            pltpu.SemaphoreType.DMA((5,)),
            pltpu.SemaphoreType.DMA((31,)),
            pltpu.SemaphoreType.DMA((31,)),
        ],
        compiler_params=pltpu.CompilerParams(
            collective_id=identity_of("feed", gu, down, *after),
            has_side_effects=True,
            vmem_limit_bytes=24 * 2**20,
        ),
        cost_estimate=BRIEF,
        name="feed",
    )(gu, down, partial, *after)


def opening_kernel(
    x_ref,
    small_ref,
    text_ref,
    w_ref,
    v_ref,
    t_ref,
    all_ref,
    mine_ref,
    wo_ref,
    vo_ref,
    held,
    local_sem,
    send_sem,
    recv_sem,
):
    group, core, _, _ = near()
    member = group * 2 + core
    plane = lax.axis_index("z")
    step = x_ref.shape[0] // 4
    text_rows = mine_ref.shape[0]
    teacher = jnp.logical_and(group == plane, core == 0)

    def frames(ref, j):
        return ref.at[pl.ds(pl.multiple_of(j * step, 16), step), :]

    peers = plane_peers()
    line = [lax.rem(plane + k, 4) for k in range(1, 4)]
    greet([member_at(peer) for peer in peers] + [{"z": there} for there in line])

    near_copy = mover(send_sem, recv_sem)
    line_copy = mover(send_sem, recv_sem, 7)
    small_local = pltpu.make_async_copy(small_ref, all_ref.at[plane, member], local_sem.at[0])
    small_local.start()
    first = [
        near_copy(k, small_ref, all_ref.at[plane, member], member_at(peer))
        for k, peer in enumerate(peers)
    ]
    for moving in first:
        moving.start()

    others = [lax.rem(group + k, 4) for k in range(1, 4)]
    keep = pltpu.make_async_copy(frames(x_ref, group), frames(held, group), local_sem.at[1])
    keep.start()

    def spread(owner, landing):
        return pltpu.make_async_remote_copy(
            src_ref=frames(x_ref, owner),
            dst_ref=frames(held, landing),
            send_sem=send_sem.at[10 + owner],
            recv_sem=recv_sem.at[10 + landing],
            device_id={"dp": owner},
            device_id_type=MESH_ID,
        )

    for owner in others:
        spread(owner, group).start()

    def rise(row):
        return pltpu.make_async_remote_copy(
            src_ref=frames(held, row),
            dst_ref=frames(t_ref, plane),
            send_sem=send_sem.at[28 + row],
            recv_sem=recv_sem.at[28 + plane],
            device_id={"z": row},
            device_id_type=MESH_ID,
        )

    stay = pltpu.make_async_copy(frames(held, plane), frames(t_ref, plane), local_sem.at[4])

    def pass_on(row):
        pl.when(row == plane)(stay.start)
        pl.when(row != plane)(rise(row).start)

    first_done = exchange_steps(
        block, block, w_ref, wo_ref, local_sem.at[2], mover(send_sem, recv_sem, 14)
    )
    second_done = exchange_steps(
        block, block, v_ref, vo_ref, local_sem.at[5], mover(send_sem, recv_sem, 32)
    )

    def text_copy(k, peer):
        return pltpu.make_async_remote_copy(
            src_ref=text_ref.at[pl.ds(pl.multiple_of(peer * text_rows, 16), text_rows), :],
            dst_ref=mine_ref,
            send_sem=send_sem.at[21 + k],
            recv_sem=recv_sem.at[21],
            device_id=member_at(peer),
            device_id_type=MESH_ID,
        )

    own_text = text_ref.at[pl.ds(pl.multiple_of(member * text_rows, 16), text_rows), :]
    text_local = pltpu.make_async_copy(own_text, mine_ref, local_sem.at[3])

    @pl.when(teacher)
    def _():
        text_local.start()
        for k, peer in enumerate(peers):
            text_copy(k, peer).start()

    keep.wait()
    pass_on(group)
    for owner in others:
        spread(owner, owner).wait_recv()
        pass_on(owner)

    for k in range(7):
        landed = all_ref.at[plane, lax.rem(member + 7 - k, 8)]
        near_copy(k, landed, landed, member_at(peers[k])).wait_recv()
    small_local.wait()
    second = [
        line_copy(k, all_ref.at[plane], all_ref.at[plane], {"z": there})
        for k, there in enumerate(line)
    ]
    for moving in second:
        moving.start()
    for k in range(3):
        landed = all_ref.at[lax.rem(plane + 3 - k, 4)]
        line_copy(k, landed, landed, {"z": line[k]}).wait_recv()

    for there in line:
        landed = frames(t_ref, there)
        pltpu.make_async_remote_copy(
            src_ref=landed,
            dst_ref=landed,
            send_sem=send_sem.at[28 + there],
            recv_sem=recv_sem.at[28 + there],
            device_id={"z": there},
            device_id_type=MESH_ID,
        ).wait_recv()
    stay.wait()
    first_done()
    second_done()

    @pl.when(teacher)
    def _():
        text_local.wait()
        for k, peer in enumerate(peers):
            text_copy(k, peer).wait_send()

    @pl.when(jnp.logical_not(teacher))
    def _():
        text_copy(0, peers[0]).wait_recv()

    for moving in first + second:
        moving.wait_send()
    for owner in others:
        spread(owner, group).wait_send()
    for there in line:
        rise(there).wait_send()


def opening(local, small, text, first, second):
    return pl.pallas_call(
        opening_kernel,
        out_shape=(
            jax.ShapeDtypeStruct(local.shape, local.dtype),
            jax.ShapeDtypeStruct((4, 8) + small.shape, small.dtype),
            jax.ShapeDtypeStruct((text.shape[0] // 8, text.shape[1]), text.dtype),
            jax.ShapeDtypeStruct(first.shape, first.dtype),
            jax.ShapeDtypeStruct(second.shape, second.dtype),
        ),
        in_specs=[IN_HBM] * 5,
        out_specs=(IN_HBM,) * 5,
        scratch_shapes=[
            pltpu.VMEM(local.shape, local.dtype),
            pltpu.SemaphoreType.DMA((6,)),
            pltpu.SemaphoreType.DMA((39,)),
            pltpu.SemaphoreType.DMA((39,)),
        ],
        compiler_params=pltpu.CompilerParams(
            collective_id=identity_of("opening", local), has_side_effects=True
        ),
        cost_estimate=BRIEF,
        name="opening",
    )(local, small, text, first, second)


def first_gather_kernel(
    x_ref, sheet_ref, o_ref, w_ref, v_ref, local_sem, send_sem, recv_sem
):
    place = member_lanes(x_ref.shape[1])
    width = FF // 8
    greet([member_at(peer) for peer in plane_peers()])
    finish = [
        gather_steps(place, x_ref, o_ref, local_sem.at[0], mover(send_sem, recv_sem))
    ]
    for k, (ref, start) in enumerate(((w_ref, 0), (w_ref, width), (v_ref, 0))):
        source, target = sheet_part(6 * D + k * FF, width), block_part(start, width)
        copy = mover(send_sem, recv_sem, 14 + 7 * k)
        finish.append(exchange_steps(source, target, sheet_ref, ref, local_sem.at[1 + k], copy))
    for end in finish:
        end()


def first_gather(shard, sheet):
    rows, width = shard.shape
    return pl.pallas_call(
        first_gather_kernel,
        out_shape=(
            jax.ShapeDtypeStruct((rows, 8 * width), shard.dtype),
            jax.ShapeDtypeStruct((8, sheet.shape[0], FF // 4), sheet.dtype),
            jax.ShapeDtypeStruct((8, sheet.shape[0], FF // 8), sheet.dtype),
        ),
        in_specs=[IN_HBM] * 2,
        out_specs=(IN_HBM,) * 3,
        scratch_shapes=[
            pltpu.SemaphoreType.DMA((4,)),
            pltpu.SemaphoreType.DMA((35,)),
            pltpu.SemaphoreType.DMA((35,)),
        ],
        compiler_params=pltpu.CompilerParams(
            collective_id=identity_of("first gather", shard, sheet), has_side_effects=True
        ),
        cost_estimate=BRIEF,
        name="first_gather",
    )(shard, sheet)


def closing_kernel(
    x_ref,
    w_ref,
    v_ref,
    g_ref,
    q_ref,
    t_ref,
    o_ref,
    vo_ref,
    s_ref,
    all_ref,
    held,
    tall,
    local_sem,
    send_sem,
    recv_sem,
):
    group, core, _, _ = near()
    member = group * 2 + core
    plane = lax.axis_index("z")
    step = x_ref.shape[0] // 4
    line = [lax.rem(plane + k, 4) for k in range(1, 4)]
    back = [lax.rem(plane + 3 - k, 4) for k in range(3)]
    groups = [lax.rem(group + k, 4) for k in range(1, 4)]
    peers = plane_peers()
    greet([member_at(peer) for peer in peers] + [{"z": there} for there in line])

    def frames(ref, j):
        return ref.at[pl.ds(pl.multiple_of(j * step, 16), step), :]

    copy = mover(send_sem, recv_sem)
    gain_line = mover(send_sem, recv_sem, 14)
    gain_plane = mover(send_sem, recv_sem, 17)
    square_plane = mover(send_sem, recv_sem, 24)
    square_line = mover(send_sem, recv_sem, 31)
    square_local = pltpu.make_async_copy(q_ref, all_ref.at[plane, member], local_sem.at[5])
    square_local.start()
    shown = [
        square_plane(k, q_ref, all_ref.at[plane, member], member_at(peer))
        for k, peer in enumerate(peers)
    ]
    for moving in shown:
        moving.start()
    gain_local = pltpu.make_async_copy(g_ref, tall.at[plane], local_sem.at[3])
    gain_local.start()
    sent = [gain_line(k, g_ref, tall.at[plane], {"z": there}) for k, there in enumerate(line)]
    local = pltpu.make_async_copy(frames(x_ref, plane), frames(held, plane), local_sem.at[0])
    local.start()
    sent += [
        copy(k, frames(x_ref, there), frames(held, plane), {"z": there})
        for k, there in enumerate(line)
    ]
    for moving in sent:
        moving.start()
    weights_done = exchange_steps(
        block, block, w_ref, o_ref, local_sem.at[1], mover(send_sem, recv_sem, 7)
    )
    others_done = exchange_steps(
        block, block, v_ref, vo_ref, local_sem.at[6], mover(send_sem, recv_sem, 34)
    )

    gain_local.wait()
    for k, origin in enumerate(back):
        gain_line(k, tall.at[origin], tall.at[origin], {"z": origin}).wait_recv()
    tall[4] = tall[0] + tall[1] + tall[2] + tall[3]
    gain_keep = pltpu.make_async_copy(tall.at[4], s_ref.at[member], local_sem.at[4])
    gain_keep.start()
    given = [
        gain_plane(k, tall.at[4], s_ref.at[member], member_at(peer)) for k, peer in enumerate(peers)
    ]
    for moving in given:
        moving.start()

    def onward(owner):
        return pltpu.make_async_remote_copy(
            src_ref=frames(held, owner),
            dst_ref=frames(t_ref, group),
            send_sem=send_sem.at[3 + owner],
            recv_sem=recv_sem.at[3 + group],
            device_id={"dp": owner},
            device_id_type=MESH_ID,
        )

    keep = pltpu.make_async_copy(frames(held, group), frames(t_ref, group), local_sem.at[2])

    def pass_on(owner):
        pl.when(owner == group)(keep.start)
        pl.when(owner != group)(onward(owner).start)

    square_local.wait()
    for k in range(7):
        landed = all_ref.at[plane, lax.rem(member + 7 - k, 8)]
        square_plane(k, landed, landed, member_at(peers[k])).wait_recv()
    for k, there in enumerate(line):
        shown.append(square_line(k, all_ref.at[plane], all_ref.at[plane], {"z": there}))
        shown[-1].start()
    local.wait()
    pass_on(plane)
    for k, origin in enumerate(back):
        landed = frames(held, origin)
        copy(k, landed, landed, {"z": origin}).wait_recv()
        pass_on(origin)
    for origin in groups:
        landed = frames(t_ref, origin)
        pltpu.make_async_remote_copy(
            src_ref=landed,
            dst_ref=landed,
            send_sem=send_sem.at[3 + origin],
            recv_sem=recv_sem.at[3 + origin],
            device_id={"dp": origin},
            device_id_type=MESH_ID,
        ).wait_recv()
    keep.wait()
    weights_done()
    others_done()
    gain_keep.wait()
    for k in range(7):
        landed = s_ref.at[lax.rem(member + 7 - k, 8)]
        gain_plane(k, landed, landed, member_at(peers[k])).wait_recv()
    for k, origin in enumerate(back):
        square_line(k, all_ref.at[origin], all_ref.at[origin], {"z": origin}).wait_recv()
    for moving in sent + given + shown:
        moving.wait_send()
    for origin in groups:
        onward(origin).wait_send()


def closing(local, weights, others, gains, squares):
    return pl.pallas_call(
        closing_kernel,
        out_shape=(
            jax.ShapeDtypeStruct(local.shape, local.dtype),
            jax.ShapeDtypeStruct(weights.shape, weights.dtype),
            jax.ShapeDtypeStruct(others.shape, others.dtype),
            jax.ShapeDtypeStruct((8,) + gains.shape, gains.dtype),
            jax.ShapeDtypeStruct((4, 8) + squares.shape, squares.dtype),
        ),
        in_specs=[IN_HBM] * 5,
        out_specs=(IN_HBM,) * 5,
        scratch_shapes=[
            pltpu.VMEM(local.shape, local.dtype),
            pltpu.VMEM((5,) + gains.shape, gains.dtype),
            pltpu.SemaphoreType.DMA((7,)),
            pltpu.SemaphoreType.DMA((41,)),
            pltpu.SemaphoreType.DMA((41,)),
        ],
        compiler_params=pltpu.CompilerParams(
            collective_id=identity_of("closing", local), has_side_effects=True
        ),
        cost_estimate=BRIEF,
        name="closing",
    )(local, weights, others, gains, squares)


def update_kernel(
    scale_ref, rate_ref, one_ref, two_ref, feed_ref, gain_ref, sheet_ref, first_ref, second_ref, *refs
):
    grad_out, first_out, second_out, sheet_out, copy_out, grad = refs
    step = pl.program_id(0)
    part = D // 8
    text = CTXW // 8
    for k in range(6):

        @pl.when(step == k)
        def _(k=k):
            ref, start = (one_ref, k * part) if k < 4 else (two_ref, (k - 4) * part)
            for m in range(8):
                grad[:, m * part : (m + 1) * part] = wide(ref.at[m, :, start : start + part])

    @pl.when(jnp.logical_and(step >= 6, step < 18))
    def _():
        grad[...] = wide(feed_ref)

    @pl.when(step == 18)
    def _():
        for m in range(8):
            for k in range(2):
                start = 2 * part + k * text
                place = k * CTXW + m * text
                grad[:, place : place + text] = wide(two_ref.at[m, :, start : start + text])

    @pl.when(step == 19)
    def _():
        grad[:, :128] = gain_ref[...]

    clipped = grad[...] * scale_ref[0]
    sheet = sheet_ref[...]
    first_new = BETA_ONE * first_ref[...] + (1.0 - BETA_ONE) * clipped
    second_new = BETA_TWO * second_ref[...] + (1.0 - BETA_TWO) * clipped * clipped
    mean_hat = first_new / (1.0 - BETA_ONE**STEP)
    square_hat = second_new / (1.0 - BETA_TWO**STEP)
    sheet_new = sheet - rate_ref[step] * (
        mean_hat / (jnp.sqrt(square_hat) + EPS_ADAM) + WEIGHT_DECAY * sheet
    )
    grad_out[...] = clipped
    first_out[...] = first_new
    second_out[...] = second_new
    sheet_out[...] = sheet_new
    copy_out[...] = sheet_new.astype(copy_out.dtype)


def sheet_update(scale, length, one, two, feed_part, gains, sheet, first, second):
    rows = sheet.shape[0]
    rates = column_spread(length)[jnp.minimum(jnp.arange(20) * D, SHEET - 1)]
    column_block = pl.BlockSpec((rows, D), lambda i: (0, i))
    like = jax.ShapeDtypeStruct(sheet.shape, sheet.dtype)
    return pl.pallas_call(
        update_kernel,
        grid=(20,),
        out_shape=(like, like, like, like, jax.ShapeDtypeStruct(sheet.shape, jnp.bfloat16)),
        in_specs=[
            IN_SMEM,
            IN_SMEM,
            pl.BlockSpec(one.shape, lambda i: (0, 0, 0)),
            pl.BlockSpec(two.shape, lambda i: (0, 0, 0)),
            pl.BlockSpec((rows, D), lambda i: (0, jnp.clip(i - 6, 0, 11))),
            pl.BlockSpec(gains.shape, lambda i: (0, 0)),
            column_block,
            column_block,
            column_block,
        ],
        out_specs=(column_block,) * 5,
        scratch_shapes=[pltpu.VMEM((rows, D), jnp.float32)],
        compiler_params=pltpu.CompilerParams(vmem_limit_bytes=24 * 2**20),
        name="sheet_update",
    )(scale.reshape(1), rates, one, two, feed_part, gains, sheet, first, second)


def split_columns(block, members):
    rows, columns = block.shape
    return block.reshape(rows, members, columns // members)


def pick_blocks(blocks, order):
    return blocks.at[order].get(mode="promise_in_bounds")


def gather_line(mine, order):
    blocks = lax.all_gather(mine, "z", axis=0, tiled=True)
    return pick_blocks(blocks, order).reshape(-1, mine.shape[-1])


def gather_slots(mine):
    return lax.all_gather(mine, "z", axis=0, tiled=True).reshape(-1, mine.shape[-1])


def sort_blocks(array, order):
    blocks = array.reshape(order.shape[0], -1, array.shape[-1])
    return pick_blocks(blocks, order).reshape(array.shape)


def as_blocks(grad, order):
    return grad.reshape(order.shape[0], -1, grad.shape[-1])


def scatter_line(blocks):
    return lax.psum_scatter(blocks, "z", scatter_dimension=0, tiled=True)


def plane_plan(latents, context, clip_starts, buckets, owners, cotangent, sheet, first, second):
    groups = lax.axis_size("dp")
    planes = lax.axis_size("z")
    cores = lax.axis_size("core")
    members = groups * cores
    frames = latents.shape[1]
    length = frames * members
    rows = sheet.shape[0]
    blocks = owners.shape[0]
    head_count = D // HEAD // members
    span = D // members
    units = FF // members
    score_scale = HEAD ** (-0.5)
    tail_col = 6 * D + 3 * FF
    gain_col = tail_col + 2 * CTXW
    plane = lax.axis_index("z")

    group_ids = jnp.arange(blocks, dtype=jnp.int32)
    inverse = jnp.sum(
        jnp.where(owners[None, :] == group_ids[:, None], group_ids[None, :], 0), axis=1
    )
    slot = group_ids.reshape(groups, planes, cores).swapaxes(0, 1).reshape(-1)
    slot_of = jnp.sum(
        jnp.where(slot[None, :] == group_ids[:, None], group_ids[None, :], 0), axis=1
    )
    to_logical = jnp.take(slot_of, inverse)
    to_slots = jnp.take(owners, slot)

    orders = jnp.stack([to_slots, to_logical])
    low_sheet = sheet.astype(jnp.bfloat16)

    def columns_of(start, width):
        return split_columns(low_sheet[:, start : start + width], members)

    def member_blocks(*pieces):
        return jnp.swapaxes(jnp.concatenate(pieces, axis=2), 0, 1)

    blocks_qkv = member_blocks(*[columns_of(k * D, D) for k in range(3)])
    blocks_two = member_blocks(
        columns_of(3 * D, D),
        columns_of(4 * D, D),
        columns_of(5 * D, D),
        columns_of(tail_col, CTXW),
        columns_of(tail_col + CTXW, CTXW),
    )
    small = jnp.concatenate(
        [
            jnp.pad(low_sheet[:, gain_col:].astype(jnp.float32).T, ((0, 0), (0, 64 - rows))),
            jnp.pad(clip_starts.astype(jnp.float32), ((0, 7), (0, 64 - clip_starts.shape[1]))),
        ],
        axis=1,
    )
    both, small, text_mine, mine_qkv, mine_two = opening(
        jnp.concatenate([latents[0], cotangent[0]], axis=1),
        small,
        context[0].T,
        blocks_qkv,
        blocks_two,
    )
    weight_qkv = gather_slots(mine_qkv)
    weight_two = gather_line(mine_two, to_logical)
    weight_ao = weight_two[:, :span]
    weight_cq = weight_two[:, span : 2 * span]
    weight_co = weight_two[:, 2 * span : 3 * span]
    weight_text = weight_two[:, 3 * span :]
    gains = pick_blocks(small[..., :rows].reshape(blocks, 8, rows), to_logical)
    gains = gains.swapaxes(1, 2).reshape(D, 8)
    starts = lax.dynamic_index_in_dim(
        small[0, :, 0, 64 : 64 + clip_starts.shape[1]], plane * cores, 0, False
    )
    starts = starts.astype(jnp.int32)

    bucket_ids = jnp.arange(NB, dtype=jnp.int32)
    bucket_pick = (bucket_ids == buckets[plane]).astype(jnp.float32)
    counts = jnp.sum((buckets[:, None] == bucket_ids[None, :]).astype(jnp.float32), axis=0)
    row_weight = buckets.shape[0] / (NB * jnp.sum(bucket_pick * counts))
    gain_one = gains[:, 0:1]
    gain_two = gains[:, 1:2]
    gain_three = gains[:, 2:3]
    time_gain = jnp.sum(gains[:, 3:] * bucket_pick[None, :], axis=1, keepdims=True)

    tokens = both[:, :D].astype(jnp.float32).T
    grad_out = both[:, D:].astype(jnp.float32).T * row_weight

    rest = frames // planes
    place = jnp.arange(length, dtype=jnp.int32).reshape(planes, cores, groups, rest)
    positions = place.transpose(2, 1, 0, 3).reshape(-1)
    segments = segment_ids(starts, positions)
    same_clip = segments[:, None] == segments[None, :]
    frequency = jnp.exp(
        -math.log(10000.0) * jnp.arange(HEAD // 2, dtype=jnp.float32) / (HEAD // 2)
    )
    angles = frequency[:, None] * positions.astype(jnp.float32)[None, :]
    cosine = jnp.cos(angles)[None]
    sine_table = jnp.sin(angles)[None]

    normed_one, inverse_one = norm_columns(tokens)
    scaled_one = gain_one * time_gain
    h_one, mine_gu, mine_down = first_gather(
        sort_blocks((normed_one * scaled_one).astype(jnp.bfloat16), to_slots), low_sheet
    )
    weight_gu = gather_slots(mine_gu)
    line_down = gather_slots(mine_down)

    joint = contract_rows(weight_qkv, h_one).reshape(3, head_count, HEAD, length)
    queries = rotate_columns(joint[0], cosine, sine_table).astype(jnp.bfloat16)
    keys = rotate_columns(joint[1], cosine, sine_table).astype(jnp.bfloat16)
    values = joint[2].astype(jnp.bfloat16)
    scores = (
        jnp.einsum("hdq,hdk->hqk", queries, keys, preferred_element_type=jnp.float32) * score_scale
    )
    attn_probs = softmax_rows(jnp.where(same_clip[None], scores, MASKED_SCORE))
    probs_low = attn_probs.astype(jnp.bfloat16)
    attn_out = jnp.einsum("hqk,hdk->hdq", probs_low, values, preferred_element_type=jnp.float32)
    text_width = CTXW // members
    text_kv = jnp.stack(
        [
            matmul(weight_text[:, :text_width], text_mine),
            matmul(weight_text[:, text_width:], text_mine),
        ],
        axis=1,
    ).reshape(D, 2 * CTX)
    attn_out, x_one, normed_two, inverse_two, h_two, text_kv = project(
        "sum",
        orders,
        attn_out.reshape(span, length).astype(jnp.bfloat16),
        weight_ao,
        tokens,
        gain_two,
        text_kv.astype(jnp.bfloat16),
    )

    text_kv = text_kv.reshape(head_count, HEAD, 2, CTX)
    text_keys = text_kv[:, :, 0]
    text_values = text_kv[:, :, 1]
    cross_q = contract_rows(weight_cq, h_two).astype(jnp.bfloat16).reshape(head_count, HEAD, length)
    cross_scores = (
        jnp.einsum("hdq,hdk->hqk", cross_q, text_keys, preferred_element_type=jnp.float32)
        * score_scale
    )
    cross_probs = softmax_rows(cross_scores)
    cross_low = cross_probs.astype(jnp.bfloat16)
    cross_out = jnp.einsum(
        "hqk,hdk->hdq", cross_low, text_values, preferred_element_type=jnp.float32
    )
    cross_out, x_two, normed_three, inverse_three, h_three, grad_ff = project(
        "gather",
        orders,
        cross_out.reshape(span, length).astype(jnp.bfloat16),
        weight_co,
        x_one,
        gain_three,
        sort_blocks(grad_out.astype(jnp.bfloat16), to_slots),
    )

    gate_up = contract_rows(weight_gu, h_three)
    gate_pre = gate_up[:units]
    up_part = gate_up[units:]
    sigmoid_gate = jax.nn.sigmoid(gate_pre)
    silu_gate = gate_pre * sigmoid_gate
    hidden = (silu_gate * up_part).astype(jnp.bfloat16)

    grad_blocks_down = as_blocks(contract_last(grad_ff, hidden).astype(jnp.bfloat16), to_slots)
    weight_down, grad_blocks_down = lax.optimization_barrier((line_down, grad_blocks_down))
    sums_down = scatter_line(grad_blocks_down)
    grad_hidden = contract_rows(weight_down, grad_ff)
    grad_gate = grad_hidden * up_part * (sigmoid_gate * (1.0 + gate_pre * (1.0 - sigmoid_gate)))
    grad_up = grad_hidden * silu_gate
    grad_gu = jnp.concatenate([grad_gate, grad_up], axis=0).astype(jnp.bfloat16)
    grad_x_two, grad_weight_gu, sum_three, grad_cross = back(
        orders,
        weight_gu,
        grad_gu,
        h_three,
        (normed_three, inverse_three, gain_three, grad_out),
        send_rows=True,
        in_slots=True,
        after=[grad_blocks_down],
    )
    grad_blocks_gu = as_blocks(grad_weight_gu, to_slots)
    sums_gu = scatter_line(grad_blocks_gu)
    grad_cross_out, grad_weight_co = back(
        orders, weight_co, grad_cross, cross_out
    )
    grad_cross_out = grad_cross_out.reshape(head_count, HEAD, length)
    grad_cross_probs = jnp.einsum(
        "hdq,hdk->hqk", grad_cross_out, text_values, preferred_element_type=jnp.float32
    )
    grad_cross_scores = (
        cross_probs
        * (grad_cross_probs - jnp.sum(cross_probs * grad_cross_probs, axis=-1, keepdims=True))
    ).astype(jnp.bfloat16)
    grad_cross_q = (
        jnp.einsum("hqk,hdk->hdq", grad_cross_scores, text_keys, preferred_element_type=jnp.float32)
        * score_scale
    )
    grad_cross_q = grad_cross_q.reshape(span, length).astype(jnp.bfloat16)
    grad_text_keys = (
        jnp.einsum("hqk,hdq->hdk", grad_cross_scores, cross_q, preferred_element_type=jnp.float32)
        * score_scale
    )
    grad_text_values = jnp.einsum(
        "hqk,hdq->hdk", cross_low, grad_cross_out, preferred_element_type=jnp.float32
    )
    grad_text = jnp.concatenate(
        [grad_text_keys.reshape(span, CTX), grad_text_values.reshape(span, CTX)], axis=1
    )
    grad_x_one, grad_weight_cq, sum_two, grad_attn, grad_text = back(
        orders,
        weight_cq,
        grad_cross_q,
        h_two,
        (normed_two, inverse_two, gain_two, grad_x_two),
        send_rows=True,
        text=grad_text.astype(jnp.bfloat16),
        after=[sums_down],
    )
    grad_text = sort_blocks(grad_text, to_slots)
    grad_weight_text = [
        contract_last(grad_text[:, :CTX], text_mine),
        contract_last(grad_text[:, CTX:], text_mine),
    ]
    grad_blocks_two = as_blocks(
        jnp.concatenate(
            [grad_weight_cq, grad_weight_co]
            + [grad.astype(jnp.bfloat16) for grad in grad_weight_text],
            axis=1,
        ),
        to_slots,
    )
    sums_two = scatter_line(grad_blocks_two)
    grad_attn_out, grad_weight_ao = back(
        orders, weight_ao, grad_attn, attn_out, after=[grad_blocks_two]
    )
    grad_attn_out = grad_attn_out.reshape(head_count, HEAD, length)
    grad_probs = jnp.einsum(
        "hdq,hdk->hqk", grad_attn_out, values, preferred_element_type=jnp.float32
    )
    grad_scores = (
        attn_probs * (grad_probs - jnp.sum(attn_probs * grad_probs, axis=-1, keepdims=True))
    ).astype(jnp.bfloat16)
    grad_queries = (
        jnp.einsum("hqk,hdk->hdq", grad_scores, keys, preferred_element_type=jnp.float32)
        * score_scale
    )
    grad_keys = (
        jnp.einsum("hqk,hdq->hdk", grad_scores, queries, preferred_element_type=jnp.float32)
        * score_scale
    )
    grad_values = jnp.einsum(
        "hqk,hdq->hdk", probs_low, grad_attn_out, preferred_element_type=jnp.float32
    )
    grad_qkv = jnp.stack(
        [
            rotate_columns(grad_queries, cosine, -sine_table),
            rotate_columns(grad_keys, cosine, -sine_table),
            grad_values,
        ]
    )
    grad_qkv = grad_qkv.reshape(3 * span, length).astype(jnp.bfloat16)
    latent_grad, grad_weight_qkv, sum_one = back(
        orders,
        weight_qkv,
        grad_qkv,
        h_one,
        (normed_one, inverse_one, scaled_one, grad_x_one),
        in_slots=True,
        after=[sums_gu],
    )
    grad_blocks_one = as_blocks(
        jnp.concatenate([grad_weight_qkv, grad_weight_ao], axis=1), to_slots
    )
    sums_one = scatter_line(grad_blocks_one)
    sums_feed, ff_out = feed(
        sums_gu,
        sums_down,
        matmul(weight_down, hidden).astype(jnp.bfloat16),
        [grad_blocks_one],
    )
    result = x_two + sort_blocks(ff_out, to_logical)
    sum_one = sum_one[0:1]
    grad_gain_one = sum_one * time_gain.T
    grad_time = sum_one * gain_one.T
    gain_grads = jnp.concatenate(
        [
            grad_gain_one,
            sum_two[0:1],
            sum_three[0:1],
            bucket_pick[:, None] * grad_time,
        ],
        axis=0,
    )
    squares = sum(
        jnp.sum(jnp.square(part.astype(jnp.float32)))
        for part in (sums_gu, sums_down, sums_two, sums_one)
    )
    out_pair, sums_one, sums_two, gain_sums, squares = closing(
        jnp.concatenate([result.T, latent_grad.T], axis=1).astype(jnp.bfloat16),
        sums_one,
        sums_two,
        gain_grads,
        jnp.pad(squares.reshape(1, 1), ((0, 7), (0, 127))),
    )
    output = out_pair[:, :D]
    latent_grad = out_pair[:, D:].astype(jnp.float32)
    place = lax.axis_index("dp") * (planes * cores) + plane * cores + lax.axis_index("core")
    gain_sums = jnp.sum(gain_sums, axis=0)
    grad_norm = jnp.sqrt(jnp.sum(squares) + jnp.sum(gain_sums * gain_sums))
    scale = 1.0 / jnp.maximum(grad_norm, 1.0)
    gain_sums = lax.dynamic_index_in_dim(
        gain_sums.reshape(8, blocks, rows), owners[place], 1, False
    ).T
    clipped, first_new, second_new, sheet_new, sheet_copy = sheet_update(
        scale,
        length,
        sums_one,
        sums_two,
        sums_feed,
        jnp.pad(gain_sums, ((0, 0), (0, 120))),
        sheet,
        first,
        second,
    )
    return (
        output[None],
        latent_grad[None],
        grad_norm,
        clipped,
        gain_sums * scale,
        first_new,
        second_new,
        sheet_new,
        sheet_copy,
    )


def solution(mesh):
    groups, seq_count = mesh.shape["dp"], mesh.shape["seq"]
    by_plane = groups == 4 and seq_count == 8
    if by_plane:
        mesh = Mesh(mesh.devices.reshape(groups, seq_count // 2, 2), ("dp", "z", "core"))
    seq = ("z", "core") if by_plane else "seq"
    both = ("dp", "z", "core") if by_plane else ("dp", "seq")
    in_specs = (
        P("dp", seq, None),
        P("dp", None, None),
        P("dp", None),
        P(),
        P(),
        P("dp", seq, None),
        P(both, None),
        P(both, None),
        P(both, None),
    )
    out_specs = (
        P("dp", seq, None),
        P("dp", seq, None),
        P(),
        P(both, None),
        P(both, None),
        P(both, None),
        P(both, None),
        P(both, None),
        P(both, None),
    )
    return jax.shard_map(
        plane_plan if by_plane else gather_plan,
        mesh=mesh,
        in_specs=in_specs,
        out_specs=out_specs,
        check_vma=False,
    )
```

```python
import functools
import math

import jax
import jax.numpy as jnp
from jax import lax
from jax.experimental import pallas as pl
from jax.experimental.pallas import tpu as pltpu
from jax.sharding import Mesh
from jax.sharding import PartitionSpec as P

D = 1536
FF = 6144
HEAD = 64
CTXW = 768
CTX = 128
NB = 5
STEP = 10
SHEET = 29192


HIGHEST = lax.Precision.HIGHEST
EPS_NORM = 1e-05
EPS_ADAM = 1e-08
MASKED_SCORE = -1e30
BETA_ONE = 0.5
BETA_TWO = 0.5
WEIGHT_DECAY = 0.01


def reorder(values, ordering):
    leading = values.shape[:-1]
    groups = ordering.shape[0]
    blocks = values.reshape(leading + (groups, values.shape[-1] // groups))
    return jnp.take(blocks, ordering, axis=-2).reshape(values.shape)


def norm_parts(values):
    average = jnp.mean(values, axis=-1, keepdims=True)
    centered = values - average
    variance = jnp.mean(centered * centered, axis=-1, keepdims=True)
    inverse_std = lax.rsqrt(variance + EPS_NORM)
    return (centered * inverse_std, inverse_std)


def norm_back(grad_normed, normed, inverse_std):
    return inverse_std * (
        grad_normed
        - jnp.mean(grad_normed, axis=-1, keepdims=True)
        - normed * jnp.mean(grad_normed * normed, axis=-1, keepdims=True)
    )


def softmax_rows(scores):
    row_max = jnp.max(scores, axis=-1, keepdims=True)
    exponent = jnp.exp(scores - row_max)
    return exponent / jnp.sum(exponent, axis=-1, keepdims=True)


def rope_tables(positions, head_dim):
    half_dim = head_dim // 2
    frequency = jnp.exp(-math.log(10000.0) * jnp.arange(half_dim, dtype=jnp.float32) / half_dim)
    angles = positions.astype(jnp.float32)[:, None] * frequency[None, :]
    return (jnp.cos(angles)[:, None, :], jnp.sin(angles)[:, None, :])


def rotate(values, cosine, sine_table):
    half_dim = values.shape[-1] // 2
    first_half = values[..., :half_dim]
    second_half = values[..., half_dim:]
    return jnp.concatenate(
        [
            first_half * cosine - second_half * sine_table,
            second_half * cosine + first_half * sine_table,
        ],
        axis=-1,
    )


def unrotate(grads, cosine, sine_table):
    half_dim = grads.shape[-1] // 2
    first_half = grads[..., :half_dim]
    second_half = grads[..., half_dim:]
    return jnp.concatenate(
        [
            first_half * cosine + second_half * sine_table,
            second_half * cosine - first_half * sine_table,
        ],
        axis=-1,
    )


def segment_ids(starts, positions):
    return jnp.sum((starts[None, :] <= positions[:, None]).astype(jnp.int32), axis=1) - 1


def column_spread(length):
    column = jnp.arange(SHEET, dtype=jnp.int32)
    base_std = D ** (-0.5)
    spread = jnp.full((SHEET,), base_std, jnp.float32)
    spread = jnp.where(
        (column >= 3 * D) & (column < 4 * D), base_std * math.sqrt(length) / 4.0, spread
    )
    spread = jnp.where((column >= 5 * D) & (column < 6 * D), base_std * math.sqrt(CTX), spread)
    spread = jnp.where((column >= 6 * D + 2 * FF) & (column < 6 * D + 3 * FF), FF ** (-0.5), spread)
    spread = jnp.where(
        (column >= 6 * D + 3 * FF) & (column < 6 * D + 3 * FF + 2 * CTXW), CTXW ** (-0.5), spread
    )
    spread = jnp.where(column >= 6 * D + 3 * FF + 2 * CTXW, 0.3, spread)
    return spread


def inner_rows(left, right):
    return lax.dot_general(
        left, right, (((0,), (0,)), ((), ())), preferred_element_type=jnp.float32
    )


def inner_rows_high(left, right):
    return lax.dot_general(
        left, right, (((0,), (0,)), ((), ())), precision=HIGHEST, preferred_element_type=jnp.float32
    )


def gather_plan(latents, context, clip_starts, buckets, owners, cotangent, sheet, first, second):
    frames = latents.shape[1]
    seq_count = lax.axis_size("seq")
    length = frames * seq_count
    head_count = D // HEAD
    score_scale = HEAD ** (-0.5)
    group_ids = jnp.arange(owners.shape[0], dtype=jnp.int32)
    inverse = jnp.sum(
        jnp.where(owners[None, :] == group_ids[:, None], group_ids[None, :], 0), axis=1
    )
    gathered = lax.all_gather(sheet.astype(jnp.bfloat16), ("dp", "seq"), axis=0, tiled=True)
    tail_col = 6 * D + 3 * FF
    gain_col = tail_col + 2 * CTXW
    gain_rows = reorder(gathered[:, gain_col:].astype(jnp.float32).T, inverse)
    row_index = lax.axis_index("dp")
    bucket_ids = jnp.arange(NB, dtype=jnp.int32)
    bucket_pick = (bucket_ids == buckets[row_index]).astype(jnp.float32)
    counts = jnp.sum((buckets[:, None] == bucket_ids[None, :]).astype(jnp.float32), axis=0)
    row_weight = buckets.shape[0] / (NB * jnp.sum(bucket_pick * counts))
    gain_one = gain_rows[0]
    gain_two = gain_rows[1]
    gain_three = gain_rows[2]
    time_gain = jnp.sum(gain_rows[3:] * bucket_pick[:, None], axis=0)
    tokens = latents[0].astype(jnp.float32)
    positions = lax.axis_index("seq") * frames + jnp.arange(frames, dtype=jnp.int32)
    all_positions = jnp.arange(length, dtype=jnp.int32)
    starts = clip_starts[0]
    same_clip = (
        segment_ids(starts, positions)[:, None] == segment_ids(starts, all_positions)[None, :]
    )[None]
    cosine, sine_table = rope_tables(positions, HEAD)
    normed_one, inverse_one = norm_parts(tokens)
    scaled_one = gain_one * time_gain
    h_one_st = reorder((normed_one * scaled_one).astype(jnp.bfloat16), owners)
    joint_qkv = jnp.dot(h_one_st, gathered[:, : 3 * D], preferred_element_type=jnp.float32)
    queries = rotate(joint_qkv[:, :D].reshape(frames, head_count, HEAD), cosine, sine_table).astype(
        jnp.bfloat16
    )
    key_local = rotate(
        joint_qkv[:, D : 2 * D].reshape(frames, head_count, HEAD), cosine, sine_table
    ).astype(jnp.bfloat16)
    value_local = joint_qkv[:, 2 * D :].reshape(frames, head_count, HEAD).astype(jnp.bfloat16)
    key_all, value_all = (
        lax.all_gather(key_local, "seq", axis=0, tiled=True),
        lax.all_gather(value_local, "seq", axis=0, tiled=True),
    )
    scores = (
        jnp.einsum("qhd,khd->hqk", queries, key_all, preferred_element_type=jnp.float32)
        * score_scale
    )
    attn_probs = softmax_rows(jnp.where(same_clip, scores, MASKED_SCORE))
    probs_low = attn_probs.astype(jnp.bfloat16)
    attn_out = (
        jnp.einsum("hqk,khd->qhd", probs_low, value_all, preferred_element_type=jnp.float32)
        .reshape(frames, D)
        .astype(jnp.bfloat16)
    )
    attn_st = reorder(attn_out, owners)
    x_one = tokens + jnp.dot(
        attn_st, gathered[:, 3 * D : 4 * D], preferred_element_type=jnp.float32
    )
    normed_two, inverse_two = norm_parts(x_one)
    h_two_st = reorder((normed_two * gain_two).astype(jnp.bfloat16), owners)
    cross_q = (
        jnp.dot(h_two_st, gathered[:, 4 * D : 5 * D], preferred_element_type=jnp.float32)
        .astype(jnp.bfloat16)
        .reshape(frames, head_count, HEAD)
    )
    text_tokens = context[0]
    text_kv = jnp.einsum(
        "tc,dec->etd",
        text_tokens,
        gathered[:, tail_col:gain_col].reshape(D, 2, CTXW),
        preferred_element_type=jnp.float32,
    )
    text_kv = reorder(text_kv, inverse).astype(jnp.bfloat16).reshape(2, CTX, head_count, HEAD)
    text_keys = text_kv[0]
    text_values = text_kv[1]
    cross_scores = (
        jnp.einsum("qhd,khd->hqk", cross_q, text_keys, preferred_element_type=jnp.float32)
        * score_scale
    )
    cross_probs = softmax_rows(cross_scores)
    cross_low = cross_probs.astype(jnp.bfloat16)
    cross_out = (
        jnp.einsum("hqk,khd->qhd", cross_low, text_values, preferred_element_type=jnp.float32)
        .reshape(frames, D)
        .astype(jnp.bfloat16)
    )
    cross_st = reorder(cross_out, owners)
    x_two = x_one + jnp.dot(
        cross_st, gathered[:, 5 * D : 6 * D], preferred_element_type=jnp.float32
    )
    normed_three, inverse_three = norm_parts(x_two)
    h_three_st = reorder((normed_three * gain_three).astype(jnp.bfloat16), owners)
    grad_out = cotangent[0].astype(jnp.float32) * row_weight
    grad_ff_st = reorder(grad_out.astype(jnp.bfloat16), owners)
    gate_weight = gathered[:, 6 * D : 6 * D + 2 * FF]
    down_weight = gathered[:, 6 * D + 2 * FF : 6 * D + 3 * FF]
    units = down_weight.shape[1]
    gate_up = jnp.dot(h_three_st, gate_weight, preferred_element_type=jnp.float32)
    gate_pre = gate_up[:, :units]
    up_part = gate_up[:, units:]
    sigmoid_gate = jax.nn.sigmoid(gate_pre)
    silu_gate = gate_pre * sigmoid_gate
    hidden = (silu_gate * up_part).astype(jnp.bfloat16)
    ff_out = reorder(
        jnp.einsum("nf,df->nd", hidden, down_weight, preferred_element_type=jnp.float32), inverse
    )
    result = x_two + ff_out
    grad_hidden = jnp.dot(grad_ff_st, down_weight, preferred_element_type=jnp.float32)
    grad_gate = grad_hidden * up_part * (sigmoid_gate * (1.0 + gate_pre * (1.0 - sigmoid_gate)))
    grad_up = grad_hidden * silu_gate
    grad_gu = jnp.concatenate([grad_gate, grad_up], axis=1).astype(jnp.bfloat16)
    grad_h_three = reorder(
        jnp.einsum("nf,df->nd", grad_gu, gate_weight, preferred_element_type=jnp.float32), inverse
    )
    grad_gain_three = jnp.sum(grad_h_three * normed_three, axis=0)
    grad_x_two = grad_out + norm_back(grad_h_three * gain_three, normed_three, inverse_three)
    grad_cross = grad_x_two.astype(jnp.bfloat16)
    grad_cross_out = (
        reorder(
            jnp.einsum(
                "nd,ed->ne",
                grad_cross,
                gathered[:, 5 * D : 6 * D],
                preferred_element_type=jnp.float32,
            ),
            inverse,
        )
        .astype(jnp.bfloat16)
        .reshape(frames, head_count, HEAD)
    )
    grad_cross_probs = jnp.einsum(
        "qhd,khd->hqk", grad_cross_out, text_values, preferred_element_type=jnp.float32
    )
    grad_cross_scores = (
        cross_probs
        * (grad_cross_probs - jnp.sum(cross_probs * grad_cross_probs, axis=-1, keepdims=True))
    ).astype(jnp.bfloat16)
    grad_cross_q = (
        (
            jnp.einsum(
                "hqk,khd->qhd", grad_cross_scores, text_keys, preferred_element_type=jnp.float32
            )
            * score_scale
        )
        .reshape(frames, D)
        .astype(jnp.bfloat16)
    )
    grad_text_keys = (
        jnp.einsum("hqk,qhd->khd", grad_cross_scores, cross_q, preferred_element_type=jnp.float32)
        * score_scale
    )
    grad_text_values = jnp.einsum(
        "hqk,qhd->khd", cross_low, grad_cross_out, preferred_element_type=jnp.float32
    )
    grad_text = reorder(
        jnp.stack([grad_text_keys.reshape(CTX, D), grad_text_values.reshape(CTX, D)]), owners
    )
    grad_h_two = reorder(
        jnp.einsum(
            "ne,de->nd",
            grad_cross_q,
            gathered[:, 4 * D : 5 * D],
            preferred_element_type=jnp.float32,
        ),
        inverse,
    )
    grad_gain_two = jnp.sum(grad_h_two * normed_two, axis=0)
    grad_x_one = grad_x_two + norm_back(grad_h_two * gain_two, normed_two, inverse_two)
    grad_attn = grad_x_one.astype(jnp.bfloat16)
    grad_attn_out = (
        reorder(
            jnp.einsum(
                "nd,ed->ne",
                grad_attn,
                gathered[:, 3 * D : 4 * D],
                preferred_element_type=jnp.float32,
            ),
            inverse,
        )
        .astype(jnp.bfloat16)
        .reshape(frames, head_count, HEAD)
    )
    key_back, value_back = (key_all, value_all)

    def head_grads(head_items):
        head_probs, head_grad_out, head_values = head_items
        grad_probs = jnp.einsum(
            "qd,kd->qk", head_grad_out, head_values, preferred_element_type=jnp.float32
        )
        return (
            head_probs * (grad_probs - jnp.sum(head_probs * grad_probs, axis=-1, keepdims=True))
        ).astype(jnp.bfloat16)

    grad_scores_low = lax.map(
        head_grads, (attn_probs, jnp.swapaxes(grad_attn_out, 0, 1), jnp.swapaxes(value_back, 0, 1))
    )
    grad_queries = (
        jnp.einsum("hqk,khd->qhd", grad_scores_low, key_back, preferred_element_type=jnp.float32)
        * score_scale
    )
    grad_keys = (
        jnp.einsum("hqk,qhd->khd", grad_scores_low, queries, preferred_element_type=jnp.float32)
        * score_scale
    )
    grad_values = jnp.einsum(
        "hqk,qhd->khd", probs_low, grad_attn_out, preferred_element_type=jnp.float32
    )
    key_sums = lax.psum_scatter(
        jnp.concatenate(
            [
                grad_keys.reshape(frames * lax.axis_size("seq"), D),
                grad_values.reshape(frames * lax.axis_size("seq"), D),
            ],
            axis=1,
        ).astype(jnp.bfloat16),
        "seq",
        scatter_dimension=0,
        tiled=True,
    ).astype(jnp.float32)
    grad_q_raw = unrotate(grad_queries, cosine, sine_table).reshape(frames, D)
    grad_k_raw = unrotate(
        key_sums[:, :D].reshape(frames, head_count, HEAD), cosine, sine_table
    ).reshape(frames, D)
    grad_qkv = jnp.concatenate([grad_q_raw, grad_k_raw, key_sums[:, D:]], axis=1).astype(
        jnp.bfloat16
    )
    grad_h_one = reorder(
        jnp.einsum("ne,de->nd", grad_qkv, gathered[:, : 3 * D], preferred_element_type=jnp.float32),
        inverse,
    )
    grad_gain_one = jnp.sum(grad_h_one * normed_one * time_gain, axis=0)
    grad_time = jnp.sum(grad_h_one * normed_one * gain_one, axis=0)
    latent_grad = grad_x_one + norm_back(grad_h_one * scaled_one, normed_one, inverse_one)
    gain_grads = jnp.concatenate(
        [
            jnp.stack([grad_gain_one, grad_gain_two, grad_gain_three]),
            bucket_pick[:, None] * grad_time[None, :],
        ],
        axis=0,
    )
    gain_grads = reorder(gain_grads, owners).T
    text_float = text_tokens.astype(jnp.float32)
    pieces = [
        inner_rows(h_one_st, grad_qkv),
        inner_rows(attn_st, grad_attn),
        inner_rows(h_two_st, grad_cross_q),
        inner_rows(cross_st, grad_cross),
    ]
    pieces = pieces + [inner_rows(h_three_st, grad_gu), inner_rows(grad_ff_st, hidden)]
    pieces = pieces + [
        inner_rows_high(grad_text[0], text_float),
        inner_rows_high(grad_text[1], text_float),
        gain_grads,
    ]
    other_shard = lax.psum_scatter(
        jnp.concatenate(pieces, axis=1), ("dp", "seq"), scatter_dimension=0, tiled=True
    )
    total_squares = lax.psum(jnp.sum(other_shard * other_shard), ("dp", "seq"))
    grad_norm = jnp.sqrt(total_squares)
    clipped = other_shard / jnp.maximum(grad_norm, 1.0)
    gain_grad = clipped[:, 6 * D + 3 * FF + 2 * CTXW :]
    first_new = BETA_ONE * first + (1.0 - BETA_ONE) * clipped
    second_new = BETA_TWO * second + (1.0 - BETA_TWO) * clipped * clipped
    mean_hat = first_new / (1.0 - BETA_ONE**STEP)
    square_hat = second_new / (1.0 - BETA_TWO**STEP)
    rates = column_spread(length)[None, :]
    sheet_new = sheet - rates * (
        mean_hat / (jnp.sqrt(square_hat) + EPS_ADAM) + WEIGHT_DECAY * sheet
    )
    return (
        result.astype(jnp.bfloat16)[None],
        latent_grad[None],
        grad_norm,
        clipped,
        gain_grad,
        first_new,
        second_new,
        sheet_new,
        sheet_new.astype(jnp.bfloat16),
    )


PLANE = ("dp", "core")


def norm_columns(values):
    average = jnp.mean(values, axis=0, keepdims=True)
    centered = values - average
    variance = jnp.mean(centered * centered, axis=0, keepdims=True)
    inverse_std = lax.rsqrt(variance + EPS_NORM)
    return (centered * inverse_std, inverse_std)


def norm_columns_back(grad_normed, normed, inverse_std):
    return inverse_std * (
        grad_normed
        - jnp.mean(grad_normed, axis=0, keepdims=True)
        - normed * jnp.mean(grad_normed * normed, axis=0, keepdims=True)
    )


def contract_rows(left, right):
    return lax.dot_general(
        left, right, (((0,), (0,)), ((), ())), preferred_element_type=jnp.float32
    )


def contract_last(left, right):
    return lax.dot_general(
        left, right, (((1,), (1,)), ((), ())), preferred_element_type=jnp.float32
    )


def matmul(left, right):
    return jnp.dot(left, right, preferred_element_type=jnp.float32)


MESH_ID = pl.DeviceIdType.MESH
IDENTITIES = {}


def identity_of(name, *arrays):
    key = (name,) + tuple((array.shape, str(array.dtype)) for array in arrays)
    return IDENTITIES.setdefault(key, len(IDENTITIES))


IN_HBM = pl.BlockSpec(memory_space=pltpu.HBM)
IN_SMEM = pl.BlockSpec(memory_space=pltpu.SMEM)
IN_VMEM = pl.BlockSpec(memory_space=pltpu.VMEM)
BRIEF = pl.CostEstimate(flops=0, bytes_accessed=1024, transcendentals=0)


def reorder_blocks(source, target, order):
    rows = source.shape[1]

    @pl.loop(0, source.shape[0])
    def _(b):
        target[pl.ds(pl.multiple_of(b * rows, 16), rows), :] = source[order(b)]


def wide(ref):
    return ref[...].astype(jnp.float32)


def greet(peers):
    barrier = pltpu.get_barrier_semaphore()
    for peer in peers:
        pl.semaphore_signal(barrier, inc=1, device_id=peer, device_id_type=MESH_ID)
    pl.semaphore_wait(barrier, len(peers))


def near():
    group, core = lax.axis_index("dp"), lax.axis_index("core")
    across = group + 1 - 2 * lax.rem(group, 2)
    along = lax.rem(group + 2, 4)
    return group, core, across, along


def member_rows(width):
    def place(ref, member, start, count):
        first_row = pl.multiple_of(member * width + start, 16)
        return ref.at[pl.ds(first_row, count), :]

    return place


def member_lanes(width):
    def place(ref, member, start, count):
        return ref.at[pl.ds(start, count), pl.ds(pl.multiple_of(member * width, 128), width)]

    return place


def mover(send_sem, recv_sem, first=0):
    def copy(k, source, target, peer):
        return pltpu.make_async_remote_copy(
            src_ref=source,
            dst_ref=target,
            send_sem=send_sem.at[first + k],
            recv_sem=recv_sem.at[first + k],
            device_id=peer,
            device_id_type=MESH_ID,
        )

    return copy


def member_at(member):
    return {"dp": lax.div(member, 2), "core": lax.rem(member, 2)}


def plane_peers():
    group, core, _, _ = near()
    member = group * 2 + core
    return [lax.rem(member + step, 8) for step in range(1, 8)]


def gather_steps(place, x_ref, o_ref, local_sem, copy, arrived_whole=lambda member: None):
    group, core, across, along = near()
    beyond = across + along - group
    other = 1 - core
    sibling, by_x, by_y = {"core": other}, {"dp": across}, {"dp": along}
    half = x_ref.shape[0] // 2

    def part(owner, owner_core, piece):
        return place(o_ref, owner * 2 + owner_core, piece * half, half)

    sent = []

    def send(k, source, target, peer):
        moving = copy(k, source, target, peer)
        moving.start()
        sent.append(moving)

    def own(k, piece, peer):
        send(k, x_ref.at[pl.ds(piece * half, half), :], part(group, core, piece), peer)

    def relay(k, owner, piece, peer):
        send(k, part(owner, core, piece), part(owner, core, piece), peer)

    def arrived(k, owner, owner_core, piece):
        landed = part(owner, owner_core, piece)
        copy(k, landed, landed, sibling).wait_recv()

    local = pltpu.make_async_copy(
        x_ref, place(o_ref, group * 2 + core, 0, 2 * half), local_sem
    )
    local.start()
    own(0, 0, by_x)
    own(1, 1, by_y)
    own(2, 1, by_x)
    own(3, 0, by_y)
    own(4, 0, sibling)
    own(5, 1, sibling)

    def finish():
        local.wait()
        arrived_whole(group * 2 + core)
        arrived(4, group, other, 0)
        arrived(5, group, other, 1)
        arrived_whole(group * 2 + other)
        arrived(0, across, core, 0)
        relay(6, across, 0, by_y)
        relay(7, across, 0, sibling)
        arrived(1, along, core, 1)
        relay(8, along, 1, by_x)
        relay(9, along, 1, sibling)
        arrived(2, across, core, 1)
        relay(10, across, 1, sibling)
        arrived_whole(across * 2 + core)
        arrived(3, along, core, 0)
        relay(11, along, 0, sibling)
        arrived_whole(along * 2 + core)
        arrived(7, across, other, 0)
        arrived(10, across, other, 1)
        arrived_whole(across * 2 + other)
        arrived(6, beyond, core, 0)
        relay(12, beyond, 0, sibling)
        arrived(8, beyond, core, 1)
        relay(13, beyond, 1, sibling)
        arrived_whole(beyond * 2 + core)
        arrived(9, along, other, 1)
        arrived(11, along, other, 0)
        arrived_whole(along * 2 + other)
        arrived(12, beyond, other, 0)
        arrived(13, beyond, other, 1)
        arrived_whole(beyond * 2 + other)
        for moving in sent:
            moving.wait_send()

    return finish


def exchange_steps(source, target, x_ref, o_ref, local_sem, copy):
    group, core, _, _ = near()
    member = group * 2 + core
    local = pltpu.make_async_copy(source(x_ref, member), target(o_ref, member), local_sem)
    local.start()
    sent = []
    for k, peer in enumerate(plane_peers()):
        sent.append(copy(k, source(x_ref, peer), target(o_ref, member), member_at(peer)))
        sent[-1].start()

    def finish():
        for k in range(7):
            sender = lax.rem(member + 7 - k, 8)
            landed = target(o_ref, sender)
            copy(k, landed, landed, member_at(sender)).wait_recv()
        local.wait()
        for moving in sent:
            moving.wait_send()

    return finish


def gather_kernel(place, x_ref, *refs):
    o_ref, local_sem, send_sem, recv_sem = refs[-4:]
    _, core, across, along = near()
    greet([{"dp": across}, {"dp": along}, {"core": 1 - core}])
    gather_steps(place, x_ref, o_ref, local_sem, mover(send_sem, recv_sem))()


def plane_gather_call(shard, shape, place, kind, after):
    return pl.pallas_call(
        functools.partial(gather_kernel, place),
        out_shape=jax.ShapeDtypeStruct(shape, shard.dtype),
        in_specs=[IN_HBM] * (1 + len(after)),
        out_specs=IN_HBM,
        scratch_shapes=[
            pltpu.SemaphoreType.DMA,
            pltpu.SemaphoreType.DMA((14,)),
            pltpu.SemaphoreType.DMA((14,)),
        ],
        compiler_params=pltpu.CompilerParams(
            collective_id=identity_of(kind, shard, *after), has_side_effects=True
        ),
        cost_estimate=BRIEF,
        name="plane_gather",
    )(shard, *after)


def plane_gather(shard, after=()):
    rows, width = shard.shape
    return plane_gather_call(shard, (rows, 8 * width), member_lanes(width), "gather lanes", after)


def plane_gather_rows(shard, after=()):
    rows, width = shard.shape
    return plane_gather_call(shard, (8 * rows, width), member_rows(rows), "gather rows", after)


def scatter_steps(place, p_ref, bufs, copy):
    pair, total, from_x, from_y, relay = bufs
    group, core, across, along = near()
    beyond = across + along - group
    other = 1 - core
    sibling, by_x, by_y = {"core": other}, {"dp": across}, {"dp": along}
    rows = total.shape[1]
    half = rows // 2
    low, high = pl.ds(0, half), pl.ds(half, half)
    sent = []

    def send(k, source, target, peer):
        moving = copy(k, source, target, peer)
        moving.start()
        sent.append(moving)

    def arrived(k, target):
        copy(k, target, target, sibling).wait_recv()

    def both_cores(k, owner):
        arrived(k, pair.at[k])
        summed = wide(place(p_ref, owner * 2 + core, 0, rows)) + wide(pair.at[k])
        total[k] = summed.astype(total.dtype)

    def cores():
        for k, owner in enumerate((beyond, across, along, group)):
            send(k, place(p_ref, owner * 2 + other, 0, rows), pair.at[k], sibling)

    def chips():
        both_cores(0, beyond)
        send(4, total.at[0, low], relay.at[0], by_x)
        send(5, total.at[0, high], relay.at[1], by_y)
        both_cores(1, across)
        send(6, total.at[1, low], from_x.at[low], by_x)
        both_cores(2, along)
        send(7, total.at[2, high], from_y.at[high], by_y)
        both_cores(3, group)

    def relays():
        arrived(5, relay.at[1])
        total[1, high] = (wide(total.at[1, high]) + wide(relay.at[1])).astype(total.dtype)
        send(8, total.at[1, high], from_x.at[high], by_x)
        arrived(4, relay.at[0])
        total[2, low] = (wide(total.at[2, low]) + wide(relay.at[0])).astype(total.dtype)
        send(9, total.at[2, low], from_y.at[low], by_y)

    def finish():
        arrived(6, from_x.at[low])
        arrived(7, from_y.at[high])
        arrived(8, from_x.at[high])
        arrived(9, from_y.at[low])
        summed = wide(total.at[3]) + wide(from_x) + wide(from_y)
        for moving in sent:
            moving.wait_send()
        return summed

    return cores, chips, relays, finish


def scatter_bufs(rows, width):
    slot = pltpu.VMEM((rows, width), jnp.bfloat16)
    four = pltpu.VMEM((4, rows, width), jnp.bfloat16)
    return [four, four, slot, slot, pltpu.VMEM((2, rows // 2, width), jnp.bfloat16)]


def scatter_kernel(place, p_ref, *refs):
    o_ref, *bufs, send_sem, recv_sem = refs[-8:]
    _, core, across, along = near()
    greet([{"dp": across}, {"dp": along}, {"core": 1 - core}])
    cores, chips, relays, finish = scatter_steps(place, p_ref, bufs, mover(send_sem, recv_sem))
    cores()
    chips()
    relays()
    o_ref[...] = finish().astype(o_ref.dtype)


def plane_scatter_call(partial, shape, place, dtype, kind, after):
    rows, width = shape
    return pl.pallas_call(
        functools.partial(scatter_kernel, place),
        out_shape=jax.ShapeDtypeStruct(shape, dtype),
        in_specs=[IN_VMEM] + [IN_HBM] * len(after),
        out_specs=IN_VMEM,
        scratch_shapes=scatter_bufs(rows, width)
        + [
            pltpu.SemaphoreType.DMA((10,)),
            pltpu.SemaphoreType.DMA((10,)),
        ],
        compiler_params=pltpu.CompilerParams(
            collective_id=identity_of(kind, partial, *after),
            has_side_effects=True,
            vmem_limit_bytes=24 * 2**20,
        ),
        cost_estimate=BRIEF,
        name="plane_scatter",
    )(partial, *after)


def plane_scatter_frames(partial, after=()):
    rows, width = partial.shape[0], partial.shape[1] // 8
    place = member_lanes(width)
    return plane_scatter_call(partial, (rows, width), place, jnp.float32, "scatter lanes", after)


def plane_scatter_rows(partial, after=()):
    rows, width = partial.shape[0] // 8, partial.shape[1]
    place = member_rows(rows)
    return plane_scatter_call(partial, (rows, width), place, jnp.bfloat16, "scatter rows", after)


def project_kernel(kind, column, order_ref, s_ref, w_ref, base_ref, gain_ref, *refs):
    if kind == "sum":
        side_ref, full_ref, x_ref, n_ref, i_ref, h_ref, side_out, *refs = refs
    else:
        full_ref, x_ref, n_ref, i_ref, h_ref, *refs = refs
    full, total, part, landed, shard, by_block, base, gain, residual, normed, *refs = refs
    heads, weight, *bufs, local_sem, send_sem, recv_sem = refs
    rows, length = s_ref.shape
    width = base_ref.shape[1]
    fetches = [
        pltpu.make_async_copy(ref, held, local_sem.at[8 + k])
        for k, (ref, held) in enumerate(
            [(s_ref, heads), (w_ref, weight), (base_ref, base), (gain_ref, gain)]
            + ([(side_ref, bufs[-1])] if kind == "sum" else [])
        )
    ]
    for fetch in fetches:
        fetch.start()
    greet([member_at(peer) for peer in plane_peers()])
    side = mover(send_sem, recv_sem, 35)
    if kind == "sum":
        cores, chips, relays, finish = scatter_steps(
            member_rows(side_out.shape[0]), bufs[-1], bufs[:-1], side
        )
        fetches[4].wait()
        cores()
    fetches[0].wait()
    fetches[1].wait()
    total[...] = jnp.zeros_like(total)

    def add(member):
        of = pl.ds(pl.multiple_of(member * rows, 16), rows)

        @pl.loop(0, length // 256)
        def _(i):
            at = pl.ds(pl.multiple_of(i * 256, 256), 256)
            total[:, at] += contract_rows(weight[of, column : column + rows], full[of, at])

    gathered = gather_steps(
        member_rows(rows), heads, full, local_sem.at[0], mover(send_sem, recv_sem), add
    )
    if kind == "sum":
        chips()
    gathered()
    kept = pltpu.make_async_copy(full, full_ref, local_sem.at[0])
    kept.start()
    part[...] = total[...].astype(part.dtype)
    exchanged = exchange_steps(
        whole_lanes(rows, width),
        whole_rows(rows),
        part,
        landed,
        local_sem.at[3],
        mover(send_sem, recv_sem, 14),
    )
    if kind == "sum":
        relays()
    exchanged()
    fetches[2].wait()
    fetches[3].wait()
    residual[...] = base[...] + wide(landed)
    standard, inverse_std = norm_columns(residual[...])
    normed[...] = standard
    i_ref[...] = inverse_std
    scaled = (standard * gain[...]).astype(shard.dtype)
    if kind == "slots":
        by_block[...] = scaled.reshape(by_block.shape)
        reorder_blocks(by_block, shard, lambda b: order_ref[0, b])
    else:
        shard[...] = scaled
    gathered = gather_steps(
        member_lanes(width), shard, h_ref, local_sem.at[4], mover(send_sem, recv_sem, 21)
    )
    x_copy = pltpu.make_async_copy(residual, x_ref, local_sem.at[5])
    x_copy.start()
    n_copy = pltpu.make_async_copy(normed, n_ref, local_sem.at[6])
    n_copy.start()
    if kind == "sum":
        side_out[...] = finish().astype(side_out.dtype)
    gathered()
    kept.wait()
    x_copy.wait()
    n_copy.wait()


def project(kind, column, orders, heads, weight, base, gain, *side):
    rows, length = heads.shape
    features, width = base.shape
    whole = jax.ShapeDtypeStruct((features, length), jnp.bfloat16)
    frames = jax.ShapeDtypeStruct(base.shape, jnp.float32)
    side_outs, bufs = (), []
    if kind == "sum":
        (text,) = side
        side_outs = (jax.ShapeDtypeStruct((text.shape[0] // 8, text.shape[1]), text.dtype),)
        bufs = scatter_bufs(*side_outs[0].shape) + [pltpu.VMEM(text.shape, text.dtype)]
    low, high = pltpu.VMEM(base.shape, jnp.bfloat16), pltpu.VMEM(base.shape, jnp.float32)
    return pl.pallas_call(
        functools.partial(project_kernel, kind, column),
        out_shape=(whole, frames, frames, jax.ShapeDtypeStruct((1, width), jnp.float32), whole)
        + side_outs,
        in_specs=[IN_SMEM] + [IN_HBM] * (4 + len(side)),
        out_specs=(IN_HBM, IN_HBM, IN_HBM, IN_VMEM, IN_HBM) + (IN_VMEM,) * len(side),
        scratch_shapes=[
            pltpu.VMEM((features, length), jnp.bfloat16),
            pltpu.VMEM((rows, length), jnp.float32),
            pltpu.VMEM((rows, length), jnp.bfloat16),
            low,
            low,
            pltpu.VMEM((orders.shape[1], features // orders.shape[1], width), jnp.bfloat16),
            high,
            pltpu.VMEM(gain.shape, jnp.float32),
            high,
            high,
            pltpu.VMEM(heads.shape, heads.dtype),
            pltpu.VMEM(weight.shape, weight.dtype),
        ]
        + bufs
        + [
            pltpu.SemaphoreType.DMA((13,)),
            pltpu.SemaphoreType.DMA((49,)),
            pltpu.SemaphoreType.DMA((49,)),
        ],
        compiler_params=pltpu.CompilerParams(
            collective_id=identity_of("project " + kind, heads),
            has_side_effects=True,
            vmem_limit_bytes=32 * 2**20,
        ),
        cost_estimate=BRIEF,
        name="project_" + kind,
    )(orders, heads, weight, base, gain, *side)


def back_kernel(plan, *refs):
    by_rows, send_rows, text, in_slots, column, beside, after = plan
    refs = list(refs)

    def take(count):
        taken = refs[:count]
        del refs[:count]
        return taken

    order_ref = take(1)[0]
    sources = take(3 if by_rows else 7)
    text_ref = take(1)[0] if text else None
    beside_refs = take(4 if beside else 0)
    take(after)
    o_ref, own_out = take(2)
    sum_ref = None if by_rows else take(1)[0]
    rows_ref = take(1)[0] if send_rows else None
    text_out = take(1)[0] if text else None
    held = take(len(sources))
    w_ref, g_ref, act, *norms = held
    results = take(0 if by_rows else 2)
    mine, theirs, pair, from_x, from_y, relay, shard, slots, own_ref = take(9)
    besides = take(4 if beside else 0)
    local_sem, send_sem, recv_sem = refs
    fetches = [
        pltpu.make_async_copy(ref, here, local_sem.at[4 + k])
        for k, (ref, here) in enumerate(zip(sources + beside_refs, held + besides))
    ]
    for fetch in fetches:
        fetch.start()

    group, core, across, along = near()
    beyond = across + along - group
    sibling, by_x, by_y = {"core": 1 - core}, {"dp": across}, {"dp": along}
    rows, width = mine.shape[1:]
    columns = slice(column, column + g_ref.shape[0])
    half = rows // 2
    low, high = pl.ds(0, half), pl.ds(half, half)
    copy = mover(send_sem, recv_sem)
    sent = []

    def send(k, source, target, peer):
        moving = copy(k, source, target, peer)
        moving.start()
        sent.append(moving)

    def arrived(k, target):
        copy(k, target, target, sibling).wait_recv()

    def split(k, at_rows, at_lanes, first, second):
        mine[k, at_rows, at_lanes] = jnp.where(core == 0, first, second).astype(mine.dtype)
        theirs[k, at_rows, at_lanes] = jnp.where(core == 0, second, first).astype(mine.dtype)

    def work_out(k, owner):
        if by_rows:

            @pl.loop(0, width // 256)
            def _(i):
                at = pl.ds(pl.multiple_of(i * 256, 256), 256)
                both = jnp.dot(
                    w_ref[pl.ds(pl.multiple_of(owner * 2 * rows, 16), 2 * rows), columns],
                    g_ref[:, at],
                    preferred_element_type=jnp.float32,
                )
                split(k, slice(None), at, both[:rows], both[rows:])

        else:

            @pl.loop(0, rows // 256)
            def _(i):
                at = pl.ds(pl.multiple_of(i * 256, 256), 256)
                both = jnp.dot(
                    w_ref[at, columns],
                    g_ref[:, pl.ds(pl.multiple_of(owner * 2 * width, 256), 2 * width)],
                    preferred_element_type=jnp.float32,
                )
                split(k, at, slice(None), both[:, :width], both[:, width:])

        send(k, theirs.at[k], pair.at[k], sibling)

    def both_cores(k):
        arrived(k, pair.at[k])
        mine[k] = (wide(mine.at[k]) + wide(pair.at[k])).astype(mine.dtype)

    def weight_grads(first, last):
        rows_of = act if in_slots else slots
        tile, count = rows_of.shape[0] // 6, g_ref.shape[0]

        @pl.loop(first, last)
        def _(i):
            at = pl.ds(pl.multiple_of(i * tile, tile), tile)
            for j in range(0, count, 256):
                of = slice(j, min(j + 256, count))
                own_ref[at, of] = contract_last(rows_of[at, :], g_ref[of, :]).astype(
                    own_ref.dtype
                )

    if send_rows or text:
        greet([member_at(peer) for peer in plane_peers()])
    else:
        greet([by_x, by_y, sibling])
    fetches[0].wait()
    fetches[1].wait()
    for k, owner in enumerate((beyond, across, along, group)):
        work_out(k, owner)
        if k == 1:
            both_cores(0)
            send(4, mine.at[0, low], relay.at[0], by_x)
            send(5, mine.at[0, high], relay.at[1], by_y)
        if k == 2:
            both_cores(1)
            send(6, mine.at[1, low], from_x.at[low], by_x)
        if k == 3:
            both_cores(2)
            send(7, mine.at[2, high], from_y.at[high], by_y)
    if text:
        text_done = gather_steps(
            member_rows(text_ref.shape[0]),
            text_ref,
            text_out,
            local_sem.at[1],
            mover(send_sem, recv_sem, 17),
        )
    def put_beside():
        cq, co, text_grad, text_mine = besides
        count, rows = g_ref.shape[0], text_grad.shape[1]
        part = text_mine.shape[0]
        tokens = text_mine.shape[1]

        @pl.loop(0, text_grad.shape[0])
        def _(b):
            at = pl.ds(pl.multiple_of(b * rows, 16), rows)
            own_ref[at, count : 2 * count] = cq[at, :]
            own_ref[at, 2 * count : 3 * count] = co[at, :]
            slots[at, : 2 * tokens] = text_grad[order_ref[0, b]]

        @pl.loop(0, 6)
        def _(i):
            at = pl.ds(pl.multiple_of(i * 256, 256), 256)
            for k in range(2):
                grads = contract_last(
                    slots[at, k * tokens : (k + 1) * tokens], text_mine[...]
                )
                start = 3 * count + k * part
                own_ref[at, start : start + part] = grads.astype(own_ref.dtype)

    fetches[2].wait()
    if not in_slots:
        reorder_blocks(act, slots, lambda b: order_ref[0, b])
    weight_grads(0, 2)
    arrived(5, relay.at[1])
    mine[1, high] = (wide(mine.at[1, high]) + wide(relay.at[1])).astype(mine.dtype)
    send(8, mine.at[1, high], from_x.at[high], by_x)
    arrived(4, relay.at[0])
    mine[2, low] = (wide(mine.at[2, low]) + wide(relay.at[0])).astype(mine.dtype)
    send(9, mine.at[2, low], from_y.at[low], by_y)
    both_cores(3)
    weight_grads(2, 6)
    if beside:
        for fetch in fetches[len(sources) :]:
            fetch.wait()
        put_beside()
    if text:
        text_done()
    own_copy = pltpu.make_async_copy(own_ref, own_out, local_sem.at[2])
    own_copy.start()
    arrived(6, from_x.at[low])
    arrived(7, from_y.at[high])
    arrived(8, from_x.at[high])
    arrived(9, from_y.at[low])
    summed = wide(mine.at[3]) + wide(from_x) + wide(from_y)
    if by_rows:
        shard[...] = summed.astype(shard.dtype)
        result_copy = pltpu.make_async_copy(shard, o_ref, local_sem.at[3])
        result_copy.start()
    else:
        for fetch in fetches[3 : len(sources)]:
            fetch.wait()
        normed, inverse_std, gain, base = norms
        result, by_block = results
        if in_slots:
            by_block[...] = summed.reshape(by_block.shape)
            reorder_blocks(by_block, result, lambda b: order_ref[1, b])
            summed = result[...]
        result[...] = base[...] + norm_columns_back(
            summed * gain[...], normed[...], inverse_std[...]
        )
        result_copy = pltpu.make_async_copy(result, o_ref, local_sem.at[3])
        result_copy.start()
        if send_rows:
            shard[...] = result[...].astype(shard.dtype)
            rows_done = exchange_steps(
                whole_rows(rows // 8),
                whole_lanes(rows // 8, width),
                shard,
                rows_ref,
                local_sem.at[0],
                mover(send_sem, recv_sem, 10),
            )
        sum_ref[...] = lax.dot_general(
            jnp.ones((8, width), jnp.float32),
            summed * normed[...],
            (((1,), (1,)), ((), ())),
            precision=HIGHEST,
            preferred_element_type=jnp.float32,
        )
        if send_rows:
            rows_done()
    result_copy.wait()
    own_copy.wait()
    for moving in sent:
        moving.wait_send()


def back(
    orders,
    weight,
    grad,
    act,
    norm=None,
    column=0,
    send_rows=False,
    text=None,
    in_slots=False,
    beside=(),
    after=(),
):
    by_rows = norm is None
    features, length = weight.shape[0], grad.shape[1]
    shape = (features // 8, length) if by_rows else (features, length // 8)
    small = jnp.bfloat16
    own_width = grad.shape[0] * (4 if beside else 1)
    own = jax.ShapeDtypeStruct((features, own_width), small)
    outs = [jax.ShapeDtypeStruct(shape, small if by_rows else jnp.float32), own]
    specs = [IN_HBM, IN_HBM]
    if not by_rows:
        outs.append(jax.ShapeDtypeStruct((8, features), jnp.float32))
        specs.append(IN_VMEM)
    if send_rows:
        outs.append(jax.ShapeDtypeStruct((features // 8, length), small))
        specs.append(IN_HBM)
    count = orders.shape[1]
    if not in_slots:
        act = act.reshape(count, features // count, length)
    sources = [weight, grad, act] + list(norm or ())
    operands = [orders] + sources
    if text is not None:
        operands.append(text)
        outs.append(jax.ShapeDtypeStruct((8 * text.shape[0], text.shape[1]), text.dtype))
        specs.append(IN_HBM)
    if beside:
        cq, co, text_grad, text_mine = beside
        beside = (cq, co, text_grad.reshape(count, features // count, -1), text_mine)
        operands += list(beside)
    operands += list(after)
    plan = (by_rows, send_rows, text is not None, in_slots, column, bool(beside), len(after))
    rows, width = shape
    four, slot = pltpu.VMEM((4, rows, width), small), pltpu.VMEM((rows, width), small)
    return pl.pallas_call(
        functools.partial(back_kernel, plan),
        out_shape=tuple(outs),
        in_specs=[IN_SMEM] + [IN_HBM] * (len(operands) - 1),
        out_specs=tuple(specs),
        scratch_shapes=[pltpu.VMEM(array.shape, array.dtype) for array in sources]
        + (
            []
            if by_rows
            else [
                pltpu.VMEM(shape, jnp.float32),
                pltpu.VMEM((count, rows // count, width), jnp.float32),
            ]
        )
        + [four, four, four, slot, slot, pltpu.VMEM((2, rows // 2, width), small), slot]
        + [
            pltpu.VMEM((16, 128) if in_slots else (features, length), small),
            pltpu.VMEM(own.shape, small),
        ]
        + [pltpu.VMEM(array.shape, array.dtype) for array in beside]
        + [
            pltpu.SemaphoreType.DMA((11,)),
            pltpu.SemaphoreType.DMA((31,)),
            pltpu.SemaphoreType.DMA((31,)),
        ],
        compiler_params=pltpu.CompilerParams(
            collective_id=identity_of("back" + str(plan), *operands),
            has_side_effects=True,
            vmem_limit_bytes=44 * 2**20,
        ),
        cost_estimate=BRIEF,
        name="back",
    )(*operands)


def exchange_kernel(source, target, x_ref, *refs):
    o_ref, local_sem, send_sem, recv_sem = refs[-4:]
    greet([member_at(peer) for peer in plane_peers()])
    exchange_steps(source, target, x_ref, o_ref, local_sem, mover(send_sem, recv_sem))()


def exchange(array, shape, source, target, kind, after=()):
    return pl.pallas_call(
        functools.partial(exchange_kernel, source, target),
        out_shape=jax.ShapeDtypeStruct(shape, array.dtype),
        in_specs=[IN_HBM] * (1 + len(after)),
        out_specs=IN_HBM,
        scratch_shapes=[
            pltpu.SemaphoreType.DMA,
            pltpu.SemaphoreType.DMA((7,)),
            pltpu.SemaphoreType.DMA((7,)),
        ],
        compiler_params=pltpu.CompilerParams(
            collective_id=identity_of(kind, array, *after), has_side_effects=True
        ),
        cost_estimate=BRIEF,
        name="plane_exchange",
    )(array, *after)


def whole_rows(rows):
    place = member_rows(rows)
    return lambda ref, member: place(ref, member, 0, rows)


def whole_lanes(rows, width):
    place = member_lanes(width)
    return lambda ref, member: place(ref, member, 0, rows)


def to_frames(part):
    rows, width = part.shape[0], part.shape[1] // 8
    return exchange(part, (8 * rows, width), whole_lanes(rows, width), whole_rows(rows), "to frames")


def to_rows(part):
    rows, width = part.shape[0] // 8, part.shape[1]
    return exchange(part, (rows, 8 * width), whole_rows(rows), whole_lanes(rows, width), "to rows")


def block(ref, member):
    return ref.at[member]


def exchange_blocks(blocks, after=()):
    return exchange(blocks, blocks.shape, block, block, "blocks", after)


def lanes(ref, start, width):
    return ref.at[:, pl.ds(pl.multiple_of(start, 128), width)]


def sheet_part(start, width):
    return lambda ref, member: lanes(ref, start + member * width, width)


def block_part(start, width):
    return lambda ref, member: lanes(ref.at[member], start, width)


def feed_kernel(gu_ref, down_ref, w_ref, h_ref, *refs):
    o_ref, y_ref, weight, hidden, part, summed, *bufs, local_sem, send_sem, recv_sem = refs[-14:]
    width = down_ref.shape[-1]
    fetches = [
        pltpu.make_async_copy(w_ref, weight, local_sem.at[3]),
        pltpu.make_async_copy(h_ref, hidden, local_sem.at[5]),
    ]
    for fetch in fetches:
        fetch.start()
    greet([member_at(peer) for peer in plane_peers()])
    finish = []
    for k, (ref, start) in enumerate(((gu_ref, 0), (gu_ref, width), (down_ref, 0))):
        source, target = block_part(start, width), sheet_part(8 * k * width, width)
        copy = mover(send_sem, recv_sem, 7 * k)
        finish.append(exchange_steps(source, target, ref, o_ref, local_sem.at[k], copy))
    for fetch in fetches:
        fetch.wait()

    @pl.loop(0, part.shape[0] // 256)
    def _(i):
        at = pl.ds(pl.multiple_of(i * 256, 256), 256)
        for j in range(0, part.shape[1], 256):
            product = jnp.dot(
                weight[at, :], hidden[:, j : j + 256], preferred_element_type=jnp.float32
            )
            part[at, j : j + 256] = product.astype(part.dtype)

    cores, chips, relays, ended = scatter_steps(
        member_lanes(y_ref.shape[1]), part, bufs, mover(send_sem, recv_sem, 21)
    )
    cores()
    chips()
    relays()
    summed[...] = ended()
    kept = pltpu.make_async_copy(summed, y_ref, local_sem.at[4])
    kept.start()
    for end in finish:
        end()
    kept.wait()


def feed(gu, down, weight, hidden, after=()):
    rows, length = weight.shape[0], hidden.shape[1]
    width = length // 8
    return pl.pallas_call(
        feed_kernel,
        out_shape=(
            jax.ShapeDtypeStruct((gu.shape[1], 24 * down.shape[-1]), gu.dtype),
            jax.ShapeDtypeStruct((rows, width), jnp.float32),
        ),
        in_specs=[IN_HBM] * (4 + len(after)),
        out_specs=(IN_HBM, IN_HBM),
        scratch_shapes=[
            pltpu.VMEM(weight.shape, weight.dtype),
            pltpu.VMEM(hidden.shape, hidden.dtype),
            pltpu.VMEM((rows, length), jnp.bfloat16),
            pltpu.VMEM((rows, width), jnp.float32),
        ]
        + scatter_bufs(rows, width)
        + [
            pltpu.SemaphoreType.DMA((6,)),
            pltpu.SemaphoreType.DMA((31,)),
            pltpu.SemaphoreType.DMA((31,)),
        ],
        compiler_params=pltpu.CompilerParams(
            collective_id=identity_of("feed", gu, down, weight, *after),
            has_side_effects=True,
            vmem_limit_bytes=28 * 2**20,
        ),
        cost_estimate=BRIEF,
        name="feed",
    )(gu, down, weight, hidden, *after)


def opening_kernel(
    latents_ref,
    cotangent_ref,
    small_ref,
    text_ref,
    sheet_ref,
    t_ref,
    all_ref,
    mine_ref,
    one_ref,
    x_ref,
    held,
    columns,
    one,
    local_sem,
    send_sem,
    recv_sem,
):
    features = latents_ref.shape[1]
    part, text = D // 8, CTXW // 8
    tail = 6 * D + 3 * FF
    fetches = [
        pltpu.make_async_copy(latents_ref, x_ref.at[:, :features], local_sem.at[5]),
        pltpu.make_async_copy(cotangent_ref, x_ref.at[:, features:], local_sem.at[6]),
        pltpu.make_async_copy(
            sheet_ref.at[:, : 6 * D], columns.at[:, : 6 * D], local_sem.at[7]
        ),
        pltpu.make_async_copy(
            sheet_ref.at[:, tail : tail + 2 * CTXW], columns.at[:, 6 * D :], local_sem.at[8]
        ),
    ]
    for fetch in fetches:
        fetch.start()
    group, core, _, _ = near()
    member = group * 2 + core
    plane = lax.axis_index("z")
    step = x_ref.shape[0] // 4
    text_rows = mine_ref.shape[0]
    teacher = jnp.logical_and(group == plane, core == 0)

    def frames(ref, j):
        return ref.at[pl.ds(pl.multiple_of(j * step, 16), step), :]

    peers = plane_peers()
    line = [lax.rem(plane + k, 4) for k in range(1, 4)]
    greet([member_at(peer) for peer in peers] + [{"z": there} for there in line])

    fetches[0].wait()
    fetches[1].wait()

    near_copy = mover(send_sem, recv_sem)
    line_copy = mover(send_sem, recv_sem, 7)
    small_local = pltpu.make_async_copy(small_ref, all_ref.at[plane, member], local_sem.at[0])
    small_local.start()
    first = [
        near_copy(k, small_ref, all_ref.at[plane, member], member_at(peer))
        for k, peer in enumerate(peers)
    ]
    for moving in first:
        moving.start()

    others = [lax.rem(group + k, 4) for k in range(1, 4)]
    keep = pltpu.make_async_copy(frames(x_ref, group), frames(held, group), local_sem.at[1])
    keep.start()

    def spread(owner, landing):
        return pltpu.make_async_remote_copy(
            src_ref=frames(x_ref, owner),
            dst_ref=frames(held, landing),
            send_sem=send_sem.at[10 + owner],
            recv_sem=recv_sem.at[10 + landing],
            device_id={"dp": owner},
            device_id_type=MESH_ID,
        )

    for owner in others:
        spread(owner, group).start()

    def rise(row):
        return pltpu.make_async_remote_copy(
            src_ref=frames(held, row),
            dst_ref=frames(t_ref, plane),
            send_sem=send_sem.at[28 + row],
            recv_sem=recv_sem.at[28 + plane],
            device_id={"z": row},
            device_id_type=MESH_ID,
        )

    stay = pltpu.make_async_copy(frames(held, plane), frames(t_ref, plane), local_sem.at[4])

    def pass_on(row):
        pl.when(row == plane)(stay.start)
        pl.when(row != plane)(rise(row).start)

    fetches[2].wait()
    fetches[3].wait()

    def move(m, at, start, width):
        one[m, :, at : at + width] = columns[:, start : start + width].astype(one.dtype)

    for m in range(8):
        for k in range(6):
            move(m, (4 * part if k < 3 else -3 * part) + k * part, k * D + m * part, part)
        for k in range(2):
            move(m, 3 * part + k * text, 6 * D + k * CTXW + m * text, text)
    weights_done = exchange_steps(
        block, block, one, one_ref, local_sem.at[2], mover(send_sem, recv_sem, 14)
    )

    def text_copy(k, peer):
        return pltpu.make_async_remote_copy(
            src_ref=text_ref.at[pl.ds(pl.multiple_of(peer * text_rows, 16), text_rows), :],
            dst_ref=mine_ref,
            send_sem=send_sem.at[21 + k],
            recv_sem=recv_sem.at[21],
            device_id=member_at(peer),
            device_id_type=MESH_ID,
        )

    own_text = text_ref.at[pl.ds(pl.multiple_of(member * text_rows, 16), text_rows), :]
    text_local = pltpu.make_async_copy(own_text, mine_ref, local_sem.at[3])

    @pl.when(teacher)
    def _():
        text_local.start()
        for k, peer in enumerate(peers):
            text_copy(k, peer).start()

    keep.wait()
    pass_on(group)
    for owner in others:
        spread(owner, owner).wait_recv()
        pass_on(owner)

    for k in range(7):
        landed = all_ref.at[plane, lax.rem(member + 7 - k, 8)]
        near_copy(k, landed, landed, member_at(peers[k])).wait_recv()
    small_local.wait()
    second = [
        line_copy(k, all_ref.at[plane], all_ref.at[plane], {"z": there})
        for k, there in enumerate(line)
    ]
    for moving in second:
        moving.start()
    for k in range(3):
        landed = all_ref.at[lax.rem(plane + 3 - k, 4)]
        line_copy(k, landed, landed, {"z": line[k]}).wait_recv()

    for there in line:
        landed = frames(t_ref, there)
        pltpu.make_async_remote_copy(
            src_ref=landed,
            dst_ref=landed,
            send_sem=send_sem.at[28 + there],
            recv_sem=recv_sem.at[28 + there],
            device_id={"z": there},
            device_id_type=MESH_ID,
        ).wait_recv()
    stay.wait()
    weights_done()

    @pl.when(teacher)
    def _():
        text_local.wait()
        for k, peer in enumerate(peers):
            text_copy(k, peer).wait_send()

    @pl.when(jnp.logical_not(teacher))
    def _():
        text_copy(0, peers[0]).wait_recv()

    for moving in first + second:
        moving.wait_send()
    for owner in others:
        spread(owner, group).wait_send()
    for there in line:
        rise(there).wait_send()


def opening(latents, cotangent, small, text, sheet):
    frames, features = latents.shape
    local = (frames, 2 * features)
    one = (8, sheet.shape[0], (6 * D + 2 * CTXW) // 8)
    low = jnp.bfloat16
    return pl.pallas_call(
        opening_kernel,
        out_shape=(
            jax.ShapeDtypeStruct(local, low),
            jax.ShapeDtypeStruct((4, 8) + small.shape, small.dtype),
            jax.ShapeDtypeStruct((text.shape[0] // 8, text.shape[1]), text.dtype),
            jax.ShapeDtypeStruct(one, low),
        ),
        in_specs=[IN_HBM] * 5,
        out_specs=(IN_HBM,) * 4,
        scratch_shapes=[
            pltpu.VMEM(local, low),
            pltpu.VMEM(local, low),
            pltpu.VMEM((sheet.shape[0], 6 * D + 2 * CTXW), jnp.float32),
            pltpu.VMEM(one, low),
            pltpu.SemaphoreType.DMA((9,)),
            pltpu.SemaphoreType.DMA((32,)),
            pltpu.SemaphoreType.DMA((32,)),
        ],
        compiler_params=pltpu.CompilerParams(
            collective_id=identity_of("opening", sheet),
            has_side_effects=True,
            vmem_limit_bytes=16 * 2**20,
        ),
        cost_estimate=BRIEF,
        name="opening",
    )(latents, cotangent, small, text, sheet)


def first_gather_kernel(
    x_ref, y_ref, sheet_ref, ox_ref, oy_ref, gu_ref, down_ref, local_sem, send_sem, recv_sem
):
    place = member_lanes(x_ref.shape[1])
    width = FF // 8
    greet([member_at(peer) for peer in plane_peers()])
    finish = [
        gather_steps(place, x_ref, ox_ref, local_sem.at[0], mover(send_sem, recv_sem)),
        gather_steps(place, y_ref, oy_ref, local_sem.at[1], mover(send_sem, recv_sem, 14)),
    ]
    for k, (ref, start) in enumerate(((gu_ref, 0), (gu_ref, width), (down_ref, 0))):
        source, target = sheet_part(6 * D + k * FF, width), block_part(start, width)
        copy = mover(send_sem, recv_sem, 28 + 7 * k)
        finish.append(exchange_steps(source, target, sheet_ref, ref, local_sem.at[2 + k], copy))
    for end in finish:
        end()


def first_gather(shard, other, sheet):
    rows, width = shard.shape
    whole = jax.ShapeDtypeStruct((rows, 8 * width), shard.dtype)
    return pl.pallas_call(
        first_gather_kernel,
        out_shape=(
            whole,
            whole,
            jax.ShapeDtypeStruct((8, sheet.shape[0], FF // 4), sheet.dtype),
            jax.ShapeDtypeStruct((8, sheet.shape[0], FF // 8), sheet.dtype),
        ),
        in_specs=[IN_HBM] * 3,
        out_specs=(IN_HBM,) * 4,
        scratch_shapes=[
            pltpu.SemaphoreType.DMA((5,)),
            pltpu.SemaphoreType.DMA((49,)),
            pltpu.SemaphoreType.DMA((49,)),
        ],
        compiler_params=pltpu.CompilerParams(
            collective_id=identity_of("first gather", shard, sheet), has_side_effects=True
        ),
        cost_estimate=BRIEF,
        name="first_gather",
    )(shard, other, sheet)


def closing_kernel(
    order_ref,
    y_ref,
    base_ref,
    grad_ref,
    w_ref,
    v_ref,
    gu_ref,
    down_ref,
    g_ref,
    t_ref,
    o_ref,
    vo_ref,
    s_ref,
    all_ref,
    by_block,
    sorted_y,
    base,
    grad,
    x_ref,
    held,
    tall,
    q_ref,
    one,
    two,
    gu,
    down,
    local_sem,
    send_sem,
    recv_sem,
):
    fetches = [
        pltpu.make_async_copy(ref, here, local_sem.at[7 + k])
        for k, (ref, here) in enumerate(
            [(y_ref, by_block), (base_ref, base), (grad_ref, grad)]
            + [(w_ref, one), (v_ref, two), (gu_ref, gu), (down_ref, down)]
        )
    ]
    for fetch in fetches:
        fetch.start()
    group, core, _, _ = near()
    member = group * 2 + core
    plane = lax.axis_index("z")
    step = x_ref.shape[0] // 4
    line = [lax.rem(plane + k, 4) for k in range(1, 4)]
    back = [lax.rem(plane + 3 - k, 4) for k in range(3)]
    groups = [lax.rem(group + k, 4) for k in range(1, 4)]
    peers = plane_peers()
    greet([member_at(peer) for peer in peers] + [{"z": there} for there in line])

    def frames(ref, j):
        return ref.at[pl.ds(pl.multiple_of(j * step, 16), step), :]

    copy = mover(send_sem, recv_sem)
    gain_line = mover(send_sem, recv_sem, 14)
    gain_plane = mover(send_sem, recv_sem, 17)
    square_plane = mover(send_sem, recv_sem, 24)
    square_line = mover(send_sem, recv_sem, 31)
    gain_local = pltpu.make_async_copy(g_ref, tall.at[plane], local_sem.at[3])
    gain_local.start()
    sent = [gain_line(k, g_ref, tall.at[plane], {"z": there}) for k, there in enumerate(line)]
    for fetch in fetches[:3]:
        fetch.wait()
    reorder_blocks(by_block, sorted_y, lambda b: order_ref[1, b])
    features = base.shape[0]
    x_ref[:, :features] = (base[...] + sorted_y[...]).T.astype(x_ref.dtype)
    x_ref[:, features:] = grad[...].T.astype(x_ref.dtype)
    local = pltpu.make_async_copy(frames(x_ref, plane), frames(held, plane), local_sem.at[0])
    local.start()
    sent += [
        copy(k, frames(x_ref, there), frames(held, plane), {"z": there})
        for k, there in enumerate(line)
    ]
    for moving in sent:
        moving.start()
    weights_done = exchange_steps(
        block, block, w_ref, o_ref, local_sem.at[1], mover(send_sem, recv_sem, 7)
    )
    others_done = exchange_steps(
        block, block, v_ref, vo_ref, local_sem.at[6], mover(send_sem, recv_sem, 34)
    )

    for fetch in fetches[3:]:
        fetch.wait()
    total = jnp.zeros((), jnp.float32)
    for ref in (one, two, gu, down):
        line_sum = jnp.zeros((1, ref.shape[2]), jnp.float32)
        for m in range(8):
            line_sum += jnp.sum(jnp.square(wide(ref.at[m])), axis=0, keepdims=True)
        total += jnp.sum(line_sum)
    q_ref[...] = jnp.full(q_ref.shape, total, jnp.float32)
    square_local = pltpu.make_async_copy(q_ref, all_ref.at[plane, member], local_sem.at[5])
    square_local.start()
    shown = [
        square_plane(k, q_ref, all_ref.at[plane, member], member_at(peer))
        for k, peer in enumerate(peers)
    ]
    for moving in shown:
        moving.start()
    gain_local.wait()
    for k, origin in enumerate(back):
        gain_line(k, tall.at[origin], tall.at[origin], {"z": origin}).wait_recv()
    tall[4] = tall[0] + tall[1] + tall[2] + tall[3]
    gain_keep = pltpu.make_async_copy(tall.at[4], s_ref.at[member], local_sem.at[4])
    gain_keep.start()
    given = [
        gain_plane(k, tall.at[4], s_ref.at[member], member_at(peer)) for k, peer in enumerate(peers)
    ]
    for moving in given:
        moving.start()

    def onward(owner):
        return pltpu.make_async_remote_copy(
            src_ref=frames(held, owner),
            dst_ref=frames(t_ref, group),
            send_sem=send_sem.at[3 + owner],
            recv_sem=recv_sem.at[3 + group],
            device_id={"dp": owner},
            device_id_type=MESH_ID,
        )

    keep = pltpu.make_async_copy(frames(held, group), frames(t_ref, group), local_sem.at[2])

    def pass_on(owner):
        pl.when(owner == group)(keep.start)
        pl.when(owner != group)(onward(owner).start)

    square_local.wait()
    for k in range(7):
        landed = all_ref.at[plane, lax.rem(member + 7 - k, 8)]
        square_plane(k, landed, landed, member_at(peers[k])).wait_recv()
    for k, there in enumerate(line):
        shown.append(square_line(k, all_ref.at[plane], all_ref.at[plane], {"z": there}))
        shown[-1].start()
    local.wait()
    pass_on(plane)
    for k, origin in enumerate(back):
        landed = frames(held, origin)
        copy(k, landed, landed, {"z": origin}).wait_recv()
        pass_on(origin)
    for origin in groups:
        landed = frames(t_ref, origin)
        pltpu.make_async_remote_copy(
            src_ref=landed,
            dst_ref=landed,
            send_sem=send_sem.at[3 + origin],
            recv_sem=recv_sem.at[3 + origin],
            device_id={"dp": origin},
            device_id_type=MESH_ID,
        ).wait_recv()
    keep.wait()
    weights_done()
    others_done()
    gain_keep.wait()
    for k in range(7):
        landed = s_ref.at[lax.rem(member + 7 - k, 8)]
        gain_plane(k, landed, landed, member_at(peers[k])).wait_recv()
    for k, origin in enumerate(back):
        square_line(k, all_ref.at[origin], all_ref.at[origin], {"z": origin}).wait_recv()
    for moving in sent + given + shown:
        moving.wait_send()
    for origin in groups:
        onward(origin).wait_send()


def closing(orders, y, base, grad, one, two, gu, down, gains):
    features, width = base.shape
    blocks = orders.shape[1]
    frames = (width, 2 * features)
    parts = (one, two, gu, down)
    return pl.pallas_call(
        closing_kernel,
        out_shape=(
            jax.ShapeDtypeStruct(frames, jnp.bfloat16),
            jax.ShapeDtypeStruct(one.shape, one.dtype),
            jax.ShapeDtypeStruct(two.shape, two.dtype),
            jax.ShapeDtypeStruct((8,) + gains.shape, gains.dtype),
            jax.ShapeDtypeStruct((4, 8, 8, 128), jnp.float32),
        ),
        in_specs=[IN_SMEM] + [IN_HBM] * 8,
        out_specs=(IN_HBM,) * 5,
        scratch_shapes=[pltpu.VMEM((blocks, features // blocks, width), jnp.float32)]
        + [pltpu.VMEM(base.shape, jnp.float32)] * 3
        + [pltpu.VMEM(frames, jnp.bfloat16)] * 2
        + [
            pltpu.VMEM((5,) + gains.shape, gains.dtype),
            pltpu.VMEM((8, 128), jnp.float32),
        ]
        + [pltpu.VMEM(part.shape, part.dtype) for part in parts]
        + [
            pltpu.SemaphoreType.DMA((14,)),
            pltpu.SemaphoreType.DMA((41,)),
            pltpu.SemaphoreType.DMA((41,)),
        ],
        compiler_params=pltpu.CompilerParams(
            collective_id=identity_of("closing", y),
            has_side_effects=True,
            vmem_limit_bytes=24 * 2**20,
        ),
        cost_estimate=BRIEF,
        name="closing",
    )(orders, y.reshape(blocks, -1, width), base, grad, one, two, gu, down, gains)


def turned(values, cosine, sine_table):
    half = HEAD // 2
    first_half, second_half = values[:half], values[half:]
    return jnp.concatenate(
        [
            first_half * cosine - second_half * sine_table,
            second_half * cosine + first_half * sine_table,
        ],
        axis=0,
    )


def attend_kernel(
    w_ref, h_ref, cos_ref, sin_ref, seg_ref, column_ref, part_ref, p_ref, o_ref, joint_ref
):
    heads, length = joint_ref.shape[1], joint_ref.shape[3]
    span = heads * HEAD
    cosine, sine_table = cos_ref[...], sin_ref[...]
    for k in range(3):
        by_row = w_ref[:, (4 + k) * span : (5 + k) * span].T

        @pl.loop(0, length // 256)
        def _(i, k=k, by_row=by_row):
            at = pl.ds(pl.multiple_of(i * 256, 256), 256)
            part = jnp.dot(by_row, h_ref[:, at], preferred_element_type=jnp.float32)
            for h in range(heads):
                joint_ref[k, h, :, at] = part[h * HEAD : (h + 1) * HEAD]

    for h in range(heads):
        queries = turned(joint_ref[0, h], cosine, sine_table)
        part_ref[0, h] = queries.astype(part_ref.dtype)
        keys = turned(joint_ref[1, h], cosine, sine_table)
        part_ref[1, h] = keys.astype(part_ref.dtype)
        part_ref[2, h] = joint_ref[2, h].astype(part_ref.dtype)
        by_key = keys.T.astype(part_ref.dtype)

        @pl.loop(0, length // 256)
        def _(i, h=h, by_key=by_key):
            at = pl.ds(pl.multiple_of(i * 256, 256), 256)
            scores = jnp.dot(
                by_key, part_ref[0, h, :, at], preferred_element_type=jnp.float32
            ) * (HEAD**-0.5)
            scores = jnp.where(column_ref[...] == seg_ref[:, at], scores, MASKED_SCORE)
            exponent = jnp.exp(scores - jnp.max(scores, axis=0, keepdims=True))
            probs = exponent * (1.0 / jnp.sum(exponent, axis=0, keepdims=True))
            p_ref[h, :, at] = probs.astype(p_ref.dtype)
            out = jnp.dot(part_ref[2, h], p_ref[h, :, at], preferred_element_type=jnp.float32)
            o_ref[h * HEAD : (h + 1) * HEAD, at] = out.astype(o_ref.dtype)


def attend(weight, frames, cosine, sine_table, segments):
    heads, length = D // HEAD // 8, frames.shape[1]
    joint = (3, heads, HEAD, length)
    small = jnp.bfloat16
    return pl.pallas_call(
        attend_kernel,
        out_shape=(
            jax.ShapeDtypeStruct(joint, small),
            jax.ShapeDtypeStruct((heads, length, length), small),
            jax.ShapeDtypeStruct((heads * HEAD, length), small),
        ),
        in_specs=[IN_VMEM] * 6,
        out_specs=(IN_VMEM,) * 3,
        scratch_shapes=[pltpu.VMEM(joint, jnp.float32)],
        compiler_params=pltpu.CompilerParams(vmem_limit_bytes=32 * 2**20),
        name="attend",
    )(weight, frames, cosine, sine_table, segments[None, :], segments[:, None])


def attend_back_kernel(part_ref, p_ref, grad_ref, cos_ref, sin_ref, o_ref, dq_ref, dk_ref, dv_ref):
    heads, length = part_ref.shape[1], part_ref.shape[3]
    cosine, sine_table = cos_ref[...], -sin_ref[...]
    scale = HEAD**-0.5
    for h in range(heads):
        of = slice(h * HEAD, (h + 1) * HEAD)
        by_key = wide(part_ref.at[2, h]).T.astype(part_ref.dtype)
        dk_ref[...] = jnp.zeros_like(dk_ref)
        dv_ref[...] = jnp.zeros_like(dv_ref)

        @pl.loop(0, length // 256)
        def _(i, h=h, of=of, by_key=by_key):
            at = pl.ds(pl.multiple_of(i * 256, 256), 256)
            grad_out = grad_ref[of, at]
            grad_probs = jnp.dot(by_key, grad_out, preferred_element_type=jnp.float32)
            low_probs = p_ref[h, :, at]
            probs = low_probs.astype(jnp.float32)
            weighted = jnp.sum(probs * grad_probs, axis=0, keepdims=True)
            grad_scores = (probs * (grad_probs - weighted)).astype(part_ref.dtype)
            dq_ref[:, at] = jnp.dot(
                part_ref[1, h], grad_scores, preferred_element_type=jnp.float32
            )
            dk_ref[...] += contract_last(part_ref[0, h, :, at], grad_scores)
            dv_ref[...] += contract_last(grad_out, low_probs)

        span = heads * HEAD
        grad_queries = turned(dq_ref[...] * scale, cosine, sine_table)
        grad_keys = turned(dk_ref[...] * scale, cosine, sine_table)
        o_ref[of, :] = grad_queries.astype(o_ref.dtype)
        o_ref[span + of.start : span + of.stop, :] = grad_keys.astype(o_ref.dtype)
        o_ref[2 * span + of.start : 2 * span + of.stop, :] = dv_ref[...].astype(o_ref.dtype)


def attend_back(parts, probs, grad, cosine, sine_table):
    _, heads, _, length = parts.shape
    return pl.pallas_call(
        attend_back_kernel,
        out_shape=jax.ShapeDtypeStruct((3 * heads * HEAD, length), jnp.bfloat16),
        in_specs=[IN_VMEM] * 5,
        out_specs=IN_VMEM,
        scratch_shapes=[pltpu.VMEM((HEAD, length), jnp.float32)] * 3,
        compiler_params=pltpu.CompilerParams(vmem_limit_bytes=32 * 2**20),
        name="attend_back",
    )(parts, probs, grad, cosine, sine_table)


def update_kernel(
    block_ref,
    rate_ref,
    one_ref,
    two_ref,
    feed_ref,
    all_ref,
    gain_ref,
    sheet_ref,
    first_ref,
    second_ref,
    grad_out,
    first_out,
    second_out,
    sheet_out,
    copy_out,
    norm_out,
    gain_out,
    grad,
    gain,
    scale,
):
    step = pl.program_id(0)
    part = D // 8
    text = CTXW // 8

    @pl.when(step == 0)
    def _():
        summed = jnp.sum(gain_ref[...], axis=0)
        rows = grad.shape[0]
        here = lax.broadcasted_iota(jnp.int32, (rows, D), 1) == (
            lax.broadcasted_iota(jnp.int32, (rows, D), 0) + block_ref[0] * rows
        )
        gain[...] = lax.dot_general(
            here.astype(jnp.float32),
            summed,
            (((1,), (1,)), ((), ())),
            precision=HIGHEST,
            preferred_element_type=jnp.float32,
        )
        norm = jnp.sqrt(jnp.sum(all_ref[:, :, 0:1, 0:1]) + jnp.sum(summed * summed))
        norm_out[0] = norm
        scale[0] = 1.0 / jnp.maximum(norm, 1.0)
        gain_out[...] = gain[...] * scale[0]

    for k in range(6):

        @pl.when(step == k)
        def _(k=k):
            ref, start = (one_ref, k * part) if k < 3 else (two_ref, (k - 3) * part)
            for m in range(8):
                grad[:, m * part : (m + 1) * part] = wide(ref.at[m, :, start : start + part])

    @pl.when(jnp.logical_and(step >= 6, step < 18))
    def _():
        grad[...] = wide(feed_ref)

    @pl.when(step == 18)
    def _():
        for m in range(8):
            for k in range(2):
                start = 3 * part + k * text
                place = k * CTXW + m * text
                grad[:, place : place + text] = wide(two_ref.at[m, :, start : start + text])

    @pl.when(step == 19)
    def _():
        grad[:, :8] = gain[...]

    clipped = grad[...] * scale[0]
    sheet = sheet_ref[...]
    first_new = BETA_ONE * first_ref[...] + (1.0 - BETA_ONE) * clipped
    second_new = BETA_TWO * second_ref[...] + (1.0 - BETA_TWO) * clipped * clipped
    mean_hat = first_new * (1.0 / (1.0 - BETA_ONE**STEP))
    square_hat = second_new * (1.0 / (1.0 - BETA_TWO**STEP))
    sheet_new = sheet - rate_ref[step] * (
        mean_hat / (jnp.sqrt(square_hat) + EPS_ADAM) + WEIGHT_DECAY * sheet
    )
    grad_out[...] = clipped
    first_out[...] = first_new
    second_out[...] = second_new
    sheet_out[...] = sheet_new
    copy_out[...] = sheet_new.astype(copy_out.dtype)


def sheet_update(block_index, length, one, two, feed_part, squares, gains, sheet, first, second):
    rows = sheet.shape[0]
    rates = column_spread(length)[jnp.minimum(jnp.arange(20) * D, SHEET - 1)]
    column_block = pl.BlockSpec((rows, D), lambda i: (0, i))
    like = jax.ShapeDtypeStruct(sheet.shape, sheet.dtype)

    def whole(array):
        return pl.BlockSpec(array.shape, lambda i: (0,) * array.ndim)

    sheet, first, second = (
        pltpu.with_memory_space_constraint(array, pltpu.HBM) for array in (sheet, first, second)
    )
    return pl.pallas_call(
        update_kernel,
        grid=(20,),
        out_shape=(like, like, like, like, jax.ShapeDtypeStruct(sheet.shape, jnp.bfloat16))
        + (jax.ShapeDtypeStruct((1,), jnp.float32), jax.ShapeDtypeStruct((rows, 8), jnp.float32)),
        in_specs=[
            IN_SMEM,
            IN_SMEM,
            whole(one),
            whole(two),
            pl.BlockSpec((rows, D), lambda i: (0, jnp.clip(i - 6, 0, 11))),
            whole(squares),
            whole(gains),
            column_block,
            column_block,
            column_block,
        ],
        out_specs=(column_block,) * 5 + (IN_SMEM, pl.BlockSpec((rows, 8), lambda i: (0, 0))),
        scratch_shapes=[
            pltpu.VMEM((rows, D), jnp.float32),
            pltpu.VMEM((rows, 8), jnp.float32),
            pltpu.SMEM((1,), jnp.float32),
        ],
        compiler_params=pltpu.CompilerParams(vmem_limit_bytes=24 * 2**20),
        name="sheet_update",
    )(block_index, rates, one, two, feed_part, squares, gains, sheet, first, second)


def pick_blocks(blocks, order):
    return blocks.at[order].get(mode="promise_in_bounds")


def gather_line(mine, order):
    blocks = lax.all_gather(mine, "z", axis=0, tiled=True)
    return pick_blocks(blocks, order).reshape(-1, mine.shape[-1])


def gather_slots(mine):
    return lax.all_gather(mine, "z", axis=0, tiled=True).reshape(-1, mine.shape[-1])


def sort_blocks(array, order):
    blocks = array.reshape(order.shape[0], -1, array.shape[-1])
    return pick_blocks(blocks, order).reshape(array.shape)


def as_blocks(grad, order):
    return grad.reshape(order.shape[0], -1, grad.shape[-1])


def scatter_line(blocks):
    return lax.psum_scatter(blocks, "z", scatter_dimension=0, tiled=True)


def plane_plan(latents, context, clip_starts, buckets, owners, cotangent, sheet, first, second):
    groups = lax.axis_size("dp")
    planes = lax.axis_size("z")
    cores = lax.axis_size("core")
    members = groups * cores
    frames = latents.shape[1]
    length = frames * members
    rows = sheet.shape[0]
    blocks = owners.shape[0]
    head_count = D // HEAD // members
    span = D // members
    units = FF // members
    score_scale = HEAD ** (-0.5)
    tail_col = 6 * D + 3 * FF
    gain_col = tail_col + 2 * CTXW
    plane = lax.axis_index("z")

    group_ids = jnp.arange(blocks, dtype=jnp.int32)
    inverse = jnp.sum(
        jnp.where(owners[None, :] == group_ids[:, None], group_ids[None, :], 0), axis=1
    )
    slot = group_ids.reshape(groups, planes, cores).swapaxes(0, 1).reshape(-1)
    slot_of = jnp.sum(
        jnp.where(slot[None, :] == group_ids[:, None], group_ids[None, :], 0), axis=1
    )
    to_logical = jnp.take(slot_of, inverse)
    to_slots = jnp.take(owners, slot)

    orders = jnp.stack([to_slots, to_logical])
    small = jnp.concatenate(
        [
            jnp.pad(
                sheet[:, gain_col:].astype(jnp.bfloat16).astype(jnp.float32).T,
                ((0, 0), (0, 64 - rows)),
            ),
            jnp.pad(clip_starts.astype(jnp.float32), ((0, 7), (0, 64 - clip_starts.shape[1]))),
        ],
        axis=1,
    )
    both, small, text_mine, mine_one = opening(
        latents[0], cotangent[0], small, context[0].T, sheet
    )
    mine_one, later = lax.optimization_barrier((mine_one, sheet))
    low_sheet = later.astype(jnp.bfloat16)
    weight_one = gather_slots(mine_one)
    weight_two = sort_blocks(weight_one[:, : 4 * span], to_logical)
    weight_cq = weight_two[:, span : 2 * span]
    weight_text = weight_two[:, 3 * span :]
    gains = pick_blocks(small[..., :rows].reshape(blocks, 8, rows), to_logical)
    gains = gains.swapaxes(1, 2).reshape(D, 8)
    starts = lax.dynamic_index_in_dim(
        small[0, :, 0, 64 : 64 + clip_starts.shape[1]], plane * cores, 0, False
    )
    starts = starts.astype(jnp.int32)

    bucket_ids = jnp.arange(NB, dtype=jnp.int32)
    bucket_pick = (bucket_ids == buckets[plane]).astype(jnp.float32)
    counts = jnp.sum((buckets[:, None] == bucket_ids[None, :]).astype(jnp.float32), axis=0)
    row_weight = buckets.shape[0] / (NB * jnp.sum(bucket_pick * counts))
    gain_one = gains[:, 0:1]
    gain_two = gains[:, 1:2]
    gain_three = gains[:, 2:3]
    time_gain = jnp.sum(gains[:, 3:] * bucket_pick[None, :], axis=1, keepdims=True)

    tokens = both[:, :D].astype(jnp.float32).T
    grad_out = both[:, D:].astype(jnp.float32).T * row_weight

    rest = frames // planes
    place = jnp.arange(length, dtype=jnp.int32).reshape(planes, cores, groups, rest)
    positions = place.transpose(2, 1, 0, 3).reshape(-1)
    segments = segment_ids(starts, positions)
    frequency = jnp.exp(
        -math.log(10000.0) * jnp.arange(HEAD // 2, dtype=jnp.float32) / (HEAD // 2)
    )
    angles = frequency[:, None] * positions.astype(jnp.float32)[None, :]
    cosine = jnp.cos(angles)
    sine_table = jnp.sin(angles)

    normed_one, inverse_one = norm_columns(tokens)
    scaled_one = gain_one * time_gain
    h_one, grad_ff, mine_gu, mine_down = first_gather(
        sort_blocks((normed_one * scaled_one).astype(jnp.bfloat16), to_slots),
        sort_blocks(grad_out.astype(jnp.bfloat16), to_slots),
        low_sheet,
    )
    weight_gu = gather_slots(mine_gu)
    line_down = gather_slots(mine_down)

    parts, probs, attn_out = attend(weight_one, h_one, cosine, sine_table, segments)
    text_width = CTXW // members
    text_kv = jnp.stack(
        [
            matmul(weight_text[:, :text_width], text_mine),
            matmul(weight_text[:, text_width:], text_mine),
        ],
        axis=1,
    ).reshape(D, 2 * CTX)
    attn_out, x_one, normed_two, inverse_two, h_two, text_kv = project(
        "sum",
        0,
        orders,
        attn_out,
        weight_two,
        tokens,
        gain_two,
        text_kv.astype(jnp.bfloat16),
    )

    text_kv = text_kv.reshape(head_count, HEAD, 2, CTX)
    text_keys = text_kv[:, :, 0]
    text_values = text_kv[:, :, 1]
    cross_q = contract_rows(weight_cq, h_two).astype(jnp.bfloat16).reshape(head_count, HEAD, length)
    cross_scores = (
        jnp.einsum("hdq,hdk->hqk", cross_q, text_keys, preferred_element_type=jnp.float32)
        * score_scale
    )
    cross_probs = softmax_rows(cross_scores)
    cross_low = cross_probs.astype(jnp.bfloat16)
    cross_out = jnp.einsum(
        "hqk,hdk->hdq", cross_low, text_values, preferred_element_type=jnp.float32
    )
    cross_out, x_two, normed_three, inverse_three, h_three = project(
        "slots",
        2 * span,
        orders,
        cross_out.reshape(span, length).astype(jnp.bfloat16),
        weight_two,
        x_one,
        gain_three,
    )

    gate_up = contract_rows(weight_gu, h_three)
    gate_pre = gate_up[:units]
    up_part = gate_up[units:]
    sigmoid_gate = jax.nn.sigmoid(gate_pre)
    silu_gate = gate_pre * sigmoid_gate
    hidden = (silu_gate * up_part).astype(jnp.bfloat16)

    grad_blocks_down = as_blocks(contract_last(grad_ff, hidden).astype(jnp.bfloat16), to_slots)
    weight_down, grad_blocks_down = lax.optimization_barrier((line_down, grad_blocks_down))
    sums_down = scatter_line(grad_blocks_down)
    grad_hidden = contract_rows(weight_down, grad_ff)
    grad_gate = grad_hidden * up_part * (sigmoid_gate * (1.0 + gate_pre * (1.0 - sigmoid_gate)))
    grad_up = grad_hidden * silu_gate
    grad_gu = jnp.concatenate([grad_gate, grad_up], axis=0).astype(jnp.bfloat16)
    grad_x_two, grad_weight_gu, sum_three, grad_cross = back(
        orders,
        weight_gu,
        grad_gu,
        h_three,
        (normed_three, inverse_three, gain_three, grad_out),
        send_rows=True,
        in_slots=True,
        after=[grad_blocks_down],
    )
    grad_blocks_gu = as_blocks(grad_weight_gu, to_slots)
    sums_gu = scatter_line(grad_blocks_gu)
    grad_cross_out, grad_weight_co = back(
        orders, weight_two, grad_cross, cross_out, column=2 * span
    )
    grad_cross_out = grad_cross_out.reshape(head_count, HEAD, length)
    grad_cross_probs = jnp.einsum(
        "hdq,hdk->hqk", grad_cross_out, text_values, preferred_element_type=jnp.float32
    )
    grad_cross_scores = (
        cross_probs
        * (grad_cross_probs - jnp.sum(cross_probs * grad_cross_probs, axis=-1, keepdims=True))
    ).astype(jnp.bfloat16)
    grad_cross_q = (
        jnp.einsum("hqk,hdk->hdq", grad_cross_scores, text_keys, preferred_element_type=jnp.float32)
        * score_scale
    )
    grad_cross_q = grad_cross_q.reshape(span, length).astype(jnp.bfloat16)
    grad_text_keys = (
        jnp.einsum("hqk,hdq->hdk", grad_cross_scores, cross_q, preferred_element_type=jnp.float32)
        * score_scale
    )
    grad_text_values = jnp.einsum(
        "hqk,hdq->hdk", cross_low, grad_cross_out, preferred_element_type=jnp.float32
    )
    grad_text = jnp.concatenate(
        [grad_text_keys.reshape(span, CTX), grad_text_values.reshape(span, CTX)], axis=1
    )
    grad_x_one, grad_weight_cq, sum_two, grad_attn, grad_text = back(
        orders,
        weight_two,
        grad_cross_q,
        h_two,
        (normed_two, inverse_two, gain_two, grad_x_two),
        column=span,
        send_rows=True,
        text=grad_text.astype(jnp.bfloat16),
        after=[sums_down],
    )
    grad_attn_out, grad_weight_two = back(
        orders,
        weight_two,
        grad_attn,
        attn_out,
        beside=(grad_weight_cq, grad_weight_co, grad_text, text_mine),
    )
    grad_blocks_two = as_blocks(grad_weight_two, to_slots)
    sums_two = scatter_line(grad_blocks_two)
    grad_qkv = attend_back(parts, probs, grad_attn_out, cosine, sine_table)
    latent_grad, grad_weight_qkv, sum_one = back(
        orders,
        weight_one,
        grad_qkv,
        h_one,
        (normed_one, inverse_one, scaled_one, grad_x_one),
        column=4 * span,
        in_slots=True,
        after=[sums_gu],
    )
    grad_blocks_one = as_blocks(grad_weight_qkv, to_slots)
    sums_one = scatter_line(grad_blocks_one)
    sums_feed, ff_out = feed(
        sums_gu,
        sums_down,
        weight_down,
        hidden,
        [grad_blocks_one],
    )
    sum_one = sum_one[0:1]
    grad_gain_one = sum_one * time_gain.T
    grad_time = sum_one * gain_one.T
    gain_grads = jnp.concatenate(
        [
            grad_gain_one,
            sum_two[0:1],
            sum_three[0:1],
            bucket_pick[:, None] * grad_time,
        ],
        axis=0,
    )
    out_pair, sums_one, sums_two, gain_sums, squares = closing(
        orders, ff_out, x_two, latent_grad, sums_one, sums_two, sums_gu, sums_down, gain_grads
    )
    output = out_pair[:, :D]
    latent_grad = out_pair[:, D:].astype(jnp.float32)
    place = lax.axis_index("dp") * (planes * cores) + plane * cores + lax.axis_index("core")
    clipped, first_new, second_new, sheet_new, sheet_copy, grad_norm, gain_grad = sheet_update(
        lax.dynamic_slice_in_dim(owners, place, 1),
        length,
        sums_one,
        sums_two,
        sums_feed,
        squares,
        gain_sums,
        sheet,
        first,
        second,
    )
    return (
        output[None],
        latent_grad[None],
        grad_norm[0],
        clipped,
        gain_grad,
        first_new,
        second_new,
        sheet_new,
        sheet_copy,
    )


def solution(mesh):
    groups, seq_count = mesh.shape["dp"], mesh.shape["seq"]
    by_plane = groups == 4 and seq_count == 8
    if by_plane:
        mesh = Mesh(mesh.devices.reshape(groups, seq_count // 2, 2), ("dp", "z", "core"))
    seq = ("z", "core") if by_plane else "seq"
    both = ("dp", "z", "core") if by_plane else ("dp", "seq")
    in_specs = (
        P("dp", seq, None),
        P("dp", None, None),
        P("dp", None),
        P(),
        P(),
        P("dp", seq, None),
        P(both, None),
        P(both, None),
        P(both, None),
    )
    out_specs = (
        P("dp", seq, None),
        P("dp", seq, None),
        P(),
        P(both, None),
        P(both, None),
        P(both, None),
        P(both, None),
        P(both, None),
        P(both, None),
    )
    return jax.shard_map(
        plane_plan if by_plane else gather_plan,
        mesh=mesh,
        in_specs=in_specs,
        out_specs=out_specs,
        check_vma=False,
    )
```

```python
import functools
import math

import jax
import jax.numpy as jnp
from jax import lax
from jax.experimental import pallas as pl
from jax.experimental.pallas import tpu as pltpu
from jax.sharding import Mesh
from jax.sharding import PartitionSpec as P

D = 1536
FF = 6144
HEAD = 64
CTXW = 768
CTX = 128
NB = 5
STEP = 10
SHEET = 29192


HIGHEST = lax.Precision.HIGHEST
EPS_NORM = 1e-05
EPS_ADAM = 1e-08
MASKED_SCORE = -1e30
BETA_ONE = 0.5
BETA_TWO = 0.5
WEIGHT_DECAY = 0.01


def reorder(values, ordering):
    leading = values.shape[:-1]
    groups = ordering.shape[0]
    blocks = values.reshape(leading + (groups, values.shape[-1] // groups))
    return jnp.take(blocks, ordering, axis=-2).reshape(values.shape)


def norm_parts(values):
    average = jnp.mean(values, axis=-1, keepdims=True)
    centered = values - average
    variance = jnp.mean(centered * centered, axis=-1, keepdims=True)
    inverse_std = lax.rsqrt(variance + EPS_NORM)
    return (centered * inverse_std, inverse_std)


def norm_back(grad_normed, normed, inverse_std):
    return inverse_std * (
        grad_normed
        - jnp.mean(grad_normed, axis=-1, keepdims=True)
        - normed * jnp.mean(grad_normed * normed, axis=-1, keepdims=True)
    )


def softmax_rows(scores):
    row_max = jnp.max(scores, axis=-1, keepdims=True)
    exponent = jnp.exp(scores - row_max)
    return exponent / jnp.sum(exponent, axis=-1, keepdims=True)


def rope_tables(positions, head_dim):
    half_dim = head_dim // 2
    frequency = jnp.exp(-math.log(10000.0) * jnp.arange(half_dim, dtype=jnp.float32) / half_dim)
    angles = positions.astype(jnp.float32)[:, None] * frequency[None, :]
    return (jnp.cos(angles)[:, None, :], jnp.sin(angles)[:, None, :])


def rotate(values, cosine, sine_table):
    half_dim = values.shape[-1] // 2
    first_half = values[..., :half_dim]
    second_half = values[..., half_dim:]
    return jnp.concatenate(
        [
            first_half * cosine - second_half * sine_table,
            second_half * cosine + first_half * sine_table,
        ],
        axis=-1,
    )


def unrotate(grads, cosine, sine_table):
    half_dim = grads.shape[-1] // 2
    first_half = grads[..., :half_dim]
    second_half = grads[..., half_dim:]
    return jnp.concatenate(
        [
            first_half * cosine + second_half * sine_table,
            second_half * cosine - first_half * sine_table,
        ],
        axis=-1,
    )


def segment_ids(starts, positions):
    return jnp.sum((starts[None, :] <= positions[:, None]).astype(jnp.int32), axis=1) - 1


def column_spread(length):
    column = jnp.arange(SHEET, dtype=jnp.int32)
    base_std = D ** (-0.5)
    spread = jnp.full((SHEET,), base_std, jnp.float32)
    spread = jnp.where(
        (column >= 3 * D) & (column < 4 * D), base_std * math.sqrt(length) / 4.0, spread
    )
    spread = jnp.where((column >= 5 * D) & (column < 6 * D), base_std * math.sqrt(CTX), spread)
    spread = jnp.where((column >= 6 * D + 2 * FF) & (column < 6 * D + 3 * FF), FF ** (-0.5), spread)
    spread = jnp.where(
        (column >= 6 * D + 3 * FF) & (column < 6 * D + 3 * FF + 2 * CTXW), CTXW ** (-0.5), spread
    )
    spread = jnp.where(column >= 6 * D + 3 * FF + 2 * CTXW, 0.3, spread)
    return spread


def inner_rows(left, right):
    return lax.dot_general(
        left, right, (((0,), (0,)), ((), ())), preferred_element_type=jnp.float32
    )


def inner_rows_high(left, right):
    return lax.dot_general(
        left, right, (((0,), (0,)), ((), ())), precision=HIGHEST, preferred_element_type=jnp.float32
    )


def gather_plan(latents, context, clip_starts, buckets, owners, cotangent, sheet, first, second):
    frames = latents.shape[1]
    seq_count = lax.axis_size("seq")
    length = frames * seq_count
    head_count = D // HEAD
    score_scale = HEAD ** (-0.5)
    group_ids = jnp.arange(owners.shape[0], dtype=jnp.int32)
    inverse = jnp.sum(
        jnp.where(owners[None, :] == group_ids[:, None], group_ids[None, :], 0), axis=1
    )
    gathered = lax.all_gather(sheet.astype(jnp.bfloat16), ("dp", "seq"), axis=0, tiled=True)
    tail_col = 6 * D + 3 * FF
    gain_col = tail_col + 2 * CTXW
    gain_rows = reorder(gathered[:, gain_col:].astype(jnp.float32).T, inverse)
    row_index = lax.axis_index("dp")
    bucket_ids = jnp.arange(NB, dtype=jnp.int32)
    bucket_pick = (bucket_ids == buckets[row_index]).astype(jnp.float32)
    counts = jnp.sum((buckets[:, None] == bucket_ids[None, :]).astype(jnp.float32), axis=0)
    row_weight = buckets.shape[0] / (NB * jnp.sum(bucket_pick * counts))
    gain_one = gain_rows[0]
    gain_two = gain_rows[1]
    gain_three = gain_rows[2]
    time_gain = jnp.sum(gain_rows[3:] * bucket_pick[:, None], axis=0)
    tokens = latents[0].astype(jnp.float32)
    positions = lax.axis_index("seq") * frames + jnp.arange(frames, dtype=jnp.int32)
    all_positions = jnp.arange(length, dtype=jnp.int32)
    starts = clip_starts[0]
    same_clip = (
        segment_ids(starts, positions)[:, None] == segment_ids(starts, all_positions)[None, :]
    )[None]
    cosine, sine_table = rope_tables(positions, HEAD)
    normed_one, inverse_one = norm_parts(tokens)
    scaled_one = gain_one * time_gain
    h_one_st = reorder((normed_one * scaled_one).astype(jnp.bfloat16), owners)
    joint_qkv = jnp.dot(h_one_st, gathered[:, : 3 * D], preferred_element_type=jnp.float32)
    queries = rotate(joint_qkv[:, :D].reshape(frames, head_count, HEAD), cosine, sine_table).astype(
        jnp.bfloat16
    )
    key_local = rotate(
        joint_qkv[:, D : 2 * D].reshape(frames, head_count, HEAD), cosine, sine_table
    ).astype(jnp.bfloat16)
    value_local = joint_qkv[:, 2 * D :].reshape(frames, head_count, HEAD).astype(jnp.bfloat16)
    key_all, value_all = (
        lax.all_gather(key_local, "seq", axis=0, tiled=True),
        lax.all_gather(value_local, "seq", axis=0, tiled=True),
    )
    scores = (
        jnp.einsum("qhd,khd->hqk", queries, key_all, preferred_element_type=jnp.float32)
        * score_scale
    )
    attn_probs = softmax_rows(jnp.where(same_clip, scores, MASKED_SCORE))
    probs_low = attn_probs.astype(jnp.bfloat16)
    attn_out = (
        jnp.einsum("hqk,khd->qhd", probs_low, value_all, preferred_element_type=jnp.float32)
        .reshape(frames, D)
        .astype(jnp.bfloat16)
    )
    attn_st = reorder(attn_out, owners)
    x_one = tokens + jnp.dot(
        attn_st, gathered[:, 3 * D : 4 * D], preferred_element_type=jnp.float32
    )
    normed_two, inverse_two = norm_parts(x_one)
    h_two_st = reorder((normed_two * gain_two).astype(jnp.bfloat16), owners)
    cross_q = (
        jnp.dot(h_two_st, gathered[:, 4 * D : 5 * D], preferred_element_type=jnp.float32)
        .astype(jnp.bfloat16)
        .reshape(frames, head_count, HEAD)
    )
    text_tokens = context[0]
    text_kv = jnp.einsum(
        "tc,dec->etd",
        text_tokens,
        gathered[:, tail_col:gain_col].reshape(D, 2, CTXW),
        preferred_element_type=jnp.float32,
    )
    text_kv = reorder(text_kv, inverse).astype(jnp.bfloat16).reshape(2, CTX, head_count, HEAD)
    text_keys = text_kv[0]
    text_values = text_kv[1]
    cross_scores = (
        jnp.einsum("qhd,khd->hqk", cross_q, text_keys, preferred_element_type=jnp.float32)
        * score_scale
    )
    cross_probs = softmax_rows(cross_scores)
    cross_low = cross_probs.astype(jnp.bfloat16)
    cross_out = (
        jnp.einsum("hqk,khd->qhd", cross_low, text_values, preferred_element_type=jnp.float32)
        .reshape(frames, D)
        .astype(jnp.bfloat16)
    )
    cross_st = reorder(cross_out, owners)
    x_two = x_one + jnp.dot(
        cross_st, gathered[:, 5 * D : 6 * D], preferred_element_type=jnp.float32
    )
    normed_three, inverse_three = norm_parts(x_two)
    h_three_st = reorder((normed_three * gain_three).astype(jnp.bfloat16), owners)
    grad_out = cotangent[0].astype(jnp.float32) * row_weight
    grad_ff_st = reorder(grad_out.astype(jnp.bfloat16), owners)
    gate_weight = gathered[:, 6 * D : 6 * D + 2 * FF]
    down_weight = gathered[:, 6 * D + 2 * FF : 6 * D + 3 * FF]
    units = down_weight.shape[1]
    gate_up = jnp.dot(h_three_st, gate_weight, preferred_element_type=jnp.float32)
    gate_pre = gate_up[:, :units]
    up_part = gate_up[:, units:]
    sigmoid_gate = jax.nn.sigmoid(gate_pre)
    silu_gate = gate_pre * sigmoid_gate
    hidden = (silu_gate * up_part).astype(jnp.bfloat16)
    ff_out = reorder(
        jnp.einsum("nf,df->nd", hidden, down_weight, preferred_element_type=jnp.float32), inverse
    )
    result = x_two + ff_out
    grad_hidden = jnp.dot(grad_ff_st, down_weight, preferred_element_type=jnp.float32)
    grad_gate = grad_hidden * up_part * (sigmoid_gate * (1.0 + gate_pre * (1.0 - sigmoid_gate)))
    grad_up = grad_hidden * silu_gate
    grad_gu = jnp.concatenate([grad_gate, grad_up], axis=1).astype(jnp.bfloat16)
    grad_h_three = reorder(
        jnp.einsum("nf,df->nd", grad_gu, gate_weight, preferred_element_type=jnp.float32), inverse
    )
    grad_gain_three = jnp.sum(grad_h_three * normed_three, axis=0)
    grad_x_two = grad_out + norm_back(grad_h_three * gain_three, normed_three, inverse_three)
    grad_cross = grad_x_two.astype(jnp.bfloat16)
    grad_cross_out = (
        reorder(
            jnp.einsum(
                "nd,ed->ne",
                grad_cross,
                gathered[:, 5 * D : 6 * D],
                preferred_element_type=jnp.float32,
            ),
            inverse,
        )
        .astype(jnp.bfloat16)
        .reshape(frames, head_count, HEAD)
    )
    grad_cross_probs = jnp.einsum(
        "qhd,khd->hqk", grad_cross_out, text_values, preferred_element_type=jnp.float32
    )
    grad_cross_scores = (
        cross_probs
        * (grad_cross_probs - jnp.sum(cross_probs * grad_cross_probs, axis=-1, keepdims=True))
    ).astype(jnp.bfloat16)
    grad_cross_q = (
        (
            jnp.einsum(
                "hqk,khd->qhd", grad_cross_scores, text_keys, preferred_element_type=jnp.float32
            )
            * score_scale
        )
        .reshape(frames, D)
        .astype(jnp.bfloat16)
    )
    grad_text_keys = (
        jnp.einsum("hqk,qhd->khd", grad_cross_scores, cross_q, preferred_element_type=jnp.float32)
        * score_scale
    )
    grad_text_values = jnp.einsum(
        "hqk,qhd->khd", cross_low, grad_cross_out, preferred_element_type=jnp.float32
    )
    grad_text = reorder(
        jnp.stack([grad_text_keys.reshape(CTX, D), grad_text_values.reshape(CTX, D)]), owners
    )
    grad_h_two = reorder(
        jnp.einsum(
            "ne,de->nd",
            grad_cross_q,
            gathered[:, 4 * D : 5 * D],
            preferred_element_type=jnp.float32,
        ),
        inverse,
    )
    grad_gain_two = jnp.sum(grad_h_two * normed_two, axis=0)
    grad_x_one = grad_x_two + norm_back(grad_h_two * gain_two, normed_two, inverse_two)
    grad_attn = grad_x_one.astype(jnp.bfloat16)
    grad_attn_out = (
        reorder(
            jnp.einsum(
                "nd,ed->ne",
                grad_attn,
                gathered[:, 3 * D : 4 * D],
                preferred_element_type=jnp.float32,
            ),
            inverse,
        )
        .astype(jnp.bfloat16)
        .reshape(frames, head_count, HEAD)
    )
    key_back, value_back = (key_all, value_all)

    def head_grads(head_items):
        head_probs, head_grad_out, head_values = head_items
        grad_probs = jnp.einsum(
            "qd,kd->qk", head_grad_out, head_values, preferred_element_type=jnp.float32
        )
        return (
            head_probs * (grad_probs - jnp.sum(head_probs * grad_probs, axis=-1, keepdims=True))
        ).astype(jnp.bfloat16)

    grad_scores_low = lax.map(
        head_grads, (attn_probs, jnp.swapaxes(grad_attn_out, 0, 1), jnp.swapaxes(value_back, 0, 1))
    )
    grad_queries = (
        jnp.einsum("hqk,khd->qhd", grad_scores_low, key_back, preferred_element_type=jnp.float32)
        * score_scale
    )
    grad_keys = (
        jnp.einsum("hqk,qhd->khd", grad_scores_low, queries, preferred_element_type=jnp.float32)
        * score_scale
    )
    grad_values = jnp.einsum(
        "hqk,qhd->khd", probs_low, grad_attn_out, preferred_element_type=jnp.float32
    )
    key_sums = lax.psum_scatter(
        jnp.concatenate(
            [
                grad_keys.reshape(frames * lax.axis_size("seq"), D),
                grad_values.reshape(frames * lax.axis_size("seq"), D),
            ],
            axis=1,
        ).astype(jnp.bfloat16),
        "seq",
        scatter_dimension=0,
        tiled=True,
    ).astype(jnp.float32)
    grad_q_raw = unrotate(grad_queries, cosine, sine_table).reshape(frames, D)
    grad_k_raw = unrotate(
        key_sums[:, :D].reshape(frames, head_count, HEAD), cosine, sine_table
    ).reshape(frames, D)
    grad_qkv = jnp.concatenate([grad_q_raw, grad_k_raw, key_sums[:, D:]], axis=1).astype(
        jnp.bfloat16
    )
    grad_h_one = reorder(
        jnp.einsum("ne,de->nd", grad_qkv, gathered[:, : 3 * D], preferred_element_type=jnp.float32),
        inverse,
    )
    grad_gain_one = jnp.sum(grad_h_one * normed_one * time_gain, axis=0)
    grad_time = jnp.sum(grad_h_one * normed_one * gain_one, axis=0)
    latent_grad = grad_x_one + norm_back(grad_h_one * scaled_one, normed_one, inverse_one)
    gain_grads = jnp.concatenate(
        [
            jnp.stack([grad_gain_one, grad_gain_two, grad_gain_three]),
            bucket_pick[:, None] * grad_time[None, :],
        ],
        axis=0,
    )
    gain_grads = reorder(gain_grads, owners).T
    text_float = text_tokens.astype(jnp.float32)
    pieces = [
        inner_rows(h_one_st, grad_qkv),
        inner_rows(attn_st, grad_attn),
        inner_rows(h_two_st, grad_cross_q),
        inner_rows(cross_st, grad_cross),
    ]
    pieces = pieces + [inner_rows(h_three_st, grad_gu), inner_rows(grad_ff_st, hidden)]
    pieces = pieces + [
        inner_rows_high(grad_text[0], text_float),
        inner_rows_high(grad_text[1], text_float),
        gain_grads,
    ]
    other_shard = lax.psum_scatter(
        jnp.concatenate(pieces, axis=1), ("dp", "seq"), scatter_dimension=0, tiled=True
    )
    total_squares = lax.psum(jnp.sum(other_shard * other_shard), ("dp", "seq"))
    grad_norm = jnp.sqrt(total_squares)
    clipped = other_shard / jnp.maximum(grad_norm, 1.0)
    gain_grad = clipped[:, 6 * D + 3 * FF + 2 * CTXW :]
    first_new = BETA_ONE * first + (1.0 - BETA_ONE) * clipped
    second_new = BETA_TWO * second + (1.0 - BETA_TWO) * clipped * clipped
    mean_hat = first_new / (1.0 - BETA_ONE**STEP)
    square_hat = second_new / (1.0 - BETA_TWO**STEP)
    rates = column_spread(length)[None, :]
    sheet_new = sheet - rates * (
        mean_hat / (jnp.sqrt(square_hat) + EPS_ADAM) + WEIGHT_DECAY * sheet
    )
    return (
        result.astype(jnp.bfloat16)[None],
        latent_grad[None],
        grad_norm,
        clipped,
        gain_grad,
        first_new,
        second_new,
        sheet_new,
        sheet_new.astype(jnp.bfloat16),
    )


PLANE = ("dp", "core")


def norm_columns(values):
    average = jnp.mean(values, axis=0, keepdims=True)
    centered = values - average
    variance = jnp.mean(centered * centered, axis=0, keepdims=True)
    inverse_std = lax.rsqrt(variance + EPS_NORM)
    return (centered * inverse_std, inverse_std)


def norm_columns_back(grad_normed, normed, inverse_std):
    return inverse_std * (
        grad_normed
        - jnp.mean(grad_normed, axis=0, keepdims=True)
        - normed * jnp.mean(grad_normed * normed, axis=0, keepdims=True)
    )


def contract_rows(left, right):
    return lax.dot_general(
        left, right, (((0,), (0,)), ((), ())), preferred_element_type=jnp.float32
    )


def contract_last(left, right):
    return lax.dot_general(
        left, right, (((1,), (1,)), ((), ())), preferred_element_type=jnp.float32
    )


def matmul(left, right):
    return jnp.dot(left, right, preferred_element_type=jnp.float32)


MESH_ID = pl.DeviceIdType.MESH
IDENTITIES = {}


def identity_of(name, *arrays):
    key = (name,) + tuple((array.shape, str(array.dtype)) for array in arrays)
    return IDENTITIES.setdefault(key, len(IDENTITIES))


IN_HBM = pl.BlockSpec(memory_space=pltpu.HBM)
IN_SMEM = pl.BlockSpec(memory_space=pltpu.SMEM)
IN_VMEM = pl.BlockSpec(memory_space=pltpu.VMEM)
BRIEF = pl.CostEstimate(flops=0, bytes_accessed=1024, transcendentals=0)


def kernel_call(kernel, *, out_shape, in_specs, out_specs, **options):
    single = not isinstance(out_shape, tuple)
    shapes = (out_shape,) if single else out_shape
    places = (out_specs,) if single else out_specs
    shapes = tuple(
        pltpu.HBM(shape.shape, shape.dtype) if place is IN_HBM else shape
        for shape, place in zip(shapes, places)
    )
    call = pl.pallas_call(
        kernel,
        out_shape=shapes[0] if single else shapes,
        in_specs=in_specs,
        out_specs=out_specs,
        **options,
    )

    def run(*operands):
        return call(
            *[
                pltpu.with_memory_space_constraint(operand, pltpu.HBM)
                if place is IN_HBM
                else operand
                for operand, place in zip(operands, in_specs)
            ]
        )

    return run


def reorder_blocks(source, target, order, column=0):
    rows = source.shape[1]
    columns = slice(column, column + target.shape[1])

    @pl.loop(0, source.shape[0])
    def _(b):
        target[pl.ds(pl.multiple_of(b * rows, 16), rows), :] = source[order(b), :, columns]


def wide(ref):
    return ref[...].astype(jnp.float32)


def greet(peers):
    barrier = pltpu.get_barrier_semaphore()
    for peer in peers:
        pl.semaphore_signal(barrier, inc=1, device_id=peer, device_id_type=MESH_ID)
    pl.semaphore_wait(barrier, len(peers))


def near():
    group, core = lax.axis_index("dp"), lax.axis_index("core")
    across = group + 1 - 2 * lax.rem(group, 2)
    along = lax.rem(group + 2, 4)
    return group, core, across, along


def member_rows(width):
    def place(ref, member, start, count):
        first_row = pl.multiple_of(member * width + start, 16)
        return ref.at[pl.ds(first_row, count), :]

    return place


def member_lanes(width):
    def place(ref, member, start, count):
        return ref.at[pl.ds(start, count), pl.ds(pl.multiple_of(member * width, 128), width)]

    return place


def mover(send_sem, recv_sem, first=0):
    def copy(k, source, target, peer):
        return pltpu.make_async_remote_copy(
            src_ref=source,
            dst_ref=target,
            send_sem=send_sem.at[first + k],
            recv_sem=recv_sem.at[first + k],
            device_id=peer,
            device_id_type=MESH_ID,
        )

    return copy


def member_at(member):
    return {"dp": lax.div(member, 2), "core": lax.rem(member, 2)}


def plane_peers():
    group, core, _, _ = near()
    member = group * 2 + core
    return [lax.rem(member + step, 8) for step in range(1, 8)]


def gather_steps(place, x_ref, o_ref, local_sem, copy, arrived_whole=lambda member: None):
    group, core, across, along = near()
    beyond = across + along - group
    other = 1 - core
    sibling, by_x, by_y = {"core": other}, {"dp": across}, {"dp": along}
    half = x_ref.shape[0] // 2

    def part(owner, owner_core, piece):
        return place(o_ref, owner * 2 + owner_core, piece * half, half)

    sent = []

    def send(k, source, target, peer):
        moving = copy(k, source, target, peer)
        moving.start()
        sent.append(moving)

    def own(k, piece, peer):
        send(k, x_ref.at[pl.ds(piece * half, half), :], part(group, core, piece), peer)

    def relay(k, owner, piece, peer):
        send(k, part(owner, core, piece), part(owner, core, piece), peer)

    def arrived(k, owner, owner_core, piece):
        landed = part(owner, owner_core, piece)
        copy(k, landed, landed, sibling).wait_recv()

    local = pltpu.make_async_copy(
        x_ref, place(o_ref, group * 2 + core, 0, 2 * half), local_sem
    )
    local.start()
    own(0, 0, by_x)
    own(1, 1, by_y)
    own(2, 1, by_x)
    own(3, 0, by_y)
    own(4, 0, sibling)
    own(5, 1, sibling)

    def finish():
        local.wait()
        arrived_whole(group * 2 + core)
        arrived(4, group, other, 0)
        arrived(5, group, other, 1)
        arrived_whole(group * 2 + other)
        arrived(0, across, core, 0)
        relay(6, across, 0, by_y)
        relay(7, across, 0, sibling)
        arrived(1, along, core, 1)
        relay(8, along, 1, by_x)
        relay(9, along, 1, sibling)
        arrived(2, across, core, 1)
        relay(10, across, 1, sibling)
        arrived_whole(across * 2 + core)
        arrived(3, along, core, 0)
        relay(11, along, 0, sibling)
        arrived_whole(along * 2 + core)
        arrived(7, across, other, 0)
        arrived(10, across, other, 1)
        arrived_whole(across * 2 + other)
        arrived(6, beyond, core, 0)
        relay(12, beyond, 0, sibling)
        arrived(8, beyond, core, 1)
        relay(13, beyond, 1, sibling)
        arrived_whole(beyond * 2 + core)
        arrived(9, along, other, 1)
        arrived(11, along, other, 0)
        arrived_whole(along * 2 + other)
        arrived(12, beyond, other, 0)
        arrived(13, beyond, other, 1)
        arrived_whole(beyond * 2 + other)
        for moving in sent:
            moving.wait_send()

    return finish


def exchange_steps(source, target, x_ref, o_ref, local_sem, copy):
    group, core, _, _ = near()
    member = group * 2 + core
    local = pltpu.make_async_copy(source(x_ref, member), target(o_ref, member), local_sem)
    local.start()
    sent = []
    for k, peer in enumerate(plane_peers()):
        sent.append(copy(k, source(x_ref, peer), target(o_ref, member), member_at(peer)))
        sent[-1].start()

    def finish():
        for k in range(7):
            sender = lax.rem(member + 7 - k, 8)
            landed = target(o_ref, sender)
            copy(k, landed, landed, member_at(sender)).wait_recv()
        local.wait()
        for moving in sent:
            moving.wait_send()

    return finish


def gather_kernel(place, x_ref, *refs):
    o_ref, local_sem, send_sem, recv_sem = refs[-4:]
    _, core, across, along = near()
    greet([{"dp": across}, {"dp": along}, {"core": 1 - core}])
    gather_steps(place, x_ref, o_ref, local_sem, mover(send_sem, recv_sem))()


def plane_gather_call(shard, shape, place, kind, after):
    return kernel_call(
        functools.partial(gather_kernel, place),
        out_shape=jax.ShapeDtypeStruct(shape, shard.dtype),
        in_specs=[IN_HBM] * (1 + len(after)),
        out_specs=IN_HBM,
        scratch_shapes=[
            pltpu.SemaphoreType.DMA,
            pltpu.SemaphoreType.DMA((14,)),
            pltpu.SemaphoreType.DMA((14,)),
        ],
        compiler_params=pltpu.CompilerParams(
            collective_id=identity_of(kind, shard, *after), has_side_effects=True
        ),
        cost_estimate=BRIEF,
        name="plane_gather",
    )(shard, *after)


def plane_gather(shard, after=()):
    rows, width = shard.shape
    return plane_gather_call(shard, (rows, 8 * width), member_lanes(width), "gather lanes", after)


def plane_gather_rows(shard, after=()):
    rows, width = shard.shape
    return plane_gather_call(shard, (8 * rows, width), member_rows(rows), "gather rows", after)


def scatter_steps(place, p_ref, bufs, copy):
    pair, total, from_x, from_y, relay = bufs
    group, core, across, along = near()
    beyond = across + along - group
    other = 1 - core
    sibling, by_x, by_y = {"core": other}, {"dp": across}, {"dp": along}
    rows = total.shape[1]
    half = rows // 2
    low, high = pl.ds(0, half), pl.ds(half, half)
    sent = []

    def send(k, source, target, peer):
        moving = copy(k, source, target, peer)
        moving.start()
        sent.append(moving)

    def arrived(k, target):
        copy(k, target, target, sibling).wait_recv()

    def both_cores(k, owner):
        arrived(k, pair.at[k])
        summed = wide(place(p_ref, owner * 2 + core, 0, rows)) + wide(pair.at[k])
        total[k] = summed.astype(total.dtype)

    def cores():
        for k, owner in enumerate((beyond, across, along, group)):
            send(k, place(p_ref, owner * 2 + other, 0, rows), pair.at[k], sibling)

    def chips():
        both_cores(0, beyond)
        send(4, total.at[0, low], relay.at[0], by_x)
        send(5, total.at[0, high], relay.at[1], by_y)
        both_cores(1, across)
        send(6, total.at[1, low], from_x.at[low], by_x)
        both_cores(2, along)
        send(7, total.at[2, high], from_y.at[high], by_y)
        both_cores(3, group)

    def relays():
        arrived(5, relay.at[1])
        total[1, high] = (wide(total.at[1, high]) + wide(relay.at[1])).astype(total.dtype)
        send(8, total.at[1, high], from_x.at[high], by_x)
        arrived(4, relay.at[0])
        total[2, low] = (wide(total.at[2, low]) + wide(relay.at[0])).astype(total.dtype)
        send(9, total.at[2, low], from_y.at[low], by_y)

    def finish():
        arrived(6, from_x.at[low])
        arrived(7, from_y.at[high])
        arrived(8, from_x.at[high])
        arrived(9, from_y.at[low])
        summed = wide(total.at[3]) + wide(from_x) + wide(from_y)
        for moving in sent:
            moving.wait_send()
        return summed

    return cores, chips, relays, finish


def scatter_bufs(rows, width):
    slot = pltpu.VMEM((rows, width), jnp.bfloat16)
    four = pltpu.VMEM((4, rows, width), jnp.bfloat16)
    return [four, four, slot, slot, pltpu.VMEM((2, rows // 2, width), jnp.bfloat16)]


def scatter_kernel(place, p_ref, *refs):
    o_ref, *bufs, send_sem, recv_sem = refs[-8:]
    _, core, across, along = near()
    greet([{"dp": across}, {"dp": along}, {"core": 1 - core}])
    cores, chips, relays, finish = scatter_steps(place, p_ref, bufs, mover(send_sem, recv_sem))
    cores()
    chips()
    relays()
    o_ref[...] = finish().astype(o_ref.dtype)


def plane_scatter_call(partial, shape, place, dtype, kind, after):
    rows, width = shape
    return kernel_call(
        functools.partial(scatter_kernel, place),
        out_shape=jax.ShapeDtypeStruct(shape, dtype),
        in_specs=[IN_VMEM] + [IN_HBM] * len(after),
        out_specs=IN_VMEM,
        scratch_shapes=scatter_bufs(rows, width)
        + [
            pltpu.SemaphoreType.DMA((10,)),
            pltpu.SemaphoreType.DMA((10,)),
        ],
        compiler_params=pltpu.CompilerParams(
            collective_id=identity_of(kind, partial, *after),
            has_side_effects=True,
            vmem_limit_bytes=24 * 2**20,
        ),
        cost_estimate=BRIEF,
        name="plane_scatter",
    )(partial, *after)


def plane_scatter_frames(partial, after=()):
    rows, width = partial.shape[0], partial.shape[1] // 8
    place = member_lanes(width)
    return plane_scatter_call(partial, (rows, width), place, jnp.float32, "scatter lanes", after)


def plane_scatter_rows(partial, after=()):
    rows, width = partial.shape[0] // 8, partial.shape[1]
    place = member_rows(rows)
    return plane_scatter_call(partial, (rows, width), place, jnp.bfloat16, "scatter rows", after)


def project_kernel(kind, column, order_ref, s_ref, w_ref, base_ref, gain_ref, *refs):
    if kind == "sum":
        side_ref, full_ref, x_ref, n_ref, i_ref, h_ref, side_out, *refs = refs
    else:
        full_ref, x_ref, n_ref, i_ref, h_ref, *refs = refs
    full, total, part, landed, shard, by_block, base, gain, residual, normed, *refs = refs
    heads, slots, weight, *bufs, local_sem, send_sem, recv_sem = refs
    rows, length = s_ref.shape
    width = base_ref.shape[1]
    fetches = [
        pltpu.make_async_copy(ref, held, local_sem.at[8 + k])
        for k, (ref, held) in enumerate(
            [(s_ref, heads), (w_ref.at[:, :, : slots.shape[2]], slots)]
            + [(base_ref, base), (gain_ref, gain)]
        )
    ]
    for fetch in fetches:
        fetch.start()
    greet([member_at(peer) for peer in plane_peers()])
    side = mover(send_sem, recv_sem, 35)
    if kind == "sum":
        cores, chips, relays, finish = scatter_steps(
            member_rows(side_out.shape[0]), bufs[-1], bufs[:-2], side
        )
        text_weight = bufs[-2]
        fetches[1].wait()
        reorder_blocks(slots, text_weight, lambda b: order_ref[1, b], 3 * rows)
        tokens = side_ref.shape[1]

        @pl.loop(0, text_weight.shape[0] // 256)
        def _(i):
            at = pl.ds(pl.multiple_of(i * 256, 256), 256)
            for k in range(2):
                half = slice(k * side_ref.shape[0], (k + 1) * side_ref.shape[0])
                bufs[-1][at, k * tokens : (k + 1) * tokens] = jnp.dot(
                    text_weight[at, half], side_ref[...], preferred_element_type=jnp.float32
                ).astype(jnp.bfloat16)

        cores()
    else:
        fetches[1].wait()
    reorder_blocks(slots, weight, lambda b: order_ref[1, b], column)
    fetches[0].wait()
    total[...] = jnp.zeros_like(total)

    def add(member):
        of = pl.ds(pl.multiple_of(member * rows, 16), rows)

        @pl.loop(0, length // 256)
        def _(i):
            at = pl.ds(pl.multiple_of(i * 256, 256), 256)
            total[:, at] += contract_rows(weight[of, :], full[of, at])

    gathered = gather_steps(
        member_rows(rows), heads, full, local_sem.at[0], mover(send_sem, recv_sem), add
    )
    if kind == "sum":
        chips()
    gathered()
    kept = pltpu.make_async_copy(full, full_ref, local_sem.at[0])
    kept.start()
    part[...] = total[...].astype(part.dtype)
    exchanged = exchange_steps(
        whole_lanes(rows, width),
        whole_rows(rows),
        part,
        landed,
        local_sem.at[3],
        mover(send_sem, recv_sem, 14),
    )
    if kind == "sum":
        relays()
    exchanged()
    fetches[2].wait()
    fetches[3].wait()
    residual[...] = base[...] + wide(landed)
    standard, inverse_std = norm_columns(residual[...])
    normed[...] = standard
    i_ref[...] = inverse_std
    by_block[...] = (standard * gain[...]).astype(shard.dtype).reshape(by_block.shape)
    reorder_blocks(by_block, shard, lambda b: order_ref[0, b])
    gathered = gather_steps(
        member_lanes(width), shard, h_ref, local_sem.at[4], mover(send_sem, recv_sem, 21)
    )
    x_copy = pltpu.make_async_copy(residual, x_ref, local_sem.at[5])
    x_copy.start()
    n_copy = pltpu.make_async_copy(normed, n_ref, local_sem.at[6])
    n_copy.start()
    if kind == "sum":
        side_out[...] = finish().astype(side_out.dtype)
    gathered()
    kept.wait()
    x_copy.wait()
    n_copy.wait()


def project(kind, column, orders, heads, weight, base, gain, *side):
    rows, length = heads.shape
    features, width = base.shape
    whole = jax.ShapeDtypeStruct((features, length), jnp.bfloat16)
    frames = jax.ShapeDtypeStruct(base.shape, jnp.float32)
    side_outs, bufs = (), []
    if kind == "sum":
        tokens = side[0].shape[1]
        side_outs = (jax.ShapeDtypeStruct((rows, 2 * tokens), jnp.bfloat16),)
        bufs = scatter_bufs(rows, 2 * tokens) + [
            pltpu.VMEM((features, rows), jnp.bfloat16),
            pltpu.VMEM((features, 2 * tokens), jnp.bfloat16),
        ]
    low, high = pltpu.VMEM(base.shape, jnp.bfloat16), pltpu.VMEM(base.shape, jnp.float32)
    return kernel_call(
        functools.partial(project_kernel, kind, column),
        out_shape=(whole, frames, frames, jax.ShapeDtypeStruct((1, width), jnp.float32), whole)
        + side_outs,
        in_specs=[IN_SMEM] + [IN_HBM] * 4 + [IN_VMEM] * len(side),
        out_specs=(IN_HBM, IN_HBM, IN_HBM, IN_VMEM, IN_HBM) + (IN_VMEM,) * len(side),
        scratch_shapes=[
            pltpu.VMEM((features, length), jnp.bfloat16),
            pltpu.VMEM((rows, length), jnp.float32),
            pltpu.VMEM((rows, length), jnp.bfloat16),
            low,
            low,
            pltpu.VMEM((orders.shape[1], features // orders.shape[1], width), jnp.bfloat16),
            high,
            pltpu.VMEM(gain.shape, jnp.float32),
            high,
            high,
            pltpu.VMEM(heads.shape, heads.dtype),
            pltpu.VMEM((orders.shape[1], features // orders.shape[1], 4 * rows), weight.dtype),
            pltpu.VMEM((features, rows), weight.dtype),
        ]
        + bufs
        + [
            pltpu.SemaphoreType.DMA((13,)),
            pltpu.SemaphoreType.DMA((49,)),
            pltpu.SemaphoreType.DMA((49,)),
        ],
        compiler_params=pltpu.CompilerParams(
            collective_id=identity_of("project " + kind, heads),
            has_side_effects=True,
            vmem_limit_bytes=32 * 2**20,
        ),
        cost_estimate=BRIEF,
        name="project_" + kind,
    )(orders, heads, weight.reshape(orders.shape[1], -1, weight.shape[1]), base, gain, *side)


def back_kernel(plan, *refs):
    by_rows, send_rows, text, in_slots, column, beside, after = plan
    refs = list(refs)

    def take(count):
        taken = refs[:count]
        del refs[:count]
        return taken

    order_ref = take(1)[0]
    sources = take(3 if by_rows else 7)
    text_ref = take(1)[0] if text else None
    beside_refs = take(4 if beside else 0)
    take(after)
    o_ref, own_out = take(2)
    sum_ref = None if by_rows else take(1)[0]
    rows_ref = take(1)[0] if send_rows else None
    text_out = take(1)[0] if text else None
    held = take(len(sources))
    w_ref, g_ref, act, *norms = held
    results = take(0 if by_rows else 2)
    mine, theirs, pair, from_x, from_y, relay, shard, slots, own_ref = take(9)
    besides = take(4 if beside else 0)
    by_head = take(1 if by_rows else 0)
    local_sem, send_sem, recv_sem = refs
    if by_rows:
        w_slots, w_ref = w_ref, by_head[0]
    source = sources[0]
    if by_rows:
        sources[0] = source.at[:, :, : w_slots.shape[2]]
    elif w_ref.shape[1] < source.shape[1]:
        sources[0] = source.at[:, : w_ref.shape[1]]
    fetches = [
        pltpu.make_async_copy(ref, here, local_sem.at[4 + k])
        for k, (ref, here) in enumerate(zip(sources + beside_refs, held + besides))
    ]
    for fetch in fetches:
        fetch.start()

    group, core, across, along = near()
    beyond = across + along - group
    sibling, by_x, by_y = {"core": 1 - core}, {"dp": across}, {"dp": along}
    rows, width = mine.shape[1:]
    columns = slice(0, g_ref.shape[0]) if by_rows else slice(column, column + g_ref.shape[0])
    half = rows // 2
    low, high = pl.ds(0, half), pl.ds(half, half)
    copy = mover(send_sem, recv_sem)
    sent = []

    def send(k, source, target, peer):
        moving = copy(k, source, target, peer)
        moving.start()
        sent.append(moving)

    def arrived(k, target):
        copy(k, target, target, sibling).wait_recv()

    def split(k, at_rows, at_lanes, first, second):
        mine[k, at_rows, at_lanes] = jnp.where(core == 0, first, second).astype(mine.dtype)
        theirs[k, at_rows, at_lanes] = jnp.where(core == 0, second, first).astype(mine.dtype)

    def work_out(k, owner):
        if by_rows:

            @pl.loop(0, width // 256)
            def _(i):
                at = pl.ds(pl.multiple_of(i * 256, 256), 256)
                both = jnp.dot(
                    w_ref[pl.ds(pl.multiple_of(owner * 2 * rows, 16), 2 * rows), columns],
                    g_ref[:, at],
                    preferred_element_type=jnp.float32,
                )
                split(k, slice(None), at, both[:rows], both[rows:])

        else:

            @pl.loop(0, rows // 256)
            def _(i):
                at = pl.ds(pl.multiple_of(i * 256, 256), 256)
                both = jnp.dot(
                    w_ref[at, columns],
                    g_ref[:, pl.ds(pl.multiple_of(owner * 2 * width, 256), 2 * width)],
                    preferred_element_type=jnp.float32,
                )
                split(k, at, slice(None), both[:, :width], both[:, width:])

        send(k, theirs.at[k], pair.at[k], sibling)

    def both_cores(k):
        arrived(k, pair.at[k])
        mine[k] = (wide(mine.at[k]) + wide(pair.at[k])).astype(mine.dtype)

    def weight_grads(first, last):
        rows_of = act if in_slots else slots
        tile, count = rows_of.shape[0] // 6, g_ref.shape[0]

        @pl.loop(first, last)
        def _(i):
            at = pl.ds(pl.multiple_of(i * tile, tile), tile)
            for j in range(0, count, 256):
                of = slice(j, min(j + 256, count))
                own_ref[at, of] = contract_last(rows_of[at, :], g_ref[of, :]).astype(
                    own_ref.dtype
                )

    if send_rows or text:
        greet([member_at(peer) for peer in plane_peers()])
    else:
        greet([by_x, by_y, sibling])
    fetches[0].wait()
    if by_rows:
        reorder_blocks(w_slots, w_ref, lambda b: order_ref[1, b], column)
    fetches[1].wait()
    for k, owner in enumerate((beyond, across, along, group)):
        work_out(k, owner)
        if k == 1:
            both_cores(0)
            send(4, mine.at[0, low], relay.at[0], by_x)
            send(5, mine.at[0, high], relay.at[1], by_y)
        if k == 2:
            both_cores(1)
            send(6, mine.at[1, low], from_x.at[low], by_x)
        if k == 3:
            both_cores(2)
            send(7, mine.at[2, high], from_y.at[high], by_y)
    if text:
        text_done = gather_steps(
            member_rows(text_ref.shape[0]),
            text_ref,
            text_out,
            local_sem.at[1],
            mover(send_sem, recv_sem, 17),
        )
    def put_beside():
        cq, co, text_grad, text_mine = besides
        count, rows = g_ref.shape[0], text_grad.shape[1]
        part = text_mine.shape[0]
        tokens = text_mine.shape[1]

        @pl.loop(0, text_grad.shape[0])
        def _(b):
            at = pl.ds(pl.multiple_of(b * rows, 16), rows)
            own_ref[at, count : 2 * count] = cq[at, :]
            own_ref[at, 2 * count : 3 * count] = co[at, :]
            slots[at, : 2 * tokens] = text_grad[order_ref[0, b]]

        @pl.loop(0, 6)
        def _(i):
            at = pl.ds(pl.multiple_of(i * 256, 256), 256)
            for k in range(2):
                grads = contract_last(
                    slots[at, k * tokens : (k + 1) * tokens], text_mine[...]
                )
                start = 3 * count + k * part
                own_ref[at, start : start + part] = grads.astype(own_ref.dtype)

    fetches[2].wait()
    if not in_slots:
        reorder_blocks(act, slots, lambda b: order_ref[0, b])
    weight_grads(0, 2)
    arrived(5, relay.at[1])
    mine[1, high] = (wide(mine.at[1, high]) + wide(relay.at[1])).astype(mine.dtype)
    send(8, mine.at[1, high], from_x.at[high], by_x)
    arrived(4, relay.at[0])
    mine[2, low] = (wide(mine.at[2, low]) + wide(relay.at[0])).astype(mine.dtype)
    send(9, mine.at[2, low], from_y.at[low], by_y)
    both_cores(3)
    weight_grads(2, 6)
    if beside:
        for fetch in fetches[len(sources) :]:
            fetch.wait()
        put_beside()
    if text:
        text_done()
    own_copy = pltpu.make_async_copy(own_ref, own_out, local_sem.at[2])
    own_copy.start()
    arrived(6, from_x.at[low])
    arrived(7, from_y.at[high])
    arrived(8, from_x.at[high])
    arrived(9, from_y.at[low])
    summed = wide(mine.at[3]) + wide(from_x) + wide(from_y)
    if by_rows:
        shard[...] = summed.astype(shard.dtype)
        result_copy = pltpu.make_async_copy(shard, o_ref, local_sem.at[3])
        result_copy.start()
    else:
        for fetch in fetches[3 : len(sources)]:
            fetch.wait()
        normed, inverse_std, gain, base = norms
        result, by_block = results
        if in_slots:
            by_block[...] = summed.reshape(by_block.shape)
            reorder_blocks(by_block, result, lambda b: order_ref[1, b])
            summed = result[...]
        result[...] = base[...] + norm_columns_back(
            summed * gain[...], normed[...], inverse_std[...]
        )
        result_copy = pltpu.make_async_copy(result, o_ref, local_sem.at[3])
        result_copy.start()
        if send_rows:
            shard[...] = result[...].astype(shard.dtype)
            rows_done = exchange_steps(
                whole_rows(rows // 8),
                whole_lanes(rows // 8, width),
                shard,
                rows_ref,
                local_sem.at[0],
                mover(send_sem, recv_sem, 10),
            )
        sum_ref[...] = lax.dot_general(
            jnp.ones((8, width), jnp.float32),
            summed * normed[...],
            (((1,), (1,)), ((), ())),
            precision=HIGHEST,
            preferred_element_type=jnp.float32,
        )
        if send_rows:
            rows_done()
    result_copy.wait()
    own_copy.wait()
    for moving in sent:
        moving.wait_send()


def back(
    orders,
    weight,
    grad,
    act,
    norm=None,
    column=0,
    send_rows=False,
    text=None,
    in_slots=False,
    beside=(),
    after=(),
):
    by_rows = norm is None
    features, length = weight.shape[0], grad.shape[1]
    shape = (features // 8, length) if by_rows else (features, length // 8)
    small = jnp.bfloat16
    own_width = grad.shape[0] * (4 if beside else 1)
    own = jax.ShapeDtypeStruct((features, own_width), small)
    outs = [jax.ShapeDtypeStruct(shape, small if by_rows else jnp.float32), own]
    specs = [IN_HBM, IN_HBM]
    if not by_rows:
        outs.append(jax.ShapeDtypeStruct((8, features), jnp.float32))
        specs.append(IN_VMEM)
    if send_rows:
        outs.append(jax.ShapeDtypeStruct((features // 8, length), small))
        specs.append(IN_HBM)
    count = orders.shape[1]
    if not in_slots:
        act = act.reshape(count, features // count, length)
    few = weight.shape[1] if column + grad.shape[0] > 4 * (features // 8) else 4 * (features // 8)
    if by_rows:
        weight = weight.reshape(count, features // count, weight.shape[1])
        held = jax.ShapeDtypeStruct((count, features // count, few), small)
    else:
        held = jax.ShapeDtypeStruct((features, few), small)
    sources = [weight, grad, act] + list(norm or ())
    operands = [orders] + sources
    if text is not None:
        operands.append(text)
        outs.append(jax.ShapeDtypeStruct((8 * text.shape[0], text.shape[1]), text.dtype))
        specs.append(IN_HBM)
    if beside:
        cq, co, text_grad, text_mine = beside
        beside = (cq, co, text_grad.reshape(count, features // count, -1), text_mine)
        operands += list(beside)
    operands += list(after)
    plan = (by_rows, send_rows, text is not None, in_slots, column, bool(beside), len(after))
    rows, width = shape
    four, slot = pltpu.VMEM((4, rows, width), small), pltpu.VMEM((rows, width), small)
    return kernel_call(
        functools.partial(back_kernel, plan),
        out_shape=tuple(outs),
        in_specs=[IN_SMEM] + [IN_HBM] * (len(operands) - 1),
        out_specs=tuple(specs),
        scratch_shapes=[pltpu.VMEM(array.shape, array.dtype) for array in [held] + sources[1:]]
        + (
            []
            if by_rows
            else [
                pltpu.VMEM(shape, jnp.float32),
                pltpu.VMEM((count, rows // count, width), jnp.float32),
            ]
        )
        + [four, four, four, slot, slot, pltpu.VMEM((2, rows // 2, width), small), slot]
        + [
            pltpu.VMEM((16, 128) if in_slots else (features, length), small),
            pltpu.VMEM(own.shape, small),
        ]
        + [pltpu.VMEM(array.shape, array.dtype) for array in beside]
        + ([pltpu.VMEM((features, grad.shape[0]), small)] if by_rows else [])
        + [
            pltpu.SemaphoreType.DMA((11,)),
            pltpu.SemaphoreType.DMA((31,)),
            pltpu.SemaphoreType.DMA((31,)),
        ],
        compiler_params=pltpu.CompilerParams(
            collective_id=identity_of("back" + str(plan), *operands),
            has_side_effects=True,
            vmem_limit_bytes=44 * 2**20,
        ),
        cost_estimate=BRIEF,
        name="back",
    )(*operands)


def exchange_kernel(source, target, x_ref, *refs):
    o_ref, local_sem, send_sem, recv_sem = refs[-4:]
    greet([member_at(peer) for peer in plane_peers()])
    exchange_steps(source, target, x_ref, o_ref, local_sem, mover(send_sem, recv_sem))()


def exchange(array, shape, source, target, kind, after=()):
    return kernel_call(
        functools.partial(exchange_kernel, source, target),
        out_shape=jax.ShapeDtypeStruct(shape, array.dtype),
        in_specs=[IN_HBM] * (1 + len(after)),
        out_specs=IN_HBM,
        scratch_shapes=[
            pltpu.SemaphoreType.DMA,
            pltpu.SemaphoreType.DMA((7,)),
            pltpu.SemaphoreType.DMA((7,)),
        ],
        compiler_params=pltpu.CompilerParams(
            collective_id=identity_of(kind, array, *after), has_side_effects=True
        ),
        cost_estimate=BRIEF,
        name="plane_exchange",
    )(array, *after)


def whole_rows(rows):
    place = member_rows(rows)
    return lambda ref, member: place(ref, member, 0, rows)


def whole_lanes(rows, width):
    place = member_lanes(width)
    return lambda ref, member: place(ref, member, 0, rows)


def to_frames(part):
    rows, width = part.shape[0], part.shape[1] // 8
    return exchange(part, (8 * rows, width), whole_lanes(rows, width), whole_rows(rows), "to frames")


def to_rows(part):
    rows, width = part.shape[0] // 8, part.shape[1]
    return exchange(part, (rows, 8 * width), whole_rows(rows), whole_lanes(rows, width), "to rows")


def block(ref, member):
    return ref.at[member]


def exchange_blocks(blocks, after=()):
    return exchange(blocks, blocks.shape, block, block, "blocks", after)


def lanes(ref, start, width):
    return ref.at[:, pl.ds(pl.multiple_of(start, 128), width)]


def sheet_part(start, width):
    return lambda ref, member: lanes(ref, start + member * width, width)


def block_part(start, width):
    return lambda ref, member: lanes(ref.at[member], start, width)


def feed_kernel(gu_ref, down_ref, w_ref, h_ref, *refs):
    o_ref, y_ref, weight, hidden, part, summed, *bufs, local_sem, send_sem, recv_sem = refs[-14:]
    width = down_ref.shape[-1]
    fetches = [
        pltpu.make_async_copy(w_ref, weight, local_sem.at[3]),
        pltpu.make_async_copy(h_ref, hidden, local_sem.at[5]),
    ]
    for fetch in fetches:
        fetch.start()
    greet([member_at(peer) for peer in plane_peers()])
    finish = []
    for k, (ref, start) in enumerate(((gu_ref, 0), (gu_ref, width), (down_ref, 0))):
        source, target = block_part(start, width), sheet_part(8 * k * width, width)
        copy = mover(send_sem, recv_sem, 7 * k)
        finish.append(exchange_steps(source, target, ref, o_ref, local_sem.at[k], copy))
    for fetch in fetches:
        fetch.wait()

    @pl.loop(0, part.shape[0] // 256)
    def _(i):
        at = pl.ds(pl.multiple_of(i * 256, 256), 256)
        for j in range(0, part.shape[1], 256):
            product = jnp.dot(
                weight[at, :], hidden[:, j : j + 256], preferred_element_type=jnp.float32
            )
            part[at, j : j + 256] = product.astype(part.dtype)

    cores, chips, relays, ended = scatter_steps(
        member_lanes(y_ref.shape[1]), part, bufs, mover(send_sem, recv_sem, 21)
    )
    cores()
    chips()
    relays()
    summed[...] = ended()
    kept = pltpu.make_async_copy(summed, y_ref, local_sem.at[4])
    kept.start()
    for end in finish:
        end()
    kept.wait()


def feed(gu, down, weight, hidden, after=()):
    rows, length = weight.shape[0], hidden.shape[1]
    width = length // 8
    return kernel_call(
        feed_kernel,
        out_shape=(
            jax.ShapeDtypeStruct((gu.shape[1], 24 * down.shape[-1]), gu.dtype),
            jax.ShapeDtypeStruct((rows, width), jnp.float32),
        ),
        in_specs=[IN_HBM] * (4 + len(after)),
        out_specs=(IN_HBM, IN_HBM),
        scratch_shapes=[
            pltpu.VMEM(weight.shape, weight.dtype),
            pltpu.VMEM(hidden.shape, hidden.dtype),
            pltpu.VMEM((rows, length), jnp.bfloat16),
            pltpu.VMEM((rows, width), jnp.float32),
        ]
        + scatter_bufs(rows, width)
        + [
            pltpu.SemaphoreType.DMA((6,)),
            pltpu.SemaphoreType.DMA((31,)),
            pltpu.SemaphoreType.DMA((31,)),
        ],
        compiler_params=pltpu.CompilerParams(
            collective_id=identity_of("feed", gu, down, weight, *after),
            has_side_effects=True,
            vmem_limit_bytes=28 * 2**20,
        ),
        cost_estimate=BRIEF,
        name="feed",
    )(gu, down, weight, hidden, *after)


def opening_kernel(
    latents_ref,
    cotangent_ref,
    small_ref,
    text_ref,
    sheet_ref,
    t_ref,
    all_ref,
    mine_ref,
    one_ref,
    x_ref,
    held,
    columns,
    one,
    local_sem,
    send_sem,
    recv_sem,
):
    features = latents_ref.shape[1]
    part, text = D // 8, CTXW // 8
    tail = 6 * D + 3 * FF
    fetches = [
        pltpu.make_async_copy(latents_ref, x_ref.at[:, :features], local_sem.at[5]),
        pltpu.make_async_copy(cotangent_ref, x_ref.at[:, features:], local_sem.at[6]),
        pltpu.make_async_copy(
            sheet_ref.at[:, : 6 * D], columns.at[:, : 6 * D], local_sem.at[7]
        ),
        pltpu.make_async_copy(
            sheet_ref.at[:, tail : tail + 2 * CTXW], columns.at[:, 6 * D :], local_sem.at[8]
        ),
    ]
    for fetch in fetches:
        fetch.start()
    group, core, _, _ = near()
    member = group * 2 + core
    plane = lax.axis_index("z")
    step = x_ref.shape[0] // 4
    text_rows = mine_ref.shape[0]
    teacher = jnp.logical_and(group == plane, core == 0)

    def frames(ref, j):
        return ref.at[pl.ds(pl.multiple_of(j * step, 16), step), :]

    peers = plane_peers()
    line = [lax.rem(plane + k, 4) for k in range(1, 4)]
    greet([member_at(peer) for peer in peers] + [{"z": there} for there in line])

    fetches[0].wait()
    fetches[1].wait()

    near_copy = mover(send_sem, recv_sem)
    line_copy = mover(send_sem, recv_sem, 7)
    small_local = pltpu.make_async_copy(small_ref, all_ref.at[plane, member], local_sem.at[0])
    small_local.start()
    first = [
        near_copy(k, small_ref, all_ref.at[plane, member], member_at(peer))
        for k, peer in enumerate(peers)
    ]
    for moving in first:
        moving.start()

    others = [lax.rem(group + k, 4) for k in range(1, 4)]
    keep = pltpu.make_async_copy(frames(x_ref, group), frames(held, group), local_sem.at[1])
    keep.start()

    def spread(owner, landing):
        return pltpu.make_async_remote_copy(
            src_ref=frames(x_ref, owner),
            dst_ref=frames(held, landing),
            send_sem=send_sem.at[10 + owner],
            recv_sem=recv_sem.at[10 + landing],
            device_id={"dp": owner},
            device_id_type=MESH_ID,
        )

    for owner in others:
        spread(owner, group).start()

    def rise(row):
        return pltpu.make_async_remote_copy(
            src_ref=frames(held, row),
            dst_ref=frames(t_ref, plane),
            send_sem=send_sem.at[28 + row],
            recv_sem=recv_sem.at[28 + plane],
            device_id={"z": row},
            device_id_type=MESH_ID,
        )

    stay = pltpu.make_async_copy(frames(held, plane), frames(t_ref, plane), local_sem.at[4])

    def pass_on(row):
        pl.when(row == plane)(stay.start)
        pl.when(row != plane)(rise(row).start)

    fetches[2].wait()
    fetches[3].wait()

    def move(m, at, start, width):
        one[m, :, at : at + width] = columns[:, start : start + width].astype(one.dtype)

    for m in range(8):
        for k in range(6):
            move(m, (4 * part if k < 3 else -3 * part) + k * part, k * D + m * part, part)
        for k in range(2):
            move(m, 3 * part + k * text, 6 * D + k * CTXW + m * text, text)
    weights_done = exchange_steps(
        block, block, one, one_ref, local_sem.at[2], mover(send_sem, recv_sem, 14)
    )

    def text_copy(k, peer):
        return pltpu.make_async_remote_copy(
            src_ref=text_ref.at[pl.ds(pl.multiple_of(peer * text_rows, 16), text_rows), :],
            dst_ref=mine_ref,
            send_sem=send_sem.at[21 + k],
            recv_sem=recv_sem.at[21],
            device_id=member_at(peer),
            device_id_type=MESH_ID,
        )

    own_text = text_ref.at[pl.ds(pl.multiple_of(member * text_rows, 16), text_rows), :]
    text_local = pltpu.make_async_copy(own_text, mine_ref, local_sem.at[3])

    @pl.when(teacher)
    def _():
        text_local.start()
        for k, peer in enumerate(peers):
            text_copy(k, peer).start()

    keep.wait()
    pass_on(group)
    for owner in others:
        spread(owner, owner).wait_recv()
        pass_on(owner)

    for k in range(7):
        landed = all_ref.at[plane, lax.rem(member + 7 - k, 8)]
        near_copy(k, landed, landed, member_at(peers[k])).wait_recv()
    small_local.wait()
    second = [
        line_copy(k, all_ref.at[plane], all_ref.at[plane], {"z": there})
        for k, there in enumerate(line)
    ]
    for moving in second:
        moving.start()
    for k in range(3):
        landed = all_ref.at[lax.rem(plane + 3 - k, 4)]
        line_copy(k, landed, landed, {"z": line[k]}).wait_recv()

    for there in line:
        landed = frames(t_ref, there)
        pltpu.make_async_remote_copy(
            src_ref=landed,
            dst_ref=landed,
            send_sem=send_sem.at[28 + there],
            recv_sem=recv_sem.at[28 + there],
            device_id={"z": there},
            device_id_type=MESH_ID,
        ).wait_recv()
    stay.wait()
    weights_done()

    @pl.when(teacher)
    def _():
        text_local.wait()
        for k, peer in enumerate(peers):
            text_copy(k, peer).wait_send()

    @pl.when(jnp.logical_not(teacher))
    def _():
        text_copy(0, peers[0]).wait_recv()

    for moving in first + second:
        moving.wait_send()
    for owner in others:
        spread(owner, group).wait_send()
    for there in line:
        rise(there).wait_send()


def opening(latents, cotangent, small, text, sheet):
    frames, features = latents.shape
    local = (frames, 2 * features)
    one = (8, sheet.shape[0], (6 * D + 2 * CTXW) // 8)
    low = jnp.bfloat16
    return kernel_call(
        opening_kernel,
        out_shape=(
            jax.ShapeDtypeStruct(local, low),
            jax.ShapeDtypeStruct((4, 8) + small.shape, small.dtype),
            jax.ShapeDtypeStruct((text.shape[0] // 8, text.shape[1]), text.dtype),
            jax.ShapeDtypeStruct(one, low),
        ),
        in_specs=[IN_HBM] * 5,
        out_specs=(IN_HBM,) * 4,
        scratch_shapes=[
            pltpu.VMEM(local, low),
            pltpu.VMEM(local, low),
            pltpu.VMEM((sheet.shape[0], 6 * D + 2 * CTXW), jnp.float32),
            pltpu.VMEM(one, low),
            pltpu.SemaphoreType.DMA((9,)),
            pltpu.SemaphoreType.DMA((32,)),
            pltpu.SemaphoreType.DMA((32,)),
        ],
        compiler_params=pltpu.CompilerParams(
            collective_id=identity_of("opening", sheet),
            has_side_effects=True,
            vmem_limit_bytes=16 * 2**20,
        ),
        cost_estimate=BRIEF,
        name="opening",
    )(latents, cotangent, small, text, sheet)


def first_gather_kernel(
    x_ref, y_ref, sheet_ref, ox_ref, oy_ref, gu_ref, down_ref, local_sem, send_sem, recv_sem
):
    place = member_lanes(x_ref.shape[1])
    width = FF // 8
    greet([member_at(peer) for peer in plane_peers()])
    finish = [
        gather_steps(place, x_ref, ox_ref, local_sem.at[0], mover(send_sem, recv_sem)),
        gather_steps(place, y_ref, oy_ref, local_sem.at[1], mover(send_sem, recv_sem, 14)),
    ]
    for k, (ref, start) in enumerate(((gu_ref, 0), (gu_ref, width), (down_ref, 0))):
        source, target = sheet_part(6 * D + k * FF, width), block_part(start, width)
        copy = mover(send_sem, recv_sem, 28 + 7 * k)
        finish.append(exchange_steps(source, target, sheet_ref, ref, local_sem.at[2 + k], copy))
    for end in finish:
        end()


def first_gather(shard, other, sheet):
    rows, width = shard.shape
    whole = jax.ShapeDtypeStruct((rows, 8 * width), shard.dtype)
    return kernel_call(
        first_gather_kernel,
        out_shape=(
            whole,
            whole,
            jax.ShapeDtypeStruct((8, sheet.shape[0], FF // 4), sheet.dtype),
            jax.ShapeDtypeStruct((8, sheet.shape[0], FF // 8), sheet.dtype),
        ),
        in_specs=[IN_HBM] * 3,
        out_specs=(IN_HBM,) * 4,
        scratch_shapes=[
            pltpu.SemaphoreType.DMA((5,)),
            pltpu.SemaphoreType.DMA((49,)),
            pltpu.SemaphoreType.DMA((49,)),
        ],
        compiler_params=pltpu.CompilerParams(
            collective_id=identity_of("first gather", shard, sheet), has_side_effects=True
        ),
        cost_estimate=BRIEF,
        name="first_gather",
    )(shard, other, sheet)


def closing_kernel(
    order_ref,
    y_ref,
    base_ref,
    grad_ref,
    w_ref,
    v_ref,
    gu_ref,
    down_ref,
    g_ref,
    t_ref,
    o_ref,
    vo_ref,
    s_ref,
    all_ref,
    by_block,
    sorted_y,
    base,
    grad,
    x_ref,
    held,
    tall,
    q_ref,
    one,
    two,
    gu,
    down,
    local_sem,
    send_sem,
    recv_sem,
):
    fetches = [
        pltpu.make_async_copy(ref, here, local_sem.at[7 + k])
        for k, (ref, here) in enumerate(
            [(y_ref, by_block), (base_ref, base), (grad_ref, grad)]
            + [(w_ref, one), (v_ref, two), (gu_ref, gu), (down_ref, down)]
        )
    ]
    for fetch in fetches:
        fetch.start()
    group, core, _, _ = near()
    member = group * 2 + core
    plane = lax.axis_index("z")
    step = x_ref.shape[0] // 4
    line = [lax.rem(plane + k, 4) for k in range(1, 4)]
    back = [lax.rem(plane + 3 - k, 4) for k in range(3)]
    groups = [lax.rem(group + k, 4) for k in range(1, 4)]
    peers = plane_peers()
    greet([member_at(peer) for peer in peers] + [{"z": there} for there in line])

    def frames(ref, j):
        return ref.at[pl.ds(pl.multiple_of(j * step, 16), step), :]

    copy = mover(send_sem, recv_sem)
    gain_line = mover(send_sem, recv_sem, 14)
    gain_plane = mover(send_sem, recv_sem, 17)
    square_plane = mover(send_sem, recv_sem, 24)
    square_line = mover(send_sem, recv_sem, 31)
    gain_local = pltpu.make_async_copy(g_ref, tall.at[plane], local_sem.at[3])
    gain_local.start()
    sent = [gain_line(k, g_ref, tall.at[plane], {"z": there}) for k, there in enumerate(line)]
    for fetch in fetches[:3]:
        fetch.wait()
    reorder_blocks(by_block, sorted_y, lambda b: order_ref[1, b])
    features = base.shape[0]
    x_ref[:, :features] = (base[...] + sorted_y[...]).T.astype(x_ref.dtype)
    x_ref[:, features:] = grad[...].T.astype(x_ref.dtype)
    local = pltpu.make_async_copy(frames(x_ref, plane), frames(held, plane), local_sem.at[0])
    local.start()
    sent += [
        copy(k, frames(x_ref, there), frames(held, plane), {"z": there})
        for k, there in enumerate(line)
    ]
    for moving in sent:
        moving.start()
    weights_done = exchange_steps(
        block, block, w_ref, o_ref, local_sem.at[1], mover(send_sem, recv_sem, 7)
    )
    others_done = exchange_steps(
        block, block, v_ref, vo_ref, local_sem.at[6], mover(send_sem, recv_sem, 34)
    )

    for fetch in fetches[3:]:
        fetch.wait()
    total = jnp.zeros((), jnp.float32)
    for ref in (one, two, gu, down):
        line_sum = jnp.zeros((1, ref.shape[2]), jnp.float32)
        for m in range(8):
            line_sum += jnp.sum(jnp.square(wide(ref.at[m])), axis=0, keepdims=True)
        total += jnp.sum(line_sum)
    q_ref[...] = jnp.full(q_ref.shape, total, jnp.float32)
    square_local = pltpu.make_async_copy(q_ref, all_ref.at[plane, member], local_sem.at[5])
    square_local.start()
    shown = [
        square_plane(k, q_ref, all_ref.at[plane, member], member_at(peer))
        for k, peer in enumerate(peers)
    ]
    for moving in shown:
        moving.start()
    gain_local.wait()
    for k, origin in enumerate(back):
        gain_line(k, tall.at[origin], tall.at[origin], {"z": origin}).wait_recv()
    tall[4] = tall[0] + tall[1] + tall[2] + tall[3]
    gain_keep = pltpu.make_async_copy(tall.at[4], s_ref.at[member], local_sem.at[4])
    gain_keep.start()
    given = [
        gain_plane(k, tall.at[4], s_ref.at[member], member_at(peer)) for k, peer in enumerate(peers)
    ]
    for moving in given:
        moving.start()

    def onward(owner):
        return pltpu.make_async_remote_copy(
            src_ref=frames(held, owner),
            dst_ref=frames(t_ref, group),
            send_sem=send_sem.at[3 + owner],
            recv_sem=recv_sem.at[3 + group],
            device_id={"dp": owner},
            device_id_type=MESH_ID,
        )

    keep = pltpu.make_async_copy(frames(held, group), frames(t_ref, group), local_sem.at[2])

    def pass_on(owner):
        pl.when(owner == group)(keep.start)
        pl.when(owner != group)(onward(owner).start)

    square_local.wait()
    for k in range(7):
        landed = all_ref.at[plane, lax.rem(member + 7 - k, 8)]
        square_plane(k, landed, landed, member_at(peers[k])).wait_recv()
    for k, there in enumerate(line):
        shown.append(square_line(k, all_ref.at[plane], all_ref.at[plane], {"z": there}))
        shown[-1].start()
    local.wait()
    pass_on(plane)
    for k, origin in enumerate(back):
        landed = frames(held, origin)
        copy(k, landed, landed, {"z": origin}).wait_recv()
        pass_on(origin)
    for origin in groups:
        landed = frames(t_ref, origin)
        pltpu.make_async_remote_copy(
            src_ref=landed,
            dst_ref=landed,
            send_sem=send_sem.at[3 + origin],
            recv_sem=recv_sem.at[3 + origin],
            device_id={"dp": origin},
            device_id_type=MESH_ID,
        ).wait_recv()
    keep.wait()
    weights_done()
    others_done()
    gain_keep.wait()
    for k in range(7):
        landed = s_ref.at[lax.rem(member + 7 - k, 8)]
        gain_plane(k, landed, landed, member_at(peers[k])).wait_recv()
    for k, origin in enumerate(back):
        square_line(k, all_ref.at[origin], all_ref.at[origin], {"z": origin}).wait_recv()
    for moving in sent + given + shown:
        moving.wait_send()
    for origin in groups:
        onward(origin).wait_send()


def closing(orders, y, base, grad, one, two, gu, down, gains):
    features, width = base.shape
    blocks = orders.shape[1]
    frames = (width, 2 * features)
    parts = (one, two, gu, down)
    return kernel_call(
        closing_kernel,
        out_shape=(
            jax.ShapeDtypeStruct(frames, jnp.bfloat16),
            jax.ShapeDtypeStruct(one.shape, one.dtype),
            jax.ShapeDtypeStruct(two.shape, two.dtype),
            jax.ShapeDtypeStruct((8,) + gains.shape, gains.dtype),
            jax.ShapeDtypeStruct((4, 8, 8, 128), jnp.float32),
        ),
        in_specs=[IN_SMEM] + [IN_HBM] * 8,
        out_specs=(IN_HBM,) * 5,
        scratch_shapes=[pltpu.VMEM((blocks, features // blocks, width), jnp.float32)]
        + [pltpu.VMEM(base.shape, jnp.float32)] * 3
        + [pltpu.VMEM(frames, jnp.bfloat16)] * 2
        + [
            pltpu.VMEM((5,) + gains.shape, gains.dtype),
            pltpu.VMEM((8, 128), jnp.float32),
        ]
        + [pltpu.VMEM(part.shape, part.dtype) for part in parts]
        + [
            pltpu.SemaphoreType.DMA((14,)),
            pltpu.SemaphoreType.DMA((41,)),
            pltpu.SemaphoreType.DMA((41,)),
        ],
        compiler_params=pltpu.CompilerParams(
            collective_id=identity_of("closing", y),
            has_side_effects=True,
            vmem_limit_bytes=24 * 2**20,
        ),
        cost_estimate=BRIEF,
        name="closing",
    )(orders, y.reshape(blocks, -1, width), base, grad, one, two, gu, down, gains)


def turned(values, cosine, sine_table):
    half = HEAD // 2
    first_half, second_half = values[:half], values[half:]
    return jnp.concatenate(
        [
            first_half * cosine - second_half * sine_table,
            second_half * cosine + first_half * sine_table,
        ],
        axis=0,
    )


def attend_kernel(
    w_ref,
    h_ref,
    cos_ref,
    sin_ref,
    seg_ref,
    column_ref,
    part_out,
    p_out,
    o_ref,
    weight,
    frames,
    joint_ref,
    part_ref,
    p_ref,
    sems,
):
    heads, length = joint_ref.shape[1], joint_ref.shape[3]
    span = heads * HEAD
    tiles = length // 256
    fetches = [pltpu.make_async_copy(w_ref, weight, sems.at[0])]
    fetches += [
        pltpu.make_async_copy(
            h_ref.at[:, i * 256 : (i + 1) * 256], frames.at[:, i * 256 : (i + 1) * 256], sems.at[1 + i]
        )
        for i in range(tiles)
    ]
    for fetch in fetches:
        fetch.start()
    cosine, sine_table = cos_ref[...], sin_ref[...]
    fetches[0].wait()
    by_row = [weight[:, (4 + k) * span : (5 + k) * span].T for k in range(3)]
    for i in range(tiles):
        fetches[1 + i].wait()
        at = slice(i * 256, (i + 1) * 256)
        for k in range(3):
            part = jnp.dot(by_row[k], frames[:, at], preferred_element_type=jnp.float32)
            for h in range(heads):
                joint_ref[k, h, :, at] = part[h * HEAD : (h + 1) * HEAD]

    kept = []
    for h in range(heads):
        queries = turned(joint_ref[0, h], cosine, sine_table)
        part_ref[0, h] = queries.astype(part_ref.dtype)
        keys = turned(joint_ref[1, h], cosine, sine_table)
        part_ref[1, h] = keys.astype(part_ref.dtype)
        part_ref[2, h] = joint_ref[2, h].astype(part_ref.dtype)
        by_key = keys.T.astype(part_ref.dtype)

        @pl.loop(0, tiles)
        def _(i, h=h, by_key=by_key):
            at = pl.ds(pl.multiple_of(i * 256, 256), 256)
            scores = jnp.dot(
                by_key, part_ref[0, h, :, at], preferred_element_type=jnp.float32
            ) * (HEAD**-0.5)
            scores = jnp.where(column_ref[...] == seg_ref[:, at], scores, MASKED_SCORE)
            exponent = jnp.exp(scores - jnp.max(scores, axis=0, keepdims=True))
            probs = exponent * (1.0 / jnp.sum(exponent, axis=0, keepdims=True))
            p_ref[h, :, at] = probs.astype(p_ref.dtype)
            out = jnp.dot(part_ref[2, h], p_ref[h, :, at], preferred_element_type=jnp.float32)
            o_ref[h * HEAD : (h + 1) * HEAD, at] = out.astype(o_ref.dtype)

        kept.append(pltpu.make_async_copy(p_ref.at[h], p_out.at[h], sems.at[1 + tiles + h]))
        kept[-1].start()
    kept.append(pltpu.make_async_copy(part_ref, part_out, sems.at[1 + tiles + heads]))
    kept[-1].start()
    for keep in kept:
        keep.wait()


def attend(weight, frames, cosine, sine_table, segments):
    heads, length = D // HEAD // 8, frames.shape[1]
    joint = (3, heads, HEAD, length)
    small = jnp.bfloat16
    return kernel_call(
        attend_kernel,
        out_shape=(
            jax.ShapeDtypeStruct(joint, small),
            jax.ShapeDtypeStruct((heads, length, length), small),
            jax.ShapeDtypeStruct((heads * HEAD, length), small),
        ),
        in_specs=[IN_HBM] * 2 + [IN_VMEM] * 4,
        out_specs=(IN_HBM, IN_HBM, IN_VMEM),
        scratch_shapes=[
            pltpu.VMEM(weight.shape, small),
            pltpu.VMEM(frames.shape, small),
            pltpu.VMEM(joint, jnp.float32),
            pltpu.VMEM(joint, small),
            pltpu.VMEM((heads, length, length), small),
            pltpu.SemaphoreType.DMA((2 + length // 256 + heads,)),
        ],
        compiler_params=pltpu.CompilerParams(vmem_limit_bytes=36 * 2**20),
        name="attend",
    )(weight, frames, cosine, sine_table, segments[None, :], segments[:, None])


def cross_kernel(w_ref, h_ref, kv_ref, cq_ref, p_ref, o_ref, weight, frames, sems):
    heads, text, length = p_ref.shape
    span = heads * HEAD
    tiles = length // 256
    fetches = [pltpu.make_async_copy(w_ref.at[:, 128:384], weight, sems.at[0])]
    fetches += [
        pltpu.make_async_copy(
            h_ref.at[:, i * 256 : (i + 1) * 256], frames.at[:, i * 256 : (i + 1) * 256], sems.at[1 + i]
        )
        for i in range(tiles)
    ]
    for fetch in fetches:
        fetch.start()
    keys = [
        wide(kv_ref.at[h * HEAD : (h + 1) * HEAD, :text]).T.astype(cq_ref.dtype)
        for h in range(heads)
    ]
    fetches[0].wait()
    by_row = weight[:, span - 128 : 2 * span - 128].T
    for i in range(tiles):
        fetches[1 + i].wait()
        at = slice(i * 256, (i + 1) * 256)
        cq_ref[:, at] = jnp.dot(
            by_row, frames[:, at], preferred_element_type=jnp.float32
        ).astype(cq_ref.dtype)
        for h in range(heads):
            of = slice(h * HEAD, (h + 1) * HEAD)
            scores = jnp.dot(keys[h], cq_ref[of, at], preferred_element_type=jnp.float32) * (
                HEAD**-0.5
            )
            exponent = jnp.exp(scores - jnp.max(scores, axis=0, keepdims=True))
            probs = exponent * (1.0 / jnp.sum(exponent, axis=0, keepdims=True))
            p_ref[h, :, at] = probs.astype(p_ref.dtype)
            out = jnp.dot(
                kv_ref[of, text:], p_ref[h, :, at], preferred_element_type=jnp.float32
            )
            o_ref[of, at] = out.astype(o_ref.dtype)


def cross(weight, frames, text_kv):
    rows, length = text_kv.shape[0], frames.shape[1]
    text, small = text_kv.shape[1] // 2, jnp.bfloat16
    return kernel_call(
        cross_kernel,
        out_shape=(
            jax.ShapeDtypeStruct((rows, length), small),
            jax.ShapeDtypeStruct((rows // HEAD, text, length), small),
            jax.ShapeDtypeStruct((rows, length), small),
        ),
        in_specs=[IN_HBM, IN_HBM, IN_VMEM],
        out_specs=(IN_VMEM,) * 3,
        scratch_shapes=[
            pltpu.VMEM((weight.shape[0], 256), small),
            pltpu.VMEM(frames.shape, small),
            pltpu.SemaphoreType.DMA((1 + length // 256,)),
        ],
        compiler_params=pltpu.CompilerParams(vmem_limit_bytes=16 * 2**20),
        name="cross",
    )(weight, frames, text_kv)


def cross_back_kernel(cq_ref, p_ref, kv_ref, grad_ref, dq_ref, dkv_ref):
    heads, text, length = p_ref.shape
    scale = HEAD**-0.5
    for h in range(heads):
        of = slice(h * HEAD, (h + 1) * HEAD)
        by_key = wide(kv_ref.at[of, text:]).T.astype(cq_ref.dtype)
        grad_out = grad_ref[of, :]
        grad_probs = jnp.dot(by_key, grad_out, preferred_element_type=jnp.float32)
        probs = wide(p_ref.at[h])
        weighted = jnp.sum(probs * grad_probs, axis=0, keepdims=True)
        grad_scores = (probs * (grad_probs - weighted)).astype(cq_ref.dtype)
        dq_ref[of, :] = (
            jnp.dot(kv_ref[of, :text], grad_scores, preferred_element_type=jnp.float32) * scale
        ).astype(dq_ref.dtype)
        dkv_ref[of, :text] = (contract_last(cq_ref[of, :], grad_scores) * scale).astype(
            dkv_ref.dtype
        )
        dkv_ref[of, text:] = contract_last(grad_out, p_ref[h]).astype(dkv_ref.dtype)


def cross_back(cross_q, probs, text_kv, grad):
    return kernel_call(
        cross_back_kernel,
        out_shape=(
            jax.ShapeDtypeStruct(cross_q.shape, cross_q.dtype),
            jax.ShapeDtypeStruct(text_kv.shape, text_kv.dtype),
        ),
        in_specs=[IN_VMEM] * 4,
        out_specs=(IN_VMEM,) * 2,
        compiler_params=pltpu.CompilerParams(vmem_limit_bytes=16 * 2**20),
        name="cross_back",
    )(cross_q, probs, text_kv, grad)


def attend_back_kernel(
    part_in, p_in, g_in, cos_ref, sin_ref, o_ref, part_ref, p_ref, grad_ref, dq_ref, dk_ref, dv_ref, sems
):
    heads, length = part_ref.shape[1], part_ref.shape[3]
    fetches = [
        pltpu.make_async_copy(part_in, part_ref, sems.at[0]),
        pltpu.make_async_copy(g_in, grad_ref, sems.at[1]),
    ]
    fetches += [
        pltpu.make_async_copy(p_in.at[h], p_ref.at[h], sems.at[2 + h]) for h in range(heads)
    ]
    for fetch in fetches:
        fetch.start()
    cosine, sine_table = cos_ref[...], -sin_ref[...]
    scale = HEAD**-0.5
    fetches[0].wait()
    fetches[1].wait()
    for h in range(heads):
        of = slice(h * HEAD, (h + 1) * HEAD)
        by_key = wide(part_ref.at[2, h]).T.astype(part_ref.dtype)
        dk_ref[...] = jnp.zeros_like(dk_ref)
        dv_ref[...] = jnp.zeros_like(dv_ref)
        fetches[2 + h].wait()

        @pl.loop(0, length // 256)
        def _(i, h=h, of=of, by_key=by_key):
            at = pl.ds(pl.multiple_of(i * 256, 256), 256)
            grad_out = grad_ref[of, at]
            grad_probs = jnp.dot(by_key, grad_out, preferred_element_type=jnp.float32)
            low_probs = p_ref[h, :, at]
            probs = low_probs.astype(jnp.float32)
            weighted = jnp.sum(probs * grad_probs, axis=0, keepdims=True)
            grad_scores = (probs * (grad_probs - weighted)).astype(part_ref.dtype)
            dq_ref[:, at] = jnp.dot(
                part_ref[1, h], grad_scores, preferred_element_type=jnp.float32
            )
            dk_ref[...] += contract_last(part_ref[0, h, :, at], grad_scores)
            dv_ref[...] += contract_last(grad_out, low_probs)

        span = heads * HEAD
        grad_queries = turned(dq_ref[...] * scale, cosine, sine_table)
        grad_keys = turned(dk_ref[...] * scale, cosine, sine_table)
        o_ref[of, :] = grad_queries.astype(o_ref.dtype)
        o_ref[span + of.start : span + of.stop, :] = grad_keys.astype(o_ref.dtype)
        o_ref[2 * span + of.start : 2 * span + of.stop, :] = dv_ref[...].astype(o_ref.dtype)


def attend_back(parts, probs, grad, cosine, sine_table):
    _, heads, _, length = parts.shape
    return kernel_call(
        attend_back_kernel,
        out_shape=jax.ShapeDtypeStruct((3 * heads * HEAD, length), jnp.bfloat16),
        in_specs=[IN_HBM] * 3 + [IN_VMEM] * 2,
        out_specs=IN_VMEM,
        scratch_shapes=[pltpu.VMEM(array.shape, array.dtype) for array in (parts, probs, grad)]
        + [pltpu.VMEM((HEAD, length), jnp.float32)] * 3
        + [pltpu.SemaphoreType.DMA((2 + heads,))],
        compiler_params=pltpu.CompilerParams(vmem_limit_bytes=32 * 2**20),
        name="attend_back",
    )(parts, probs, grad, cosine, sine_table)


def update_kernel(
    block_ref,
    rate_ref,
    one_ref,
    two_ref,
    feed_ref,
    all_ref,
    gain_ref,
    pair_ref,
    sheet_ref,
    first_ref,
    second_ref,
    grad_out,
    first_out,
    second_out,
    sheet_out,
    copy_out,
    norm_out,
    gain_out,
    output_out,
    latent_out,
    grad,
    gain,
    scale,
):
    step = pl.program_id(0)
    part = D // 8
    text = CTXW // 8

    @pl.when(step == 0)
    def _():
        summed = jnp.sum(gain_ref[...], axis=0)
        rows = grad.shape[0]
        here = lax.broadcasted_iota(jnp.int32, (rows, D), 1) == (
            lax.broadcasted_iota(jnp.int32, (rows, D), 0) + block_ref[0] * rows
        )
        gain[...] = lax.dot_general(
            here.astype(jnp.float32),
            summed,
            (((1,), (1,)), ((), ())),
            precision=HIGHEST,
            preferred_element_type=jnp.float32,
        )
        norm = jnp.sqrt(jnp.sum(all_ref[:, :, 0:1, 0:1]) + jnp.sum(summed * summed))
        norm_out[0] = norm
        scale[0] = 1.0 / jnp.maximum(norm, 1.0)
        gain_out[...] = gain[...] * scale[0]
        output_out[...] = pair_ref[:, :D]
        latent_out[...] = wide(pair_ref.at[:, D:])

    for k in range(6):

        @pl.when(step == k // 2)
        def _(k=k):
            ref, start = (one_ref, k * part) if k < 3 else (two_ref, (k - 3) * part)
            for m in range(8):
                at = (k % 2) * D + m * part
                grad[:, at : at + part] = wide(ref.at[m, :, start : start + part])

    @pl.when(jnp.logical_and(step >= 3, step < 9))
    def _():
        grad[...] = wide(feed_ref)

    @pl.when(step == 9)
    def _():
        for m in range(8):
            for k in range(2):
                start = 3 * part + k * text
                at = k * CTXW + m * text
                grad[:, at : at + text] = wide(two_ref.at[m, :, start : start + text])
        grad[:, D : D + 8] = gain[...]

    for half in range(2):
        at = slice(half * D, (half + 1) * D)
        clipped = grad[:, at] * scale[0]
        sheet = sheet_ref[:, at]
        first_new = BETA_ONE * first_ref[:, at] + (1.0 - BETA_ONE) * clipped
        second_new = BETA_TWO * second_ref[:, at] + (1.0 - BETA_TWO) * clipped * clipped
        mean_hat = first_new * (1.0 / (1.0 - BETA_ONE**STEP))
        square_hat = second_new * (1.0 / (1.0 - BETA_TWO**STEP))
        sheet_new = sheet - rate_ref[2 * step + half] * (
            mean_hat / (jnp.sqrt(square_hat) + EPS_ADAM) + WEIGHT_DECAY * sheet
        )
        grad_out[:, at] = clipped
        first_out[:, at] = first_new
        second_out[:, at] = second_new
        sheet_out[:, at] = sheet_new
        copy_out[:, at] = sheet_new.astype(copy_out.dtype)


def sheet_update(block_index, length, one, two, feed_part, squares, gains, pair, sheet, first, second):
    rows = sheet.shape[0]
    frames = (pair.shape[0], D)
    rates = column_spread(length)[jnp.minimum(jnp.arange(20) * D, SHEET - 1)]
    column_block = pl.BlockSpec((rows, 2 * D), lambda i: (0, i))
    like = jax.ShapeDtypeStruct(sheet.shape, sheet.dtype)

    def whole(shape):
        return pl.BlockSpec(shape, lambda i: (0,) * len(shape))

    sheet, first, second, feed_part = (
        pltpu.with_memory_space_constraint(array, pltpu.HBM)
        for array in (sheet, first, second, feed_part)
    )
    return pl.pallas_call(
        update_kernel,
        grid=(10,),
        out_shape=(like, like, like, like, jax.ShapeDtypeStruct(sheet.shape, jnp.bfloat16))
        + (jax.ShapeDtypeStruct((1,), jnp.float32), jax.ShapeDtypeStruct((rows, 8), jnp.float32))
        + (
            jax.ShapeDtypeStruct(frames, jnp.bfloat16),
            jax.ShapeDtypeStruct(frames, jnp.float32),
        ),
        in_specs=[
            IN_SMEM,
            IN_SMEM,
            whole(one.shape),
            whole(two.shape),
            pl.BlockSpec((rows, 2 * D), lambda i: (0, jnp.clip(i - 3, 0, 5))),
            whole(squares.shape),
            whole(gains.shape),
            whole(pair.shape),
            column_block,
            column_block,
            column_block,
        ],
        out_specs=(column_block,) * 5
        + (IN_SMEM, whole((rows, 8)), whole(frames), whole(frames)),
        scratch_shapes=[
            pltpu.VMEM((rows, 2 * D), jnp.float32),
            pltpu.VMEM((rows, 8), jnp.float32),
            pltpu.SMEM((1,), jnp.float32),
        ],
        compiler_params=pltpu.CompilerParams(vmem_limit_bytes=32 * 2**20),
        name="sheet_update",
    )(block_index, rates, one, two, feed_part, squares, gains, pair, sheet, first, second)


def pick_blocks(blocks, order):
    return blocks.at[order].get(mode="promise_in_bounds")


def gather_line(mine, order):
    blocks = lax.all_gather(mine, "z", axis=0, tiled=True)
    return pick_blocks(blocks, order).reshape(-1, mine.shape[-1])


def gather_slots(mine):
    return lax.all_gather(mine, "z", axis=0, tiled=True).reshape(-1, mine.shape[-1])


def sort_blocks(array, order):
    blocks = array.reshape(order.shape[0], -1, array.shape[-1])
    return pick_blocks(blocks, order).reshape(array.shape)


def as_blocks(grad, order):
    return grad.reshape(order.shape[0], -1, grad.shape[-1])


def scatter_line(blocks):
    return lax.psum_scatter(blocks, "z", scatter_dimension=0, tiled=True)


def plane_plan(latents, context, clip_starts, buckets, owners, cotangent, sheet, first, second):
    groups = lax.axis_size("dp")
    planes = lax.axis_size("z")
    cores = lax.axis_size("core")
    members = groups * cores
    frames = latents.shape[1]
    length = frames * members
    rows = sheet.shape[0]
    blocks = owners.shape[0]
    head_count = D // HEAD // members
    span = D // members
    units = FF // members
    score_scale = HEAD ** (-0.5)
    tail_col = 6 * D + 3 * FF
    gain_col = tail_col + 2 * CTXW
    plane = lax.axis_index("z")

    group_ids = jnp.arange(blocks, dtype=jnp.int32)
    inverse = jnp.sum(
        jnp.where(owners[None, :] == group_ids[:, None], group_ids[None, :], 0), axis=1
    )
    slot = group_ids.reshape(groups, planes, cores).swapaxes(0, 1).reshape(-1)
    slot_of = jnp.sum(
        jnp.where(slot[None, :] == group_ids[:, None], group_ids[None, :], 0), axis=1
    )
    to_logical = jnp.take(slot_of, inverse)
    to_slots = jnp.take(owners, slot)

    orders = jnp.stack([to_slots, to_logical])
    small = jnp.concatenate(
        [
            jnp.pad(
                sheet[:, gain_col:].astype(jnp.bfloat16).astype(jnp.float32).T,
                ((0, 0), (0, 64 - rows)),
            ),
            jnp.pad(clip_starts.astype(jnp.float32), ((0, 7), (0, 64 - clip_starts.shape[1]))),
        ],
        axis=1,
    )
    both, small, text_mine, mine_one = opening(
        latents[0], cotangent[0], small, context[0].T, sheet
    )
    mine_one, later = lax.optimization_barrier((mine_one, sheet))
    low_sheet = later.astype(jnp.bfloat16)
    weight_one = gather_slots(mine_one)
    gains = pick_blocks(small[..., :rows].reshape(blocks, 8, rows), to_logical)
    gains = gains.swapaxes(1, 2).reshape(D, 8)
    starts = lax.dynamic_index_in_dim(
        small[0, :, 0, 64 : 64 + clip_starts.shape[1]], plane * cores, 0, False
    )
    starts = starts.astype(jnp.int32)

    bucket_ids = jnp.arange(NB, dtype=jnp.int32)
    bucket_pick = (bucket_ids == buckets[plane]).astype(jnp.float32)
    counts = jnp.sum((buckets[:, None] == bucket_ids[None, :]).astype(jnp.float32), axis=0)
    row_weight = buckets.shape[0] / (NB * jnp.sum(bucket_pick * counts))
    gain_one = gains[:, 0:1]
    gain_two = gains[:, 1:2]
    gain_three = gains[:, 2:3]
    time_gain = jnp.sum(gains[:, 3:] * bucket_pick[None, :], axis=1, keepdims=True)

    tokens = both[:, :D].astype(jnp.float32).T
    grad_out = both[:, D:].astype(jnp.float32).T * row_weight

    rest = frames // planes
    place = jnp.arange(length, dtype=jnp.int32).reshape(planes, cores, groups, rest)
    positions = place.transpose(2, 1, 0, 3).reshape(-1)
    segments = segment_ids(starts, positions)
    frequency = jnp.exp(
        -math.log(10000.0) * jnp.arange(HEAD // 2, dtype=jnp.float32) / (HEAD // 2)
    )
    angles = frequency[:, None] * positions.astype(jnp.float32)[None, :]
    cosine = jnp.cos(angles)
    sine_table = jnp.sin(angles)

    normed_one, inverse_one = norm_columns(tokens)
    scaled_one = gain_one * time_gain
    h_one, grad_ff, mine_gu, mine_down = first_gather(
        sort_blocks((normed_one * scaled_one).astype(jnp.bfloat16), to_slots),
        sort_blocks(grad_out.astype(jnp.bfloat16), to_slots),
        low_sheet,
    )
    weight_gu = gather_slots(mine_gu)
    line_down = gather_slots(mine_down)

    parts, probs, attn_out = attend(weight_one, h_one, cosine, sine_table, segments)
    attn_out, x_one, normed_two, inverse_two, h_two, text_kv = project(
        "sum",
        0,
        orders,
        attn_out,
        weight_one,
        tokens,
        gain_two,
        text_mine,
    )

    cross_q, cross_probs, cross_out = cross(weight_one, h_two, text_kv)
    cross_out, x_two, normed_three, inverse_three, h_three = project(
        "slots",
        2 * span,
        orders,
        cross_out,
        weight_one,
        x_one,
        gain_three,
    )

    gate_up = contract_rows(weight_gu, h_three)
    gate_pre = gate_up[:units]
    up_part = gate_up[units:]
    sigmoid_gate = jax.nn.sigmoid(gate_pre)
    silu_gate = gate_pre * sigmoid_gate
    hidden = (silu_gate * up_part).astype(jnp.bfloat16)

    grad_blocks_down = as_blocks(contract_last(grad_ff, hidden).astype(jnp.bfloat16), to_slots)
    weight_down, grad_blocks_down = lax.optimization_barrier((line_down, grad_blocks_down))
    sums_down = scatter_line(grad_blocks_down)
    grad_hidden = contract_rows(weight_down, grad_ff)
    grad_gate = grad_hidden * up_part * (sigmoid_gate * (1.0 + gate_pre * (1.0 - sigmoid_gate)))
    grad_up = grad_hidden * silu_gate
    grad_gu = jnp.concatenate([grad_gate, grad_up], axis=0).astype(jnp.bfloat16)
    grad_x_two, grad_weight_gu, sum_three, grad_cross = back(
        orders,
        weight_gu,
        grad_gu,
        h_three,
        (normed_three, inverse_three, gain_three, grad_out),
        send_rows=True,
        in_slots=True,
        after=[grad_blocks_down],
    )
    grad_blocks_gu = as_blocks(grad_weight_gu, to_slots)
    sums_gu = scatter_line(grad_blocks_gu)
    grad_cross_out, grad_weight_co = back(
        orders, weight_one, grad_cross, cross_out, column=2 * span
    )
    grad_cross_q, grad_text = cross_back(cross_q, cross_probs, text_kv, grad_cross_out)
    grad_x_one, grad_weight_cq, sum_two, grad_attn, grad_text = back(
        orders,
        weight_one,
        grad_cross_q,
        h_two,
        (normed_two, inverse_two, gain_two, grad_x_two),
        column=span,
        send_rows=True,
        text=grad_text,
        in_slots=True,
        after=[sums_down],
    )
    grad_attn_out, grad_weight_two = back(
        orders,
        weight_one,
        grad_attn,
        attn_out,
        beside=(grad_weight_cq, grad_weight_co, grad_text, text_mine),
    )
    grad_blocks_two = as_blocks(grad_weight_two, to_slots)
    sums_two = scatter_line(grad_blocks_two)
    grad_qkv = attend_back(parts, probs, grad_attn_out, cosine, sine_table)
    latent_grad, grad_weight_qkv, sum_one = back(
        orders,
        weight_one,
        grad_qkv,
        h_one,
        (normed_one, inverse_one, scaled_one, grad_x_one),
        column=4 * span,
        in_slots=True,
        after=[sums_gu],
    )
    grad_blocks_one = as_blocks(grad_weight_qkv, to_slots)
    sums_one = scatter_line(grad_blocks_one)
    sums_feed, ff_out = feed(
        sums_gu,
        sums_down,
        weight_down,
        hidden,
        [grad_blocks_one],
    )
    sum_one = sum_one[0:1]
    grad_gain_one = sum_one * time_gain.T
    grad_time = sum_one * gain_one.T
    gain_grads = jnp.concatenate(
        [
            grad_gain_one,
            sum_two[0:1],
            sum_three[0:1],
            bucket_pick[:, None] * grad_time,
        ],
        axis=0,
    )
    out_pair, sums_one, sums_two, gain_sums, squares = closing(
        orders, ff_out, x_two, latent_grad, sums_one, sums_two, sums_gu, sums_down, gain_grads
    )
    place = lax.axis_index("dp") * (planes * cores) + plane * cores + lax.axis_index("core")
    (
        clipped,
        first_new,
        second_new,
        sheet_new,
        sheet_copy,
        grad_norm,
        gain_grad,
        output,
        latent_grad,
    ) = sheet_update(
        lax.dynamic_slice_in_dim(owners, place, 1),
        length,
        sums_one,
        sums_two,
        sums_feed,
        squares,
        gain_sums,
        out_pair,
        sheet,
        first,
        second,
    )
    return (
        output[None],
        latent_grad[None],
        grad_norm[0],
        clipped,
        gain_grad,
        first_new,
        second_new,
        sheet_new,
        sheet_copy,
    )


def solution(mesh):
    groups, seq_count = mesh.shape["dp"], mesh.shape["seq"]
    by_plane = groups == 4 and seq_count == 8
    if by_plane:
        mesh = Mesh(mesh.devices.reshape(groups, seq_count // 2, 2), ("dp", "z", "core"))
    seq = ("z", "core") if by_plane else "seq"
    both = ("dp", "z", "core") if by_plane else ("dp", "seq")
    in_specs = (
        P("dp", seq, None),
        P("dp", None, None),
        P("dp", None),
        P(),
        P(),
        P("dp", seq, None),
        P(both, None),
        P(both, None),
        P(both, None),
    )
    out_specs = (
        P("dp", seq, None),
        P("dp", seq, None),
        P(),
        P(both, None),
        P(both, None),
        P(both, None),
        P(both, None),
        P(both, None),
        P(both, None),
    )
    return jax.shard_map(
        plane_plan if by_plane else gather_plan,
        mesh=mesh,
        in_specs=in_specs,
        out_specs=out_specs,
        check_vma=False,
    )
```

```python
import functools
import math

import jax
import jax.numpy as jnp
from jax import lax
from jax.experimental import pallas as pl
from jax.experimental.pallas import tpu as pltpu
from jax.sharding import Mesh
from jax.sharding import PartitionSpec as P

D = 1536
FF = 6144
HEAD = 64
CTXW = 768
CTX = 128
NB = 5
STEP = 10
SHEET = 29192


HIGHEST = lax.Precision.HIGHEST
EPS_NORM = 1e-05
EPS_ADAM = 1e-08
MASKED_SCORE = -1e30
BETA_ONE = 0.5
BETA_TWO = 0.5
WEIGHT_DECAY = 0.01


def reorder(values, ordering):
    leading = values.shape[:-1]
    groups = ordering.shape[0]
    blocks = values.reshape(leading + (groups, values.shape[-1] // groups))
    return jnp.take(blocks, ordering, axis=-2).reshape(values.shape)


def norm_parts(values):
    average = jnp.mean(values, axis=-1, keepdims=True)
    centered = values - average
    variance = jnp.mean(centered * centered, axis=-1, keepdims=True)
    inverse_std = lax.rsqrt(variance + EPS_NORM)
    return (centered * inverse_std, inverse_std)


def norm_back(grad_normed, normed, inverse_std):
    return inverse_std * (
        grad_normed
        - jnp.mean(grad_normed, axis=-1, keepdims=True)
        - normed * jnp.mean(grad_normed * normed, axis=-1, keepdims=True)
    )


def softmax_rows(scores):
    row_max = jnp.max(scores, axis=-1, keepdims=True)
    exponent = jnp.exp(scores - row_max)
    return exponent / jnp.sum(exponent, axis=-1, keepdims=True)


def rope_tables(positions, head_dim):
    half_dim = head_dim // 2
    frequency = jnp.exp(-math.log(10000.0) * jnp.arange(half_dim, dtype=jnp.float32) / half_dim)
    angles = positions.astype(jnp.float32)[:, None] * frequency[None, :]
    return (jnp.cos(angles)[:, None, :], jnp.sin(angles)[:, None, :])


def rotate(values, cosine, sine_table):
    half_dim = values.shape[-1] // 2
    first_half = values[..., :half_dim]
    second_half = values[..., half_dim:]
    return jnp.concatenate(
        [
            first_half * cosine - second_half * sine_table,
            second_half * cosine + first_half * sine_table,
        ],
        axis=-1,
    )


def unrotate(grads, cosine, sine_table):
    half_dim = grads.shape[-1] // 2
    first_half = grads[..., :half_dim]
    second_half = grads[..., half_dim:]
    return jnp.concatenate(
        [
            first_half * cosine + second_half * sine_table,
            second_half * cosine - first_half * sine_table,
        ],
        axis=-1,
    )


def segment_ids(starts, positions):
    return jnp.sum((starts[None, :] <= positions[:, None]).astype(jnp.int32), axis=1) - 1


def column_spread(length):
    column = jnp.arange(SHEET, dtype=jnp.int32)
    base_std = D ** (-0.5)
    spread = jnp.full((SHEET,), base_std, jnp.float32)
    spread = jnp.where(
        (column >= 3 * D) & (column < 4 * D), base_std * math.sqrt(length) / 4.0, spread
    )
    spread = jnp.where((column >= 5 * D) & (column < 6 * D), base_std * math.sqrt(CTX), spread)
    spread = jnp.where((column >= 6 * D + 2 * FF) & (column < 6 * D + 3 * FF), FF ** (-0.5), spread)
    spread = jnp.where(
        (column >= 6 * D + 3 * FF) & (column < 6 * D + 3 * FF + 2 * CTXW), CTXW ** (-0.5), spread
    )
    spread = jnp.where(column >= 6 * D + 3 * FF + 2 * CTXW, 0.3, spread)
    return spread


def inner_rows(left, right):
    return lax.dot_general(
        left, right, (((0,), (0,)), ((), ())), preferred_element_type=jnp.float32
    )


def inner_rows_high(left, right):
    return lax.dot_general(
        left, right, (((0,), (0,)), ((), ())), precision=HIGHEST, preferred_element_type=jnp.float32
    )


def gather_plan(latents, context, clip_starts, buckets, owners, cotangent, sheet, first, second):
    frames = latents.shape[1]
    seq_count = lax.axis_size("seq")
    length = frames * seq_count
    head_count = D // HEAD
    score_scale = HEAD ** (-0.5)
    group_ids = jnp.arange(owners.shape[0], dtype=jnp.int32)
    inverse = jnp.sum(
        jnp.where(owners[None, :] == group_ids[:, None], group_ids[None, :], 0), axis=1
    )
    gathered = lax.all_gather(sheet.astype(jnp.bfloat16), ("dp", "seq"), axis=0, tiled=True)
    tail_col = 6 * D + 3 * FF
    gain_col = tail_col + 2 * CTXW
    gain_rows = reorder(gathered[:, gain_col:].astype(jnp.float32).T, inverse)
    row_index = lax.axis_index("dp")
    bucket_ids = jnp.arange(NB, dtype=jnp.int32)
    bucket_pick = (bucket_ids == buckets[row_index]).astype(jnp.float32)
    counts = jnp.sum((buckets[:, None] == bucket_ids[None, :]).astype(jnp.float32), axis=0)
    row_weight = buckets.shape[0] / (NB * jnp.sum(bucket_pick * counts))
    gain_one = gain_rows[0]
    gain_two = gain_rows[1]
    gain_three = gain_rows[2]
    time_gain = jnp.sum(gain_rows[3:] * bucket_pick[:, None], axis=0)
    tokens = latents[0].astype(jnp.float32)
    positions = lax.axis_index("seq") * frames + jnp.arange(frames, dtype=jnp.int32)
    all_positions = jnp.arange(length, dtype=jnp.int32)
    starts = clip_starts[0]
    same_clip = (
        segment_ids(starts, positions)[:, None] == segment_ids(starts, all_positions)[None, :]
    )[None]
    cosine, sine_table = rope_tables(positions, HEAD)
    normed_one, inverse_one = norm_parts(tokens)
    scaled_one = gain_one * time_gain
    h_one_st = reorder((normed_one * scaled_one).astype(jnp.bfloat16), owners)
    joint_qkv = jnp.dot(h_one_st, gathered[:, : 3 * D], preferred_element_type=jnp.float32)
    queries = rotate(joint_qkv[:, :D].reshape(frames, head_count, HEAD), cosine, sine_table).astype(
        jnp.bfloat16
    )
    key_local = rotate(
        joint_qkv[:, D : 2 * D].reshape(frames, head_count, HEAD), cosine, sine_table
    ).astype(jnp.bfloat16)
    value_local = joint_qkv[:, 2 * D :].reshape(frames, head_count, HEAD).astype(jnp.bfloat16)
    key_all, value_all = (
        lax.all_gather(key_local, "seq", axis=0, tiled=True),
        lax.all_gather(value_local, "seq", axis=0, tiled=True),
    )
    scores = (
        jnp.einsum("qhd,khd->hqk", queries, key_all, preferred_element_type=jnp.float32)
        * score_scale
    )
    attn_probs = softmax_rows(jnp.where(same_clip, scores, MASKED_SCORE))
    probs_low = attn_probs.astype(jnp.bfloat16)
    attn_out = (
        jnp.einsum("hqk,khd->qhd", probs_low, value_all, preferred_element_type=jnp.float32)
        .reshape(frames, D)
        .astype(jnp.bfloat16)
    )
    attn_st = reorder(attn_out, owners)
    x_one = tokens + jnp.dot(
        attn_st, gathered[:, 3 * D : 4 * D], preferred_element_type=jnp.float32
    )
    normed_two, inverse_two = norm_parts(x_one)
    h_two_st = reorder((normed_two * gain_two).astype(jnp.bfloat16), owners)
    cross_q = (
        jnp.dot(h_two_st, gathered[:, 4 * D : 5 * D], preferred_element_type=jnp.float32)
        .astype(jnp.bfloat16)
        .reshape(frames, head_count, HEAD)
    )
    text_tokens = context[0]
    text_kv = jnp.einsum(
        "tc,dec->etd",
        text_tokens,
        gathered[:, tail_col:gain_col].reshape(D, 2, CTXW),
        preferred_element_type=jnp.float32,
    )
    text_kv = reorder(text_kv, inverse).astype(jnp.bfloat16).reshape(2, CTX, head_count, HEAD)
    text_keys = text_kv[0]
    text_values = text_kv[1]
    cross_scores = (
        jnp.einsum("qhd,khd->hqk", cross_q, text_keys, preferred_element_type=jnp.float32)
        * score_scale
    )
    cross_probs = softmax_rows(cross_scores)
    cross_low = cross_probs.astype(jnp.bfloat16)
    cross_out = (
        jnp.einsum("hqk,khd->qhd", cross_low, text_values, preferred_element_type=jnp.float32)
        .reshape(frames, D)
        .astype(jnp.bfloat16)
    )
    cross_st = reorder(cross_out, owners)
    x_two = x_one + jnp.dot(
        cross_st, gathered[:, 5 * D : 6 * D], preferred_element_type=jnp.float32
    )
    normed_three, inverse_three = norm_parts(x_two)
    h_three_st = reorder((normed_three * gain_three).astype(jnp.bfloat16), owners)
    grad_out = cotangent[0].astype(jnp.float32) * row_weight
    grad_ff_st = reorder(grad_out.astype(jnp.bfloat16), owners)
    gate_weight = gathered[:, 6 * D : 6 * D + 2 * FF]
    down_weight = gathered[:, 6 * D + 2 * FF : 6 * D + 3 * FF]
    units = down_weight.shape[1]
    gate_up = jnp.dot(h_three_st, gate_weight, preferred_element_type=jnp.float32)
    gate_pre = gate_up[:, :units]
    up_part = gate_up[:, units:]
    sigmoid_gate = jax.nn.sigmoid(gate_pre)
    silu_gate = gate_pre * sigmoid_gate
    hidden = (silu_gate * up_part).astype(jnp.bfloat16)
    ff_out = reorder(
        jnp.einsum("nf,df->nd", hidden, down_weight, preferred_element_type=jnp.float32), inverse
    )
    result = x_two + ff_out
    grad_hidden = jnp.dot(grad_ff_st, down_weight, preferred_element_type=jnp.float32)
    grad_gate = grad_hidden * up_part * (sigmoid_gate * (1.0 + gate_pre * (1.0 - sigmoid_gate)))
    grad_up = grad_hidden * silu_gate
    grad_gu = jnp.concatenate([grad_gate, grad_up], axis=1).astype(jnp.bfloat16)
    grad_h_three = reorder(
        jnp.einsum("nf,df->nd", grad_gu, gate_weight, preferred_element_type=jnp.float32), inverse
    )
    grad_gain_three = jnp.sum(grad_h_three * normed_three, axis=0)
    grad_x_two = grad_out + norm_back(grad_h_three * gain_three, normed_three, inverse_three)
    grad_cross = grad_x_two.astype(jnp.bfloat16)
    grad_cross_out = (
        reorder(
            jnp.einsum(
                "nd,ed->ne",
                grad_cross,
                gathered[:, 5 * D : 6 * D],
                preferred_element_type=jnp.float32,
            ),
            inverse,
        )
        .astype(jnp.bfloat16)
        .reshape(frames, head_count, HEAD)
    )
    grad_cross_probs = jnp.einsum(
        "qhd,khd->hqk", grad_cross_out, text_values, preferred_element_type=jnp.float32
    )
    grad_cross_scores = (
        cross_probs
        * (grad_cross_probs - jnp.sum(cross_probs * grad_cross_probs, axis=-1, keepdims=True))
    ).astype(jnp.bfloat16)
    grad_cross_q = (
        (
            jnp.einsum(
                "hqk,khd->qhd", grad_cross_scores, text_keys, preferred_element_type=jnp.float32
            )
            * score_scale
        )
        .reshape(frames, D)
        .astype(jnp.bfloat16)
    )
    grad_text_keys = (
        jnp.einsum("hqk,qhd->khd", grad_cross_scores, cross_q, preferred_element_type=jnp.float32)
        * score_scale
    )
    grad_text_values = jnp.einsum(
        "hqk,qhd->khd", cross_low, grad_cross_out, preferred_element_type=jnp.float32
    )
    grad_text = reorder(
        jnp.stack([grad_text_keys.reshape(CTX, D), grad_text_values.reshape(CTX, D)]), owners
    )
    grad_h_two = reorder(
        jnp.einsum(
            "ne,de->nd",
            grad_cross_q,
            gathered[:, 4 * D : 5 * D],
            preferred_element_type=jnp.float32,
        ),
        inverse,
    )
    grad_gain_two = jnp.sum(grad_h_two * normed_two, axis=0)
    grad_x_one = grad_x_two + norm_back(grad_h_two * gain_two, normed_two, inverse_two)
    grad_attn = grad_x_one.astype(jnp.bfloat16)
    grad_attn_out = (
        reorder(
            jnp.einsum(
                "nd,ed->ne",
                grad_attn,
                gathered[:, 3 * D : 4 * D],
                preferred_element_type=jnp.float32,
            ),
            inverse,
        )
        .astype(jnp.bfloat16)
        .reshape(frames, head_count, HEAD)
    )
    key_back, value_back = (key_all, value_all)

    def head_grads(head_items):
        head_probs, head_grad_out, head_values = head_items
        grad_probs = jnp.einsum(
            "qd,kd->qk", head_grad_out, head_values, preferred_element_type=jnp.float32
        )
        return (
            head_probs * (grad_probs - jnp.sum(head_probs * grad_probs, axis=-1, keepdims=True))
        ).astype(jnp.bfloat16)

    grad_scores_low = lax.map(
        head_grads, (attn_probs, jnp.swapaxes(grad_attn_out, 0, 1), jnp.swapaxes(value_back, 0, 1))
    )
    grad_queries = (
        jnp.einsum("hqk,khd->qhd", grad_scores_low, key_back, preferred_element_type=jnp.float32)
        * score_scale
    )
    grad_keys = (
        jnp.einsum("hqk,qhd->khd", grad_scores_low, queries, preferred_element_type=jnp.float32)
        * score_scale
    )
    grad_values = jnp.einsum(
        "hqk,qhd->khd", probs_low, grad_attn_out, preferred_element_type=jnp.float32
    )
    key_sums = lax.psum_scatter(
        jnp.concatenate(
            [
                grad_keys.reshape(frames * lax.axis_size("seq"), D),
                grad_values.reshape(frames * lax.axis_size("seq"), D),
            ],
            axis=1,
        ).astype(jnp.bfloat16),
        "seq",
        scatter_dimension=0,
        tiled=True,
    ).astype(jnp.float32)
    grad_q_raw = unrotate(grad_queries, cosine, sine_table).reshape(frames, D)
    grad_k_raw = unrotate(
        key_sums[:, :D].reshape(frames, head_count, HEAD), cosine, sine_table
    ).reshape(frames, D)
    grad_qkv = jnp.concatenate([grad_q_raw, grad_k_raw, key_sums[:, D:]], axis=1).astype(
        jnp.bfloat16
    )
    grad_h_one = reorder(
        jnp.einsum("ne,de->nd", grad_qkv, gathered[:, : 3 * D], preferred_element_type=jnp.float32),
        inverse,
    )
    grad_gain_one = jnp.sum(grad_h_one * normed_one * time_gain, axis=0)
    grad_time = jnp.sum(grad_h_one * normed_one * gain_one, axis=0)
    latent_grad = grad_x_one + norm_back(grad_h_one * scaled_one, normed_one, inverse_one)
    gain_grads = jnp.concatenate(
        [
            jnp.stack([grad_gain_one, grad_gain_two, grad_gain_three]),
            bucket_pick[:, None] * grad_time[None, :],
        ],
        axis=0,
    )
    gain_grads = reorder(gain_grads, owners).T
    text_float = text_tokens.astype(jnp.float32)
    pieces = [
        inner_rows(h_one_st, grad_qkv),
        inner_rows(attn_st, grad_attn),
        inner_rows(h_two_st, grad_cross_q),
        inner_rows(cross_st, grad_cross),
    ]
    pieces = pieces + [inner_rows(h_three_st, grad_gu), inner_rows(grad_ff_st, hidden)]
    pieces = pieces + [
        inner_rows_high(grad_text[0], text_float),
        inner_rows_high(grad_text[1], text_float),
        gain_grads,
    ]
    other_shard = lax.psum_scatter(
        jnp.concatenate(pieces, axis=1), ("dp", "seq"), scatter_dimension=0, tiled=True
    )
    total_squares = lax.psum(jnp.sum(other_shard * other_shard), ("dp", "seq"))
    grad_norm = jnp.sqrt(total_squares)
    clipped = other_shard / jnp.maximum(grad_norm, 1.0)
    gain_grad = clipped[:, 6 * D + 3 * FF + 2 * CTXW :]
    first_new = BETA_ONE * first + (1.0 - BETA_ONE) * clipped
    second_new = BETA_TWO * second + (1.0 - BETA_TWO) * clipped * clipped
    mean_hat = first_new / (1.0 - BETA_ONE**STEP)
    square_hat = second_new / (1.0 - BETA_TWO**STEP)
    rates = column_spread(length)[None, :]
    sheet_new = sheet - rates * (
        mean_hat / (jnp.sqrt(square_hat) + EPS_ADAM) + WEIGHT_DECAY * sheet
    )
    return (
        result.astype(jnp.bfloat16)[None],
        latent_grad[None],
        grad_norm,
        clipped,
        gain_grad,
        first_new,
        second_new,
        sheet_new,
        sheet_new.astype(jnp.bfloat16),
    )


PLANE = ("dp", "core")


def norm_columns(values):
    average = jnp.mean(values, axis=0, keepdims=True)
    centered = values - average
    variance = jnp.mean(centered * centered, axis=0, keepdims=True)
    inverse_std = lax.rsqrt(variance + EPS_NORM)
    return (centered * inverse_std, inverse_std)


def norm_columns_back(grad_normed, normed, inverse_std):
    return inverse_std * (
        grad_normed
        - jnp.mean(grad_normed, axis=0, keepdims=True)
        - normed * jnp.mean(grad_normed * normed, axis=0, keepdims=True)
    )


def contract_rows(left, right):
    return lax.dot_general(
        left, right, (((0,), (0,)), ((), ())), preferred_element_type=jnp.float32
    )


def contract_last(left, right):
    return lax.dot_general(
        left, right, (((1,), (1,)), ((), ())), preferred_element_type=jnp.float32
    )


def matmul(left, right):
    return jnp.dot(left, right, preferred_element_type=jnp.float32)


MESH_ID = pl.DeviceIdType.MESH
IDENTITIES = {}


def identity_of(name, *arrays):
    key = (name,) + tuple((array.shape, str(array.dtype)) for array in arrays)
    return IDENTITIES.setdefault(key, len(IDENTITIES))


IN_HBM = pl.BlockSpec(memory_space=pltpu.HBM)
IN_SMEM = pl.BlockSpec(memory_space=pltpu.SMEM)
IN_VMEM = pl.BlockSpec(memory_space=pltpu.VMEM)
BRIEF = pl.CostEstimate(flops=0, bytes_accessed=1024, transcendentals=0)


def kernel_call(kernel, *, out_shape, in_specs, out_specs, **options):
    single = not isinstance(out_shape, tuple)
    shapes = (out_shape,) if single else out_shape
    places = (out_specs,) if single else out_specs
    shapes = tuple(
        pltpu.HBM(shape.shape, shape.dtype) if place is IN_HBM else shape
        for shape, place in zip(shapes, places)
    )
    call = pl.pallas_call(
        kernel,
        out_shape=shapes[0] if single else shapes,
        in_specs=in_specs,
        out_specs=out_specs,
        **options,
    )

    def run(*operands):
        return call(
            *[
                pltpu.with_memory_space_constraint(operand, pltpu.HBM)
                if place is IN_HBM
                else operand
                for operand, place in zip(operands, in_specs)
            ]
        )

    return run


def reorder_blocks(source, target, order, column=0):
    rows = source.shape[1]
    columns = slice(column, column + target.shape[1])

    @pl.loop(0, source.shape[0])
    def _(b):
        target[pl.ds(pl.multiple_of(b * rows, 16), rows), :] = source[order(b), :, columns]


def wide(ref):
    return ref[...].astype(jnp.float32)


def greet(peers):
    barrier = pltpu.get_barrier_semaphore()
    for peer in peers:
        pl.semaphore_signal(barrier, inc=1, device_id=peer, device_id_type=MESH_ID)
    pl.semaphore_wait(barrier, len(peers))


def near():
    group, core = lax.axis_index("dp"), lax.axis_index("core")
    across = group + 1 - 2 * lax.rem(group, 2)
    along = lax.rem(group + 2, 4)
    return group, core, across, along


def member_rows(width):
    def place(ref, member, start, count):
        first_row = pl.multiple_of(member * width + start, 16)
        return ref.at[pl.ds(first_row, count), :]

    return place


def member_lanes(width):
    def place(ref, member, start, count):
        return ref.at[pl.ds(start, count), pl.ds(pl.multiple_of(member * width, 128), width)]

    return place


def mover(send_sem, recv_sem, first=0):
    def copy(k, source, target, peer):
        return pltpu.make_async_remote_copy(
            src_ref=source,
            dst_ref=target,
            send_sem=send_sem.at[first + k],
            recv_sem=recv_sem.at[first + k],
            device_id=peer,
            device_id_type=MESH_ID,
        )

    return copy


def member_at(member):
    return {"dp": lax.div(member, 2), "core": lax.rem(member, 2)}


def plane_peers():
    group, core, _, _ = near()
    member = group * 2 + core
    return [lax.rem(member + step, 8) for step in range(1, 8)]


def gather_steps(place, x_ref, o_ref, local_sem, copy, arrived_whole=lambda member: None):
    group, core, across, along = near()
    beyond = across + along - group
    other = 1 - core
    sibling, by_x, by_y = {"core": other}, {"dp": across}, {"dp": along}
    half = x_ref.shape[0] // 2

    def part(owner, owner_core, piece):
        return place(o_ref, owner * 2 + owner_core, piece * half, half)

    sent = []

    def send(k, source, target, peer):
        moving = copy(k, source, target, peer)
        moving.start()
        sent.append(moving)

    def own(k, piece, peer):
        send(k, x_ref.at[pl.ds(piece * half, half), :], part(group, core, piece), peer)

    def relay(k, owner, piece, peer):
        send(k, part(owner, core, piece), part(owner, core, piece), peer)

    def arrived(k, owner, owner_core, piece):
        landed = part(owner, owner_core, piece)
        copy(k, landed, landed, sibling).wait_recv()

    local = pltpu.make_async_copy(
        x_ref, place(o_ref, group * 2 + core, 0, 2 * half), local_sem
    )
    local.start()
    own(0, 0, by_x)
    own(1, 1, by_y)
    own(2, 1, by_x)
    own(3, 0, by_y)
    own(4, 0, sibling)
    own(5, 1, sibling)

    def finish():
        local.wait()
        arrived_whole(group * 2 + core)
        arrived(4, group, other, 0)
        arrived(5, group, other, 1)
        arrived_whole(group * 2 + other)
        arrived(0, across, core, 0)
        relay(6, across, 0, by_y)
        relay(7, across, 0, sibling)
        arrived(1, along, core, 1)
        relay(8, along, 1, by_x)
        relay(9, along, 1, sibling)
        arrived(2, across, core, 1)
        relay(10, across, 1, sibling)
        arrived_whole(across * 2 + core)
        arrived(3, along, core, 0)
        relay(11, along, 0, sibling)
        arrived_whole(along * 2 + core)
        arrived(7, across, other, 0)
        arrived(10, across, other, 1)
        arrived_whole(across * 2 + other)
        arrived(6, beyond, core, 0)
        relay(12, beyond, 0, sibling)
        arrived(8, beyond, core, 1)
        relay(13, beyond, 1, sibling)
        arrived_whole(beyond * 2 + core)
        arrived(9, along, other, 1)
        arrived(11, along, other, 0)
        arrived_whole(along * 2 + other)
        arrived(12, beyond, other, 0)
        arrived(13, beyond, other, 1)
        arrived_whole(beyond * 2 + other)
        for moving in sent:
            moving.wait_send()

    return finish


def exchange_steps(source, target, x_ref, o_ref, local_sem, copy):
    group, core, _, _ = near()
    member = group * 2 + core
    local = pltpu.make_async_copy(source(x_ref, member), target(o_ref, member), local_sem)
    local.start()
    sent = []
    for k, peer in enumerate(plane_peers()):
        sent.append(copy(k, source(x_ref, peer), target(o_ref, member), member_at(peer)))
        sent[-1].start()

    def finish():
        for k in range(7):
            sender = lax.rem(member + 7 - k, 8)
            landed = target(o_ref, sender)
            copy(k, landed, landed, member_at(sender)).wait_recv()
        local.wait()
        for moving in sent:
            moving.wait_send()

    return finish


def gather_kernel(place, x_ref, *refs):
    o_ref, local_sem, send_sem, recv_sem = refs[-4:]
    _, core, across, along = near()
    greet([{"dp": across}, {"dp": along}, {"core": 1 - core}])
    gather_steps(place, x_ref, o_ref, local_sem, mover(send_sem, recv_sem))()


def plane_gather_call(shard, shape, place, kind, after):
    return kernel_call(
        functools.partial(gather_kernel, place),
        out_shape=jax.ShapeDtypeStruct(shape, shard.dtype),
        in_specs=[IN_HBM] * (1 + len(after)),
        out_specs=IN_HBM,
        scratch_shapes=[
            pltpu.SemaphoreType.DMA,
            pltpu.SemaphoreType.DMA((14,)),
            pltpu.SemaphoreType.DMA((14,)),
        ],
        compiler_params=pltpu.CompilerParams(
            collective_id=identity_of(kind, shard, *after), has_side_effects=True
        ),
        cost_estimate=BRIEF,
        name="plane_gather",
    )(shard, *after)


def plane_gather(shard, after=()):
    rows, width = shard.shape
    return plane_gather_call(shard, (rows, 8 * width), member_lanes(width), "gather lanes", after)


def plane_gather_rows(shard, after=()):
    rows, width = shard.shape
    return plane_gather_call(shard, (8 * rows, width), member_rows(rows), "gather rows", after)


def scatter_steps(place, p_ref, bufs, copy):
    pair, total, from_x, from_y, relay = bufs
    group, core, across, along = near()
    beyond = across + along - group
    other = 1 - core
    sibling, by_x, by_y = {"core": other}, {"dp": across}, {"dp": along}
    rows = total.shape[1]
    half = rows // 2
    low, high = pl.ds(0, half), pl.ds(half, half)
    sent = []

    def send(k, source, target, peer):
        moving = copy(k, source, target, peer)
        moving.start()
        sent.append(moving)

    def arrived(k, target):
        copy(k, target, target, sibling).wait_recv()

    def both_cores(k, owner):
        arrived(k, pair.at[k])
        summed = wide(place(p_ref, owner * 2 + core, 0, rows)) + wide(pair.at[k])
        total[k] = summed.astype(total.dtype)

    def cores():
        for k, owner in enumerate((beyond, across, along, group)):
            send(k, place(p_ref, owner * 2 + other, 0, rows), pair.at[k], sibling)

    def chips():
        both_cores(0, beyond)
        send(4, total.at[0, low], relay.at[0], by_x)
        send(5, total.at[0, high], relay.at[1], by_y)
        both_cores(1, across)
        send(6, total.at[1, low], from_x.at[low], by_x)
        both_cores(2, along)
        send(7, total.at[2, high], from_y.at[high], by_y)
        both_cores(3, group)

    def relays():
        arrived(5, relay.at[1])
        total[1, high] = (wide(total.at[1, high]) + wide(relay.at[1])).astype(total.dtype)
        send(8, total.at[1, high], from_x.at[high], by_x)
        arrived(4, relay.at[0])
        total[2, low] = (wide(total.at[2, low]) + wide(relay.at[0])).astype(total.dtype)
        send(9, total.at[2, low], from_y.at[low], by_y)

    def finish():
        arrived(6, from_x.at[low])
        arrived(7, from_y.at[high])
        arrived(8, from_x.at[high])
        arrived(9, from_y.at[low])
        summed = wide(total.at[3]) + wide(from_x) + wide(from_y)
        for moving in sent:
            moving.wait_send()
        return summed

    return cores, chips, relays, finish


def scatter_bufs(rows, width):
    slot = pltpu.VMEM((rows, width), jnp.bfloat16)
    four = pltpu.VMEM((4, rows, width), jnp.bfloat16)
    return [four, four, slot, slot, pltpu.VMEM((2, rows // 2, width), jnp.bfloat16)]


def scatter_kernel(place, p_ref, *refs):
    o_ref, *bufs, send_sem, recv_sem = refs[-8:]
    _, core, across, along = near()
    greet([{"dp": across}, {"dp": along}, {"core": 1 - core}])
    cores, chips, relays, finish = scatter_steps(place, p_ref, bufs, mover(send_sem, recv_sem))
    cores()
    chips()
    relays()
    o_ref[...] = finish().astype(o_ref.dtype)


def plane_scatter_call(partial, shape, place, dtype, kind, after):
    rows, width = shape
    return kernel_call(
        functools.partial(scatter_kernel, place),
        out_shape=jax.ShapeDtypeStruct(shape, dtype),
        in_specs=[IN_VMEM] + [IN_HBM] * len(after),
        out_specs=IN_VMEM,
        scratch_shapes=scatter_bufs(rows, width)
        + [
            pltpu.SemaphoreType.DMA((10,)),
            pltpu.SemaphoreType.DMA((10,)),
        ],
        compiler_params=pltpu.CompilerParams(
            collective_id=identity_of(kind, partial, *after),
            has_side_effects=True,
            vmem_limit_bytes=24 * 2**20,
        ),
        cost_estimate=BRIEF,
        name="plane_scatter",
    )(partial, *after)


def plane_scatter_frames(partial, after=()):
    rows, width = partial.shape[0], partial.shape[1] // 8
    place = member_lanes(width)
    return plane_scatter_call(partial, (rows, width), place, jnp.float32, "scatter lanes", after)


def plane_scatter_rows(partial, after=()):
    rows, width = partial.shape[0] // 8, partial.shape[1]
    place = member_rows(rows)
    return plane_scatter_call(partial, (rows, width), place, jnp.bfloat16, "scatter rows", after)


def project_kernel(kind, column, order_ref, s_ref, w_ref, base_ref, gain_ref, *refs):
    if kind == "sum":
        side_ref, full_ref, x_ref, n_ref, i_ref, h_ref, side_out, *refs = refs
    else:
        full_ref, x_ref, n_ref, i_ref, h_ref, *refs = refs
    full, total, part, landed, shard, by_block, base, gain, residual, normed, *refs = refs
    heads, slots, weight, *bufs, local_sem, send_sem, recv_sem = refs
    rows, length = s_ref.shape
    width = base_ref.shape[1]
    fetches = [
        pltpu.make_async_copy(ref, held, local_sem.at[8 + k])
        for k, (ref, held) in enumerate(
            [(s_ref, heads), (w_ref.at[:, :, : slots.shape[2]], slots)]
            + [(base_ref, base), (gain_ref, gain)]
        )
    ]
    for fetch in fetches:
        fetch.start()
    greet([member_at(peer) for peer in plane_peers()])
    side = mover(send_sem, recv_sem, 35)
    if kind == "sum":
        cores, chips, relays, finish = scatter_steps(
            member_rows(side_out.shape[0]), bufs[-1], bufs[:-2], side
        )
        text_weight = bufs[-2]
        fetches[1].wait()
        reorder_blocks(slots, text_weight, lambda b: order_ref[1, b], 3 * rows)
        tokens = side_ref.shape[1]

        @pl.loop(0, text_weight.shape[0] // 256)
        def _(i):
            at = pl.ds(pl.multiple_of(i * 256, 256), 256)
            for k in range(2):
                half = slice(k * side_ref.shape[0], (k + 1) * side_ref.shape[0])
                bufs[-1][at, k * tokens : (k + 1) * tokens] = jnp.dot(
                    text_weight[at, half], side_ref[...], preferred_element_type=jnp.float32
                ).astype(jnp.bfloat16)

        cores()
    else:
        fetches[1].wait()
    reorder_blocks(slots, weight, lambda b: order_ref[1, b], column)
    fetches[0].wait()
    total[...] = jnp.zeros_like(total)

    def add(member):
        of = pl.ds(pl.multiple_of(member * rows, 16), rows)

        @pl.loop(0, length // 256)
        def _(i):
            at = pl.ds(pl.multiple_of(i * 256, 256), 256)
            total[:, at] += contract_rows(weight[of, :], full[of, at])

    gathered = gather_steps(
        member_rows(rows), heads, full, local_sem.at[0], mover(send_sem, recv_sem), add
    )
    if kind == "sum":
        chips()
    gathered()
    kept = pltpu.make_async_copy(full, full_ref, local_sem.at[0])
    kept.start()
    part[...] = total[...].astype(part.dtype)
    exchanged = exchange_steps(
        whole_lanes(rows, width),
        whole_rows(rows),
        part,
        landed,
        local_sem.at[3],
        mover(send_sem, recv_sem, 14),
    )
    if kind == "sum":
        relays()
    exchanged()
    fetches[2].wait()
    fetches[3].wait()
    residual[...] = base[...] + wide(landed)
    standard, inverse_std = norm_columns(residual[...])
    normed[...] = standard
    i_ref[...] = inverse_std
    by_block[...] = (standard * gain[...]).astype(shard.dtype).reshape(by_block.shape)
    reorder_blocks(by_block, shard, lambda b: order_ref[0, b])
    gathered = gather_steps(
        member_lanes(width), shard, h_ref, local_sem.at[4], mover(send_sem, recv_sem, 21)
    )
    x_copy = pltpu.make_async_copy(residual, x_ref, local_sem.at[5])
    x_copy.start()
    n_copy = pltpu.make_async_copy(normed, n_ref, local_sem.at[6])
    n_copy.start()
    if kind == "sum":
        side_out[...] = finish().astype(side_out.dtype)
    gathered()
    kept.wait()
    x_copy.wait()
    n_copy.wait()


def project(kind, column, orders, heads, weight, base, gain, *side):
    rows, length = heads.shape
    features, width = base.shape
    whole = jax.ShapeDtypeStruct((features, length), jnp.bfloat16)
    frames = jax.ShapeDtypeStruct(base.shape, jnp.float32)
    side_outs, bufs = (), []
    if kind == "sum":
        tokens = side[0].shape[1]
        side_outs = (jax.ShapeDtypeStruct((rows, 2 * tokens), jnp.bfloat16),)
        bufs = scatter_bufs(rows, 2 * tokens) + [
            pltpu.VMEM((features, rows), jnp.bfloat16),
            pltpu.VMEM((features, 2 * tokens), jnp.bfloat16),
        ]
    low, high = pltpu.VMEM(base.shape, jnp.bfloat16), pltpu.VMEM(base.shape, jnp.float32)
    return kernel_call(
        functools.partial(project_kernel, kind, column),
        out_shape=(whole, frames, frames, jax.ShapeDtypeStruct((1, width), jnp.float32), whole)
        + side_outs,
        in_specs=[IN_SMEM] + [IN_HBM] * 4 + [IN_VMEM] * len(side),
        out_specs=(IN_HBM, IN_HBM, IN_HBM, IN_VMEM, IN_HBM) + (IN_VMEM,) * len(side),
        scratch_shapes=[
            pltpu.VMEM((features, length), jnp.bfloat16),
            pltpu.VMEM((rows, length), jnp.float32),
            pltpu.VMEM((rows, length), jnp.bfloat16),
            low,
            low,
            pltpu.VMEM((orders.shape[1], features // orders.shape[1], width), jnp.bfloat16),
            high,
            pltpu.VMEM(gain.shape, jnp.float32),
            high,
            high,
            pltpu.VMEM(heads.shape, heads.dtype),
            pltpu.VMEM((orders.shape[1], features // orders.shape[1], 4 * rows), weight.dtype),
            pltpu.VMEM((features, rows), weight.dtype),
        ]
        + bufs
        + [
            pltpu.SemaphoreType.DMA((13,)),
            pltpu.SemaphoreType.DMA((49,)),
            pltpu.SemaphoreType.DMA((49,)),
        ],
        compiler_params=pltpu.CompilerParams(
            collective_id=identity_of("project " + kind, heads),
            has_side_effects=True,
            vmem_limit_bytes=32 * 2**20,
        ),
        cost_estimate=BRIEF,
        name="project_" + kind,
    )(orders, heads, weight.reshape(orders.shape[1], -1, weight.shape[1]), base, gain, *side)


def back_kernel(plan, *refs):
    by_rows, send_rows, text, in_slots, column, beside, after = plan
    refs = list(refs)

    def take(count):
        taken = refs[:count]
        del refs[:count]
        return taken

    order_ref = take(1)[0]
    sources = take(3 if by_rows else 7)
    text_ref = take(1)[0] if text else None
    beside_refs = take(4 if beside else 0)
    take(after)
    o_ref, own_out = take(2)
    sum_ref = None if by_rows else take(1)[0]
    rows_ref = take(1)[0] if send_rows else None
    text_out = take(1)[0] if text else None
    held = take(len(sources))
    w_ref, g_ref, act, *norms = held
    results = take(0 if by_rows else 2)
    mine, theirs, pair, from_x, from_y, relay, shard, slots, own_ref = take(9)
    besides = take(4 if beside else 0)
    by_head = take(1 if by_rows else 0)
    local_sem, send_sem, recv_sem = refs
    if by_rows:
        w_slots, w_ref = w_ref, by_head[0]
    source = sources[0]
    if by_rows:
        sources[0] = source.at[:, :, : w_slots.shape[2]]
    elif w_ref.shape[1] < source.shape[1]:
        sources[0] = source.at[:, : w_ref.shape[1]]
    fetches = [
        pltpu.make_async_copy(ref, here, local_sem.at[4 + k])
        for k, (ref, here) in enumerate(zip(sources + beside_refs, held + besides))
    ]
    for fetch in fetches:
        fetch.start()

    group, core, across, along = near()
    beyond = across + along - group
    sibling, by_x, by_y = {"core": 1 - core}, {"dp": across}, {"dp": along}
    rows, width = mine.shape[1:]
    columns = slice(0, g_ref.shape[0]) if by_rows else slice(column, column + g_ref.shape[0])
    half = rows // 2
    low, high = pl.ds(0, half), pl.ds(half, half)
    copy = mover(send_sem, recv_sem)
    sent = []

    def send(k, source, target, peer):
        moving = copy(k, source, target, peer)
        moving.start()
        sent.append(moving)

    def arrived(k, target):
        copy(k, target, target, sibling).wait_recv()

    def split(k, at_rows, at_lanes, first, second):
        mine[k, at_rows, at_lanes] = jnp.where(core == 0, first, second).astype(mine.dtype)
        theirs[k, at_rows, at_lanes] = jnp.where(core == 0, second, first).astype(mine.dtype)

    def work_out(k, owner):
        if by_rows:

            @pl.loop(0, width // 256)
            def _(i):
                at = pl.ds(pl.multiple_of(i * 256, 256), 256)
                both = jnp.dot(
                    w_ref[pl.ds(pl.multiple_of(owner * 2 * rows, 16), 2 * rows), columns],
                    g_ref[:, at],
                    preferred_element_type=jnp.float32,
                )
                split(k, slice(None), at, both[:rows], both[rows:])

        else:

            @pl.loop(0, rows // 256)
            def _(i):
                at = pl.ds(pl.multiple_of(i * 256, 256), 256)
                both = jnp.dot(
                    w_ref[at, columns],
                    g_ref[:, pl.ds(pl.multiple_of(owner * 2 * width, 256), 2 * width)],
                    preferred_element_type=jnp.float32,
                )
                split(k, at, slice(None), both[:, :width], both[:, width:])

        send(k, theirs.at[k], pair.at[k], sibling)

    def both_cores(k):
        arrived(k, pair.at[k])
        mine[k] = (wide(mine.at[k]) + wide(pair.at[k])).astype(mine.dtype)

    def weight_grads(first, last):
        rows_of = act if in_slots else slots
        tile, count = rows_of.shape[0] // 6, g_ref.shape[0]

        @pl.loop(first, last)
        def _(i):
            at = pl.ds(pl.multiple_of(i * tile, tile), tile)
            for j in range(0, count, 256):
                of = slice(j, min(j + 256, count))
                own_ref[at, of] = contract_last(rows_of[at, :], g_ref[of, :]).astype(
                    own_ref.dtype
                )

    if send_rows or text:
        greet([member_at(peer) for peer in plane_peers()])
    else:
        greet([by_x, by_y, sibling])
    fetches[0].wait()
    if by_rows:
        reorder_blocks(w_slots, w_ref, lambda b: order_ref[1, b], column)
    fetches[1].wait()
    for k, owner in enumerate((beyond, across, along, group)):
        work_out(k, owner)
        if k == 1:
            both_cores(0)
            send(4, mine.at[0, low], relay.at[0], by_x)
            send(5, mine.at[0, high], relay.at[1], by_y)
        if k == 2:
            both_cores(1)
            send(6, mine.at[1, low], from_x.at[low], by_x)
        if k == 3:
            both_cores(2)
            send(7, mine.at[2, high], from_y.at[high], by_y)
    if text:
        text_done = gather_steps(
            member_rows(text_ref.shape[0]),
            text_ref,
            text_out,
            local_sem.at[1],
            mover(send_sem, recv_sem, 17),
        )
    def put_beside():
        cq, co, text_grad, text_mine = besides
        count, rows = g_ref.shape[0], text_grad.shape[1]
        part = text_mine.shape[0]
        tokens = text_mine.shape[1]

        @pl.loop(0, text_grad.shape[0])
        def _(b):
            at = pl.ds(pl.multiple_of(b * rows, 16), rows)
            own_ref[at, count : 2 * count] = cq[at, :]
            own_ref[at, 2 * count : 3 * count] = co[at, :]
            slots[at, : 2 * tokens] = text_grad[order_ref[0, b]]

        @pl.loop(0, 6)
        def _(i):
            at = pl.ds(pl.multiple_of(i * 256, 256), 256)
            for k in range(2):
                grads = contract_last(
                    slots[at, k * tokens : (k + 1) * tokens], text_mine[...]
                )
                start = 3 * count + k * part
                own_ref[at, start : start + part] = grads.astype(own_ref.dtype)

    fetches[2].wait()
    if not in_slots:
        reorder_blocks(act, slots, lambda b: order_ref[0, b])
    weight_grads(0, 2)
    arrived(5, relay.at[1])
    mine[1, high] = (wide(mine.at[1, high]) + wide(relay.at[1])).astype(mine.dtype)
    send(8, mine.at[1, high], from_x.at[high], by_x)
    arrived(4, relay.at[0])
    mine[2, low] = (wide(mine.at[2, low]) + wide(relay.at[0])).astype(mine.dtype)
    send(9, mine.at[2, low], from_y.at[low], by_y)
    both_cores(3)
    weight_grads(2, 6)
    if beside:
        for fetch in fetches[len(sources) :]:
            fetch.wait()
        put_beside()
    if text:
        text_done()
    own_copy = pltpu.make_async_copy(own_ref, own_out, local_sem.at[2])
    own_copy.start()
    arrived(6, from_x.at[low])
    arrived(7, from_y.at[high])
    arrived(8, from_x.at[high])
    arrived(9, from_y.at[low])
    summed = wide(mine.at[3]) + wide(from_x) + wide(from_y)
    if by_rows:
        shard[...] = summed.astype(shard.dtype)
        result_copy = pltpu.make_async_copy(shard, o_ref, local_sem.at[3])
        result_copy.start()
    else:
        for fetch in fetches[3 : len(sources)]:
            fetch.wait()
        normed, inverse_std, gain, base = norms
        result, by_block = results
        if in_slots:
            by_block[...] = summed.reshape(by_block.shape)
            reorder_blocks(by_block, result, lambda b: order_ref[1, b])
            summed = result[...]
        result[...] = base[...] + norm_columns_back(
            summed * gain[...], normed[...], inverse_std[...]
        )
        result_copy = pltpu.make_async_copy(result, o_ref, local_sem.at[3])
        result_copy.start()
        if send_rows:
            shard[...] = result[...].astype(shard.dtype)
            rows_done = exchange_steps(
                whole_rows(rows // 8),
                whole_lanes(rows // 8, width),
                shard,
                rows_ref,
                local_sem.at[0],
                mover(send_sem, recv_sem, 10),
            )
        sum_ref[...] = lax.dot_general(
            jnp.ones((8, width), jnp.float32),
            summed * normed[...],
            (((1,), (1,)), ((), ())),
            precision=HIGHEST,
            preferred_element_type=jnp.float32,
        )
        if send_rows:
            rows_done()
    result_copy.wait()
    own_copy.wait()
    for moving in sent:
        moving.wait_send()


def back(
    orders,
    weight,
    grad,
    act,
    norm=None,
    column=0,
    send_rows=False,
    text=None,
    in_slots=False,
    beside=(),
    after=(),
):
    by_rows = norm is None
    features, length = weight.shape[0], grad.shape[1]
    shape = (features // 8, length) if by_rows else (features, length // 8)
    small = jnp.bfloat16
    own_width = grad.shape[0] * (4 if beside else 1)
    own = jax.ShapeDtypeStruct((features, own_width), small)
    outs = [jax.ShapeDtypeStruct(shape, small if by_rows else jnp.float32), own]
    specs = [IN_HBM, IN_HBM]
    if not by_rows:
        outs.append(jax.ShapeDtypeStruct((8, features), jnp.float32))
        specs.append(IN_VMEM)
    if send_rows:
        outs.append(jax.ShapeDtypeStruct((features // 8, length), small))
        specs.append(IN_HBM)
    count = orders.shape[1]
    if not in_slots:
        act = act.reshape(count, features // count, length)
    few = weight.shape[1] if column + grad.shape[0] > 4 * (features // 8) else 4 * (features // 8)
    if by_rows:
        weight = weight.reshape(count, features // count, weight.shape[1])
        held = jax.ShapeDtypeStruct((count, features // count, few), small)
    else:
        held = jax.ShapeDtypeStruct((features, few), small)
    sources = [weight, grad, act] + list(norm or ())
    operands = [orders] + sources
    if text is not None:
        operands.append(text)
        outs.append(jax.ShapeDtypeStruct((8 * text.shape[0], text.shape[1]), text.dtype))
        specs.append(IN_HBM)
    if beside:
        cq, co, text_grad, text_mine = beside
        beside = (cq, co, text_grad.reshape(count, features // count, -1), text_mine)
        operands += list(beside)
    operands += list(after)
    plan = (by_rows, send_rows, text is not None, in_slots, column, bool(beside), len(after))
    rows, width = shape
    four, slot = pltpu.VMEM((4, rows, width), small), pltpu.VMEM((rows, width), small)
    return kernel_call(
        functools.partial(back_kernel, plan),
        out_shape=tuple(outs),
        in_specs=[IN_SMEM] + [IN_HBM] * (len(operands) - 1),
        out_specs=tuple(specs),
        scratch_shapes=[pltpu.VMEM(array.shape, array.dtype) for array in [held] + sources[1:]]
        + (
            []
            if by_rows
            else [
                pltpu.VMEM(shape, jnp.float32),
                pltpu.VMEM((count, rows // count, width), jnp.float32),
            ]
        )
        + [four, four, four, slot, slot, pltpu.VMEM((2, rows // 2, width), small), slot]
        + [
            pltpu.VMEM((16, 128) if in_slots else (features, length), small),
            pltpu.VMEM(own.shape, small),
        ]
        + [pltpu.VMEM(array.shape, array.dtype) for array in beside]
        + ([pltpu.VMEM((features, grad.shape[0]), small)] if by_rows else [])
        + [
            pltpu.SemaphoreType.DMA((11,)),
            pltpu.SemaphoreType.DMA((31,)),
            pltpu.SemaphoreType.DMA((31,)),
        ],
        compiler_params=pltpu.CompilerParams(
            collective_id=identity_of("back" + str(plan), *operands),
            has_side_effects=True,
            vmem_limit_bytes=44 * 2**20,
        ),
        cost_estimate=BRIEF,
        name="back",
    )(*operands)


def exchange_kernel(source, target, x_ref, *refs):
    o_ref, local_sem, send_sem, recv_sem = refs[-4:]
    greet([member_at(peer) for peer in plane_peers()])
    exchange_steps(source, target, x_ref, o_ref, local_sem, mover(send_sem, recv_sem))()


def exchange(array, shape, source, target, kind, after=()):
    return kernel_call(
        functools.partial(exchange_kernel, source, target),
        out_shape=jax.ShapeDtypeStruct(shape, array.dtype),
        in_specs=[IN_HBM] * (1 + len(after)),
        out_specs=IN_HBM,
        scratch_shapes=[
            pltpu.SemaphoreType.DMA,
            pltpu.SemaphoreType.DMA((7,)),
            pltpu.SemaphoreType.DMA((7,)),
        ],
        compiler_params=pltpu.CompilerParams(
            collective_id=identity_of(kind, array, *after), has_side_effects=True
        ),
        cost_estimate=BRIEF,
        name="plane_exchange",
    )(array, *after)


def whole_rows(rows):
    place = member_rows(rows)
    return lambda ref, member: place(ref, member, 0, rows)


def whole_lanes(rows, width):
    place = member_lanes(width)
    return lambda ref, member: place(ref, member, 0, rows)


def to_frames(part):
    rows, width = part.shape[0], part.shape[1] // 8
    return exchange(part, (8 * rows, width), whole_lanes(rows, width), whole_rows(rows), "to frames")


def to_rows(part):
    rows, width = part.shape[0] // 8, part.shape[1]
    return exchange(part, (rows, 8 * width), whole_rows(rows), whole_lanes(rows, width), "to rows")


def block(ref, member):
    return ref.at[member]


def exchange_blocks(blocks, after=()):
    return exchange(blocks, blocks.shape, block, block, "blocks", after)


def lanes(ref, start, width):
    return ref.at[:, pl.ds(pl.multiple_of(start, 128), width)]


def sheet_part(start, width):
    return lambda ref, member: lanes(ref, start + member * width, width)


def block_part(start, width):
    return lambda ref, member: lanes(ref.at[member], start, width)


def feed_kernel(gu_ref, down_ref, w_ref, h_ref, *refs):
    o_ref, y_ref, weight, hidden, part, summed, *bufs, local_sem, send_sem, recv_sem = refs[-14:]
    width = down_ref.shape[-1]
    fetches = [
        pltpu.make_async_copy(w_ref, weight, local_sem.at[3]),
        pltpu.make_async_copy(h_ref, hidden, local_sem.at[5]),
    ]
    for fetch in fetches:
        fetch.start()
    greet([member_at(peer) for peer in plane_peers()])
    finish = []
    for k, (ref, start) in enumerate(((gu_ref, 0), (gu_ref, width), (down_ref, 0))):
        source, target = block_part(start, width), sheet_part(8 * k * width, width)
        copy = mover(send_sem, recv_sem, 7 * k)
        finish.append(exchange_steps(source, target, ref, o_ref, local_sem.at[k], copy))
    for fetch in fetches:
        fetch.wait()

    @pl.loop(0, part.shape[0] // 256)
    def _(i):
        at = pl.ds(pl.multiple_of(i * 256, 256), 256)
        for j in range(0, part.shape[1], 256):
            product = jnp.dot(
                weight[at, :], hidden[:, j : j + 256], preferred_element_type=jnp.float32
            )
            part[at, j : j + 256] = product.astype(part.dtype)

    cores, chips, relays, ended = scatter_steps(
        member_lanes(y_ref.shape[1]), part, bufs, mover(send_sem, recv_sem, 21)
    )
    cores()
    chips()
    relays()
    summed[...] = ended()
    kept = pltpu.make_async_copy(summed, y_ref, local_sem.at[4])
    kept.start()
    for end in finish:
        end()
    kept.wait()


def feed(gu, down, weight, hidden, after=()):
    rows, length = weight.shape[0], hidden.shape[1]
    width = length // 8
    return kernel_call(
        feed_kernel,
        out_shape=(
            jax.ShapeDtypeStruct((gu.shape[1], 24 * down.shape[-1]), gu.dtype),
            jax.ShapeDtypeStruct((rows, width), jnp.float32),
        ),
        in_specs=[IN_HBM] * (4 + len(after)),
        out_specs=(IN_HBM, IN_HBM),
        scratch_shapes=[
            pltpu.VMEM(weight.shape, weight.dtype),
            pltpu.VMEM(hidden.shape, hidden.dtype),
            pltpu.VMEM((rows, length), jnp.bfloat16),
            pltpu.VMEM((rows, width), jnp.float32),
        ]
        + scatter_bufs(rows, width)
        + [
            pltpu.SemaphoreType.DMA((6,)),
            pltpu.SemaphoreType.DMA((31,)),
            pltpu.SemaphoreType.DMA((31,)),
        ],
        compiler_params=pltpu.CompilerParams(
            collective_id=identity_of("feed", gu, down, weight, *after),
            has_side_effects=True,
            vmem_limit_bytes=28 * 2**20,
        ),
        cost_estimate=BRIEF,
        name="feed",
    )(gu, down, weight, hidden, *after)


def opening_kernel(
    latents_ref,
    cotangent_ref,
    small_ref,
    text_ref,
    sheet_ref,
    t_ref,
    all_ref,
    mine_ref,
    one_ref,
    x_ref,
    held,
    columns,
    one,
    local_sem,
    send_sem,
    recv_sem,
):
    features = latents_ref.shape[1]
    part, text = D // 8, CTXW // 8
    tail = 6 * D + 3 * FF
    fetches = [
        pltpu.make_async_copy(latents_ref, x_ref.at[:, :features], local_sem.at[5]),
        pltpu.make_async_copy(cotangent_ref, x_ref.at[:, features:], local_sem.at[6]),
        pltpu.make_async_copy(
            sheet_ref.at[:, : 6 * D], columns.at[:, : 6 * D], local_sem.at[7]
        ),
        pltpu.make_async_copy(
            sheet_ref.at[:, tail : tail + 2 * CTXW], columns.at[:, 6 * D :], local_sem.at[8]
        ),
    ]
    for fetch in fetches:
        fetch.start()
    group, core, across, along = near()
    member = group * 2 + core
    plane = lax.axis_index("z")
    step = x_ref.shape[0] // 4
    text_rows = mine_ref.shape[0]
    teacher = jnp.logical_and(group == plane, core == 0)

    def frames(ref, j):
        return ref.at[pl.ds(pl.multiple_of(j * step, 16), step), :]

    peers = plane_peers()
    line = [lax.rem(plane + k, 4) for k in range(1, 4)]
    greet([member_at(peer) for peer in peers] + [{"z": there} for there in line])

    fetches[0].wait()
    fetches[1].wait()

    near_copy = mover(send_sem, recv_sem)
    line_copy = mover(send_sem, recv_sem, 7)
    small_local = pltpu.make_async_copy(small_ref, all_ref.at[plane, member], local_sem.at[0])
    small_local.start()
    first = [
        near_copy(k, small_ref, all_ref.at[plane, member], member_at(peer))
        for k, peer in enumerate(peers)
    ]
    for moving in first:
        moving.start()

    others = [across, along, across + along - group]
    keep = pltpu.make_async_copy(frames(x_ref, group), frames(held, group), local_sem.at[1])
    keep.start()

    def piece(ref, j, a):
        at = pl.ds(pl.multiple_of(j * step, 16), step)
        return ref.at[at, a * features : (a + 1) * features]

    def spread(owner, landing, a):
        return pltpu.make_async_remote_copy(
            src_ref=piece(x_ref, owner, a),
            dst_ref=piece(held, landing, a),
            send_sem=send_sem.at[(10, 36)[a] + owner],
            recv_sem=recv_sem.at[(10, 36)[a] + landing],
            device_id={"dp": owner},
            device_id_type=MESH_ID,
        )

    for a in range(2):
        for owner in others:
            spread(owner, group, a).start()

    def rise(row, a):
        return pltpu.make_async_remote_copy(
            src_ref=piece(held, row, a),
            dst_ref=piece(t_ref, plane, a),
            send_sem=send_sem.at[(28, 32)[a] + row],
            recv_sem=recv_sem.at[(28, 32)[a] + plane],
            device_id={"z": row},
            device_id_type=MESH_ID,
        )

    stay = [
        pltpu.make_async_copy(piece(held, plane, a), piece(t_ref, plane, a), local_sem.at[(4, 9)[a]])
        for a in range(2)
    ]

    def pass_on(row, a):
        pl.when(row == plane)(stay[a].start)
        pl.when(row != plane)(rise(row, a).start)

    keep.wait()
    for a in range(2):
        pass_on(group, a)

    fetches[2].wait()
    fetches[3].wait()

    def move(m, at, start, width):
        one[m, :, at : at + width] = columns[:, start : start + width].astype(one.dtype)

    for m in range(8):
        for k in range(6):
            move(m, (4 * part if k < 3 else -3 * part) + k * part, k * D + m * part, part)
        for k in range(2):
            move(m, 3 * part + k * text, 6 * D + k * CTXW + m * text, text)
    for owner in others:
        spread(owner, owner, 0).wait_recv()
        pass_on(owner, 0)
    weights_done = exchange_steps(
        block, block, one, one_ref, local_sem.at[2], mover(send_sem, recv_sem, 14)
    )

    def text_copy(k, peer):
        return pltpu.make_async_remote_copy(
            src_ref=text_ref.at[pl.ds(pl.multiple_of(peer * text_rows, 16), text_rows), :],
            dst_ref=mine_ref,
            send_sem=send_sem.at[21 + k],
            recv_sem=recv_sem.at[21],
            device_id=member_at(peer),
            device_id_type=MESH_ID,
        )

    own_text = text_ref.at[pl.ds(pl.multiple_of(member * text_rows, 16), text_rows), :]
    text_local = pltpu.make_async_copy(own_text, mine_ref, local_sem.at[3])

    @pl.when(teacher)
    def _():
        text_local.start()
        for k, peer in enumerate(peers):
            text_copy(k, peer).start()

    for owner in others:
        spread(owner, owner, 1).wait_recv()
        pass_on(owner, 1)

    for k in range(7):
        landed = all_ref.at[plane, lax.rem(member + 7 - k, 8)]
        near_copy(k, landed, landed, member_at(peers[k])).wait_recv()
    small_local.wait()
    second = [
        line_copy(k, all_ref.at[plane], all_ref.at[plane], {"z": there})
        for k, there in enumerate(line)
    ]
    for moving in second:
        moving.start()
    for k in range(3):
        landed = all_ref.at[lax.rem(plane + 3 - k, 4)]
        line_copy(k, landed, landed, {"z": line[k]}).wait_recv()

    for a in range(2):
        for there in line:
            landed = piece(t_ref, there, a)
            pltpu.make_async_remote_copy(
                src_ref=landed,
                dst_ref=landed,
                send_sem=send_sem.at[(28, 32)[a] + there],
                recv_sem=recv_sem.at[(28, 32)[a] + there],
                device_id={"z": there},
                device_id_type=MESH_ID,
            ).wait_recv()
        stay[a].wait()
    weights_done()

    @pl.when(teacher)
    def _():
        text_local.wait()
        for k, peer in enumerate(peers):
            text_copy(k, peer).wait_send()

    @pl.when(jnp.logical_not(teacher))
    def _():
        text_copy(0, peers[0]).wait_recv()

    for moving in first + second:
        moving.wait_send()
    for a in range(2):
        for owner in others:
            spread(owner, group, a).wait_send()
        for there in line:
            rise(there, a).wait_send()


def opening(latents, cotangent, small, text, sheet):
    frames, features = latents.shape
    local = (frames, 2 * features)
    one = (8, sheet.shape[0], (6 * D + 2 * CTXW) // 8)
    low = jnp.bfloat16
    return kernel_call(
        opening_kernel,
        out_shape=(
            jax.ShapeDtypeStruct(local, low),
            jax.ShapeDtypeStruct((4, 8) + small.shape, small.dtype),
            jax.ShapeDtypeStruct((text.shape[0] // 8, text.shape[1]), text.dtype),
            jax.ShapeDtypeStruct(one, low),
        ),
        in_specs=[IN_HBM] * 5,
        out_specs=(IN_HBM,) * 4,
        scratch_shapes=[
            pltpu.VMEM(local, low),
            pltpu.VMEM(local, low),
            pltpu.VMEM((sheet.shape[0], 6 * D + 2 * CTXW), jnp.float32),
            pltpu.VMEM(one, low),
            pltpu.SemaphoreType.DMA((10,)),
            pltpu.SemaphoreType.DMA((40,)),
            pltpu.SemaphoreType.DMA((40,)),
        ],
        compiler_params=pltpu.CompilerParams(
            collective_id=identity_of("opening", sheet),
            has_side_effects=True,
            vmem_limit_bytes=16 * 2**20,
        ),
        cost_estimate=BRIEF,
        name="opening",
    )(latents, cotangent, small, text, sheet)


def first_gather_kernel(
    x_ref, y_ref, sheet_ref, ox_ref, oy_ref, gu_ref, down_ref, local_sem, send_sem, recv_sem
):
    place = member_lanes(x_ref.shape[1])
    width = FF // 8
    greet([member_at(peer) for peer in plane_peers()])
    finish = [
        gather_steps(place, x_ref, ox_ref, local_sem.at[0], mover(send_sem, recv_sem)),
        gather_steps(place, y_ref, oy_ref, local_sem.at[1], mover(send_sem, recv_sem, 14)),
    ]
    for k, (ref, start) in enumerate(((gu_ref, 0), (gu_ref, width), (down_ref, 0))):
        source, target = sheet_part(6 * D + k * FF, width), block_part(start, width)
        copy = mover(send_sem, recv_sem, 28 + 7 * k)
        finish.append(exchange_steps(source, target, sheet_ref, ref, local_sem.at[2 + k], copy))
    for end in finish:
        end()


def first_gather(shard, other, sheet):
    rows, width = shard.shape
    whole = jax.ShapeDtypeStruct((rows, 8 * width), shard.dtype)
    return kernel_call(
        first_gather_kernel,
        out_shape=(
            whole,
            whole,
            jax.ShapeDtypeStruct((8, sheet.shape[0], FF // 4), sheet.dtype),
            jax.ShapeDtypeStruct((8, sheet.shape[0], FF // 8), sheet.dtype),
        ),
        in_specs=[IN_HBM] * 3,
        out_specs=(IN_HBM,) * 4,
        scratch_shapes=[
            pltpu.SemaphoreType.DMA((5,)),
            pltpu.SemaphoreType.DMA((49,)),
            pltpu.SemaphoreType.DMA((49,)),
        ],
        compiler_params=pltpu.CompilerParams(
            collective_id=identity_of("first gather", shard, sheet), has_side_effects=True
        ),
        cost_estimate=BRIEF,
        name="first_gather",
    )(shard, other, sheet)


def prepare_kernel(order_ref, y_ref, base_ref, grad_ref, gu_ref, down_ref, two_ref, x_ref, q_ref, y):
    features = base_ref.shape[0]
    reorder_blocks(y_ref, y, lambda b: order_ref[1, b])
    x_ref[:, :features] = (base_ref[...] + y[...]).T.astype(x_ref.dtype)
    x_ref[:, features:] = grad_ref[...].T.astype(x_ref.dtype)
    q_ref[...] = jnp.full(q_ref.shape, square_sum((gu_ref, down_ref, two_ref)), jnp.float32)


def prepare(orders, y, base, grad, gu, down, two):
    features, width = base.shape
    return kernel_call(
        prepare_kernel,
        out_shape=(
            jax.ShapeDtypeStruct((width, 2 * features), jnp.bfloat16),
            jax.ShapeDtypeStruct((8, 128), jnp.float32),
        ),
        in_specs=[IN_SMEM] + [IN_VMEM] * 6,
        out_specs=(IN_VMEM,) * 2,
        scratch_shapes=[pltpu.VMEM(base.shape, jnp.float32)],
        compiler_params=pltpu.CompilerParams(vmem_limit_bytes=16 * 2**20),
        name="prepare",
    )(orders, y.reshape(orders.shape[1], -1, width), base, grad, gu, down, two)


def square_sum(refs):
    total = jnp.zeros((), jnp.float32)
    for ref in refs:
        line_sum = jnp.zeros((1, ref.shape[2]), jnp.float32)
        for m in range(8):
            line_sum += jnp.sum(jnp.square(wide(ref.at[m])), axis=0, keepdims=True)
        total += jnp.sum(line_sum)
    return total


def closing_kernel(
    x_ref,
    p_ref,
    w_ref,
    g_ref,
    _,
    t_ref,
    o_ref,
    s_ref,
    all_ref,
    held,
    tall,
    q_ref,
    one,
    local_sem,
    send_sem,
    recv_sem,
):
    fetch = pltpu.make_async_copy(w_ref, one, local_sem.at[0])
    fetch.start()
    group, core, across, along = near()
    member = group * 2 + core
    plane = lax.axis_index("z")
    step, features = x_ref.shape[0] // 4, x_ref.shape[1] // 2
    groups = [across, along, across + along - group]
    inner = lax.div(plane * (3 - plane), 2)
    two_off, mirrored = lax.rem(plane + 2, 4), 3 - plane
    line = [
        plane + 1 - 2 * lax.rem(plane, 2),
        inner * mirrored + (1 - inner) * two_off,
        inner * two_off + (1 - inner) * mirrored,
    ]
    peers = plane_peers()
    greet([member_at(peer) for peer in peers] + [{"z": there} for there in line])

    def piece(ref, j, a):
        at = pl.ds(pl.multiple_of(j * step, 16), step)
        return ref.at[at, a * features : (a + 1) * features]

    def cross_line(there, a):
        return pltpu.make_async_remote_copy(
            src_ref=piece(x_ref, there, a),
            dst_ref=piece(held, plane, a),
            send_sem=send_sem.at[4 * a + there],
            recv_sem=recv_sem.at[4 * a + plane],
            device_id={"z": there},
            device_id_type=MESH_ID,
        )

    def onward(owner, a):
        return pltpu.make_async_remote_copy(
            src_ref=piece(held, owner, a),
            dst_ref=piece(t_ref, group, a),
            send_sem=send_sem.at[8 + 4 * a + owner],
            recv_sem=recv_sem.at[8 + 4 * a + group],
            device_id={"dp": owner},
            device_id_type=MESH_ID,
        )

    def landed(ref, j, a, sem, peer):
        at = piece(ref, j, a)
        pltpu.make_async_remote_copy(
            src_ref=at,
            dst_ref=at,
            send_sem=send_sem.at[sem],
            recv_sem=recv_sem.at[sem],
            device_id=peer,
            device_id_type=MESH_ID,
        ).wait_recv()

    keep = [
        pltpu.make_async_copy(piece(held, group, a), piece(t_ref, group, a), local_sem.at[1 + a])
        for a in range(2)
    ]

    def pass_on(owner, a):
        pl.when(owner == group)(keep[a].start)
        pl.when(owner != group)(onward(owner, a).start)

    gain_line = mover(send_sem, recv_sem, 23)
    gain_plane = mover(send_sem, recv_sem, 26)
    square_plane = mover(send_sem, recv_sem, 33)
    square_line = mover(send_sem, recv_sem, 40)
    turned_line = [lax.rem(plane + k, 4) for k in range(1, 4)]
    back_line = [lax.rem(plane + 3 - k, 4) for k in range(3)]
    gain_local = pltpu.make_async_copy(g_ref, tall.at[plane], local_sem.at[3])
    gain_local.start()
    sent = [
        gain_line(k, g_ref, tall.at[plane], {"z": there}) for k, there in enumerate(turned_line)
    ]
    for moving in sent:
        moving.start()
    local = pltpu.make_async_copy(
        x_ref.at[pl.ds(pl.multiple_of(plane * step, 16), step), :],
        held.at[pl.ds(pl.multiple_of(plane * step, 16), step), :],
        local_sem.at[4],
    )
    local.start()
    for a in range(2):
        for there in line:
            cross_line(there, a).start()
    fetch.wait()
    weights_done = exchange_steps(
        block, block, one, o_ref, local_sem.at[5], mover(send_sem, recv_sem, 16)
    )
    q_ref[...] = p_ref[...] + square_sum((one,))
    square_local = pltpu.make_async_copy(q_ref, all_ref.at[plane, member], local_sem.at[6])
    square_local.start()
    shown = [
        square_plane(k, q_ref, all_ref.at[plane, member], member_at(peer))
        for k, peer in enumerate(peers)
    ]
    for moving in shown:
        moving.start()
    local.wait()
    for a in range(2):
        pass_on(plane, a)
    gain_local.wait()
    for k, origin in enumerate(back_line):
        gain_line(k, tall.at[origin], tall.at[origin], {"z": origin}).wait_recv()
    tall[4] = tall[0] + tall[1] + tall[2] + tall[3]
    gain_keep = pltpu.make_async_copy(tall.at[4], s_ref.at[member], local_sem.at[7])
    gain_keep.start()
    given = [
        gain_plane(k, tall.at[4], s_ref.at[member], member_at(peer)) for k, peer in enumerate(peers)
    ]
    for moving in given:
        moving.start()
    square_local.wait()
    for k in range(7):
        shown_here = all_ref.at[plane, lax.rem(member + 7 - k, 8)]
        square_plane(k, shown_here, shown_here, member_at(peers[k])).wait_recv()
    for k, there in enumerate(turned_line):
        shown.append(square_line(k, all_ref.at[plane], all_ref.at[plane], {"z": there}))
        shown[-1].start()
    for a in range(2):
        for origin in line:
            landed(held, origin, a, 4 * a + origin, {"z": origin})
            pass_on(origin, a)
    for a in range(2):
        for origin in groups:
            landed(t_ref, origin, a, 8 + 4 * a + origin, {"dp": origin})
        keep[a].wait()
    weights_done()
    gain_keep.wait()
    for k in range(7):
        given_here = s_ref.at[lax.rem(member + 7 - k, 8)]
        gain_plane(k, given_here, given_here, member_at(peers[k])).wait_recv()
    for k, origin in enumerate(back_line):
        square_line(k, all_ref.at[origin], all_ref.at[origin], {"z": origin}).wait_recv()
    for moving in sent + given + shown:
        moving.wait_send()
    for a in range(2):
        for there in line:
            cross_line(there, a).wait_send()
        for owner in groups:
            onward(owner, a).wait_send()


def closing(local, squares, one, gains, after):
    return kernel_call(
        closing_kernel,
        out_shape=(
            jax.ShapeDtypeStruct(local.shape, local.dtype),
            jax.ShapeDtypeStruct(one.shape, one.dtype),
            jax.ShapeDtypeStruct((8,) + gains.shape, gains.dtype),
            jax.ShapeDtypeStruct((4, 8) + squares.shape, jnp.float32),
        ),
        in_specs=[IN_VMEM, IN_VMEM] + [IN_HBM] * 3,
        out_specs=(IN_VMEM,) * 4,
        scratch_shapes=[
            pltpu.VMEM(local.shape, local.dtype),
            pltpu.VMEM((5,) + gains.shape, gains.dtype),
            pltpu.VMEM(squares.shape, jnp.float32),
            pltpu.VMEM(one.shape, one.dtype),
            pltpu.SemaphoreType.DMA((8,)),
            pltpu.SemaphoreType.DMA((43,)),
            pltpu.SemaphoreType.DMA((43,)),
        ],
        compiler_params=pltpu.CompilerParams(
            collective_id=identity_of("closing", one),
            has_side_effects=True,
            vmem_limit_bytes=8 * 2**20,
        ),
        cost_estimate=BRIEF,
        name="closing",
    )(local, squares, one, gains, after)


def turned(values, cosine, sine_table):
    half = HEAD // 2
    first_half, second_half = values[:half], values[half:]
    return jnp.concatenate(
        [
            first_half * cosine - second_half * sine_table,
            second_half * cosine + first_half * sine_table,
        ],
        axis=0,
    )


def attend_kernel(
    w_ref,
    h_ref,
    cos_ref,
    sin_ref,
    seg_ref,
    column_ref,
    part_out,
    p_out,
    o_ref,
    weight,
    frames,
    joint_ref,
    part_ref,
    p_ref,
    sems,
):
    heads, length = joint_ref.shape[1], joint_ref.shape[3]
    span = heads * HEAD
    tiles = length // 256
    fetches = [pltpu.make_async_copy(w_ref, weight, sems.at[0])]
    fetches += [
        pltpu.make_async_copy(
            h_ref.at[:, i * 256 : (i + 1) * 256], frames.at[:, i * 256 : (i + 1) * 256], sems.at[1 + i]
        )
        for i in range(tiles)
    ]
    for fetch in fetches:
        fetch.start()
    cosine, sine_table = cos_ref[...], sin_ref[...]
    fetches[0].wait()
    by_row = [weight[:, (4 + k) * span : (5 + k) * span].T for k in range(3)]
    for i in range(tiles):
        fetches[1 + i].wait()
        at = slice(i * 256, (i + 1) * 256)
        for k in range(3):
            part = jnp.dot(by_row[k], frames[:, at], preferred_element_type=jnp.float32)
            for h in range(heads):
                joint_ref[k, h, :, at] = part[h * HEAD : (h + 1) * HEAD]

    kept = []
    for h in range(heads):
        queries = turned(joint_ref[0, h], cosine, sine_table)
        part_ref[0, h] = queries.astype(part_ref.dtype)
        keys = turned(joint_ref[1, h], cosine, sine_table)
        part_ref[1, h] = keys.astype(part_ref.dtype)
        part_ref[2, h] = joint_ref[2, h].astype(part_ref.dtype)
        by_key = keys.T.astype(part_ref.dtype)

        @pl.loop(0, tiles)
        def _(i, h=h, by_key=by_key):
            at = pl.ds(pl.multiple_of(i * 256, 256), 256)
            scores = jnp.dot(
                by_key, part_ref[0, h, :, at], preferred_element_type=jnp.float32
            ) * (HEAD**-0.5)
            scores = jnp.where(column_ref[...] == seg_ref[:, at], scores, MASKED_SCORE)
            exponent = jnp.exp(scores - jnp.max(scores, axis=0, keepdims=True))
            probs = exponent * (1.0 / jnp.sum(exponent, axis=0, keepdims=True))
            p_ref[h, :, at] = probs.astype(p_ref.dtype)
            out = jnp.dot(part_ref[2, h], p_ref[h, :, at], preferred_element_type=jnp.float32)
            o_ref[h * HEAD : (h + 1) * HEAD, at] = out.astype(o_ref.dtype)

        kept.append(pltpu.make_async_copy(p_ref.at[h], p_out.at[h], sems.at[1 + tiles + h]))
        kept[-1].start()
    kept.append(pltpu.make_async_copy(part_ref, part_out, sems.at[1 + tiles + heads]))
    kept[-1].start()
    for keep in kept:
        keep.wait()


def attend(weight, frames, cosine, sine_table, segments):
    heads, length = D // HEAD // 8, frames.shape[1]
    joint = (3, heads, HEAD, length)
    small = jnp.bfloat16
    return kernel_call(
        attend_kernel,
        out_shape=(
            jax.ShapeDtypeStruct(joint, small),
            jax.ShapeDtypeStruct((heads, length, length), small),
            jax.ShapeDtypeStruct((heads * HEAD, length), small),
        ),
        in_specs=[IN_HBM] * 2 + [IN_VMEM] * 4,
        out_specs=(IN_HBM, IN_HBM, IN_VMEM),
        scratch_shapes=[
            pltpu.VMEM(weight.shape, small),
            pltpu.VMEM(frames.shape, small),
            pltpu.VMEM(joint, jnp.float32),
            pltpu.VMEM(joint, small),
            pltpu.VMEM((heads, length, length), small),
            pltpu.SemaphoreType.DMA((2 + length // 256 + heads,)),
        ],
        compiler_params=pltpu.CompilerParams(vmem_limit_bytes=36 * 2**20),
        name="attend",
    )(weight, frames, cosine, sine_table, segments[None, :], segments[:, None])


def cross_kernel(w_ref, h_ref, kv_ref, cq_ref, p_ref, o_ref, weight, frames, sems):
    heads, text, length = p_ref.shape
    span = heads * HEAD
    tiles = length // 256
    fetches = [pltpu.make_async_copy(w_ref.at[:, 128:384], weight, sems.at[0])]
    fetches += [
        pltpu.make_async_copy(
            h_ref.at[:, i * 256 : (i + 1) * 256], frames.at[:, i * 256 : (i + 1) * 256], sems.at[1 + i]
        )
        for i in range(tiles)
    ]
    for fetch in fetches:
        fetch.start()
    keys = [
        wide(kv_ref.at[h * HEAD : (h + 1) * HEAD, :text]).T.astype(cq_ref.dtype)
        for h in range(heads)
    ]
    fetches[0].wait()
    by_row = weight[:, span - 128 : 2 * span - 128].T
    for i in range(tiles):
        fetches[1 + i].wait()
        at = slice(i * 256, (i + 1) * 256)
        cq_ref[:, at] = jnp.dot(
            by_row, frames[:, at], preferred_element_type=jnp.float32
        ).astype(cq_ref.dtype)
        for h in range(heads):
            of = slice(h * HEAD, (h + 1) * HEAD)
            scores = jnp.dot(keys[h], cq_ref[of, at], preferred_element_type=jnp.float32) * (
                HEAD**-0.5
            )
            exponent = jnp.exp(scores - jnp.max(scores, axis=0, keepdims=True))
            probs = exponent * (1.0 / jnp.sum(exponent, axis=0, keepdims=True))
            p_ref[h, :, at] = probs.astype(p_ref.dtype)
            out = jnp.dot(
                kv_ref[of, text:], p_ref[h, :, at], preferred_element_type=jnp.float32
            )
            o_ref[of, at] = out.astype(o_ref.dtype)


def cross(weight, frames, text_kv):
    rows, length = text_kv.shape[0], frames.shape[1]
    text, small = text_kv.shape[1] // 2, jnp.bfloat16
    return kernel_call(
        cross_kernel,
        out_shape=(
            jax.ShapeDtypeStruct((rows, length), small),
            jax.ShapeDtypeStruct((rows // HEAD, text, length), small),
            jax.ShapeDtypeStruct((rows, length), small),
        ),
        in_specs=[IN_HBM, IN_HBM, IN_VMEM],
        out_specs=(IN_VMEM,) * 3,
        scratch_shapes=[
            pltpu.VMEM((weight.shape[0], 256), small),
            pltpu.VMEM(frames.shape, small),
            pltpu.SemaphoreType.DMA((1 + length // 256,)),
        ],
        compiler_params=pltpu.CompilerParams(vmem_limit_bytes=16 * 2**20),
        name="cross",
    )(weight, frames, text_kv)


def cross_back_kernel(cq_ref, p_ref, kv_ref, grad_ref, dq_ref, dkv_ref):
    heads, text, length = p_ref.shape
    scale = HEAD**-0.5
    for h in range(heads):
        of = slice(h * HEAD, (h + 1) * HEAD)
        by_key = wide(kv_ref.at[of, text:]).T.astype(cq_ref.dtype)
        grad_out = grad_ref[of, :]
        grad_probs = jnp.dot(by_key, grad_out, preferred_element_type=jnp.float32)
        probs = wide(p_ref.at[h])
        weighted = jnp.sum(probs * grad_probs, axis=0, keepdims=True)
        grad_scores = (probs * (grad_probs - weighted)).astype(cq_ref.dtype)
        dq_ref[of, :] = (
            jnp.dot(kv_ref[of, :text], grad_scores, preferred_element_type=jnp.float32) * scale
        ).astype(dq_ref.dtype)
        dkv_ref[of, :text] = (contract_last(cq_ref[of, :], grad_scores) * scale).astype(
            dkv_ref.dtype
        )
        dkv_ref[of, text:] = contract_last(grad_out, p_ref[h]).astype(dkv_ref.dtype)


def cross_back(cross_q, probs, text_kv, grad):
    return kernel_call(
        cross_back_kernel,
        out_shape=(
            jax.ShapeDtypeStruct(cross_q.shape, cross_q.dtype),
            jax.ShapeDtypeStruct(text_kv.shape, text_kv.dtype),
        ),
        in_specs=[IN_VMEM] * 4,
        out_specs=(IN_VMEM,) * 2,
        compiler_params=pltpu.CompilerParams(vmem_limit_bytes=16 * 2**20),
        name="cross_back",
    )(cross_q, probs, text_kv, grad)


def attend_back_kernel(
    part_in, p_in, g_in, cos_ref, sin_ref, o_ref, part_ref, p_ref, grad_ref, dq_ref, dk_ref, dv_ref, sems
):
    heads, length = part_ref.shape[1], part_ref.shape[3]
    fetches = [
        pltpu.make_async_copy(part_in, part_ref, sems.at[0]),
        pltpu.make_async_copy(g_in, grad_ref, sems.at[1]),
    ]
    fetches += [
        pltpu.make_async_copy(p_in.at[h], p_ref.at[h], sems.at[2 + h]) for h in range(heads)
    ]
    for fetch in fetches:
        fetch.start()
    cosine, sine_table = cos_ref[...], -sin_ref[...]
    scale = HEAD**-0.5
    fetches[0].wait()
    fetches[1].wait()
    for h in range(heads):
        of = slice(h * HEAD, (h + 1) * HEAD)
        by_key = wide(part_ref.at[2, h]).T.astype(part_ref.dtype)
        dk_ref[...] = jnp.zeros_like(dk_ref)
        dv_ref[...] = jnp.zeros_like(dv_ref)
        fetches[2 + h].wait()

        @pl.loop(0, length // 256)
        def _(i, h=h, of=of, by_key=by_key):
            at = pl.ds(pl.multiple_of(i * 256, 256), 256)
            grad_out = grad_ref[of, at]
            grad_probs = jnp.dot(by_key, grad_out, preferred_element_type=jnp.float32)
            low_probs = p_ref[h, :, at]
            probs = low_probs.astype(jnp.float32)
            weighted = jnp.sum(probs * grad_probs, axis=0, keepdims=True)
            grad_scores = (probs * (grad_probs - weighted)).astype(part_ref.dtype)
            dq_ref[:, at] = jnp.dot(
                part_ref[1, h], grad_scores, preferred_element_type=jnp.float32
            )
            dk_ref[...] += contract_last(part_ref[0, h, :, at], grad_scores)
            dv_ref[...] += contract_last(grad_out, low_probs)

        span = heads * HEAD
        grad_queries = turned(dq_ref[...] * scale, cosine, sine_table)
        grad_keys = turned(dk_ref[...] * scale, cosine, sine_table)
        o_ref[of, :] = grad_queries.astype(o_ref.dtype)
        o_ref[span + of.start : span + of.stop, :] = grad_keys.astype(o_ref.dtype)
        o_ref[2 * span + of.start : 2 * span + of.stop, :] = dv_ref[...].astype(o_ref.dtype)


def attend_back(parts, probs, grad, cosine, sine_table):
    _, heads, _, length = parts.shape
    return kernel_call(
        attend_back_kernel,
        out_shape=jax.ShapeDtypeStruct((3 * heads * HEAD, length), jnp.bfloat16),
        in_specs=[IN_HBM] * 3 + [IN_VMEM] * 2,
        out_specs=IN_VMEM,
        scratch_shapes=[pltpu.VMEM(array.shape, array.dtype) for array in (parts, probs, grad)]
        + [pltpu.VMEM((HEAD, length), jnp.float32)] * 3
        + [pltpu.SemaphoreType.DMA((2 + heads,))],
        compiler_params=pltpu.CompilerParams(vmem_limit_bytes=32 * 2**20),
        name="attend_back",
    )(parts, probs, grad, cosine, sine_table)


def update_kernel(
    block_ref,
    rate_ref,
    one_ref,
    two_ref,
    feed_ref,
    all_ref,
    gain_ref,
    pair_ref,
    sheet_ref,
    first_ref,
    second_ref,
    grad_out,
    first_out,
    second_out,
    sheet_out,
    copy_out,
    norm_out,
    gain_out,
    output_out,
    latent_out,
    grad,
    gain,
    scale,
):
    step = pl.program_id(0)
    part = D // 8
    text = CTXW // 8

    @pl.when(step == 0)
    def _():
        summed = jnp.sum(gain_ref[...], axis=0)
        rows = grad.shape[0]
        here = lax.broadcasted_iota(jnp.int32, (rows, D), 1) == (
            lax.broadcasted_iota(jnp.int32, (rows, D), 0) + block_ref[0] * rows
        )
        gain[...] = lax.dot_general(
            here.astype(jnp.float32),
            summed,
            (((1,), (1,)), ((), ())),
            precision=HIGHEST,
            preferred_element_type=jnp.float32,
        )
        norm = jnp.sqrt(jnp.sum(all_ref[:, :, 0:1, 0:1]) + jnp.sum(summed * summed))
        norm_out[0] = norm
        scale[0] = 1.0 / jnp.maximum(norm, 1.0)
        gain_out[...] = gain[...] * scale[0]
        output_out[...] = pair_ref[:, :D]
        latent_out[...] = wide(pair_ref.at[:, D:])

    for k in range(6):

        @pl.when(step == k // 2)
        def _(k=k):
            ref, start = (one_ref, k * part) if k < 3 else (two_ref, (k - 3) * part)
            for m in range(8):
                at = (k % 2) * D + m * part
                grad[:, at : at + part] = wide(ref.at[m, :, start : start + part])

    @pl.when(jnp.logical_and(step >= 3, step < 9))
    def _():
        grad[...] = wide(feed_ref)

    @pl.when(step == 9)
    def _():
        for m in range(8):
            for k in range(2):
                start = 3 * part + k * text
                at = k * CTXW + m * text
                grad[:, at : at + text] = wide(two_ref.at[m, :, start : start + text])
        grad[:, D : D + 8] = gain[...]

    for half in range(2):
        at = slice(half * D, (half + 1) * D)
        clipped = grad[:, at] * scale[0]
        sheet = sheet_ref[:, at]
        first_new = BETA_ONE * first_ref[:, at] + (1.0 - BETA_ONE) * clipped
        second_new = BETA_TWO * second_ref[:, at] + (1.0 - BETA_TWO) * clipped * clipped
        mean_hat = first_new * (1.0 / (1.0 - BETA_ONE**STEP))
        square_hat = second_new * (1.0 / (1.0 - BETA_TWO**STEP))
        sheet_new = sheet - rate_ref[2 * step + half] * (
            mean_hat / (jnp.sqrt(square_hat) + EPS_ADAM) + WEIGHT_DECAY * sheet
        )
        grad_out[:, at] = clipped
        first_out[:, at] = first_new
        second_out[:, at] = second_new
        sheet_out[:, at] = sheet_new
        copy_out[:, at] = sheet_new.astype(copy_out.dtype)


def sheet_update(block_index, length, one, two, feed_part, squares, gains, pair, sheet, first, second):
    rows = sheet.shape[0]
    frames = (pair.shape[0], D)
    rates = column_spread(length)[jnp.minimum(jnp.arange(20) * D, SHEET - 1)]
    column_block = pl.BlockSpec((rows, 2 * D), lambda i: (0, i))
    like = jax.ShapeDtypeStruct(sheet.shape, sheet.dtype)

    def whole(shape):
        return pl.BlockSpec(shape, lambda i: (0,) * len(shape))

    sheet, first, second, feed_part = (
        pltpu.with_memory_space_constraint(array, pltpu.HBM)
        for array in (sheet, first, second, feed_part)
    )
    return pl.pallas_call(
        update_kernel,
        grid=(10,),
        out_shape=(like, like, like, like, jax.ShapeDtypeStruct(sheet.shape, jnp.bfloat16))
        + (jax.ShapeDtypeStruct((1,), jnp.float32), jax.ShapeDtypeStruct((rows, 8), jnp.float32))
        + (
            jax.ShapeDtypeStruct(frames, jnp.bfloat16),
            jax.ShapeDtypeStruct(frames, jnp.float32),
        ),
        in_specs=[
            IN_SMEM,
            IN_SMEM,
            IN_VMEM,
            IN_VMEM,
            pl.BlockSpec((rows, 2 * D), lambda i: (0, jnp.clip(i - 3, 0, 5))),
            IN_VMEM,
            IN_VMEM,
            IN_VMEM,
            column_block,
            column_block,
            column_block,
        ],
        out_specs=(column_block,) * 5
        + (IN_SMEM, whole((rows, 8)), whole(frames), whole(frames)),
        scratch_shapes=[
            pltpu.VMEM((rows, 2 * D), jnp.float32),
            pltpu.VMEM((rows, 8), jnp.float32),
            pltpu.SMEM((1,), jnp.float32),
        ],
        compiler_params=pltpu.CompilerParams(vmem_limit_bytes=32 * 2**20),
        name="sheet_update",
    )(block_index, rates, one, two, feed_part, squares, gains, pair, sheet, first, second)


def pick_blocks(blocks, order):
    return blocks.at[order].get(mode="promise_in_bounds")


def gather_line(mine, order):
    blocks = lax.all_gather(mine, "z", axis=0, tiled=True)
    return pick_blocks(blocks, order).reshape(-1, mine.shape[-1])


def gather_slots(mine):
    return lax.all_gather(mine, "z", axis=0, tiled=True).reshape(-1, mine.shape[-1])


def sort_blocks(array, order):
    blocks = array.reshape(order.shape[0], -1, array.shape[-1])
    return pick_blocks(blocks, order).reshape(array.shape)


def as_blocks(grad, order):
    return grad.reshape(order.shape[0], -1, grad.shape[-1])


def scatter_line(blocks):
    return lax.psum_scatter(blocks, "z", scatter_dimension=0, tiled=True)


def plane_plan(latents, context, clip_starts, buckets, owners, cotangent, sheet, first, second):
    groups = lax.axis_size("dp")
    planes = lax.axis_size("z")
    cores = lax.axis_size("core")
    members = groups * cores
    frames = latents.shape[1]
    length = frames * members
    rows = sheet.shape[0]
    blocks = owners.shape[0]
    head_count = D // HEAD // members
    span = D // members
    units = FF // members
    score_scale = HEAD ** (-0.5)
    tail_col = 6 * D + 3 * FF
    gain_col = tail_col + 2 * CTXW
    plane = lax.axis_index("z")

    group_ids = jnp.arange(blocks, dtype=jnp.int32)
    inverse = jnp.sum(
        jnp.where(owners[None, :] == group_ids[:, None], group_ids[None, :], 0), axis=1
    )
    slot = group_ids.reshape(groups, planes, cores).swapaxes(0, 1).reshape(-1)
    slot_of = jnp.sum(
        jnp.where(slot[None, :] == group_ids[:, None], group_ids[None, :], 0), axis=1
    )
    to_logical = jnp.take(slot_of, inverse)
    to_slots = jnp.take(owners, slot)

    orders = jnp.stack([to_slots, to_logical])
    small = jnp.concatenate(
        [
            jnp.pad(
                sheet[:, gain_col:].astype(jnp.bfloat16).astype(jnp.float32).T,
                ((0, 0), (0, 64 - rows)),
            ),
            jnp.pad(clip_starts.astype(jnp.float32), ((0, 7), (0, 64 - clip_starts.shape[1]))),
        ],
        axis=1,
    )
    both, small, text_mine, mine_one = opening(
        latents[0], cotangent[0], small, context[0].T, sheet
    )
    mine_one, later = lax.optimization_barrier((mine_one, sheet))
    low_sheet = later.astype(jnp.bfloat16)
    weight_one = gather_slots(mine_one)
    gains = pick_blocks(small[..., :rows].reshape(blocks, 8, rows), to_logical)
    gains = gains.swapaxes(1, 2).reshape(D, 8)
    starts = lax.dynamic_index_in_dim(
        small[0, :, 0, 64 : 64 + clip_starts.shape[1]], plane * cores, 0, False
    )
    starts = starts.astype(jnp.int32)

    bucket_ids = jnp.arange(NB, dtype=jnp.int32)
    bucket_pick = (bucket_ids == buckets[plane]).astype(jnp.float32)
    counts = jnp.sum((buckets[:, None] == bucket_ids[None, :]).astype(jnp.float32), axis=0)
    row_weight = buckets.shape[0] / (NB * jnp.sum(bucket_pick * counts))
    gain_one = gains[:, 0:1]
    gain_two = gains[:, 1:2]
    gain_three = gains[:, 2:3]
    time_gain = jnp.sum(gains[:, 3:] * bucket_pick[None, :], axis=1, keepdims=True)

    tokens = both[:, :D].astype(jnp.float32).T
    grad_out = both[:, D:].astype(jnp.float32).T * row_weight

    rest = frames // planes
    place = jnp.arange(length, dtype=jnp.int32).reshape(planes, cores, groups, rest)
    positions = place.transpose(2, 1, 0, 3).reshape(-1)
    segments = segment_ids(starts, positions)
    frequency = jnp.exp(
        -math.log(10000.0) * jnp.arange(HEAD // 2, dtype=jnp.float32) / (HEAD // 2)
    )
    angles = frequency[:, None] * positions.astype(jnp.float32)[None, :]
    cosine = jnp.cos(angles)
    sine_table = jnp.sin(angles)

    normed_one, inverse_one = norm_columns(tokens)
    scaled_one = gain_one * time_gain
    h_one, grad_ff, mine_gu, mine_down = first_gather(
        sort_blocks((normed_one * scaled_one).astype(jnp.bfloat16), to_slots),
        sort_blocks(grad_out.astype(jnp.bfloat16), to_slots),
        low_sheet,
    )
    weight_gu = gather_slots(mine_gu)
    line_down = gather_slots(mine_down)

    parts, probs, attn_out = attend(weight_one, h_one, cosine, sine_table, segments)
    attn_out, x_one, normed_two, inverse_two, h_two, text_kv = project(
        "sum",
        0,
        orders,
        attn_out,
        weight_one,
        tokens,
        gain_two,
        text_mine,
    )

    cross_q, cross_probs, cross_out = cross(weight_one, h_two, text_kv)
    cross_out, x_two, normed_three, inverse_three, h_three = project(
        "slots",
        2 * span,
        orders,
        cross_out,
        weight_one,
        x_one,
        gain_three,
    )

    gate_up = contract_rows(weight_gu, h_three)
    gate_pre = gate_up[:units]
    up_part = gate_up[units:]
    sigmoid_gate = jax.nn.sigmoid(gate_pre)
    silu_gate = gate_pre * sigmoid_gate
    hidden = (silu_gate * up_part).astype(jnp.bfloat16)

    grad_blocks_down = as_blocks(contract_last(grad_ff, hidden).astype(jnp.bfloat16), to_slots)
    weight_down, grad_blocks_down = lax.optimization_barrier((line_down, grad_blocks_down))
    sums_down = scatter_line(grad_blocks_down)
    grad_hidden = contract_rows(weight_down, grad_ff)
    grad_gate = grad_hidden * up_part * (sigmoid_gate * (1.0 + gate_pre * (1.0 - sigmoid_gate)))
    grad_up = grad_hidden * silu_gate
    grad_gu = jnp.concatenate([grad_gate, grad_up], axis=0).astype(jnp.bfloat16)
    grad_x_two, grad_weight_gu, sum_three, grad_cross = back(
        orders,
        weight_gu,
        grad_gu,
        h_three,
        (normed_three, inverse_three, gain_three, grad_out),
        send_rows=True,
        in_slots=True,
        after=[grad_blocks_down],
    )
    grad_blocks_gu = as_blocks(grad_weight_gu, to_slots)
    sums_gu = scatter_line(grad_blocks_gu)
    grad_cross_out, grad_weight_co = back(
        orders, weight_one, grad_cross, cross_out, column=2 * span
    )
    grad_cross_q, grad_text = cross_back(cross_q, cross_probs, text_kv, grad_cross_out)
    grad_x_one, grad_weight_cq, sum_two, grad_attn, grad_text = back(
        orders,
        weight_one,
        grad_cross_q,
        h_two,
        (normed_two, inverse_two, gain_two, grad_x_two),
        column=span,
        send_rows=True,
        text=grad_text,
        in_slots=True,
        after=[sums_down],
    )
    grad_attn_out, grad_weight_two = back(
        orders,
        weight_one,
        grad_attn,
        attn_out,
        beside=(grad_weight_cq, grad_weight_co, grad_text, text_mine),
    )
    grad_blocks_two = as_blocks(grad_weight_two, to_slots)
    sums_two = scatter_line(grad_blocks_two)
    grad_qkv = attend_back(parts, probs, grad_attn_out, cosine, sine_table)
    latent_grad, grad_weight_qkv, sum_one = back(
        orders,
        weight_one,
        grad_qkv,
        h_one,
        (normed_one, inverse_one, scaled_one, grad_x_one),
        column=4 * span,
        in_slots=True,
        after=[sums_gu],
    )
    grad_blocks_one = as_blocks(grad_weight_qkv, to_slots)
    sums_one = scatter_line(grad_blocks_one)
    sums_feed, ff_out = feed(
        sums_gu,
        sums_down,
        weight_down,
        hidden,
        [grad_blocks_one],
    )
    sum_one = sum_one[0:1]
    grad_gain_one = sum_one * time_gain.T
    grad_time = sum_one * gain_one.T
    gain_grads = jnp.concatenate(
        [
            grad_gain_one,
            sum_two[0:1],
            sum_three[0:1],
            bucket_pick[:, None] * grad_time,
        ],
        axis=0,
    )
    pair, squares = prepare(
        orders, ff_out, x_two, latent_grad, sums_gu, sums_down, sums_two
    )
    sums_two = exchange_blocks(sums_two, [sums_feed])
    out_pair, sums_one, gain_sums, squares = closing(
        pair, squares, sums_one, gain_grads, sums_two
    )
    place = lax.axis_index("dp") * (planes * cores) + plane * cores + lax.axis_index("core")
    (
        clipped,
        first_new,
        second_new,
        sheet_new,
        sheet_copy,
        grad_norm,
        gain_grad,
        output,
        latent_grad,
    ) = sheet_update(
        lax.dynamic_slice_in_dim(owners, place, 1),
        length,
        sums_one,
        sums_two,
        sums_feed,
        squares,
        gain_sums,
        out_pair,
        sheet,
        first,
        second,
    )
    return (
        output[None],
        latent_grad[None],
        grad_norm[0],
        clipped,
        gain_grad,
        first_new,
        second_new,
        sheet_new,
        sheet_copy,
    )


def solution(mesh):
    groups, seq_count = mesh.shape["dp"], mesh.shape["seq"]
    by_plane = groups == 4 and seq_count == 8
    if by_plane:
        mesh = Mesh(mesh.devices.reshape(groups, seq_count // 2, 2), ("dp", "z", "core"))
    seq = ("z", "core") if by_plane else "seq"
    both = ("dp", "z", "core") if by_plane else ("dp", "seq")
    in_specs = (
        P("dp", seq, None),
        P("dp", None, None),
        P("dp", None),
        P(),
        P(),
        P("dp", seq, None),
        P(both, None),
        P(both, None),
        P(both, None),
    )
    out_specs = (
        P("dp", seq, None),
        P("dp", seq, None),
        P(),
        P(both, None),
        P(both, None),
        P(both, None),
        P(both, None),
        P(both, None),
        P(both, None),
    )
    return jax.shard_map(
        plane_plan if by_plane else gather_plan,
        mesh=mesh,
        in_specs=in_specs,
        out_specs=out_specs,
        check_vma=False,
    )
```

```python
import functools
import math

import jax
import jax.numpy as jnp
from jax import lax
from jax.experimental import pallas as pl
from jax.experimental.pallas import tpu as pltpu
from jax.sharding import Mesh
from jax.sharding import PartitionSpec as P

D = 1536
FF = 6144
HEAD = 64
CTXW = 768
CTX = 128
NB = 5
STEP = 10
SHEET = 29192


HIGHEST = lax.Precision.HIGHEST
EPS_NORM = 1e-05
EPS_ADAM = 1e-08
MASKED_SCORE = -1e30
BETA_ONE = 0.5
BETA_TWO = 0.5
WEIGHT_DECAY = 0.01


def reorder(values, ordering):
    leading = values.shape[:-1]
    groups = ordering.shape[0]
    blocks = values.reshape(leading + (groups, values.shape[-1] // groups))
    return jnp.take(blocks, ordering, axis=-2).reshape(values.shape)


def norm_parts(values):
    average = jnp.mean(values, axis=-1, keepdims=True)
    centered = values - average
    variance = jnp.mean(centered * centered, axis=-1, keepdims=True)
    inverse_std = lax.rsqrt(variance + EPS_NORM)
    return (centered * inverse_std, inverse_std)


def norm_back(grad_normed, normed, inverse_std):
    return inverse_std * (
        grad_normed
        - jnp.mean(grad_normed, axis=-1, keepdims=True)
        - normed * jnp.mean(grad_normed * normed, axis=-1, keepdims=True)
    )


def softmax_rows(scores):
    row_max = jnp.max(scores, axis=-1, keepdims=True)
    exponent = jnp.exp(scores - row_max)
    return exponent / jnp.sum(exponent, axis=-1, keepdims=True)


def rope_tables(positions, head_dim):
    half_dim = head_dim // 2
    frequency = jnp.exp(-math.log(10000.0) * jnp.arange(half_dim, dtype=jnp.float32) / half_dim)
    angles = positions.astype(jnp.float32)[:, None] * frequency[None, :]
    return (jnp.cos(angles)[:, None, :], jnp.sin(angles)[:, None, :])


def rotate(values, cosine, sine_table):
    half_dim = values.shape[-1] // 2
    first_half = values[..., :half_dim]
    second_half = values[..., half_dim:]
    return jnp.concatenate(
        [
            first_half * cosine - second_half * sine_table,
            second_half * cosine + first_half * sine_table,
        ],
        axis=-1,
    )


def unrotate(grads, cosine, sine_table):
    half_dim = grads.shape[-1] // 2
    first_half = grads[..., :half_dim]
    second_half = grads[..., half_dim:]
    return jnp.concatenate(
        [
            first_half * cosine + second_half * sine_table,
            second_half * cosine - first_half * sine_table,
        ],
        axis=-1,
    )


def segment_ids(starts, positions):
    return jnp.sum((starts[None, :] <= positions[:, None]).astype(jnp.int32), axis=1) - 1


def column_spread(length):
    column = jnp.arange(SHEET, dtype=jnp.int32)
    base_std = D ** (-0.5)
    spread = jnp.full((SHEET,), base_std, jnp.float32)
    spread = jnp.where(
        (column >= 3 * D) & (column < 4 * D), base_std * math.sqrt(length) / 4.0, spread
    )
    spread = jnp.where((column >= 5 * D) & (column < 6 * D), base_std * math.sqrt(CTX), spread)
    spread = jnp.where((column >= 6 * D + 2 * FF) & (column < 6 * D + 3 * FF), FF ** (-0.5), spread)
    spread = jnp.where(
        (column >= 6 * D + 3 * FF) & (column < 6 * D + 3 * FF + 2 * CTXW), CTXW ** (-0.5), spread
    )
    spread = jnp.where(column >= 6 * D + 3 * FF + 2 * CTXW, 0.3, spread)
    return spread


def inner_rows(left, right):
    return lax.dot_general(
        left, right, (((0,), (0,)), ((), ())), preferred_element_type=jnp.float32
    )


def inner_rows_high(left, right):
    return lax.dot_general(
        left, right, (((0,), (0,)), ((), ())), precision=HIGHEST, preferred_element_type=jnp.float32
    )


def gather_plan(latents, context, clip_starts, buckets, owners, cotangent, sheet, first, second):
    frames = latents.shape[1]
    seq_count = lax.axis_size("seq")
    length = frames * seq_count
    head_count = D // HEAD
    score_scale = HEAD ** (-0.5)
    group_ids = jnp.arange(owners.shape[0], dtype=jnp.int32)
    inverse = jnp.sum(
        jnp.where(owners[None, :] == group_ids[:, None], group_ids[None, :], 0), axis=1
    )
    gathered = lax.all_gather(sheet.astype(jnp.bfloat16), ("dp", "seq"), axis=0, tiled=True)
    tail_col = 6 * D + 3 * FF
    gain_col = tail_col + 2 * CTXW
    gain_rows = reorder(gathered[:, gain_col:].astype(jnp.float32).T, inverse)
    row_index = lax.axis_index("dp")
    bucket_ids = jnp.arange(NB, dtype=jnp.int32)
    bucket_pick = (bucket_ids == buckets[row_index]).astype(jnp.float32)
    counts = jnp.sum((buckets[:, None] == bucket_ids[None, :]).astype(jnp.float32), axis=0)
    row_weight = buckets.shape[0] / (NB * jnp.sum(bucket_pick * counts))
    gain_one = gain_rows[0]
    gain_two = gain_rows[1]
    gain_three = gain_rows[2]
    time_gain = jnp.sum(gain_rows[3:] * bucket_pick[:, None], axis=0)
    tokens = latents[0].astype(jnp.float32)
    positions = lax.axis_index("seq") * frames + jnp.arange(frames, dtype=jnp.int32)
    all_positions = jnp.arange(length, dtype=jnp.int32)
    starts = clip_starts[0]
    same_clip = (
        segment_ids(starts, positions)[:, None] == segment_ids(starts, all_positions)[None, :]
    )[None]
    cosine, sine_table = rope_tables(positions, HEAD)
    normed_one, inverse_one = norm_parts(tokens)
    scaled_one = gain_one * time_gain
    h_one_st = reorder((normed_one * scaled_one).astype(jnp.bfloat16), owners)
    joint_qkv = jnp.dot(h_one_st, gathered[:, : 3 * D], preferred_element_type=jnp.float32)
    queries = rotate(joint_qkv[:, :D].reshape(frames, head_count, HEAD), cosine, sine_table).astype(
        jnp.bfloat16
    )
    key_local = rotate(
        joint_qkv[:, D : 2 * D].reshape(frames, head_count, HEAD), cosine, sine_table
    ).astype(jnp.bfloat16)
    value_local = joint_qkv[:, 2 * D :].reshape(frames, head_count, HEAD).astype(jnp.bfloat16)
    key_all, value_all = (
        lax.all_gather(key_local, "seq", axis=0, tiled=True),
        lax.all_gather(value_local, "seq", axis=0, tiled=True),
    )
    scores = (
        jnp.einsum("qhd,khd->hqk", queries, key_all, preferred_element_type=jnp.float32)
        * score_scale
    )
    attn_probs = softmax_rows(jnp.where(same_clip, scores, MASKED_SCORE))
    probs_low = attn_probs.astype(jnp.bfloat16)
    attn_out = (
        jnp.einsum("hqk,khd->qhd", probs_low, value_all, preferred_element_type=jnp.float32)
        .reshape(frames, D)
        .astype(jnp.bfloat16)
    )
    attn_st = reorder(attn_out, owners)
    x_one = tokens + jnp.dot(
        attn_st, gathered[:, 3 * D : 4 * D], preferred_element_type=jnp.float32
    )
    normed_two, inverse_two = norm_parts(x_one)
    h_two_st = reorder((normed_two * gain_two).astype(jnp.bfloat16), owners)
    cross_q = (
        jnp.dot(h_two_st, gathered[:, 4 * D : 5 * D], preferred_element_type=jnp.float32)
        .astype(jnp.bfloat16)
        .reshape(frames, head_count, HEAD)
    )
    text_tokens = context[0]
    text_kv = jnp.einsum(
        "tc,dec->etd",
        text_tokens,
        gathered[:, tail_col:gain_col].reshape(D, 2, CTXW),
        preferred_element_type=jnp.float32,
    )
    text_kv = reorder(text_kv, inverse).astype(jnp.bfloat16).reshape(2, CTX, head_count, HEAD)
    text_keys = text_kv[0]
    text_values = text_kv[1]
    cross_scores = (
        jnp.einsum("qhd,khd->hqk", cross_q, text_keys, preferred_element_type=jnp.float32)
        * score_scale
    )
    cross_probs = softmax_rows(cross_scores)
    cross_low = cross_probs.astype(jnp.bfloat16)
    cross_out = (
        jnp.einsum("hqk,khd->qhd", cross_low, text_values, preferred_element_type=jnp.float32)
        .reshape(frames, D)
        .astype(jnp.bfloat16)
    )
    cross_st = reorder(cross_out, owners)
    x_two = x_one + jnp.dot(
        cross_st, gathered[:, 5 * D : 6 * D], preferred_element_type=jnp.float32
    )
    normed_three, inverse_three = norm_parts(x_two)
    h_three_st = reorder((normed_three * gain_three).astype(jnp.bfloat16), owners)
    grad_out = cotangent[0].astype(jnp.float32) * row_weight
    grad_ff_st = reorder(grad_out.astype(jnp.bfloat16), owners)
    gate_weight = gathered[:, 6 * D : 6 * D + 2 * FF]
    down_weight = gathered[:, 6 * D + 2 * FF : 6 * D + 3 * FF]
    units = down_weight.shape[1]
    gate_up = jnp.dot(h_three_st, gate_weight, preferred_element_type=jnp.float32)
    gate_pre = gate_up[:, :units]
    up_part = gate_up[:, units:]
    sigmoid_gate = jax.nn.sigmoid(gate_pre)
    silu_gate = gate_pre * sigmoid_gate
    hidden = (silu_gate * up_part).astype(jnp.bfloat16)
    ff_out = reorder(
        jnp.einsum("nf,df->nd", hidden, down_weight, preferred_element_type=jnp.float32), inverse
    )
    result = x_two + ff_out
    grad_hidden = jnp.dot(grad_ff_st, down_weight, preferred_element_type=jnp.float32)
    grad_gate = grad_hidden * up_part * (sigmoid_gate * (1.0 + gate_pre * (1.0 - sigmoid_gate)))
    grad_up = grad_hidden * silu_gate
    grad_gu = jnp.concatenate([grad_gate, grad_up], axis=1).astype(jnp.bfloat16)
    grad_h_three = reorder(
        jnp.einsum("nf,df->nd", grad_gu, gate_weight, preferred_element_type=jnp.float32), inverse
    )
    grad_gain_three = jnp.sum(grad_h_three * normed_three, axis=0)
    grad_x_two = grad_out + norm_back(grad_h_three * gain_three, normed_three, inverse_three)
    grad_cross = grad_x_two.astype(jnp.bfloat16)
    grad_cross_out = (
        reorder(
            jnp.einsum(
                "nd,ed->ne",
                grad_cross,
                gathered[:, 5 * D : 6 * D],
                preferred_element_type=jnp.float32,
            ),
            inverse,
        )
        .astype(jnp.bfloat16)
        .reshape(frames, head_count, HEAD)
    )
    grad_cross_probs = jnp.einsum(
        "qhd,khd->hqk", grad_cross_out, text_values, preferred_element_type=jnp.float32
    )
    grad_cross_scores = (
        cross_probs
        * (grad_cross_probs - jnp.sum(cross_probs * grad_cross_probs, axis=-1, keepdims=True))
    ).astype(jnp.bfloat16)
    grad_cross_q = (
        (
            jnp.einsum(
                "hqk,khd->qhd", grad_cross_scores, text_keys, preferred_element_type=jnp.float32
            )
            * score_scale
        )
        .reshape(frames, D)
        .astype(jnp.bfloat16)
    )
    grad_text_keys = (
        jnp.einsum("hqk,qhd->khd", grad_cross_scores, cross_q, preferred_element_type=jnp.float32)
        * score_scale
    )
    grad_text_values = jnp.einsum(
        "hqk,qhd->khd", cross_low, grad_cross_out, preferred_element_type=jnp.float32
    )
    grad_text = reorder(
        jnp.stack([grad_text_keys.reshape(CTX, D), grad_text_values.reshape(CTX, D)]), owners
    )
    grad_h_two = reorder(
        jnp.einsum(
            "ne,de->nd",
            grad_cross_q,
            gathered[:, 4 * D : 5 * D],
            preferred_element_type=jnp.float32,
        ),
        inverse,
    )
    grad_gain_two = jnp.sum(grad_h_two * normed_two, axis=0)
    grad_x_one = grad_x_two + norm_back(grad_h_two * gain_two, normed_two, inverse_two)
    grad_attn = grad_x_one.astype(jnp.bfloat16)
    grad_attn_out = (
        reorder(
            jnp.einsum(
                "nd,ed->ne",
                grad_attn,
                gathered[:, 3 * D : 4 * D],
                preferred_element_type=jnp.float32,
            ),
            inverse,
        )
        .astype(jnp.bfloat16)
        .reshape(frames, head_count, HEAD)
    )
    key_back, value_back = (key_all, value_all)

    def head_grads(head_items):
        head_probs, head_grad_out, head_values = head_items
        grad_probs = jnp.einsum(
            "qd,kd->qk", head_grad_out, head_values, preferred_element_type=jnp.float32
        )
        return (
            head_probs * (grad_probs - jnp.sum(head_probs * grad_probs, axis=-1, keepdims=True))
        ).astype(jnp.bfloat16)

    grad_scores_low = lax.map(
        head_grads, (attn_probs, jnp.swapaxes(grad_attn_out, 0, 1), jnp.swapaxes(value_back, 0, 1))
    )
    grad_queries = (
        jnp.einsum("hqk,khd->qhd", grad_scores_low, key_back, preferred_element_type=jnp.float32)
        * score_scale
    )
    grad_keys = (
        jnp.einsum("hqk,qhd->khd", grad_scores_low, queries, preferred_element_type=jnp.float32)
        * score_scale
    )
    grad_values = jnp.einsum(
        "hqk,qhd->khd", probs_low, grad_attn_out, preferred_element_type=jnp.float32
    )
    key_sums = lax.psum_scatter(
        jnp.concatenate(
            [
                grad_keys.reshape(frames * lax.axis_size("seq"), D),
                grad_values.reshape(frames * lax.axis_size("seq"), D),
            ],
            axis=1,
        ).astype(jnp.bfloat16),
        "seq",
        scatter_dimension=0,
        tiled=True,
    ).astype(jnp.float32)
    grad_q_raw = unrotate(grad_queries, cosine, sine_table).reshape(frames, D)
    grad_k_raw = unrotate(
        key_sums[:, :D].reshape(frames, head_count, HEAD), cosine, sine_table
    ).reshape(frames, D)
    grad_qkv = jnp.concatenate([grad_q_raw, grad_k_raw, key_sums[:, D:]], axis=1).astype(
        jnp.bfloat16
    )
    grad_h_one = reorder(
        jnp.einsum("ne,de->nd", grad_qkv, gathered[:, : 3 * D], preferred_element_type=jnp.float32),
        inverse,
    )
    grad_gain_one = jnp.sum(grad_h_one * normed_one * time_gain, axis=0)
    grad_time = jnp.sum(grad_h_one * normed_one * gain_one, axis=0)
    latent_grad = grad_x_one + norm_back(grad_h_one * scaled_one, normed_one, inverse_one)
    gain_grads = jnp.concatenate(
        [
            jnp.stack([grad_gain_one, grad_gain_two, grad_gain_three]),
            bucket_pick[:, None] * grad_time[None, :],
        ],
        axis=0,
    )
    gain_grads = reorder(gain_grads, owners).T
    text_float = text_tokens.astype(jnp.float32)
    pieces = [
        inner_rows(h_one_st, grad_qkv),
        inner_rows(attn_st, grad_attn),
        inner_rows(h_two_st, grad_cross_q),
        inner_rows(cross_st, grad_cross),
    ]
    pieces = pieces + [inner_rows(h_three_st, grad_gu), inner_rows(grad_ff_st, hidden)]
    pieces = pieces + [
        inner_rows_high(grad_text[0], text_float),
        inner_rows_high(grad_text[1], text_float),
        gain_grads,
    ]
    other_shard = lax.psum_scatter(
        jnp.concatenate(pieces, axis=1), ("dp", "seq"), scatter_dimension=0, tiled=True
    )
    total_squares = lax.psum(jnp.sum(other_shard * other_shard), ("dp", "seq"))
    grad_norm = jnp.sqrt(total_squares)
    clipped = other_shard / jnp.maximum(grad_norm, 1.0)
    gain_grad = clipped[:, 6 * D + 3 * FF + 2 * CTXW :]
    first_new = BETA_ONE * first + (1.0 - BETA_ONE) * clipped
    second_new = BETA_TWO * second + (1.0 - BETA_TWO) * clipped * clipped
    mean_hat = first_new / (1.0 - BETA_ONE**STEP)
    square_hat = second_new / (1.0 - BETA_TWO**STEP)
    rates = column_spread(length)[None, :]
    sheet_new = sheet - rates * (
        mean_hat / (jnp.sqrt(square_hat) + EPS_ADAM) + WEIGHT_DECAY * sheet
    )
    return (
        result.astype(jnp.bfloat16)[None],
        latent_grad[None],
        grad_norm,
        clipped,
        gain_grad,
        first_new,
        second_new,
        sheet_new,
        sheet_new.astype(jnp.bfloat16),
    )


PLANE = ("dp", "core")


def norm_columns(values):
    average = jnp.mean(values, axis=0, keepdims=True)
    centered = values - average
    variance = jnp.mean(centered * centered, axis=0, keepdims=True)
    inverse_std = lax.rsqrt(variance + EPS_NORM)
    return (centered * inverse_std, inverse_std)


def norm_columns_back(grad_normed, normed, inverse_std):
    return inverse_std * (
        grad_normed
        - jnp.mean(grad_normed, axis=0, keepdims=True)
        - normed * jnp.mean(grad_normed * normed, axis=0, keepdims=True)
    )


def contract_rows(left, right):
    return lax.dot_general(
        left, right, (((0,), (0,)), ((), ())), preferred_element_type=jnp.float32
    )


def contract_last(left, right):
    return lax.dot_general(
        left, right, (((1,), (1,)), ((), ())), preferred_element_type=jnp.float32
    )


def matmul(left, right):
    return jnp.dot(left, right, preferred_element_type=jnp.float32)


MESH_ID = pl.DeviceIdType.MESH
IDENTITIES = {}


def identity_of(name, *arrays):
    key = (name,) + tuple((array.shape, str(array.dtype)) for array in arrays)
    return IDENTITIES.setdefault(key, len(IDENTITIES))


IN_HBM = pl.BlockSpec(memory_space=pltpu.HBM)
IN_SMEM = pl.BlockSpec(memory_space=pltpu.SMEM)
IN_VMEM = pl.BlockSpec(memory_space=pltpu.VMEM)
BRIEF = pl.CostEstimate(flops=0, bytes_accessed=1024, transcendentals=0)


def kernel_call(kernel, *, out_shape, in_specs, out_specs, **options):
    single = not isinstance(out_shape, tuple)
    shapes = (out_shape,) if single else out_shape
    places = (out_specs,) if single else out_specs
    shapes = tuple(
        pltpu.HBM(shape.shape, shape.dtype) if place is IN_HBM else shape
        for shape, place in zip(shapes, places)
    )
    call = pl.pallas_call(
        kernel,
        out_shape=shapes[0] if single else shapes,
        in_specs=in_specs,
        out_specs=out_specs,
        **options,
    )

    def run(*operands):
        return call(
            *[
                pltpu.with_memory_space_constraint(operand, pltpu.HBM)
                if place is IN_HBM
                else operand
                for operand, place in zip(operands, in_specs)
            ]
        )

    return run


def reorder_blocks(source, target, order, column=0):
    rows = source.shape[1]
    columns = slice(column, column + target.shape[1])

    @pl.loop(0, source.shape[0])
    def _(b):
        target[pl.ds(pl.multiple_of(b * rows, 16), rows), :] = source[order(b), :, columns]


def wide(ref):
    return ref[...].astype(jnp.float32)


def greet(peers):
    barrier = pltpu.get_barrier_semaphore()
    for peer in peers:
        pl.semaphore_signal(barrier, inc=1, device_id=peer, device_id_type=MESH_ID)
    pl.semaphore_wait(barrier, len(peers))


def near():
    group, core = lax.axis_index("dp"), lax.axis_index("core")
    across = group + 1 - 2 * lax.rem(group, 2)
    along = lax.rem(group + 2, 4)
    return group, core, across, along


def member_rows(width):
    def place(ref, member, start, count):
        first_row = pl.multiple_of(member * width + start, 16)
        return ref.at[pl.ds(first_row, count), :]

    return place


def member_lanes(width):
    def place(ref, member, start, count):
        return ref.at[pl.ds(start, count), pl.ds(pl.multiple_of(member * width, 128), width)]

    return place


def mover(send_sem, recv_sem, first=0):
    def copy(k, source, target, peer):
        return pltpu.make_async_remote_copy(
            src_ref=source,
            dst_ref=target,
            send_sem=send_sem.at[first + k],
            recv_sem=recv_sem.at[first + k],
            device_id=peer,
            device_id_type=MESH_ID,
        )

    return copy


def member_at(member):
    return {"dp": lax.div(member, 2), "core": lax.rem(member, 2)}


def plane_peers():
    group, core, _, _ = near()
    member = group * 2 + core
    return [lax.rem(member + step, 8) for step in range(1, 8)]


def gather_steps(place, x_ref, o_ref, local_sem, copy, arrived_whole=lambda member: None):
    group, core, across, along = near()
    beyond = across + along - group
    other = 1 - core
    sibling, by_x, by_y = {"core": other}, {"dp": across}, {"dp": along}
    half = x_ref.shape[0] // 2

    def part(owner, owner_core, piece):
        return place(o_ref, owner * 2 + owner_core, piece * half, half)

    sent = []

    def send(k, source, target, peer):
        moving = copy(k, source, target, peer)
        moving.start()
        sent.append(moving)

    def own(k, piece, peer):
        send(k, x_ref.at[pl.ds(piece * half, half), :], part(group, core, piece), peer)

    def relay(k, owner, piece, peer):
        send(k, part(owner, core, piece), part(owner, core, piece), peer)

    def arrived(k, owner, owner_core, piece):
        landed = part(owner, owner_core, piece)
        copy(k, landed, landed, sibling).wait_recv()

    local = pltpu.make_async_copy(
        x_ref, place(o_ref, group * 2 + core, 0, 2 * half), local_sem
    )
    local.start()
    own(0, 0, by_x)
    own(1, 1, by_y)
    own(2, 1, by_x)
    own(3, 0, by_y)
    own(4, 0, sibling)
    own(5, 1, sibling)

    def finish():
        local.wait()
        arrived_whole(group * 2 + core)
        arrived(4, group, other, 0)
        arrived(5, group, other, 1)
        arrived_whole(group * 2 + other)
        arrived(0, across, core, 0)
        relay(6, across, 0, by_y)
        relay(7, across, 0, sibling)
        arrived(1, along, core, 1)
        relay(8, along, 1, by_x)
        relay(9, along, 1, sibling)
        arrived(2, across, core, 1)
        relay(10, across, 1, sibling)
        arrived_whole(across * 2 + core)
        arrived(3, along, core, 0)
        relay(11, along, 0, sibling)
        arrived_whole(along * 2 + core)
        arrived(7, across, other, 0)
        arrived(10, across, other, 1)
        arrived_whole(across * 2 + other)
        arrived(6, beyond, core, 0)
        relay(12, beyond, 0, sibling)
        arrived(8, beyond, core, 1)
        relay(13, beyond, 1, sibling)
        arrived_whole(beyond * 2 + core)
        arrived(9, along, other, 1)
        arrived(11, along, other, 0)
        arrived_whole(along * 2 + other)
        arrived(12, beyond, other, 0)
        arrived(13, beyond, other, 1)
        arrived_whole(beyond * 2 + other)
        for moving in sent:
            moving.wait_send()

    return finish


def exchange_steps(source, target, x_ref, o_ref, local_sem, copy):
    group, core, _, _ = near()
    member = group * 2 + core
    local = pltpu.make_async_copy(source(x_ref, member), target(o_ref, member), local_sem)
    local.start()
    sent = []
    for k, peer in enumerate(plane_peers()):
        sent.append(copy(k, source(x_ref, peer), target(o_ref, member), member_at(peer)))
        sent[-1].start()

    def finish():
        for k in range(7):
            sender = lax.rem(member + 7 - k, 8)
            landed = target(o_ref, sender)
            copy(k, landed, landed, member_at(sender)).wait_recv()
        local.wait()
        for moving in sent:
            moving.wait_send()

    return finish


def gather_kernel(place, x_ref, *refs):
    o_ref, local_sem, send_sem, recv_sem = refs[-4:]
    _, core, across, along = near()
    greet([{"dp": across}, {"dp": along}, {"core": 1 - core}])
    gather_steps(place, x_ref, o_ref, local_sem, mover(send_sem, recv_sem))()


def plane_gather_call(shard, shape, place, kind, after):
    return kernel_call(
        functools.partial(gather_kernel, place),
        out_shape=jax.ShapeDtypeStruct(shape, shard.dtype),
        in_specs=[IN_HBM] * (1 + len(after)),
        out_specs=IN_HBM,
        scratch_shapes=[
            pltpu.SemaphoreType.DMA,
            pltpu.SemaphoreType.DMA((14,)),
            pltpu.SemaphoreType.DMA((14,)),
        ],
        compiler_params=pltpu.CompilerParams(
            collective_id=identity_of(kind, shard, *after), has_side_effects=True
        ),
        cost_estimate=BRIEF,
        name="plane_gather",
    )(shard, *after)


def plane_gather(shard, after=()):
    rows, width = shard.shape
    return plane_gather_call(shard, (rows, 8 * width), member_lanes(width), "gather lanes", after)


def plane_gather_rows(shard, after=()):
    rows, width = shard.shape
    return plane_gather_call(shard, (8 * rows, width), member_rows(rows), "gather rows", after)


def scatter_steps(place, p_ref, bufs, copy):
    pair, total, from_x, from_y, relay = bufs
    group, core, across, along = near()
    beyond = across + along - group
    other = 1 - core
    sibling, by_x, by_y = {"core": other}, {"dp": across}, {"dp": along}
    rows = total.shape[1]
    half = rows // 2
    low, high = pl.ds(0, half), pl.ds(half, half)
    sent = []

    def send(k, source, target, peer):
        moving = copy(k, source, target, peer)
        moving.start()
        sent.append(moving)

    def arrived(k, target):
        copy(k, target, target, sibling).wait_recv()

    def both_cores(k, owner):
        arrived(k, pair.at[k])
        summed = wide(place(p_ref, owner * 2 + core, 0, rows)) + wide(pair.at[k])
        total[k] = summed.astype(total.dtype)

    def cores():
        for k, owner in enumerate((beyond, across, along, group)):
            send(k, place(p_ref, owner * 2 + other, 0, rows), pair.at[k], sibling)

    def chips():
        both_cores(0, beyond)
        send(4, total.at[0, low], relay.at[0], by_x)
        send(5, total.at[0, high], relay.at[1], by_y)
        both_cores(1, across)
        send(6, total.at[1, low], from_x.at[low], by_x)
        both_cores(2, along)
        send(7, total.at[2, high], from_y.at[high], by_y)
        both_cores(3, group)

    def relays():
        arrived(5, relay.at[1])
        total[1, high] = (wide(total.at[1, high]) + wide(relay.at[1])).astype(total.dtype)
        send(8, total.at[1, high], from_x.at[high], by_x)
        arrived(4, relay.at[0])
        total[2, low] = (wide(total.at[2, low]) + wide(relay.at[0])).astype(total.dtype)
        send(9, total.at[2, low], from_y.at[low], by_y)

    def finish():
        arrived(6, from_x.at[low])
        arrived(7, from_y.at[high])
        arrived(8, from_x.at[high])
        arrived(9, from_y.at[low])
        summed = wide(total.at[3]) + wide(from_x) + wide(from_y)
        for moving in sent:
            moving.wait_send()
        return summed

    return cores, chips, relays, finish


def scatter_bufs(rows, width):
    slot = pltpu.VMEM((rows, width), jnp.bfloat16)
    four = pltpu.VMEM((4, rows, width), jnp.bfloat16)
    return [four, four, slot, slot, pltpu.VMEM((2, rows // 2, width), jnp.bfloat16)]


def scatter_kernel(place, p_ref, *refs):
    o_ref, *bufs, send_sem, recv_sem = refs[-8:]
    _, core, across, along = near()
    greet([{"dp": across}, {"dp": along}, {"core": 1 - core}])
    cores, chips, relays, finish = scatter_steps(place, p_ref, bufs, mover(send_sem, recv_sem))
    cores()
    chips()
    relays()
    o_ref[...] = finish().astype(o_ref.dtype)


def plane_scatter_call(partial, shape, place, dtype, kind, after):
    rows, width = shape
    return kernel_call(
        functools.partial(scatter_kernel, place),
        out_shape=jax.ShapeDtypeStruct(shape, dtype),
        in_specs=[IN_VMEM] + [IN_HBM] * len(after),
        out_specs=IN_VMEM,
        scratch_shapes=scatter_bufs(rows, width)
        + [
            pltpu.SemaphoreType.DMA((10,)),
            pltpu.SemaphoreType.DMA((10,)),
        ],
        compiler_params=pltpu.CompilerParams(
            collective_id=identity_of(kind, partial, *after),
            has_side_effects=True,
            vmem_limit_bytes=24 * 2**20,
        ),
        cost_estimate=BRIEF,
        name="plane_scatter",
    )(partial, *after)


def plane_scatter_frames(partial, after=()):
    rows, width = partial.shape[0], partial.shape[1] // 8
    place = member_lanes(width)
    return plane_scatter_call(partial, (rows, width), place, jnp.float32, "scatter lanes", after)


def plane_scatter_rows(partial, after=()):
    rows, width = partial.shape[0] // 8, partial.shape[1]
    place = member_rows(rows)
    return plane_scatter_call(partial, (rows, width), place, jnp.bfloat16, "scatter rows", after)


def project_kernel(kind, column, order_ref, s_ref, w_ref, base_ref, gain_ref, *refs):
    if kind == "sum":
        side_ref, full_ref, x_ref, n_ref, i_ref, h_ref, side_out, *refs = refs
    else:
        full_ref, x_ref, n_ref, i_ref, h_ref, *refs = refs
    full, total, part, landed, shard, by_block, base, gain, residual, normed, *refs = refs
    heads, slots, weight, *bufs, local_sem, send_sem, recv_sem = refs
    rows, length = s_ref.shape
    width = base_ref.shape[1]
    fetches = [
        pltpu.make_async_copy(ref, held, local_sem.at[8 + k])
        for k, (ref, held) in enumerate(
            [(s_ref, heads), (w_ref.at[:, :, : slots.shape[2]], slots)]
            + [(base_ref, base), (gain_ref, gain)]
        )
    ]
    for fetch in fetches:
        fetch.start()
    greet([member_at(peer) for peer in plane_peers()])
    side = mover(send_sem, recv_sem, 35)
    if kind == "sum":
        cores, chips, relays, finish = scatter_steps(
            member_rows(side_out.shape[0]), bufs[-1], bufs[:-2], side
        )
        text_weight = bufs[-2]
        fetches[1].wait()
        reorder_blocks(slots, text_weight, lambda b: order_ref[1, b], 3 * rows)
        tokens = side_ref.shape[1]

        @pl.loop(0, text_weight.shape[0] // 256)
        def _(i):
            at = pl.ds(pl.multiple_of(i * 256, 256), 256)
            for k in range(2):
                half = slice(k * side_ref.shape[0], (k + 1) * side_ref.shape[0])
                bufs[-1][at, k * tokens : (k + 1) * tokens] = jnp.dot(
                    text_weight[at, half], side_ref[...], preferred_element_type=jnp.float32
                ).astype(jnp.bfloat16)

        cores()
    else:
        fetches[1].wait()
    reorder_blocks(slots, weight, lambda b: order_ref[1, b], column)
    fetches[0].wait()
    total[...] = jnp.zeros_like(total)

    def add(member):
        of = pl.ds(pl.multiple_of(member * rows, 16), rows)

        @pl.loop(0, length // 256)
        def _(i):
            at = pl.ds(pl.multiple_of(i * 256, 256), 256)
            total[:, at] += contract_rows(weight[of, :], full[of, at])

    gathered = gather_steps(
        member_rows(rows), heads, full, local_sem.at[0], mover(send_sem, recv_sem), add
    )
    if kind == "sum":
        chips()
    gathered()
    kept = pltpu.make_async_copy(full, full_ref, local_sem.at[0])
    kept.start()
    part[...] = total[...].astype(part.dtype)
    exchanged = exchange_steps(
        whole_lanes(rows, width),
        whole_rows(rows),
        part,
        landed,
        local_sem.at[3],
        mover(send_sem, recv_sem, 14),
    )
    if kind == "sum":
        relays()
    exchanged()
    fetches[2].wait()
    fetches[3].wait()
    residual[...] = base[...] + wide(landed)
    standard, inverse_std = norm_columns(residual[...])
    normed[...] = standard
    i_ref[...] = inverse_std
    by_block[...] = (standard * gain[...]).astype(shard.dtype).reshape(by_block.shape)
    reorder_blocks(by_block, shard, lambda b: order_ref[0, b])
    gathered = gather_steps(
        member_lanes(width), shard, h_ref, local_sem.at[4], mover(send_sem, recv_sem, 21)
    )
    x_copy = pltpu.make_async_copy(residual, x_ref, local_sem.at[5])
    x_copy.start()
    n_copy = pltpu.make_async_copy(normed, n_ref, local_sem.at[6])
    n_copy.start()
    if kind == "sum":
        side_out[...] = finish().astype(side_out.dtype)
    gathered()
    kept.wait()
    x_copy.wait()
    n_copy.wait()


def project(kind, column, orders, heads, weight, base, gain, *side):
    rows, length = heads.shape
    features, width = base.shape
    whole = jax.ShapeDtypeStruct((features, length), jnp.bfloat16)
    frames = jax.ShapeDtypeStruct(base.shape, jnp.float32)
    side_outs, bufs = (), []
    if kind == "sum":
        tokens = side[0].shape[1]
        side_outs = (jax.ShapeDtypeStruct((rows, 2 * tokens), jnp.bfloat16),)
        bufs = scatter_bufs(rows, 2 * tokens) + [
            pltpu.VMEM((features, rows), jnp.bfloat16),
            pltpu.VMEM((features, 2 * tokens), jnp.bfloat16),
        ]
    low, high = pltpu.VMEM(base.shape, jnp.bfloat16), pltpu.VMEM(base.shape, jnp.float32)
    return kernel_call(
        functools.partial(project_kernel, kind, column),
        out_shape=(whole, frames, frames, jax.ShapeDtypeStruct((1, width), jnp.float32), whole)
        + side_outs,
        in_specs=[IN_SMEM] + [IN_HBM] * 4 + [IN_VMEM] * len(side),
        out_specs=(IN_HBM, IN_HBM, IN_HBM, IN_VMEM, IN_HBM) + (IN_VMEM,) * len(side),
        scratch_shapes=[
            pltpu.VMEM((features, length), jnp.bfloat16),
            pltpu.VMEM((rows, length), jnp.float32),
            pltpu.VMEM((rows, length), jnp.bfloat16),
            low,
            low,
            pltpu.VMEM((orders.shape[1], features // orders.shape[1], width), jnp.bfloat16),
            high,
            pltpu.VMEM(gain.shape, jnp.float32),
            high,
            high,
            pltpu.VMEM(heads.shape, heads.dtype),
            pltpu.VMEM((orders.shape[1], features // orders.shape[1], 4 * rows), weight.dtype),
            pltpu.VMEM((features, rows), weight.dtype),
        ]
        + bufs
        + [
            pltpu.SemaphoreType.DMA((13,)),
            pltpu.SemaphoreType.DMA((49,)),
            pltpu.SemaphoreType.DMA((49,)),
        ],
        compiler_params=pltpu.CompilerParams(
            collective_id=identity_of("project " + kind, heads),
            has_side_effects=True,
            vmem_limit_bytes=32 * 2**20,
        ),
        cost_estimate=BRIEF,
        name="project_" + kind,
    )(orders, heads, weight.reshape(orders.shape[1], -1, weight.shape[1]), base, gain, *side)


def back_kernel(plan, *refs):
    by_rows, send_rows, text, in_slots, column, beside, after = plan
    refs = list(refs)

    def take(count):
        taken = refs[:count]
        del refs[:count]
        return taken

    order_ref = take(1)[0]
    sources = take(3 if by_rows else 7)
    text_ref = take(1)[0] if text else None
    beside_refs = take(4 if beside else 0)
    take(after)
    o_ref, own_out = take(2)
    sum_ref = None if by_rows else take(1)[0]
    rows_ref = take(1)[0] if send_rows else None
    text_out = take(1)[0] if text else None
    held = take(len(sources))
    w_ref, g_ref, act, *norms = held
    results = take(0 if by_rows else 2)
    mine, theirs, pair, from_x, from_y, relay, shard, slots, own_ref = take(9)
    besides = take(4 if beside else 0)
    by_head = take(1 if by_rows else 0)
    local_sem, send_sem, recv_sem = refs
    if by_rows:
        w_slots, w_ref = w_ref, by_head[0]
    source = sources[0]
    if by_rows:
        sources[0] = source.at[:, :, : w_slots.shape[2]]
    elif w_ref.shape[1] < source.shape[1]:
        sources[0] = source.at[:, : w_ref.shape[1]]
    fetches = [
        pltpu.make_async_copy(ref, here, local_sem.at[4 + k])
        for k, (ref, here) in enumerate(zip(sources + beside_refs, held + besides))
    ]
    for fetch in fetches:
        fetch.start()

    group, core, across, along = near()
    beyond = across + along - group
    sibling, by_x, by_y = {"core": 1 - core}, {"dp": across}, {"dp": along}
    rows, width = mine.shape[1:]
    columns = slice(0, g_ref.shape[0]) if by_rows else slice(column, column + g_ref.shape[0])
    half = rows // 2
    low, high = pl.ds(0, half), pl.ds(half, half)
    copy = mover(send_sem, recv_sem)
    sent = []

    def send(k, source, target, peer):
        moving = copy(k, source, target, peer)
        moving.start()
        sent.append(moving)

    def arrived(k, target):
        copy(k, target, target, sibling).wait_recv()

    def split(k, at_rows, at_lanes, first, second):
        mine[k, at_rows, at_lanes] = jnp.where(core == 0, first, second).astype(mine.dtype)
        theirs[k, at_rows, at_lanes] = jnp.where(core == 0, second, first).astype(mine.dtype)

    def work_out(k, owner):
        if by_rows:

            @pl.loop(0, width // 256)
            def _(i):
                at = pl.ds(pl.multiple_of(i * 256, 256), 256)
                both = jnp.dot(
                    w_ref[pl.ds(pl.multiple_of(owner * 2 * rows, 16), 2 * rows), columns],
                    g_ref[:, at],
                    preferred_element_type=jnp.float32,
                )
                split(k, slice(None), at, both[:rows], both[rows:])

        else:

            @pl.loop(0, rows // 256)
            def _(i):
                at = pl.ds(pl.multiple_of(i * 256, 256), 256)
                both = jnp.dot(
                    w_ref[at, columns],
                    g_ref[:, pl.ds(pl.multiple_of(owner * 2 * width, 256), 2 * width)],
                    preferred_element_type=jnp.float32,
                )
                split(k, at, slice(None), both[:, :width], both[:, width:])

        send(k, theirs.at[k], pair.at[k], sibling)

    def both_cores(k):
        arrived(k, pair.at[k])
        mine[k] = (wide(mine.at[k]) + wide(pair.at[k])).astype(mine.dtype)

    def weight_grads(first, last):
        rows_of = act if in_slots else slots
        tile, count = rows_of.shape[0] // 6, g_ref.shape[0]

        @pl.loop(first, last)
        def _(i):
            at = pl.ds(pl.multiple_of(i * tile, tile), tile)
            for j in range(0, count, 256):
                of = slice(j, min(j + 256, count))
                own_ref[at, of] = contract_last(rows_of[at, :], g_ref[of, :]).astype(
                    own_ref.dtype
                )

    if send_rows or text:
        greet([member_at(peer) for peer in plane_peers()])
    else:
        greet([by_x, by_y, sibling])
    fetches[0].wait()
    if by_rows:
        reorder_blocks(w_slots, w_ref, lambda b: order_ref[1, b], column)
    fetches[1].wait()
    for k, owner in enumerate((beyond, across, along, group)):
        work_out(k, owner)
        if k == 1:
            both_cores(0)
            send(4, mine.at[0, low], relay.at[0], by_x)
            send(5, mine.at[0, high], relay.at[1], by_y)
        if k == 2:
            both_cores(1)
            send(6, mine.at[1, low], from_x.at[low], by_x)
        if k == 3:
            both_cores(2)
            send(7, mine.at[2, high], from_y.at[high], by_y)
    if text:
        text_done = gather_steps(
            member_rows(text_ref.shape[0]),
            text_ref,
            text_out,
            local_sem.at[1],
            mover(send_sem, recv_sem, 17),
        )
    def put_beside():
        cq, co, text_grad, text_mine = besides
        count, rows = g_ref.shape[0], text_grad.shape[1]
        part = text_mine.shape[0]
        tokens = text_mine.shape[1]

        @pl.loop(0, text_grad.shape[0])
        def _(b):
            at = pl.ds(pl.multiple_of(b * rows, 16), rows)
            own_ref[at, count : 2 * count] = cq[at, :]
            own_ref[at, 2 * count : 3 * count] = co[at, :]
            slots[at, : 2 * tokens] = text_grad[order_ref[0, b]]

        @pl.loop(0, 6)
        def _(i):
            at = pl.ds(pl.multiple_of(i * 256, 256), 256)
            for k in range(2):
                grads = contract_last(
                    slots[at, k * tokens : (k + 1) * tokens], text_mine[...]
                )
                start = 3 * count + k * part
                own_ref[at, start : start + part] = grads.astype(own_ref.dtype)

    fetches[2].wait()
    if not in_slots:
        reorder_blocks(act, slots, lambda b: order_ref[0, b])
    weight_grads(0, 2)
    arrived(5, relay.at[1])
    mine[1, high] = (wide(mine.at[1, high]) + wide(relay.at[1])).astype(mine.dtype)
    send(8, mine.at[1, high], from_x.at[high], by_x)
    arrived(4, relay.at[0])
    mine[2, low] = (wide(mine.at[2, low]) + wide(relay.at[0])).astype(mine.dtype)
    send(9, mine.at[2, low], from_y.at[low], by_y)
    both_cores(3)
    weight_grads(2, 6)
    if beside:
        for fetch in fetches[len(sources) :]:
            fetch.wait()
        put_beside()
    if text:
        text_done()
    own_copy = pltpu.make_async_copy(own_ref, own_out, local_sem.at[2])
    own_copy.start()
    arrived(6, from_x.at[low])
    arrived(7, from_y.at[high])
    arrived(8, from_x.at[high])
    arrived(9, from_y.at[low])
    summed = wide(mine.at[3]) + wide(from_x) + wide(from_y)
    if by_rows:
        shard[...] = summed.astype(shard.dtype)
        result_copy = pltpu.make_async_copy(shard, o_ref, local_sem.at[3])
        result_copy.start()
    else:
        for fetch in fetches[3 : len(sources)]:
            fetch.wait()
        normed, inverse_std, gain, base = norms
        result, by_block = results
        if in_slots:
            by_block[...] = summed.reshape(by_block.shape)
            reorder_blocks(by_block, result, lambda b: order_ref[1, b])
            summed = result[...]
        result[...] = base[...] + norm_columns_back(
            summed * gain[...], normed[...], inverse_std[...]
        )
        result_copy = pltpu.make_async_copy(result, o_ref, local_sem.at[3])
        result_copy.start()
        if send_rows:
            shard[...] = result[...].astype(shard.dtype)
            rows_done = exchange_steps(
                whole_rows(rows // 8),
                whole_lanes(rows // 8, width),
                shard,
                rows_ref,
                local_sem.at[0],
                mover(send_sem, recv_sem, 10),
            )
        sum_ref[...] = lax.dot_general(
            jnp.ones((8, width), jnp.float32),
            summed * normed[...],
            (((1,), (1,)), ((), ())),
            precision=HIGHEST,
            preferred_element_type=jnp.float32,
        )
        if send_rows:
            rows_done()
    result_copy.wait()
    own_copy.wait()
    for moving in sent:
        moving.wait_send()


def back(
    orders,
    weight,
    grad,
    act,
    norm=None,
    column=0,
    send_rows=False,
    text=None,
    in_slots=False,
    beside=(),
    after=(),
):
    by_rows = norm is None
    features, length = weight.shape[0], grad.shape[1]
    shape = (features // 8, length) if by_rows else (features, length // 8)
    small = jnp.bfloat16
    own_width = grad.shape[0] * (4 if beside else 1)
    own = jax.ShapeDtypeStruct((features, own_width), small)
    outs = [jax.ShapeDtypeStruct(shape, small if by_rows else jnp.float32), own]
    specs = [IN_HBM, IN_HBM]
    if not by_rows:
        outs.append(jax.ShapeDtypeStruct((8, features), jnp.float32))
        specs.append(IN_VMEM)
    if send_rows:
        outs.append(jax.ShapeDtypeStruct((features // 8, length), small))
        specs.append(IN_HBM)
    count = orders.shape[1]
    if not in_slots:
        act = act.reshape(count, features // count, length)
    few = weight.shape[1] if column + grad.shape[0] > 4 * (features // 8) else 4 * (features // 8)
    if by_rows:
        weight = weight.reshape(count, features // count, weight.shape[1])
        held = jax.ShapeDtypeStruct((count, features // count, few), small)
    else:
        held = jax.ShapeDtypeStruct((features, few), small)
    sources = [weight, grad, act] + list(norm or ())
    operands = [orders] + sources
    if text is not None:
        operands.append(text)
        outs.append(jax.ShapeDtypeStruct((8 * text.shape[0], text.shape[1]), text.dtype))
        specs.append(IN_HBM)
    if beside:
        cq, co, text_grad, text_mine = beside
        beside = (cq, co, text_grad.reshape(count, features // count, -1), text_mine)
        operands += list(beside)
    operands += list(after)
    plan = (by_rows, send_rows, text is not None, in_slots, column, bool(beside), len(after))
    rows, width = shape
    four, slot = pltpu.VMEM((4, rows, width), small), pltpu.VMEM((rows, width), small)
    return kernel_call(
        functools.partial(back_kernel, plan),
        out_shape=tuple(outs),
        in_specs=[IN_SMEM] + [IN_HBM] * (len(operands) - 1),
        out_specs=tuple(specs),
        scratch_shapes=[pltpu.VMEM(array.shape, array.dtype) for array in [held] + sources[1:]]
        + (
            []
            if by_rows
            else [
                pltpu.VMEM(shape, jnp.float32),
                pltpu.VMEM((count, rows // count, width), jnp.float32),
            ]
        )
        + [four, four, four, slot, slot, pltpu.VMEM((2, rows // 2, width), small), slot]
        + [
            pltpu.VMEM((16, 128) if in_slots else (features, length), small),
            pltpu.VMEM(own.shape, small),
        ]
        + [pltpu.VMEM(array.shape, array.dtype) for array in beside]
        + ([pltpu.VMEM((features, grad.shape[0]), small)] if by_rows else [])
        + [
            pltpu.SemaphoreType.DMA((11,)),
            pltpu.SemaphoreType.DMA((31,)),
            pltpu.SemaphoreType.DMA((31,)),
        ],
        compiler_params=pltpu.CompilerParams(
            collective_id=identity_of("back" + str(plan), *operands),
            has_side_effects=True,
            vmem_limit_bytes=44 * 2**20,
        ),
        cost_estimate=BRIEF,
        name="back",
    )(*operands)


def exchange_kernel(source, target, x_ref, *refs):
    o_ref, local_sem, send_sem, recv_sem = refs[-4:]
    greet([member_at(peer) for peer in plane_peers()])
    exchange_steps(source, target, x_ref, o_ref, local_sem, mover(send_sem, recv_sem))()


def exchange(array, shape, source, target, kind, after=()):
    return kernel_call(
        functools.partial(exchange_kernel, source, target),
        out_shape=jax.ShapeDtypeStruct(shape, array.dtype),
        in_specs=[IN_HBM] * (1 + len(after)),
        out_specs=IN_HBM,
        scratch_shapes=[
            pltpu.SemaphoreType.DMA,
            pltpu.SemaphoreType.DMA((7,)),
            pltpu.SemaphoreType.DMA((7,)),
        ],
        compiler_params=pltpu.CompilerParams(
            collective_id=identity_of(kind, array, *after), has_side_effects=True
        ),
        cost_estimate=BRIEF,
        name="plane_exchange",
    )(array, *after)


def whole_rows(rows):
    place = member_rows(rows)
    return lambda ref, member: place(ref, member, 0, rows)


def whole_lanes(rows, width):
    place = member_lanes(width)
    return lambda ref, member: place(ref, member, 0, rows)


def to_frames(part):
    rows, width = part.shape[0], part.shape[1] // 8
    return exchange(part, (8 * rows, width), whole_lanes(rows, width), whole_rows(rows), "to frames")


def to_rows(part):
    rows, width = part.shape[0] // 8, part.shape[1]
    return exchange(part, (rows, 8 * width), whole_rows(rows), whole_lanes(rows, width), "to rows")


def block(ref, member):
    return ref.at[member]


def exchange_blocks(blocks, after=()):
    return exchange(blocks, blocks.shape, block, block, "blocks", after)


def lanes(ref, start, width):
    return ref.at[:, pl.ds(pl.multiple_of(start, 128), width)]


def sheet_part(start, width):
    return lambda ref, member: lanes(ref, start + member * width, width)


def block_part(start, width):
    return lambda ref, member: lanes(ref.at[member], start, width)


def feed_kernel(gu_ref, down_ref, w_ref, h_ref, g_ref, *refs):
    o_ref, y_ref, t_ref, weight, hidden, part, summed, grad, x_ref, held, *refs = refs[-18:]
    *bufs, local_sem, send_sem, recv_sem = refs
    width = down_ref.shape[-1]
    fetches = [
        pltpu.make_async_copy(w_ref, weight, local_sem.at[3]),
        pltpu.make_async_copy(h_ref, hidden, local_sem.at[5]),
        pltpu.make_async_copy(g_ref, grad, local_sem.at[6]),
    ]
    for fetch in fetches:
        fetch.start()
    plane = lax.axis_index("z")
    greet(
        [member_at(peer) for peer in plane_peers()]
        + [{"z": lax.rem(plane + k, 4)} for k in range(1, 4)]
    )
    depart, arrive, turned_back = turn_steps(
        x_ref, held, t_ref, local_sem.at[pl.ds(7, 2)], send_sem, recv_sem, 31
    )
    fetches[2].wait()
    x_ref[...] = grad[...].T.astype(x_ref.dtype)
    finish = []
    for k, (ref, start) in enumerate(((gu_ref, 0), (gu_ref, width), (down_ref, 0))):
        source, target = block_part(start, width), sheet_part(8 * k * width, width)
        copy = mover(send_sem, recv_sem, 7 * k)
        finish.append(exchange_steps(source, target, ref, o_ref, local_sem.at[k], copy))
    for fetch in fetches[:2]:
        fetch.wait()

    @pl.loop(0, part.shape[0] // 256)
    def _(i):
        at = pl.ds(pl.multiple_of(i * 256, 256), 256)
        for j in range(0, part.shape[1], 256):
            product = jnp.dot(
                weight[at, :], hidden[:, j : j + 256], preferred_element_type=jnp.float32
            )
            part[at, j : j + 256] = product.astype(part.dtype)

    cores, chips, relays, ended = scatter_steps(
        member_lanes(y_ref.shape[1]), part, bufs, mover(send_sem, recv_sem, 21)
    )
    cores()
    chips()
    relays()
    depart()
    summed[...] = ended()
    kept = pltpu.make_async_copy(summed, y_ref, local_sem.at[4])
    kept.start()
    arrive()
    for end in finish:
        end()
    kept.wait()
    turned_back()


def feed(gu, down, weight, hidden, grad, after=()):
    rows, length = weight.shape[0], hidden.shape[1]
    width = length // 8
    return kernel_call(
        feed_kernel,
        out_shape=(
            jax.ShapeDtypeStruct((gu.shape[1], 24 * down.shape[-1]), gu.dtype),
            jax.ShapeDtypeStruct((rows, width), jnp.float32),
            jax.ShapeDtypeStruct((width, rows), jnp.bfloat16),
        ),
        in_specs=[IN_HBM] * (5 + len(after)),
        out_specs=(IN_HBM,) * 3,
        scratch_shapes=[
            pltpu.VMEM(weight.shape, weight.dtype),
            pltpu.VMEM(hidden.shape, hidden.dtype),
            pltpu.VMEM((rows, length), jnp.bfloat16),
            pltpu.VMEM((rows, width), jnp.float32),
            pltpu.VMEM((rows, width), jnp.float32),
            pltpu.VMEM((width, rows), jnp.bfloat16),
            pltpu.VMEM((width, rows), jnp.bfloat16),
        ]
        + scatter_bufs(rows, width)
        + [
            pltpu.SemaphoreType.DMA((9,)),
            pltpu.SemaphoreType.DMA((39,)),
            pltpu.SemaphoreType.DMA((39,)),
        ],
        compiler_params=pltpu.CompilerParams(
            collective_id=identity_of("feed", gu, down, weight, *after),
            has_side_effects=True,
            vmem_limit_bytes=28 * 2**20,
        ),
        cost_estimate=BRIEF,
        name="feed",
    )(gu, down, weight, hidden, grad, *after)


def opening_kernel(
    latents_ref,
    cotangent_ref,
    small_ref,
    text_ref,
    sheet_ref,
    t_ref,
    all_ref,
    mine_ref,
    one_ref,
    x_ref,
    held,
    columns,
    one,
    local_sem,
    send_sem,
    recv_sem,
):
    features = latents_ref.shape[1]
    part, text = D // 8, CTXW // 8
    tail = 6 * D + 3 * FF
    fetches = [
        pltpu.make_async_copy(latents_ref, x_ref.at[:, :features], local_sem.at[5]),
        pltpu.make_async_copy(cotangent_ref, x_ref.at[:, features:], local_sem.at[6]),
        pltpu.make_async_copy(
            sheet_ref.at[:, : 6 * D], columns.at[:, : 6 * D], local_sem.at[7]
        ),
        pltpu.make_async_copy(
            sheet_ref.at[:, tail : tail + 2 * CTXW], columns.at[:, 6 * D :], local_sem.at[8]
        ),
    ]
    for fetch in fetches:
        fetch.start()
    group, core, across, along = near()
    member = group * 2 + core
    plane = lax.axis_index("z")
    step = x_ref.shape[0] // 4
    text_rows = mine_ref.shape[0]
    teacher = jnp.logical_and(group == plane, core == 0)

    def frames(ref, j):
        return ref.at[pl.ds(pl.multiple_of(j * step, 16), step), :]

    peers = plane_peers()
    line = [lax.rem(plane + k, 4) for k in range(1, 4)]
    greet([member_at(peer) for peer in peers] + [{"z": there} for there in line])

    fetches[0].wait()
    fetches[1].wait()

    near_copy = mover(send_sem, recv_sem)
    line_copy = mover(send_sem, recv_sem, 7)
    small_local = pltpu.make_async_copy(small_ref, all_ref.at[plane, member], local_sem.at[0])
    small_local.start()
    first = [
        near_copy(k, small_ref, all_ref.at[plane, member], member_at(peer))
        for k, peer in enumerate(peers)
    ]
    for moving in first:
        moving.start()

    others = [across, along, across + along - group]
    keep = pltpu.make_async_copy(frames(x_ref, group), frames(held, group), local_sem.at[1])
    keep.start()

    def piece(ref, j, a):
        at = pl.ds(pl.multiple_of(j * step, 16), step)
        return ref.at[at, a * features : (a + 1) * features]

    def spread(owner, landing, a):
        return pltpu.make_async_remote_copy(
            src_ref=piece(x_ref, owner, a),
            dst_ref=piece(held, landing, a),
            send_sem=send_sem.at[(10, 36)[a] + owner],
            recv_sem=recv_sem.at[(10, 36)[a] + landing],
            device_id={"dp": owner},
            device_id_type=MESH_ID,
        )

    for a in range(2):
        for owner in others:
            spread(owner, group, a).start()

    def rise(row, a):
        return pltpu.make_async_remote_copy(
            src_ref=piece(held, row, a),
            dst_ref=piece(t_ref, plane, a),
            send_sem=send_sem.at[(28, 32)[a] + row],
            recv_sem=recv_sem.at[(28, 32)[a] + plane],
            device_id={"z": row},
            device_id_type=MESH_ID,
        )

    stay = [
        pltpu.make_async_copy(piece(held, plane, a), piece(t_ref, plane, a), local_sem.at[(4, 9)[a]])
        for a in range(2)
    ]

    def pass_on(row, a):
        pl.when(row == plane)(stay[a].start)
        pl.when(row != plane)(rise(row, a).start)

    keep.wait()
    for a in range(2):
        pass_on(group, a)

    fetches[2].wait()
    fetches[3].wait()

    def move(m, at, start, width):
        one[m, :, at : at + width] = columns[:, start : start + width].astype(one.dtype)

    for m in range(8):
        for k in range(6):
            move(m, (4 * part if k < 3 else -3 * part) + k * part, k * D + m * part, part)
        for k in range(2):
            move(m, 3 * part + k * text, 6 * D + k * CTXW + m * text, text)
    for owner in others:
        spread(owner, owner, 0).wait_recv()
        pass_on(owner, 0)
    weights_done = exchange_steps(
        block, block, one, one_ref, local_sem.at[2], mover(send_sem, recv_sem, 14)
    )

    def text_copy(k, peer):
        return pltpu.make_async_remote_copy(
            src_ref=text_ref.at[pl.ds(pl.multiple_of(peer * text_rows, 16), text_rows), :],
            dst_ref=mine_ref,
            send_sem=send_sem.at[21 + k],
            recv_sem=recv_sem.at[21],
            device_id=member_at(peer),
            device_id_type=MESH_ID,
        )

    own_text = text_ref.at[pl.ds(pl.multiple_of(member * text_rows, 16), text_rows), :]
    text_local = pltpu.make_async_copy(own_text, mine_ref, local_sem.at[3])

    @pl.when(teacher)
    def _():
        text_local.start()
        for k, peer in enumerate(peers):
            text_copy(k, peer).start()

    for owner in others:
        spread(owner, owner, 1).wait_recv()
        pass_on(owner, 1)

    for k in range(7):
        landed = all_ref.at[plane, lax.rem(member + 7 - k, 8)]
        near_copy(k, landed, landed, member_at(peers[k])).wait_recv()
    small_local.wait()
    second = [
        line_copy(k, all_ref.at[plane], all_ref.at[plane], {"z": there})
        for k, there in enumerate(line)
    ]
    for moving in second:
        moving.start()
    for k in range(3):
        landed = all_ref.at[lax.rem(plane + 3 - k, 4)]
        line_copy(k, landed, landed, {"z": line[k]}).wait_recv()

    for a in range(2):
        for there in line:
            landed = piece(t_ref, there, a)
            pltpu.make_async_remote_copy(
                src_ref=landed,
                dst_ref=landed,
                send_sem=send_sem.at[(28, 32)[a] + there],
                recv_sem=recv_sem.at[(28, 32)[a] + there],
                device_id={"z": there},
                device_id_type=MESH_ID,
            ).wait_recv()
        stay[a].wait()
    weights_done()

    @pl.when(teacher)
    def _():
        text_local.wait()
        for k, peer in enumerate(peers):
            text_copy(k, peer).wait_send()

    @pl.when(jnp.logical_not(teacher))
    def _():
        text_copy(0, peers[0]).wait_recv()

    for moving in first + second:
        moving.wait_send()
    for a in range(2):
        for owner in others:
            spread(owner, group, a).wait_send()
        for there in line:
            rise(there, a).wait_send()


def opening(latents, cotangent, small, text, sheet):
    frames, features = latents.shape
    local = (frames, 2 * features)
    one = (8, sheet.shape[0], (6 * D + 2 * CTXW) // 8)
    low = jnp.bfloat16
    return kernel_call(
        opening_kernel,
        out_shape=(
            jax.ShapeDtypeStruct(local, low),
            jax.ShapeDtypeStruct((4, 8) + small.shape, small.dtype),
            jax.ShapeDtypeStruct((text.shape[0] // 8, text.shape[1]), text.dtype),
            jax.ShapeDtypeStruct(one, low),
        ),
        in_specs=[IN_HBM] * 5,
        out_specs=(IN_HBM,) * 4,
        scratch_shapes=[
            pltpu.VMEM(local, low),
            pltpu.VMEM(local, low),
            pltpu.VMEM((sheet.shape[0], 6 * D + 2 * CTXW), jnp.float32),
            pltpu.VMEM(one, low),
            pltpu.SemaphoreType.DMA((10,)),
            pltpu.SemaphoreType.DMA((40,)),
            pltpu.SemaphoreType.DMA((40,)),
        ],
        compiler_params=pltpu.CompilerParams(
            collective_id=identity_of("opening", sheet),
            has_side_effects=True,
            vmem_limit_bytes=16 * 2**20,
        ),
        cost_estimate=BRIEF,
        name="opening",
    )(latents, cotangent, small, text, sheet)


def first_gather_kernel(
    x_ref, y_ref, sheet_ref, ox_ref, oy_ref, gu_ref, down_ref, local_sem, send_sem, recv_sem
):
    place = member_lanes(x_ref.shape[1])
    width = FF // 8
    greet([member_at(peer) for peer in plane_peers()])
    finish = [
        gather_steps(place, x_ref, ox_ref, local_sem.at[0], mover(send_sem, recv_sem)),
        gather_steps(place, y_ref, oy_ref, local_sem.at[1], mover(send_sem, recv_sem, 14)),
    ]
    for k, (ref, start) in enumerate(((gu_ref, 0), (gu_ref, width), (down_ref, 0))):
        source, target = sheet_part(6 * D + k * FF, width), block_part(start, width)
        copy = mover(send_sem, recv_sem, 28 + 7 * k)
        finish.append(exchange_steps(source, target, sheet_ref, ref, local_sem.at[2 + k], copy))
    for end in finish:
        end()


def first_gather(shard, other, sheet):
    rows, width = shard.shape
    whole = jax.ShapeDtypeStruct((rows, 8 * width), shard.dtype)
    return kernel_call(
        first_gather_kernel,
        out_shape=(
            whole,
            whole,
            jax.ShapeDtypeStruct((8, sheet.shape[0], FF // 4), sheet.dtype),
            jax.ShapeDtypeStruct((8, sheet.shape[0], FF // 8), sheet.dtype),
        ),
        in_specs=[IN_HBM] * 3,
        out_specs=(IN_HBM,) * 4,
        scratch_shapes=[
            pltpu.SemaphoreType.DMA((5,)),
            pltpu.SemaphoreType.DMA((49,)),
            pltpu.SemaphoreType.DMA((49,)),
        ],
        compiler_params=pltpu.CompilerParams(
            collective_id=identity_of("first gather", shard, sheet), has_side_effects=True
        ),
        cost_estimate=BRIEF,
        name="first_gather",
    )(shard, other, sheet)


def turn_steps(x_ref, held, t_ref, local_sem, send_sem, recv_sem, first):
    group, core, across, along = near()
    plane = lax.axis_index("z")
    step = x_ref.shape[0] // 4
    groups = [across, along, across + along - group]
    inner = lax.div(plane * (3 - plane), 2)
    two_off, mirrored = lax.rem(plane + 2, 4), 3 - plane
    line = [
        plane + 1 - 2 * lax.rem(plane, 2),
        inner * mirrored + (1 - inner) * two_off,
        inner * two_off + (1 - inner) * mirrored,
    ]

    def frames(ref, j):
        return ref.at[pl.ds(pl.multiple_of(j * step, 16), step), :]

    def copy(source, target, sent, landed, peer):
        return pltpu.make_async_remote_copy(
            src_ref=source,
            dst_ref=target,
            send_sem=send_sem.at[first + sent],
            recv_sem=recv_sem.at[first + landed],
            device_id=peer,
            device_id_type=MESH_ID,
        )

    def along_line(there):
        return copy(frames(x_ref, there), frames(held, plane), there, plane, {"z": there})

    def onward(owner):
        return copy(
            frames(held, owner), frames(t_ref, group), 4 + owner, 4 + group, {"dp": owner}
        )

    own = pltpu.make_async_copy(frames(x_ref, plane), frames(held, plane), local_sem.at[0])
    keep = pltpu.make_async_copy(frames(held, group), frames(t_ref, group), local_sem.at[1])

    def pass_on(owner):
        pl.when(owner == group)(keep.start)
        pl.when(owner != group)(onward(owner).start)

    def start():
        own.start()
        for there in line:
            along_line(there).start()
        own.wait()
        pass_on(plane)

    def arrive():
        for origin in line:
            at = frames(held, origin)
            copy(at, at, origin, origin, {"z": origin}).wait_recv()
            pass_on(origin)

    def finish():
        for origin in groups:
            at = frames(t_ref, origin)
            copy(at, at, 4 + origin, 4 + origin, {"dp": origin}).wait_recv()
        keep.wait()
        for there in line:
            along_line(there).wait_send()
        for owner in groups:
            onward(owner).wait_send()

    return start, arrive, finish


def prepare_kernel(order_ref, y_ref, base_ref, gu_ref, down_ref, two_ref, x_ref, q_ref, y):
    reorder_blocks(y_ref, y, lambda b: order_ref[1, b])
    x_ref[...] = (base_ref[...] + y[...]).T.astype(x_ref.dtype)
    q_ref[...] = jnp.full(q_ref.shape, square_sum((gu_ref, down_ref, two_ref)), jnp.float32)


def prepare(orders, y, base, gu, down, two):
    features, width = base.shape
    return kernel_call(
        prepare_kernel,
        out_shape=(
            jax.ShapeDtypeStruct((width, features), jnp.bfloat16),
            jax.ShapeDtypeStruct((8, 128), jnp.float32),
        ),
        in_specs=[IN_SMEM] + [IN_VMEM] * 5,
        out_specs=(IN_VMEM,) * 2,
        scratch_shapes=[pltpu.VMEM(base.shape, jnp.float32)],
        compiler_params=pltpu.CompilerParams(vmem_limit_bytes=16 * 2**20),
        name="prepare",
    )(orders, y.reshape(orders.shape[1], -1, width), base, gu, down, two)


def square_sum(refs):
    total = jnp.zeros((), jnp.float32)
    for ref in refs:
        line_sum = jnp.zeros((1, ref.shape[2]), jnp.float32)
        for m in range(8):
            line_sum += jnp.sum(jnp.square(wide(ref.at[m])), axis=0, keepdims=True)
        total += jnp.sum(line_sum)
    return total


def closing_kernel(
    x_ref,
    p_ref,
    w_ref,
    g_ref,
    _,
    t_ref,
    o_ref,
    s_ref,
    all_ref,
    held,
    tall,
    q_ref,
    one,
    local_sem,
    send_sem,
    recv_sem,
):
    fetch = pltpu.make_async_copy(w_ref, one, local_sem.at[0])
    fetch.start()
    group, core, _, _ = near()
    member = group * 2 + core
    plane = lax.axis_index("z")
    turned_line = [lax.rem(plane + k, 4) for k in range(1, 4)]
    peers = plane_peers()
    greet([member_at(peer) for peer in peers] + [{"z": there} for there in turned_line])
    start, arrive, finish = turn_steps(
        x_ref, held, t_ref, local_sem.at[pl.ds(1, 2)], send_sem, recv_sem, 0
    )
    gain_line = mover(send_sem, recv_sem, 23)
    gain_plane = mover(send_sem, recv_sem, 26)
    square_plane = mover(send_sem, recv_sem, 33)
    square_line = mover(send_sem, recv_sem, 40)
    back_line = [lax.rem(plane + 3 - k, 4) for k in range(3)]
    gain_local = pltpu.make_async_copy(g_ref, tall.at[plane], local_sem.at[3])
    gain_local.start()
    sent = [
        gain_line(k, g_ref, tall.at[plane], {"z": there}) for k, there in enumerate(turned_line)
    ]
    for moving in sent:
        moving.start()
    start()
    fetch.wait()
    weights_done = exchange_steps(
        block, block, one, o_ref, local_sem.at[5], mover(send_sem, recv_sem, 16)
    )
    q_ref[...] = p_ref[...] + square_sum((one,))
    square_local = pltpu.make_async_copy(q_ref, all_ref.at[plane, member], local_sem.at[6])
    square_local.start()
    shown = [
        square_plane(k, q_ref, all_ref.at[plane, member], member_at(peer))
        for k, peer in enumerate(peers)
    ]
    for moving in shown:
        moving.start()
    gain_local.wait()
    for k, origin in enumerate(back_line):
        gain_line(k, tall.at[origin], tall.at[origin], {"z": origin}).wait_recv()
    tall[4] = tall[0] + tall[1] + tall[2] + tall[3]
    gain_keep = pltpu.make_async_copy(tall.at[4], s_ref.at[member], local_sem.at[7])
    gain_keep.start()
    given = [
        gain_plane(k, tall.at[4], s_ref.at[member], member_at(peer)) for k, peer in enumerate(peers)
    ]
    for moving in given:
        moving.start()
    square_local.wait()
    for k in range(7):
        shown_here = all_ref.at[plane, lax.rem(member + 7 - k, 8)]
        square_plane(k, shown_here, shown_here, member_at(peers[k])).wait_recv()
    for k, there in enumerate(turned_line):
        shown.append(square_line(k, all_ref.at[plane], all_ref.at[plane], {"z": there}))
        shown[-1].start()
    arrive()
    finish()
    weights_done()
    gain_keep.wait()
    for k in range(7):
        given_here = s_ref.at[lax.rem(member + 7 - k, 8)]
        gain_plane(k, given_here, given_here, member_at(peers[k])).wait_recv()
    for k, origin in enumerate(back_line):
        square_line(k, all_ref.at[origin], all_ref.at[origin], {"z": origin}).wait_recv()
    for moving in sent + given + shown:
        moving.wait_send()

def closing(local, squares, one, gains, after):
    return kernel_call(
        closing_kernel,
        out_shape=(
            jax.ShapeDtypeStruct(local.shape, local.dtype),
            jax.ShapeDtypeStruct(one.shape, one.dtype),
            jax.ShapeDtypeStruct((8,) + gains.shape, gains.dtype),
            jax.ShapeDtypeStruct((4, 8) + squares.shape, jnp.float32),
        ),
        in_specs=[IN_VMEM, IN_VMEM] + [IN_HBM] * 3,
        out_specs=(IN_VMEM,) * 4,
        scratch_shapes=[
            pltpu.VMEM(local.shape, local.dtype),
            pltpu.VMEM((5,) + gains.shape, gains.dtype),
            pltpu.VMEM(squares.shape, jnp.float32),
            pltpu.VMEM(one.shape, one.dtype),
            pltpu.SemaphoreType.DMA((8,)),
            pltpu.SemaphoreType.DMA((43,)),
            pltpu.SemaphoreType.DMA((43,)),
        ],
        compiler_params=pltpu.CompilerParams(
            collective_id=identity_of("closing", one),
            has_side_effects=True,
            vmem_limit_bytes=8 * 2**20,
        ),
        cost_estimate=BRIEF,
        name="closing",
    )(local, squares, one, gains, after)


def turned(values, cosine, sine_table):
    half = HEAD // 2
    first_half, second_half = values[:half], values[half:]
    return jnp.concatenate(
        [
            first_half * cosine - second_half * sine_table,
            second_half * cosine + first_half * sine_table,
        ],
        axis=0,
    )


def attend_kernel(
    w_ref,
    h_ref,
    cos_ref,
    sin_ref,
    seg_ref,
    column_ref,
    part_out,
    p_out,
    o_ref,
    weight,
    frames,
    joint_ref,
    part_ref,
    p_ref,
    sems,
):
    heads, length = joint_ref.shape[1], joint_ref.shape[3]
    span = heads * HEAD
    tiles = length // 256
    fetches = [pltpu.make_async_copy(w_ref, weight, sems.at[0])]
    fetches += [
        pltpu.make_async_copy(
            h_ref.at[:, i * 256 : (i + 1) * 256], frames.at[:, i * 256 : (i + 1) * 256], sems.at[1 + i]
        )
        for i in range(tiles)
    ]
    for fetch in fetches:
        fetch.start()
    cosine, sine_table = cos_ref[...], sin_ref[...]
    fetches[0].wait()
    by_row = [weight[:, (4 + k) * span : (5 + k) * span].T for k in range(3)]
    for i in range(tiles):
        fetches[1 + i].wait()
        at = slice(i * 256, (i + 1) * 256)
        for k in range(3):
            part = jnp.dot(by_row[k], frames[:, at], preferred_element_type=jnp.float32)
            for h in range(heads):
                joint_ref[k, h, :, at] = part[h * HEAD : (h + 1) * HEAD]

    kept = []
    for h in range(heads):
        queries = turned(joint_ref[0, h], cosine, sine_table)
        part_ref[0, h] = queries.astype(part_ref.dtype)
        keys = turned(joint_ref[1, h], cosine, sine_table)
        part_ref[1, h] = keys.astype(part_ref.dtype)
        part_ref[2, h] = joint_ref[2, h].astype(part_ref.dtype)
        by_key = keys.T.astype(part_ref.dtype)

        @pl.loop(0, tiles)
        def _(i, h=h, by_key=by_key):
            at = pl.ds(pl.multiple_of(i * 256, 256), 256)
            scores = jnp.dot(
                by_key, part_ref[0, h, :, at], preferred_element_type=jnp.float32
            ) * (HEAD**-0.5)
            scores = jnp.where(column_ref[...] == seg_ref[:, at], scores, MASKED_SCORE)
            exponent = jnp.exp(scores - jnp.max(scores, axis=0, keepdims=True))
            probs = exponent * (1.0 / jnp.sum(exponent, axis=0, keepdims=True))
            p_ref[h, :, at] = probs.astype(p_ref.dtype)
            out = jnp.dot(part_ref[2, h], p_ref[h, :, at], preferred_element_type=jnp.float32)
            o_ref[h * HEAD : (h + 1) * HEAD, at] = out.astype(o_ref.dtype)

        kept.append(pltpu.make_async_copy(p_ref.at[h], p_out.at[h], sems.at[1 + tiles + h]))
        kept[-1].start()
    kept.append(pltpu.make_async_copy(part_ref, part_out, sems.at[1 + tiles + heads]))
    kept[-1].start()
    for keep in kept:
        keep.wait()


def attend(weight, frames, cosine, sine_table, segments):
    heads, length = D // HEAD // 8, frames.shape[1]
    joint = (3, heads, HEAD, length)
    small = jnp.bfloat16
    return kernel_call(
        attend_kernel,
        out_shape=(
            jax.ShapeDtypeStruct(joint, small),
            jax.ShapeDtypeStruct((heads, length, length), small),
            jax.ShapeDtypeStruct((heads * HEAD, length), small),
        ),
        in_specs=[IN_HBM] * 2 + [IN_VMEM] * 4,
        out_specs=(IN_HBM, IN_HBM, IN_VMEM),
        scratch_shapes=[
            pltpu.VMEM(weight.shape, small),
            pltpu.VMEM(frames.shape, small),
            pltpu.VMEM(joint, jnp.float32),
            pltpu.VMEM(joint, small),
            pltpu.VMEM((heads, length, length), small),
            pltpu.SemaphoreType.DMA((2 + length // 256 + heads,)),
        ],
        compiler_params=pltpu.CompilerParams(vmem_limit_bytes=36 * 2**20),
        name="attend",
    )(weight, frames, cosine, sine_table, segments[None, :], segments[:, None])


def cross_kernel(w_ref, h_ref, kv_ref, cq_ref, p_ref, o_ref, weight, frames, sems):
    heads, text, length = p_ref.shape
    span = heads * HEAD
    tiles = length // 256
    fetches = [pltpu.make_async_copy(w_ref.at[:, 128:384], weight, sems.at[0])]
    fetches += [
        pltpu.make_async_copy(
            h_ref.at[:, i * 256 : (i + 1) * 256], frames.at[:, i * 256 : (i + 1) * 256], sems.at[1 + i]
        )
        for i in range(tiles)
    ]
    for fetch in fetches:
        fetch.start()
    keys = [
        wide(kv_ref.at[h * HEAD : (h + 1) * HEAD, :text]).T.astype(cq_ref.dtype)
        for h in range(heads)
    ]
    fetches[0].wait()
    by_row = weight[:, span - 128 : 2 * span - 128].T
    for i in range(tiles):
        fetches[1 + i].wait()
        at = slice(i * 256, (i + 1) * 256)
        cq_ref[:, at] = jnp.dot(
            by_row, frames[:, at], preferred_element_type=jnp.float32
        ).astype(cq_ref.dtype)
        for h in range(heads):
            of = slice(h * HEAD, (h + 1) * HEAD)
            scores = jnp.dot(keys[h], cq_ref[of, at], preferred_element_type=jnp.float32) * (
                HEAD**-0.5
            )
            exponent = jnp.exp(scores - jnp.max(scores, axis=0, keepdims=True))
            probs = exponent * (1.0 / jnp.sum(exponent, axis=0, keepdims=True))
            p_ref[h, :, at] = probs.astype(p_ref.dtype)
            out = jnp.dot(
                kv_ref[of, text:], p_ref[h, :, at], preferred_element_type=jnp.float32
            )
            o_ref[of, at] = out.astype(o_ref.dtype)


def cross(weight, frames, text_kv):
    rows, length = text_kv.shape[0], frames.shape[1]
    text, small = text_kv.shape[1] // 2, jnp.bfloat16
    return kernel_call(
        cross_kernel,
        out_shape=(
            jax.ShapeDtypeStruct((rows, length), small),
            jax.ShapeDtypeStruct((rows // HEAD, text, length), small),
            jax.ShapeDtypeStruct((rows, length), small),
        ),
        in_specs=[IN_HBM, IN_HBM, IN_VMEM],
        out_specs=(IN_VMEM,) * 3,
        scratch_shapes=[
            pltpu.VMEM((weight.shape[0], 256), small),
            pltpu.VMEM(frames.shape, small),
            pltpu.SemaphoreType.DMA((1 + length // 256,)),
        ],
        compiler_params=pltpu.CompilerParams(vmem_limit_bytes=16 * 2**20),
        name="cross",
    )(weight, frames, text_kv)


def cross_back_kernel(cq_ref, p_ref, kv_ref, grad_ref, dq_ref, dkv_ref):
    heads, text, length = p_ref.shape
    scale = HEAD**-0.5
    for h in range(heads):
        of = slice(h * HEAD, (h + 1) * HEAD)
        by_key = wide(kv_ref.at[of, text:]).T.astype(cq_ref.dtype)
        grad_out = grad_ref[of, :]
        grad_probs = jnp.dot(by_key, grad_out, preferred_element_type=jnp.float32)
        probs = wide(p_ref.at[h])
        weighted = jnp.sum(probs * grad_probs, axis=0, keepdims=True)
        grad_scores = (probs * (grad_probs - weighted)).astype(cq_ref.dtype)
        dq_ref[of, :] = (
            jnp.dot(kv_ref[of, :text], grad_scores, preferred_element_type=jnp.float32) * scale
        ).astype(dq_ref.dtype)
        dkv_ref[of, :text] = (contract_last(cq_ref[of, :], grad_scores) * scale).astype(
            dkv_ref.dtype
        )
        dkv_ref[of, text:] = contract_last(grad_out, p_ref[h]).astype(dkv_ref.dtype)


def cross_back(cross_q, probs, text_kv, grad):
    return kernel_call(
        cross_back_kernel,
        out_shape=(
            jax.ShapeDtypeStruct(cross_q.shape, cross_q.dtype),
            jax.ShapeDtypeStruct(text_kv.shape, text_kv.dtype),
        ),
        in_specs=[IN_VMEM] * 4,
        out_specs=(IN_VMEM,) * 2,
        compiler_params=pltpu.CompilerParams(vmem_limit_bytes=16 * 2**20),
        name="cross_back",
    )(cross_q, probs, text_kv, grad)


def attend_back_kernel(
    part_in, p_in, g_in, cos_ref, sin_ref, o_ref, part_ref, p_ref, grad_ref, dq_ref, dk_ref, dv_ref, sems
):
    heads, length = part_ref.shape[1], part_ref.shape[3]
    fetches = [
        pltpu.make_async_copy(part_in, part_ref, sems.at[0]),
        pltpu.make_async_copy(g_in, grad_ref, sems.at[1]),
    ]
    fetches += [
        pltpu.make_async_copy(p_in.at[h], p_ref.at[h], sems.at[2 + h]) for h in range(heads)
    ]
    for fetch in fetches:
        fetch.start()
    cosine, sine_table = cos_ref[...], -sin_ref[...]
    scale = HEAD**-0.5
    fetches[0].wait()
    fetches[1].wait()
    for h in range(heads):
        of = slice(h * HEAD, (h + 1) * HEAD)
        by_key = wide(part_ref.at[2, h]).T.astype(part_ref.dtype)
        dk_ref[...] = jnp.zeros_like(dk_ref)
        dv_ref[...] = jnp.zeros_like(dv_ref)
        fetches[2 + h].wait()

        @pl.loop(0, length // 256)
        def _(i, h=h, of=of, by_key=by_key):
            at = pl.ds(pl.multiple_of(i * 256, 256), 256)
            grad_out = grad_ref[of, at]
            grad_probs = jnp.dot(by_key, grad_out, preferred_element_type=jnp.float32)
            low_probs = p_ref[h, :, at]
            probs = low_probs.astype(jnp.float32)
            weighted = jnp.sum(probs * grad_probs, axis=0, keepdims=True)
            grad_scores = (probs * (grad_probs - weighted)).astype(part_ref.dtype)
            dq_ref[:, at] = jnp.dot(
                part_ref[1, h], grad_scores, preferred_element_type=jnp.float32
            )
            dk_ref[...] += contract_last(part_ref[0, h, :, at], grad_scores)
            dv_ref[...] += contract_last(grad_out, low_probs)

        span = heads * HEAD
        grad_queries = turned(dq_ref[...] * scale, cosine, sine_table)
        grad_keys = turned(dk_ref[...] * scale, cosine, sine_table)
        o_ref[of, :] = grad_queries.astype(o_ref.dtype)
        o_ref[span + of.start : span + of.stop, :] = grad_keys.astype(o_ref.dtype)
        o_ref[2 * span + of.start : 2 * span + of.stop, :] = dv_ref[...].astype(o_ref.dtype)


def attend_back(parts, probs, grad, cosine, sine_table):
    _, heads, _, length = parts.shape
    return kernel_call(
        attend_back_kernel,
        out_shape=jax.ShapeDtypeStruct((3 * heads * HEAD, length), jnp.bfloat16),
        in_specs=[IN_HBM] * 3 + [IN_VMEM] * 2,
        out_specs=IN_VMEM,
        scratch_shapes=[pltpu.VMEM(array.shape, array.dtype) for array in (parts, probs, grad)]
        + [pltpu.VMEM((HEAD, length), jnp.float32)] * 3
        + [pltpu.SemaphoreType.DMA((2 + heads,))],
        compiler_params=pltpu.CompilerParams(vmem_limit_bytes=32 * 2**20),
        name="attend_back",
    )(parts, probs, grad, cosine, sine_table)


def update_kernel(
    block_ref,
    rate_ref,
    one_ref,
    two_ref,
    feed_ref,
    all_ref,
    gain_ref,
    output_ref,
    latent_ref,
    sheet_ref,
    first_ref,
    second_ref,
    grad_out,
    first_out,
    second_out,
    sheet_out,
    copy_out,
    norm_out,
    gain_out,
    output_out,
    latent_out,
    grad,
    gain,
    scale,
):
    step = pl.program_id(0)
    part = D // 8
    text = CTXW // 8

    @pl.when(step == 0)
    def _():
        summed = jnp.sum(gain_ref[...], axis=0)
        rows = grad.shape[0]
        here = lax.broadcasted_iota(jnp.int32, (rows, D), 1) == (
            lax.broadcasted_iota(jnp.int32, (rows, D), 0) + block_ref[0] * rows
        )
        gain[...] = lax.dot_general(
            here.astype(jnp.float32),
            summed,
            (((1,), (1,)), ((), ())),
            precision=HIGHEST,
            preferred_element_type=jnp.float32,
        )
        norm = jnp.sqrt(jnp.sum(all_ref[:, :, 0:1, 0:1]) + jnp.sum(summed * summed))
        norm_out[0] = norm
        scale[0] = 1.0 / jnp.maximum(norm, 1.0)
        gain_out[...] = gain[...] * scale[0]
        output_out[...] = output_ref[...]
        latent_out[...] = wide(latent_ref)

    for k in range(6):

        @pl.when(step == k // 2)
        def _(k=k):
            ref, start = (one_ref, k * part) if k < 3 else (two_ref, (k - 3) * part)
            for m in range(8):
                at = (k % 2) * D + m * part
                grad[:, at : at + part] = wide(ref.at[m, :, start : start + part])

    @pl.when(jnp.logical_and(step >= 3, step < 9))
    def _():
        grad[...] = wide(feed_ref)

    @pl.when(step == 9)
    def _():
        for m in range(8):
            for k in range(2):
                start = 3 * part + k * text
                at = k * CTXW + m * text
                grad[:, at : at + text] = wide(two_ref.at[m, :, start : start + text])
        grad[:, D : D + 8] = gain[...]

    for half in range(2):
        at = slice(half * D, (half + 1) * D)
        clipped = grad[:, at] * scale[0]
        sheet = sheet_ref[:, at]
        first_new = BETA_ONE * first_ref[:, at] + (1.0 - BETA_ONE) * clipped
        second_new = BETA_TWO * second_ref[:, at] + (1.0 - BETA_TWO) * clipped * clipped
        mean_hat = first_new * (1.0 / (1.0 - BETA_ONE**STEP))
        square_hat = second_new * (1.0 / (1.0 - BETA_TWO**STEP))
        sheet_new = sheet - rate_ref[2 * step + half] * (
            mean_hat / (jnp.sqrt(square_hat) + EPS_ADAM) + WEIGHT_DECAY * sheet
        )
        grad_out[:, at] = clipped
        first_out[:, at] = first_new
        second_out[:, at] = second_new
        sheet_out[:, at] = sheet_new
        copy_out[:, at] = sheet_new.astype(copy_out.dtype)


def sheet_update(
    block_index, length, one, two, feed_part, squares, gains, output, latent, sheet, first, second
):
    rows = sheet.shape[0]
    frames = output.shape
    rates = column_spread(length)[jnp.minimum(jnp.arange(20) * D, SHEET - 1)]
    column_block = pl.BlockSpec((rows, 2 * D), lambda i: (0, i))
    like = jax.ShapeDtypeStruct(sheet.shape, sheet.dtype)

    def whole(shape):
        return pl.BlockSpec(shape, lambda i: (0,) * len(shape))

    sheet, first, second, feed_part = (
        pltpu.with_memory_space_constraint(array, pltpu.HBM)
        for array in (sheet, first, second, feed_part)
    )
    return pl.pallas_call(
        update_kernel,
        grid=(10,),
        out_shape=(like, like, like, like, jax.ShapeDtypeStruct(sheet.shape, jnp.bfloat16))
        + (jax.ShapeDtypeStruct((1,), jnp.float32), jax.ShapeDtypeStruct((rows, 8), jnp.float32))
        + (
            jax.ShapeDtypeStruct(frames, jnp.bfloat16),
            jax.ShapeDtypeStruct(frames, jnp.float32),
        ),
        in_specs=[
            IN_SMEM,
            IN_SMEM,
            IN_VMEM,
            IN_VMEM,
            pl.BlockSpec((rows, 2 * D), lambda i: (0, jnp.clip(i - 3, 0, 5))),
            IN_VMEM,
            IN_VMEM,
            IN_VMEM,
            IN_VMEM,
            column_block,
            column_block,
            column_block,
        ],
        out_specs=(column_block,) * 5
        + (IN_SMEM, whole((rows, 8)), whole(frames), whole(frames)),
        scratch_shapes=[
            pltpu.VMEM((rows, 2 * D), jnp.float32),
            pltpu.VMEM((rows, 8), jnp.float32),
            pltpu.SMEM((1,), jnp.float32),
        ],
        compiler_params=pltpu.CompilerParams(vmem_limit_bytes=32 * 2**20),
        name="sheet_update",
    )(
        block_index,
        rates,
        one,
        two,
        feed_part,
        squares,
        gains,
        output,
        latent,
        sheet,
        first,
        second,
    )


def pick_blocks(blocks, order):
    return blocks.at[order].get(mode="promise_in_bounds")


def gather_line(mine, order):
    blocks = lax.all_gather(mine, "z", axis=0, tiled=True)
    return pick_blocks(blocks, order).reshape(-1, mine.shape[-1])


def gather_slots(mine):
    return lax.all_gather(mine, "z", axis=0, tiled=True).reshape(-1, mine.shape[-1])


def sort_blocks(array, order):
    blocks = array.reshape(order.shape[0], -1, array.shape[-1])
    return pick_blocks(blocks, order).reshape(array.shape)


def as_blocks(grad, order):
    return grad.reshape(order.shape[0], -1, grad.shape[-1])


def scatter_line(blocks):
    return lax.psum_scatter(blocks, "z", scatter_dimension=0, tiled=True)


def plane_plan(latents, context, clip_starts, buckets, owners, cotangent, sheet, first, second):
    groups = lax.axis_size("dp")
    planes = lax.axis_size("z")
    cores = lax.axis_size("core")
    members = groups * cores
    frames = latents.shape[1]
    length = frames * members
    rows = sheet.shape[0]
    blocks = owners.shape[0]
    head_count = D // HEAD // members
    span = D // members
    units = FF // members
    score_scale = HEAD ** (-0.5)
    tail_col = 6 * D + 3 * FF
    gain_col = tail_col + 2 * CTXW
    plane = lax.axis_index("z")

    group_ids = jnp.arange(blocks, dtype=jnp.int32)
    inverse = jnp.sum(
        jnp.where(owners[None, :] == group_ids[:, None], group_ids[None, :], 0), axis=1
    )
    slot = group_ids.reshape(groups, planes, cores).swapaxes(0, 1).reshape(-1)
    slot_of = jnp.sum(
        jnp.where(slot[None, :] == group_ids[:, None], group_ids[None, :], 0), axis=1
    )
    to_logical = jnp.take(slot_of, inverse)
    to_slots = jnp.take(owners, slot)

    orders = jnp.stack([to_slots, to_logical])
    small = jnp.concatenate(
        [
            jnp.pad(
                sheet[:, gain_col:].astype(jnp.bfloat16).astype(jnp.float32).T,
                ((0, 0), (0, 64 - rows)),
            ),
            jnp.pad(clip_starts.astype(jnp.float32), ((0, 7), (0, 64 - clip_starts.shape[1]))),
        ],
        axis=1,
    )
    both, small, text_mine, mine_one = opening(
        latents[0], cotangent[0], small, context[0].T, sheet
    )
    mine_one, later = lax.optimization_barrier((mine_one, sheet))
    low_sheet = later.astype(jnp.bfloat16)
    weight_one = gather_slots(mine_one)
    gains = pick_blocks(small[..., :rows].reshape(blocks, 8, rows), to_logical)
    gains = gains.swapaxes(1, 2).reshape(D, 8)
    starts = lax.dynamic_index_in_dim(
        small[0, :, 0, 64 : 64 + clip_starts.shape[1]], plane * cores, 0, False
    )
    starts = starts.astype(jnp.int32)

    bucket_ids = jnp.arange(NB, dtype=jnp.int32)
    bucket_pick = (bucket_ids == buckets[plane]).astype(jnp.float32)
    counts = jnp.sum((buckets[:, None] == bucket_ids[None, :]).astype(jnp.float32), axis=0)
    row_weight = buckets.shape[0] / (NB * jnp.sum(bucket_pick * counts))
    gain_one = gains[:, 0:1]
    gain_two = gains[:, 1:2]
    gain_three = gains[:, 2:3]
    time_gain = jnp.sum(gains[:, 3:] * bucket_pick[None, :], axis=1, keepdims=True)

    tokens = both[:, :D].astype(jnp.float32).T
    grad_out = both[:, D:].astype(jnp.float32).T * row_weight

    rest = frames // planes
    place = jnp.arange(length, dtype=jnp.int32).reshape(planes, cores, groups, rest)
    positions = place.transpose(2, 1, 0, 3).reshape(-1)
    segments = segment_ids(starts, positions)
    frequency = jnp.exp(
        -math.log(10000.0) * jnp.arange(HEAD // 2, dtype=jnp.float32) / (HEAD // 2)
    )
    angles = frequency[:, None] * positions.astype(jnp.float32)[None, :]
    cosine = jnp.cos(angles)
    sine_table = jnp.sin(angles)

    normed_one, inverse_one = norm_columns(tokens)
    scaled_one = gain_one * time_gain
    h_one, grad_ff, mine_gu, mine_down = first_gather(
        sort_blocks((normed_one * scaled_one).astype(jnp.bfloat16), to_slots),
        sort_blocks(grad_out.astype(jnp.bfloat16), to_slots),
        low_sheet,
    )
    weight_gu = gather_slots(mine_gu)
    line_down = gather_slots(mine_down)

    parts, probs, attn_out = attend(weight_one, h_one, cosine, sine_table, segments)
    attn_out, x_one, normed_two, inverse_two, h_two, text_kv = project(
        "sum",
        0,
        orders,
        attn_out,
        weight_one,
        tokens,
        gain_two,
        text_mine,
    )

    cross_q, cross_probs, cross_out = cross(weight_one, h_two, text_kv)
    cross_out, x_two, normed_three, inverse_three, h_three = project(
        "slots",
        2 * span,
        orders,
        cross_out,
        weight_one,
        x_one,
        gain_three,
    )

    gate_up = contract_rows(weight_gu, h_three)
    gate_pre = gate_up[:units]
    up_part = gate_up[units:]
    sigmoid_gate = jax.nn.sigmoid(gate_pre)
    silu_gate = gate_pre * sigmoid_gate
    hidden = (silu_gate * up_part).astype(jnp.bfloat16)

    grad_blocks_down = as_blocks(contract_last(grad_ff, hidden).astype(jnp.bfloat16), to_slots)
    weight_down, grad_blocks_down = lax.optimization_barrier((line_down, grad_blocks_down))
    sums_down = scatter_line(grad_blocks_down)
    grad_hidden = contract_rows(weight_down, grad_ff)
    grad_gate = grad_hidden * up_part * (sigmoid_gate * (1.0 + gate_pre * (1.0 - sigmoid_gate)))
    grad_up = grad_hidden * silu_gate
    grad_gu = jnp.concatenate([grad_gate, grad_up], axis=0).astype(jnp.bfloat16)
    grad_x_two, grad_weight_gu, sum_three, grad_cross = back(
        orders,
        weight_gu,
        grad_gu,
        h_three,
        (normed_three, inverse_three, gain_three, grad_out),
        send_rows=True,
        in_slots=True,
        after=[grad_blocks_down],
    )
    grad_blocks_gu = as_blocks(grad_weight_gu, to_slots)
    sums_gu = scatter_line(grad_blocks_gu)
    grad_cross_out, grad_weight_co = back(
        orders, weight_one, grad_cross, cross_out, column=2 * span
    )
    grad_cross_q, grad_text = cross_back(cross_q, cross_probs, text_kv, grad_cross_out)
    grad_x_one, grad_weight_cq, sum_two, grad_attn, grad_text = back(
        orders,
        weight_one,
        grad_cross_q,
        h_two,
        (normed_two, inverse_two, gain_two, grad_x_two),
        column=span,
        send_rows=True,
        text=grad_text,
        in_slots=True,
        after=[sums_down],
    )
    grad_attn_out, grad_weight_two = back(
        orders,
        weight_one,
        grad_attn,
        attn_out,
        beside=(grad_weight_cq, grad_weight_co, grad_text, text_mine),
    )
    grad_blocks_two = as_blocks(grad_weight_two, to_slots)
    sums_two = scatter_line(grad_blocks_two)
    grad_qkv = attend_back(parts, probs, grad_attn_out, cosine, sine_table)
    latent_grad, grad_weight_qkv, sum_one = back(
        orders,
        weight_one,
        grad_qkv,
        h_one,
        (normed_one, inverse_one, scaled_one, grad_x_one),
        column=4 * span,
        in_slots=True,
        after=[sums_gu],
    )
    grad_blocks_one = as_blocks(grad_weight_qkv, to_slots)
    sums_one = scatter_line(grad_blocks_one)
    sums_feed, ff_out, latent_grad = feed(
        sums_gu,
        sums_down,
        weight_down,
        hidden,
        latent_grad,
        [grad_blocks_one],
    )
    sum_one = sum_one[0:1]
    grad_gain_one = sum_one * time_gain.T
    grad_time = sum_one * gain_one.T
    gain_grads = jnp.concatenate(
        [
            grad_gain_one,
            sum_two[0:1],
            sum_three[0:1],
            bucket_pick[:, None] * grad_time,
        ],
        axis=0,
    )
    output, squares = prepare(orders, ff_out, x_two, sums_gu, sums_down, sums_two)
    sums_two = exchange_blocks(sums_two, [sums_feed])
    output, sums_one, gain_sums, squares = closing(
        output, squares, sums_one, gain_grads, sums_two
    )
    place = lax.axis_index("dp") * (planes * cores) + plane * cores + lax.axis_index("core")
    (
        clipped,
        first_new,
        second_new,
        sheet_new,
        sheet_copy,
        grad_norm,
        gain_grad,
        output,
        latent_grad,
    ) = sheet_update(
        lax.dynamic_slice_in_dim(owners, place, 1),
        length,
        sums_one,
        sums_two,
        sums_feed,
        squares,
        gain_sums,
        output,
        latent_grad,
        sheet,
        first,
        second,
    )
    return (
        output[None],
        latent_grad[None],
        grad_norm[0],
        clipped,
        gain_grad,
        first_new,
        second_new,
        sheet_new,
        sheet_copy,
    )


def solution(mesh):
    groups, seq_count = mesh.shape["dp"], mesh.shape["seq"]
    by_plane = groups == 4 and seq_count == 8
    if by_plane:
        mesh = Mesh(mesh.devices.reshape(groups, seq_count // 2, 2), ("dp", "z", "core"))
    seq = ("z", "core") if by_plane else "seq"
    both = ("dp", "z", "core") if by_plane else ("dp", "seq")
    in_specs = (
        P("dp", seq, None),
        P("dp", None, None),
        P("dp", None),
        P(),
        P(),
        P("dp", seq, None),
        P(both, None),
        P(both, None),
        P(both, None),
    )
    out_specs = (
        P("dp", seq, None),
        P("dp", seq, None),
        P(),
        P(both, None),
        P(both, None),
        P(both, None),
        P(both, None),
        P(both, None),
        P(both, None),
    )
    return jax.shard_map(
        plane_plan if by_plane else gather_plan,
        mesh=mesh,
        in_specs=in_specs,
        out_specs=out_specs,
        check_vma=False,
    )
```

```python
import functools
import math

import jax
import jax.numpy as jnp
from jax import lax
from jax.experimental import pallas as pl
from jax.experimental.pallas import tpu as pltpu
from jax.sharding import Mesh
from jax.sharding import PartitionSpec as P

D = 1536
FF = 6144
HEAD = 64
CTXW = 768
CTX = 128
NB = 5
STEP = 10
SHEET = 29192


HIGHEST = lax.Precision.HIGHEST
EPS_NORM = 1e-05
EPS_ADAM = 1e-08
MASKED_SCORE = -1e30
BETA_ONE = 0.5
BETA_TWO = 0.5
WEIGHT_DECAY = 0.01


def reorder(values, ordering):
    leading = values.shape[:-1]
    groups = ordering.shape[0]
    blocks = values.reshape(leading + (groups, values.shape[-1] // groups))
    return jnp.take(blocks, ordering, axis=-2).reshape(values.shape)


def norm_parts(values):
    average = jnp.mean(values, axis=-1, keepdims=True)
    centered = values - average
    variance = jnp.mean(centered * centered, axis=-1, keepdims=True)
    inverse_std = lax.rsqrt(variance + EPS_NORM)
    return (centered * inverse_std, inverse_std)


def norm_back(grad_normed, normed, inverse_std):
    return inverse_std * (
        grad_normed
        - jnp.mean(grad_normed, axis=-1, keepdims=True)
        - normed * jnp.mean(grad_normed * normed, axis=-1, keepdims=True)
    )


def softmax_rows(scores):
    row_max = jnp.max(scores, axis=-1, keepdims=True)
    exponent = jnp.exp(scores - row_max)
    return exponent / jnp.sum(exponent, axis=-1, keepdims=True)


def rope_tables(positions, head_dim):
    half_dim = head_dim // 2
    frequency = jnp.exp(-math.log(10000.0) * jnp.arange(half_dim, dtype=jnp.float32) / half_dim)
    angles = positions.astype(jnp.float32)[:, None] * frequency[None, :]
    return (jnp.cos(angles)[:, None, :], jnp.sin(angles)[:, None, :])


def rotate(values, cosine, sine_table):
    half_dim = values.shape[-1] // 2
    first_half = values[..., :half_dim]
    second_half = values[..., half_dim:]
    return jnp.concatenate(
        [
            first_half * cosine - second_half * sine_table,
            second_half * cosine + first_half * sine_table,
        ],
        axis=-1,
    )


def unrotate(grads, cosine, sine_table):
    half_dim = grads.shape[-1] // 2
    first_half = grads[..., :half_dim]
    second_half = grads[..., half_dim:]
    return jnp.concatenate(
        [
            first_half * cosine + second_half * sine_table,
            second_half * cosine - first_half * sine_table,
        ],
        axis=-1,
    )


def segment_ids(starts, positions):
    return jnp.sum((starts[None, :] <= positions[:, None]).astype(jnp.int32), axis=1) - 1


def column_spread(length):
    column = jnp.arange(SHEET, dtype=jnp.int32)
    base_std = D ** (-0.5)
    spread = jnp.full((SHEET,), base_std, jnp.float32)
    spread = jnp.where(
        (column >= 3 * D) & (column < 4 * D), base_std * math.sqrt(length) / 4.0, spread
    )
    spread = jnp.where((column >= 5 * D) & (column < 6 * D), base_std * math.sqrt(CTX), spread)
    spread = jnp.where((column >= 6 * D + 2 * FF) & (column < 6 * D + 3 * FF), FF ** (-0.5), spread)
    spread = jnp.where(
        (column >= 6 * D + 3 * FF) & (column < 6 * D + 3 * FF + 2 * CTXW), CTXW ** (-0.5), spread
    )
    spread = jnp.where(column >= 6 * D + 3 * FF + 2 * CTXW, 0.3, spread)
    return spread


def inner_rows(left, right):
    return lax.dot_general(
        left, right, (((0,), (0,)), ((), ())), preferred_element_type=jnp.float32
    )


def inner_rows_high(left, right):
    return lax.dot_general(
        left, right, (((0,), (0,)), ((), ())), precision=HIGHEST, preferred_element_type=jnp.float32
    )


def gather_plan(latents, context, clip_starts, buckets, owners, cotangent, sheet, first, second):
    frames = latents.shape[1]
    seq_count = lax.axis_size("seq")
    length = frames * seq_count
    head_count = D // HEAD
    score_scale = HEAD ** (-0.5)
    group_ids = jnp.arange(owners.shape[0], dtype=jnp.int32)
    inverse = jnp.sum(
        jnp.where(owners[None, :] == group_ids[:, None], group_ids[None, :], 0), axis=1
    )
    gathered = lax.all_gather(sheet.astype(jnp.bfloat16), ("dp", "seq"), axis=0, tiled=True)
    tail_col = 6 * D + 3 * FF
    gain_col = tail_col + 2 * CTXW
    gain_rows = reorder(gathered[:, gain_col:].astype(jnp.float32).T, inverse)
    row_index = lax.axis_index("dp")
    bucket_ids = jnp.arange(NB, dtype=jnp.int32)
    bucket_pick = (bucket_ids == buckets[row_index]).astype(jnp.float32)
    counts = jnp.sum((buckets[:, None] == bucket_ids[None, :]).astype(jnp.float32), axis=0)
    row_weight = buckets.shape[0] / (NB * jnp.sum(bucket_pick * counts))
    gain_one = gain_rows[0]
    gain_two = gain_rows[1]
    gain_three = gain_rows[2]
    time_gain = jnp.sum(gain_rows[3:] * bucket_pick[:, None], axis=0)
    tokens = latents[0].astype(jnp.float32)
    positions = lax.axis_index("seq") * frames + jnp.arange(frames, dtype=jnp.int32)
    all_positions = jnp.arange(length, dtype=jnp.int32)
    starts = clip_starts[0]
    same_clip = (
        segment_ids(starts, positions)[:, None] == segment_ids(starts, all_positions)[None, :]
    )[None]
    cosine, sine_table = rope_tables(positions, HEAD)
    normed_one, inverse_one = norm_parts(tokens)
    scaled_one = gain_one * time_gain
    h_one_st = reorder((normed_one * scaled_one).astype(jnp.bfloat16), owners)
    joint_qkv = jnp.dot(h_one_st, gathered[:, : 3 * D], preferred_element_type=jnp.float32)
    queries = rotate(joint_qkv[:, :D].reshape(frames, head_count, HEAD), cosine, sine_table).astype(
        jnp.bfloat16
    )
    key_local = rotate(
        joint_qkv[:, D : 2 * D].reshape(frames, head_count, HEAD), cosine, sine_table
    ).astype(jnp.bfloat16)
    value_local = joint_qkv[:, 2 * D :].reshape(frames, head_count, HEAD).astype(jnp.bfloat16)
    key_all, value_all = (
        lax.all_gather(key_local, "seq", axis=0, tiled=True),
        lax.all_gather(value_local, "seq", axis=0, tiled=True),
    )
    scores = (
        jnp.einsum("qhd,khd->hqk", queries, key_all, preferred_element_type=jnp.float32)
        * score_scale
    )
    attn_probs = softmax_rows(jnp.where(same_clip, scores, MASKED_SCORE))
    probs_low = attn_probs.astype(jnp.bfloat16)
    attn_out = (
        jnp.einsum("hqk,khd->qhd", probs_low, value_all, preferred_element_type=jnp.float32)
        .reshape(frames, D)
        .astype(jnp.bfloat16)
    )
    attn_st = reorder(attn_out, owners)
    x_one = tokens + jnp.dot(
        attn_st, gathered[:, 3 * D : 4 * D], preferred_element_type=jnp.float32
    )
    normed_two, inverse_two = norm_parts(x_one)
    h_two_st = reorder((normed_two * gain_two).astype(jnp.bfloat16), owners)
    cross_q = (
        jnp.dot(h_two_st, gathered[:, 4 * D : 5 * D], preferred_element_type=jnp.float32)
        .astype(jnp.bfloat16)
        .reshape(frames, head_count, HEAD)
    )
    text_tokens = context[0]
    text_kv = jnp.einsum(
        "tc,dec->etd",
        text_tokens,
        gathered[:, tail_col:gain_col].reshape(D, 2, CTXW),
        preferred_element_type=jnp.float32,
    )
    text_kv = reorder(text_kv, inverse).astype(jnp.bfloat16).reshape(2, CTX, head_count, HEAD)
    text_keys = text_kv[0]
    text_values = text_kv[1]
    cross_scores = (
        jnp.einsum("qhd,khd->hqk", cross_q, text_keys, preferred_element_type=jnp.float32)
        * score_scale
    )
    cross_probs = softmax_rows(cross_scores)
    cross_low = cross_probs.astype(jnp.bfloat16)
    cross_out = (
        jnp.einsum("hqk,khd->qhd", cross_low, text_values, preferred_element_type=jnp.float32)
        .reshape(frames, D)
        .astype(jnp.bfloat16)
    )
    cross_st = reorder(cross_out, owners)
    x_two = x_one + jnp.dot(
        cross_st, gathered[:, 5 * D : 6 * D], preferred_element_type=jnp.float32
    )
    normed_three, inverse_three = norm_parts(x_two)
    h_three_st = reorder((normed_three * gain_three).astype(jnp.bfloat16), owners)
    grad_out = cotangent[0].astype(jnp.float32) * row_weight
    grad_ff_st = reorder(grad_out.astype(jnp.bfloat16), owners)
    gate_weight = gathered[:, 6 * D : 6 * D + 2 * FF]
    down_weight = gathered[:, 6 * D + 2 * FF : 6 * D + 3 * FF]
    units = down_weight.shape[1]
    gate_up = jnp.dot(h_three_st, gate_weight, preferred_element_type=jnp.float32)
    gate_pre = gate_up[:, :units]
    up_part = gate_up[:, units:]
    sigmoid_gate = jax.nn.sigmoid(gate_pre)
    silu_gate = gate_pre * sigmoid_gate
    hidden = (silu_gate * up_part).astype(jnp.bfloat16)
    ff_out = reorder(
        jnp.einsum("nf,df->nd", hidden, down_weight, preferred_element_type=jnp.float32), inverse
    )
    result = x_two + ff_out
    grad_hidden = jnp.dot(grad_ff_st, down_weight, preferred_element_type=jnp.float32)
    grad_gate = grad_hidden * up_part * (sigmoid_gate * (1.0 + gate_pre * (1.0 - sigmoid_gate)))
    grad_up = grad_hidden * silu_gate
    grad_gu = jnp.concatenate([grad_gate, grad_up], axis=1).astype(jnp.bfloat16)
    grad_h_three = reorder(
        jnp.einsum("nf,df->nd", grad_gu, gate_weight, preferred_element_type=jnp.float32), inverse
    )
    grad_gain_three = jnp.sum(grad_h_three * normed_three, axis=0)
    grad_x_two = grad_out + norm_back(grad_h_three * gain_three, normed_three, inverse_three)
    grad_cross = grad_x_two.astype(jnp.bfloat16)
    grad_cross_out = (
        reorder(
            jnp.einsum(
                "nd,ed->ne",
                grad_cross,
                gathered[:, 5 * D : 6 * D],
                preferred_element_type=jnp.float32,
            ),
            inverse,
        )
        .astype(jnp.bfloat16)
        .reshape(frames, head_count, HEAD)
    )
    grad_cross_probs = jnp.einsum(
        "qhd,khd->hqk", grad_cross_out, text_values, preferred_element_type=jnp.float32
    )
    grad_cross_scores = (
        cross_probs
        * (grad_cross_probs - jnp.sum(cross_probs * grad_cross_probs, axis=-1, keepdims=True))
    ).astype(jnp.bfloat16)
    grad_cross_q = (
        (
            jnp.einsum(
                "hqk,khd->qhd", grad_cross_scores, text_keys, preferred_element_type=jnp.float32
            )
            * score_scale
        )
        .reshape(frames, D)
        .astype(jnp.bfloat16)
    )
    grad_text_keys = (
        jnp.einsum("hqk,qhd->khd", grad_cross_scores, cross_q, preferred_element_type=jnp.float32)
        * score_scale
    )
    grad_text_values = jnp.einsum(
        "hqk,qhd->khd", cross_low, grad_cross_out, preferred_element_type=jnp.float32
    )
    grad_text = reorder(
        jnp.stack([grad_text_keys.reshape(CTX, D), grad_text_values.reshape(CTX, D)]), owners
    )
    grad_h_two = reorder(
        jnp.einsum(
            "ne,de->nd",
            grad_cross_q,
            gathered[:, 4 * D : 5 * D],
            preferred_element_type=jnp.float32,
        ),
        inverse,
    )
    grad_gain_two = jnp.sum(grad_h_two * normed_two, axis=0)
    grad_x_one = grad_x_two + norm_back(grad_h_two * gain_two, normed_two, inverse_two)
    grad_attn = grad_x_one.astype(jnp.bfloat16)
    grad_attn_out = (
        reorder(
            jnp.einsum(
                "nd,ed->ne",
                grad_attn,
                gathered[:, 3 * D : 4 * D],
                preferred_element_type=jnp.float32,
            ),
            inverse,
        )
        .astype(jnp.bfloat16)
        .reshape(frames, head_count, HEAD)
    )
    key_back, value_back = (key_all, value_all)

    def head_grads(head_items):
        head_probs, head_grad_out, head_values = head_items
        grad_probs = jnp.einsum(
            "qd,kd->qk", head_grad_out, head_values, preferred_element_type=jnp.float32
        )
        return (
            head_probs * (grad_probs - jnp.sum(head_probs * grad_probs, axis=-1, keepdims=True))
        ).astype(jnp.bfloat16)

    grad_scores_low = lax.map(
        head_grads, (attn_probs, jnp.swapaxes(grad_attn_out, 0, 1), jnp.swapaxes(value_back, 0, 1))
    )
    grad_queries = (
        jnp.einsum("hqk,khd->qhd", grad_scores_low, key_back, preferred_element_type=jnp.float32)
        * score_scale
    )
    grad_keys = (
        jnp.einsum("hqk,qhd->khd", grad_scores_low, queries, preferred_element_type=jnp.float32)
        * score_scale
    )
    grad_values = jnp.einsum(
        "hqk,qhd->khd", probs_low, grad_attn_out, preferred_element_type=jnp.float32
    )
    key_sums = lax.psum_scatter(
        jnp.concatenate(
            [
                grad_keys.reshape(frames * lax.axis_size("seq"), D),
                grad_values.reshape(frames * lax.axis_size("seq"), D),
            ],
            axis=1,
        ).astype(jnp.bfloat16),
        "seq",
        scatter_dimension=0,
        tiled=True,
    ).astype(jnp.float32)
    grad_q_raw = unrotate(grad_queries, cosine, sine_table).reshape(frames, D)
    grad_k_raw = unrotate(
        key_sums[:, :D].reshape(frames, head_count, HEAD), cosine, sine_table
    ).reshape(frames, D)
    grad_qkv = jnp.concatenate([grad_q_raw, grad_k_raw, key_sums[:, D:]], axis=1).astype(
        jnp.bfloat16
    )
    grad_h_one = reorder(
        jnp.einsum("ne,de->nd", grad_qkv, gathered[:, : 3 * D], preferred_element_type=jnp.float32),
        inverse,
    )
    grad_gain_one = jnp.sum(grad_h_one * normed_one * time_gain, axis=0)
    grad_time = jnp.sum(grad_h_one * normed_one * gain_one, axis=0)
    latent_grad = grad_x_one + norm_back(grad_h_one * scaled_one, normed_one, inverse_one)
    gain_grads = jnp.concatenate(
        [
            jnp.stack([grad_gain_one, grad_gain_two, grad_gain_three]),
            bucket_pick[:, None] * grad_time[None, :],
        ],
        axis=0,
    )
    gain_grads = reorder(gain_grads, owners).T
    text_float = text_tokens.astype(jnp.float32)
    pieces = [
        inner_rows(h_one_st, grad_qkv),
        inner_rows(attn_st, grad_attn),
        inner_rows(h_two_st, grad_cross_q),
        inner_rows(cross_st, grad_cross),
    ]
    pieces = pieces + [inner_rows(h_three_st, grad_gu), inner_rows(grad_ff_st, hidden)]
    pieces = pieces + [
        inner_rows_high(grad_text[0], text_float),
        inner_rows_high(grad_text[1], text_float),
        gain_grads,
    ]
    other_shard = lax.psum_scatter(
        jnp.concatenate(pieces, axis=1), ("dp", "seq"), scatter_dimension=0, tiled=True
    )
    total_squares = lax.psum(jnp.sum(other_shard * other_shard), ("dp", "seq"))
    grad_norm = jnp.sqrt(total_squares)
    clipped = other_shard / jnp.maximum(grad_norm, 1.0)
    gain_grad = clipped[:, 6 * D + 3 * FF + 2 * CTXW :]
    first_new = BETA_ONE * first + (1.0 - BETA_ONE) * clipped
    second_new = BETA_TWO * second + (1.0 - BETA_TWO) * clipped * clipped
    mean_hat = first_new / (1.0 - BETA_ONE**STEP)
    square_hat = second_new / (1.0 - BETA_TWO**STEP)
    rates = column_spread(length)[None, :]
    sheet_new = sheet - rates * (
        mean_hat / (jnp.sqrt(square_hat) + EPS_ADAM) + WEIGHT_DECAY * sheet
    )
    return (
        result.astype(jnp.bfloat16)[None],
        latent_grad[None],
        grad_norm,
        clipped,
        gain_grad,
        first_new,
        second_new,
        sheet_new,
        sheet_new.astype(jnp.bfloat16),
    )


PLANE = ("dp", "core")


def norm_columns(values):
    average = jnp.mean(values, axis=0, keepdims=True)
    centered = values - average
    variance = jnp.mean(centered * centered, axis=0, keepdims=True)
    inverse_std = lax.rsqrt(variance + EPS_NORM)
    return (centered * inverse_std, inverse_std)


def norm_columns_back(grad_normed, normed, inverse_std):
    return inverse_std * (
        grad_normed
        - jnp.mean(grad_normed, axis=0, keepdims=True)
        - normed * jnp.mean(grad_normed * normed, axis=0, keepdims=True)
    )


def contract_rows(left, right):
    return lax.dot_general(
        left, right, (((0,), (0,)), ((), ())), preferred_element_type=jnp.float32
    )


def contract_last(left, right):
    return lax.dot_general(
        left, right, (((1,), (1,)), ((), ())), preferred_element_type=jnp.float32
    )


def matmul(left, right):
    return jnp.dot(left, right, preferred_element_type=jnp.float32)


MESH_ID = pl.DeviceIdType.MESH
IDENTITIES = {}


def identity_of(name, *arrays):
    key = (name,) + tuple((array.shape, str(array.dtype)) for array in arrays)
    return IDENTITIES.setdefault(key, len(IDENTITIES))


IN_HBM = pl.BlockSpec(memory_space=pltpu.HBM)
IN_SMEM = pl.BlockSpec(memory_space=pltpu.SMEM)
IN_VMEM = pl.BlockSpec(memory_space=pltpu.VMEM)
BRIEF = pl.CostEstimate(flops=0, bytes_accessed=1024, transcendentals=0)


def kernel_call(kernel, *, out_shape, in_specs, out_specs, **options):
    single = not isinstance(out_shape, tuple)
    shapes = (out_shape,) if single else out_shape
    places = (out_specs,) if single else out_specs
    shapes = tuple(
        pltpu.HBM(shape.shape, shape.dtype) if place is IN_HBM else shape
        for shape, place in zip(shapes, places)
    )
    call = pl.pallas_call(
        kernel,
        out_shape=shapes[0] if single else shapes,
        in_specs=in_specs,
        out_specs=out_specs,
        **options,
    )

    def run(*operands):
        return call(
            *[
                pltpu.with_memory_space_constraint(operand, pltpu.HBM)
                if place is IN_HBM
                else operand
                for operand, place in zip(operands, in_specs)
            ]
        )

    return run


def reorder_blocks(source, target, order, column=0):
    rows = source.shape[1]
    columns = slice(column, column + target.shape[1])

    @pl.loop(0, source.shape[0])
    def _(b):
        target[pl.ds(pl.multiple_of(b * rows, 16), rows), :] = source[order(b), :, columns]


def wide(ref):
    return ref[...].astype(jnp.float32)


def greet(peers):
    barrier = pltpu.get_barrier_semaphore()
    for peer in peers:
        pl.semaphore_signal(barrier, inc=1, device_id=peer, device_id_type=MESH_ID)
    pl.semaphore_wait(barrier, len(peers))


def near():
    group, core = lax.axis_index("dp"), lax.axis_index("core")
    across = group + 1 - 2 * lax.rem(group, 2)
    along = lax.rem(group + 2, 4)
    return group, core, across, along


def member_rows(width):
    def place(ref, member, start, count):
        first_row = pl.multiple_of(member * width + start, 16)
        return ref.at[pl.ds(first_row, count), :]

    return place


def member_lanes(width):
    def place(ref, member, start, count):
        return ref.at[pl.ds(start, count), pl.ds(pl.multiple_of(member * width, 128), width)]

    return place


def mover(send_sem, recv_sem, first=0):
    def copy(k, source, target, peer):
        return pltpu.make_async_remote_copy(
            src_ref=source,
            dst_ref=target,
            send_sem=send_sem.at[first + k],
            recv_sem=recv_sem.at[first + k],
            device_id=peer,
            device_id_type=MESH_ID,
        )

    return copy


def member_at(member):
    return {"dp": lax.div(member, 2), "core": lax.rem(member, 2)}


def plane_peers():
    group, core, _, _ = near()
    member = group * 2 + core
    return [lax.rem(member + step, 8) for step in range(1, 8)]


def gather_steps(place, x_ref, o_ref, local_sem, copy, arrived_whole=lambda member: None):
    group, core, across, along = near()
    beyond = across + along - group
    other = 1 - core
    sibling, by_x, by_y = {"core": other}, {"dp": across}, {"dp": along}
    half = x_ref.shape[0] // 2

    def part(owner, owner_core, piece):
        return place(o_ref, owner * 2 + owner_core, piece * half, half)

    sent = []

    def send(k, source, target, peer):
        moving = copy(k, source, target, peer)
        moving.start()
        sent.append(moving)

    def own(k, piece, peer):
        send(k, x_ref.at[pl.ds(piece * half, half), :], part(group, core, piece), peer)

    def relay(k, owner, piece, peer):
        send(k, part(owner, core, piece), part(owner, core, piece), peer)

    def arrived(k, owner, owner_core, piece):
        landed = part(owner, owner_core, piece)
        copy(k, landed, landed, sibling).wait_recv()

    local = pltpu.make_async_copy(
        x_ref, place(o_ref, group * 2 + core, 0, 2 * half), local_sem
    )
    local.start()
    own(0, 0, by_x)
    own(1, 1, by_y)
    own(2, 1, by_x)
    own(3, 0, by_y)
    own(4, 0, sibling)
    own(5, 1, sibling)

    def finish():
        local.wait()
        arrived_whole(group * 2 + core)
        arrived(4, group, other, 0)
        arrived(5, group, other, 1)
        arrived_whole(group * 2 + other)
        arrived(0, across, core, 0)
        relay(6, across, 0, by_y)
        relay(7, across, 0, sibling)
        arrived(1, along, core, 1)
        relay(8, along, 1, by_x)
        relay(9, along, 1, sibling)
        arrived(2, across, core, 1)
        relay(10, across, 1, sibling)
        arrived_whole(across * 2 + core)
        arrived(3, along, core, 0)
        relay(11, along, 0, sibling)
        arrived_whole(along * 2 + core)
        arrived(7, across, other, 0)
        arrived(10, across, other, 1)
        arrived_whole(across * 2 + other)
        arrived(6, beyond, core, 0)
        relay(12, beyond, 0, sibling)
        arrived(8, beyond, core, 1)
        relay(13, beyond, 1, sibling)
        arrived_whole(beyond * 2 + core)
        arrived(9, along, other, 1)
        arrived(11, along, other, 0)
        arrived_whole(along * 2 + other)
        arrived(12, beyond, other, 0)
        arrived(13, beyond, other, 1)
        arrived_whole(beyond * 2 + other)
        for moving in sent:
            moving.wait_send()

    return finish


def exchange_steps(source, target, x_ref, o_ref, local_sem, copy):
    group, core, _, _ = near()
    member = group * 2 + core
    local = pltpu.make_async_copy(source(x_ref, member), target(o_ref, member), local_sem)
    local.start()
    sent = []
    for k, peer in enumerate(plane_peers()):
        sent.append(copy(k, source(x_ref, peer), target(o_ref, member), member_at(peer)))
        sent[-1].start()

    def finish():
        for k in range(7):
            sender = lax.rem(member + 7 - k, 8)
            landed = target(o_ref, sender)
            copy(k, landed, landed, member_at(sender)).wait_recv()
        local.wait()
        for moving in sent:
            moving.wait_send()

    return finish


def gather_kernel(place, x_ref, *refs):
    o_ref, local_sem, send_sem, recv_sem = refs[-4:]
    _, core, across, along = near()
    greet([{"dp": across}, {"dp": along}, {"core": 1 - core}])
    gather_steps(place, x_ref, o_ref, local_sem, mover(send_sem, recv_sem))()


def plane_gather_call(shard, shape, place, kind, after):
    return kernel_call(
        functools.partial(gather_kernel, place),
        out_shape=jax.ShapeDtypeStruct(shape, shard.dtype),
        in_specs=[IN_HBM] * (1 + len(after)),
        out_specs=IN_HBM,
        scratch_shapes=[
            pltpu.SemaphoreType.DMA,
            pltpu.SemaphoreType.DMA((14,)),
            pltpu.SemaphoreType.DMA((14,)),
        ],
        compiler_params=pltpu.CompilerParams(
            collective_id=identity_of(kind, shard, *after), has_side_effects=True
        ),
        cost_estimate=BRIEF,
        name="plane_gather",
    )(shard, *after)


def plane_gather(shard, after=()):
    rows, width = shard.shape
    return plane_gather_call(shard, (rows, 8 * width), member_lanes(width), "gather lanes", after)


def plane_gather_rows(shard, after=()):
    rows, width = shard.shape
    return plane_gather_call(shard, (8 * rows, width), member_rows(rows), "gather rows", after)


def scatter_steps(place, p_ref, bufs, copy):
    pair, total, from_x, from_y, relay = bufs
    group, core, across, along = near()
    beyond = across + along - group
    other = 1 - core
    sibling, by_x, by_y = {"core": other}, {"dp": across}, {"dp": along}
    rows = total.shape[1]
    half = rows // 2
    low, high = pl.ds(0, half), pl.ds(half, half)
    sent = []

    def send(k, source, target, peer):
        moving = copy(k, source, target, peer)
        moving.start()
        sent.append(moving)

    def arrived(k, target):
        copy(k, target, target, sibling).wait_recv()

    def both_cores(k, owner):
        arrived(k, pair.at[k])
        summed = wide(place(p_ref, owner * 2 + core, 0, rows)) + wide(pair.at[k])
        total[k] = summed.astype(total.dtype)

    def cores():
        for k, owner in enumerate((beyond, across, along, group)):
            send(k, place(p_ref, owner * 2 + other, 0, rows), pair.at[k], sibling)

    def chips():
        both_cores(0, beyond)
        send(4, total.at[0, low], relay.at[0], by_x)
        send(5, total.at[0, high], relay.at[1], by_y)
        both_cores(1, across)
        send(6, total.at[1, low], from_x.at[low], by_x)
        both_cores(2, along)
        send(7, total.at[2, high], from_y.at[high], by_y)
        both_cores(3, group)

    def relays():
        arrived(5, relay.at[1])
        total[1, high] = (wide(total.at[1, high]) + wide(relay.at[1])).astype(total.dtype)
        send(8, total.at[1, high], from_x.at[high], by_x)
        arrived(4, relay.at[0])
        total[2, low] = (wide(total.at[2, low]) + wide(relay.at[0])).astype(total.dtype)
        send(9, total.at[2, low], from_y.at[low], by_y)

    def finish():
        arrived(6, from_x.at[low])
        arrived(7, from_y.at[high])
        arrived(8, from_x.at[high])
        arrived(9, from_y.at[low])
        summed = wide(total.at[3]) + wide(from_x) + wide(from_y)
        for moving in sent:
            moving.wait_send()
        return summed

    return cores, chips, relays, finish


def scatter_bufs(rows, width):
    slot = pltpu.VMEM((rows, width), jnp.bfloat16)
    four = pltpu.VMEM((4, rows, width), jnp.bfloat16)
    return [four, four, slot, slot, pltpu.VMEM((2, rows // 2, width), jnp.bfloat16)]


def scatter_kernel(place, p_ref, *refs):
    o_ref, *bufs, send_sem, recv_sem = refs[-8:]
    _, core, across, along = near()
    greet([{"dp": across}, {"dp": along}, {"core": 1 - core}])
    cores, chips, relays, finish = scatter_steps(place, p_ref, bufs, mover(send_sem, recv_sem))
    cores()
    chips()
    relays()
    o_ref[...] = finish().astype(o_ref.dtype)


def plane_scatter_call(partial, shape, place, dtype, kind, after):
    rows, width = shape
    return kernel_call(
        functools.partial(scatter_kernel, place),
        out_shape=jax.ShapeDtypeStruct(shape, dtype),
        in_specs=[IN_VMEM] + [IN_HBM] * len(after),
        out_specs=IN_VMEM,
        scratch_shapes=scatter_bufs(rows, width)
        + [
            pltpu.SemaphoreType.DMA((10,)),
            pltpu.SemaphoreType.DMA((10,)),
        ],
        compiler_params=pltpu.CompilerParams(
            collective_id=identity_of(kind, partial, *after),
            has_side_effects=True,
            vmem_limit_bytes=24 * 2**20,
        ),
        cost_estimate=BRIEF,
        name="plane_scatter",
    )(partial, *after)


def plane_scatter_frames(partial, after=()):
    rows, width = partial.shape[0], partial.shape[1] // 8
    place = member_lanes(width)
    return plane_scatter_call(partial, (rows, width), place, jnp.float32, "scatter lanes", after)


def plane_scatter_rows(partial, after=()):
    rows, width = partial.shape[0] // 8, partial.shape[1]
    place = member_rows(rows)
    return plane_scatter_call(partial, (rows, width), place, jnp.bfloat16, "scatter rows", after)


def project_kernel(kind, column, order_ref, s_ref, w_ref, base_ref, gain_ref, *refs):
    if kind == "sum":
        side_ref, full_ref, x_ref, n_ref, i_ref, h_ref, side_out, *refs = refs
    else:
        full_ref, x_ref, n_ref, i_ref, h_ref, *refs = refs
    full, total, part, landed, shard, by_block, base, gain, residual, normed, *refs = refs
    heads, slots, weight, *bufs, local_sem, send_sem, recv_sem = refs
    rows, length = s_ref.shape
    width = base_ref.shape[1]
    fetches = [
        pltpu.make_async_copy(ref, held, local_sem.at[8 + k])
        for k, (ref, held) in enumerate(
            [(s_ref, heads), (w_ref.at[:, :, : slots.shape[2]], slots)]
            + [(base_ref, base), (gain_ref, gain)]
        )
    ]
    for fetch in fetches:
        fetch.start()
    greet([member_at(peer) for peer in plane_peers()])
    total[...] = jnp.zeros_like(total)

    def add(member):
        of = pl.ds(pl.multiple_of(member * rows, 16), rows)

        @pl.loop(0, length // 256)
        def _(i):
            at = pl.ds(pl.multiple_of(i * 256, 256), 256)
            total[:, at] += contract_rows(weight[of, :], full[of, at])

    fetches[0].wait()
    gathered = gather_steps(
        member_rows(rows), heads, full, local_sem.at[0], mover(send_sem, recv_sem), add
    )
    side = mover(send_sem, recv_sem, 35)
    if kind == "sum":
        cores, chips, relays, finish = scatter_steps(
            member_rows(side_out.shape[0]), bufs[-1], bufs[:-2], side
        )
        text_weight = bufs[-2]
        fetches[1].wait()
        reorder_blocks(slots, text_weight, lambda b: order_ref[1, b], 3 * rows)
        tokens = side_ref.shape[1]

        @pl.loop(0, text_weight.shape[0] // 256)
        def _(i):
            at = pl.ds(pl.multiple_of(i * 256, 256), 256)
            for k in range(2):
                half = slice(k * side_ref.shape[0], (k + 1) * side_ref.shape[0])
                bufs[-1][at, k * tokens : (k + 1) * tokens] = jnp.dot(
                    text_weight[at, half], side_ref[...], preferred_element_type=jnp.float32
                ).astype(jnp.bfloat16)

        cores()
    else:
        fetches[1].wait()
    reorder_blocks(slots, weight, lambda b: order_ref[1, b], column)
    if kind == "sum":
        chips()
    gathered()
    kept = pltpu.make_async_copy(full, full_ref, local_sem.at[0])
    kept.start()
    part[...] = total[...].astype(part.dtype)
    exchanged = exchange_steps(
        whole_lanes(rows, width),
        whole_rows(rows),
        part,
        landed,
        local_sem.at[3],
        mover(send_sem, recv_sem, 14),
    )
    if kind == "sum":
        relays()
    exchanged()
    fetches[2].wait()
    fetches[3].wait()
    residual[...] = base[...] + wide(landed)
    standard, inverse_std = norm_columns(residual[...])
    normed[...] = standard
    i_ref[...] = inverse_std
    by_block[...] = (standard * gain[...]).astype(shard.dtype).reshape(by_block.shape)
    reorder_blocks(by_block, shard, lambda b: order_ref[0, b])
    gathered = gather_steps(
        member_lanes(width), shard, h_ref, local_sem.at[4], mover(send_sem, recv_sem, 21)
    )
    x_copy = pltpu.make_async_copy(residual, x_ref, local_sem.at[5])
    x_copy.start()
    n_copy = pltpu.make_async_copy(normed, n_ref, local_sem.at[6])
    n_copy.start()
    if kind == "sum":
        side_out[...] = finish().astype(side_out.dtype)
    gathered()
    kept.wait()
    x_copy.wait()
    n_copy.wait()


def project(kind, column, orders, heads, weight, base, gain, *side):
    rows, length = heads.shape
    features, width = base.shape
    whole = jax.ShapeDtypeStruct((features, length), jnp.bfloat16)
    frames = jax.ShapeDtypeStruct(base.shape, jnp.float32)
    side_outs, bufs = (), []
    if kind == "sum":
        tokens = side[0].shape[1]
        side_outs = (jax.ShapeDtypeStruct((rows, 2 * tokens), jnp.bfloat16),)
        bufs = scatter_bufs(rows, 2 * tokens) + [
            pltpu.VMEM((features, rows), jnp.bfloat16),
            pltpu.VMEM((features, 2 * tokens), jnp.bfloat16),
        ]
    low, high = pltpu.VMEM(base.shape, jnp.bfloat16), pltpu.VMEM(base.shape, jnp.float32)
    return kernel_call(
        functools.partial(project_kernel, kind, column),
        out_shape=(whole, frames, frames, jax.ShapeDtypeStruct((1, width), jnp.float32), whole)
        + side_outs,
        in_specs=[IN_SMEM] + [IN_HBM] * 4 + [IN_VMEM] * len(side),
        out_specs=(IN_HBM, IN_HBM, IN_HBM, IN_VMEM, IN_HBM) + (IN_VMEM,) * len(side),
        scratch_shapes=[
            pltpu.VMEM((features, length), jnp.bfloat16),
            pltpu.VMEM((rows, length), jnp.float32),
            pltpu.VMEM((rows, length), jnp.bfloat16),
            low,
            low,
            pltpu.VMEM((orders.shape[1], features // orders.shape[1], width), jnp.bfloat16),
            high,
            pltpu.VMEM(gain.shape, jnp.float32),
            high,
            high,
            pltpu.VMEM(heads.shape, heads.dtype),
            pltpu.VMEM((orders.shape[1], features // orders.shape[1], 4 * rows), weight.dtype),
            pltpu.VMEM((features, rows), weight.dtype),
        ]
        + bufs
        + [
            pltpu.SemaphoreType.DMA((13,)),
            pltpu.SemaphoreType.DMA((49,)),
            pltpu.SemaphoreType.DMA((49,)),
        ],
        compiler_params=pltpu.CompilerParams(
            collective_id=identity_of("project " + kind, heads),
            has_side_effects=True,
            vmem_limit_bytes=32 * 2**20,
        ),
        cost_estimate=BRIEF,
        name="project_" + kind,
    )(orders, heads, weight.reshape(orders.shape[1], -1, weight.shape[1]), base, gain, *side)


def back_kernel(plan, *refs):
    by_rows, send_rows, text, in_slots, column, beside, after = plan
    refs = list(refs)

    def take(count):
        taken = refs[:count]
        del refs[:count]
        return taken

    order_ref = take(1)[0]
    sources = take(3 if by_rows else 7)
    text_ref = take(1)[0] if text else None
    beside_refs = take(4 if beside else 0)
    take(after)
    o_ref, own_out = take(2)
    sum_ref = None if by_rows else take(1)[0]
    rows_ref = take(1)[0] if send_rows else None
    text_out = take(1)[0] if text else None
    held = take(len(sources))
    w_ref, g_ref, act, *norms = held
    results = take(0 if by_rows else 2)
    mine, theirs, pair, from_x, from_y, relay, shard, slots, own_ref = take(9)
    besides = take(4 if beside else 0)
    by_head = take(1 if by_rows else 0)
    local_sem, send_sem, recv_sem = refs
    if by_rows:
        w_slots, w_ref = w_ref, by_head[0]
    source = sources[0]
    if by_rows:
        sources[0] = source.at[:, :, : w_slots.shape[2]]
    elif w_ref.shape[1] < source.shape[1]:
        sources[0] = source.at[:, : w_ref.shape[1]]
    fetches = [
        pltpu.make_async_copy(ref, here, local_sem.at[4 + k])
        for k, (ref, here) in enumerate(zip(sources + beside_refs, held + besides))
    ]
    for fetch in fetches:
        fetch.start()

    group, core, across, along = near()
    beyond = across + along - group
    sibling, by_x, by_y = {"core": 1 - core}, {"dp": across}, {"dp": along}
    rows, width = mine.shape[1:]
    columns = slice(0, g_ref.shape[0]) if by_rows else slice(column, column + g_ref.shape[0])
    half = rows // 2
    low, high = pl.ds(0, half), pl.ds(half, half)
    copy = mover(send_sem, recv_sem)
    sent = []

    def send(k, source, target, peer):
        moving = copy(k, source, target, peer)
        moving.start()
        sent.append(moving)

    def arrived(k, target):
        copy(k, target, target, sibling).wait_recv()

    def split(k, at_rows, at_lanes, first, second):
        mine[k, at_rows, at_lanes] = jnp.where(core == 0, first, second).astype(mine.dtype)
        theirs[k, at_rows, at_lanes] = jnp.where(core == 0, second, first).astype(mine.dtype)

    def work_out(k, owner):
        if by_rows:

            @pl.loop(0, width // 256)
            def _(i):
                at = pl.ds(pl.multiple_of(i * 256, 256), 256)
                both = jnp.dot(
                    w_ref[pl.ds(pl.multiple_of(owner * 2 * rows, 16), 2 * rows), columns],
                    g_ref[:, at],
                    preferred_element_type=jnp.float32,
                )
                split(k, slice(None), at, both[:rows], both[rows:])

        else:

            @pl.loop(0, rows // 256)
            def _(i):
                at = pl.ds(pl.multiple_of(i * 256, 256), 256)
                both = jnp.dot(
                    w_ref[at, columns],
                    g_ref[:, pl.ds(pl.multiple_of(owner * 2 * width, 256), 2 * width)],
                    preferred_element_type=jnp.float32,
                )
                split(k, at, slice(None), both[:, :width], both[:, width:])

        send(k, theirs.at[k], pair.at[k], sibling)

    def both_cores(k):
        arrived(k, pair.at[k])
        mine[k] = (wide(mine.at[k]) + wide(pair.at[k])).astype(mine.dtype)

    def weight_grads(first, last):
        rows_of = act if in_slots else slots
        tile, count = rows_of.shape[0] // 6, g_ref.shape[0]

        @pl.loop(first, last)
        def _(i):
            at = pl.ds(pl.multiple_of(i * tile, tile), tile)
            for j in range(0, count, 256):
                of = slice(j, min(j + 256, count))
                own_ref[at, of] = contract_last(rows_of[at, :], g_ref[of, :]).astype(
                    own_ref.dtype
                )

    if send_rows or text:
        greet([member_at(peer) for peer in plane_peers()])
    else:
        greet([by_x, by_y, sibling])
    fetches[0].wait()
    if by_rows:
        reorder_blocks(w_slots, w_ref, lambda b: order_ref[1, b], column)
    fetches[1].wait()
    for k, owner in enumerate((beyond, across, along, group)):
        work_out(k, owner)
        if k == 1:
            both_cores(0)
            send(4, mine.at[0, low], relay.at[0], by_x)
            send(5, mine.at[0, high], relay.at[1], by_y)
        if k == 2:
            both_cores(1)
            send(6, mine.at[1, low], from_x.at[low], by_x)
        if k == 3:
            both_cores(2)
            send(7, mine.at[2, high], from_y.at[high], by_y)
    if text:
        text_done = gather_steps(
            member_rows(text_ref.shape[0]),
            text_ref,
            text_out,
            local_sem.at[1],
            mover(send_sem, recv_sem, 17),
        )
    def put_beside():
        cq, co, text_grad, text_mine = besides
        count, rows = g_ref.shape[0], text_grad.shape[1]
        part = text_mine.shape[0]
        tokens = text_mine.shape[1]

        @pl.loop(0, text_grad.shape[0])
        def _(b):
            at = pl.ds(pl.multiple_of(b * rows, 16), rows)
            own_ref[at, count : 2 * count] = cq[at, :]
            own_ref[at, 2 * count : 3 * count] = co[at, :]
            slots[at, : 2 * tokens] = text_grad[order_ref[0, b]]

        @pl.loop(0, 6)
        def _(i):
            at = pl.ds(pl.multiple_of(i * 256, 256), 256)
            for k in range(2):
                grads = contract_last(
                    slots[at, k * tokens : (k + 1) * tokens], text_mine[...]
                )
                start = 3 * count + k * part
                own_ref[at, start : start + part] = grads.astype(own_ref.dtype)

    fetches[2].wait()
    if not in_slots:
        reorder_blocks(act, slots, lambda b: order_ref[0, b])
    weight_grads(0, 2)
    arrived(5, relay.at[1])
    mine[1, high] = (wide(mine.at[1, high]) + wide(relay.at[1])).astype(mine.dtype)
    send(8, mine.at[1, high], from_x.at[high], by_x)
    arrived(4, relay.at[0])
    mine[2, low] = (wide(mine.at[2, low]) + wide(relay.at[0])).astype(mine.dtype)
    send(9, mine.at[2, low], from_y.at[low], by_y)
    both_cores(3)
    weight_grads(2, 6)
    if beside:
        for fetch in fetches[len(sources) :]:
            fetch.wait()
        put_beside()
    if text:
        text_done()
    own_copy = pltpu.make_async_copy(own_ref, own_out, local_sem.at[2])
    own_copy.start()
    arrived(6, from_x.at[low])
    arrived(7, from_y.at[high])
    arrived(8, from_x.at[high])
    arrived(9, from_y.at[low])
    summed = wide(mine.at[3]) + wide(from_x) + wide(from_y)
    if by_rows:
        shard[...] = summed.astype(shard.dtype)
        result_copy = pltpu.make_async_copy(shard, o_ref, local_sem.at[3])
        result_copy.start()
    else:
        for fetch in fetches[3 : len(sources)]:
            fetch.wait()
        normed, inverse_std, gain, base = norms
        result, by_block = results
        if in_slots:
            by_block[...] = summed.reshape(by_block.shape)
            reorder_blocks(by_block, result, lambda b: order_ref[1, b])
            summed = result[...]
        result[...] = base[...] + norm_columns_back(
            summed * gain[...], normed[...], inverse_std[...]
        )
        result_copy = pltpu.make_async_copy(result, o_ref, local_sem.at[3])
        result_copy.start()
        if send_rows:
            shard[...] = result[...].astype(shard.dtype)
            rows_done = exchange_steps(
                whole_rows(rows // 8),
                whole_lanes(rows // 8, width),
                shard,
                rows_ref,
                local_sem.at[0],
                mover(send_sem, recv_sem, 10),
            )
        sum_ref[...] = lax.dot_general(
            jnp.ones((8, width), jnp.float32),
            summed * normed[...],
            (((1,), (1,)), ((), ())),
            precision=HIGHEST,
            preferred_element_type=jnp.float32,
        )
        if send_rows:
            rows_done()
    result_copy.wait()
    own_copy.wait()
    for moving in sent:
        moving.wait_send()


def back(
    orders,
    weight,
    grad,
    act,
    norm=None,
    column=0,
    send_rows=False,
    text=None,
    in_slots=False,
    beside=(),
    after=(),
):
    by_rows = norm is None
    features, length = weight.shape[0], grad.shape[1]
    shape = (features // 8, length) if by_rows else (features, length // 8)
    small = jnp.bfloat16
    own_width = grad.shape[0] * (4 if beside else 1)
    own = jax.ShapeDtypeStruct((features, own_width), small)
    outs = [jax.ShapeDtypeStruct(shape, small if by_rows else jnp.float32), own]
    specs = [IN_HBM, IN_HBM]
    if not by_rows:
        outs.append(jax.ShapeDtypeStruct((8, features), jnp.float32))
        specs.append(IN_VMEM)
    if send_rows:
        outs.append(jax.ShapeDtypeStruct((features // 8, length), small))
        specs.append(IN_HBM)
    count = orders.shape[1]
    if not in_slots:
        act = act.reshape(count, features // count, length)
    few = weight.shape[1] if column + grad.shape[0] > 4 * (features // 8) else 4 * (features // 8)
    if by_rows:
        weight = weight.reshape(count, features // count, weight.shape[1])
        held = jax.ShapeDtypeStruct((count, features // count, few), small)
    else:
        held = jax.ShapeDtypeStruct((features, few), small)
    sources = [weight, grad, act] + list(norm or ())
    operands = [orders] + sources
    if text is not None:
        operands.append(text)
        outs.append(jax.ShapeDtypeStruct((8 * text.shape[0], text.shape[1]), text.dtype))
        specs.append(IN_HBM)
    if beside:
        cq, co, text_grad, text_mine = beside
        beside = (cq, co, text_grad.reshape(count, features // count, -1), text_mine)
        operands += list(beside)
    operands += list(after)
    plan = (by_rows, send_rows, text is not None, in_slots, column, bool(beside), len(after))
    rows, width = shape
    four, slot = pltpu.VMEM((4, rows, width), small), pltpu.VMEM((rows, width), small)
    return kernel_call(
        functools.partial(back_kernel, plan),
        out_shape=tuple(outs),
        in_specs=[IN_SMEM] + [IN_HBM] * (len(operands) - 1),
        out_specs=tuple(specs),
        scratch_shapes=[pltpu.VMEM(array.shape, array.dtype) for array in [held] + sources[1:]]
        + (
            []
            if by_rows
            else [
                pltpu.VMEM(shape, jnp.float32),
                pltpu.VMEM((count, rows // count, width), jnp.float32),
            ]
        )
        + [four, four, four, slot, slot, pltpu.VMEM((2, rows // 2, width), small), slot]
        + [
            pltpu.VMEM((16, 128) if in_slots else (features, length), small),
            pltpu.VMEM(own.shape, small),
        ]
        + [pltpu.VMEM(array.shape, array.dtype) for array in beside]
        + ([pltpu.VMEM((features, grad.shape[0]), small)] if by_rows else [])
        + [
            pltpu.SemaphoreType.DMA((11,)),
            pltpu.SemaphoreType.DMA((31,)),
            pltpu.SemaphoreType.DMA((31,)),
        ],
        compiler_params=pltpu.CompilerParams(
            collective_id=identity_of("back" + str(plan), *operands),
            has_side_effects=True,
            vmem_limit_bytes=44 * 2**20,
        ),
        cost_estimate=BRIEF,
        name="back",
    )(*operands)


def exchange_kernel(source, target, x_ref, *refs):
    o_ref, local_sem, send_sem, recv_sem = refs[-4:]
    greet([member_at(peer) for peer in plane_peers()])
    exchange_steps(source, target, x_ref, o_ref, local_sem, mover(send_sem, recv_sem))()


def exchange(array, shape, source, target, kind, after=()):
    return kernel_call(
        functools.partial(exchange_kernel, source, target),
        out_shape=jax.ShapeDtypeStruct(shape, array.dtype),
        in_specs=[IN_HBM] * (1 + len(after)),
        out_specs=IN_HBM,
        scratch_shapes=[
            pltpu.SemaphoreType.DMA,
            pltpu.SemaphoreType.DMA((7,)),
            pltpu.SemaphoreType.DMA((7,)),
        ],
        compiler_params=pltpu.CompilerParams(
            collective_id=identity_of(kind, array, *after), has_side_effects=True
        ),
        cost_estimate=BRIEF,
        name="plane_exchange",
    )(array, *after)


def whole_rows(rows):
    place = member_rows(rows)
    return lambda ref, member: place(ref, member, 0, rows)


def whole_lanes(rows, width):
    place = member_lanes(width)
    return lambda ref, member: place(ref, member, 0, rows)


def to_frames(part):
    rows, width = part.shape[0], part.shape[1] // 8
    return exchange(part, (8 * rows, width), whole_lanes(rows, width), whole_rows(rows), "to frames")


def to_rows(part):
    rows, width = part.shape[0] // 8, part.shape[1]
    return exchange(part, (rows, 8 * width), whole_rows(rows), whole_lanes(rows, width), "to rows")


def block(ref, member):
    return ref.at[member]


def exchange_blocks(blocks, after=()):
    return exchange(blocks, blocks.shape, block, block, "blocks", after)


def lanes(ref, start, width):
    return ref.at[:, pl.ds(pl.multiple_of(start, 128), width)]


def sheet_part(start, width):
    return lambda ref, member: lanes(ref, start + member * width, width)


def block_part(start, width):
    return lambda ref, member: lanes(ref.at[member], start, width)


def feed_kernel(gu_ref, down_ref, w_ref, h_ref, g_ref, *refs):
    o_ref, y_ref, t_ref, weight, hidden, part, summed, grad, x_ref, held, *refs = refs[-18:]
    *bufs, local_sem, send_sem, recv_sem = refs
    width = down_ref.shape[-1]
    fetches = [
        pltpu.make_async_copy(w_ref, weight, local_sem.at[3]),
        pltpu.make_async_copy(h_ref, hidden, local_sem.at[5]),
        pltpu.make_async_copy(g_ref, grad, local_sem.at[6]),
    ]
    for fetch in fetches:
        fetch.start()
    plane = lax.axis_index("z")
    greet(
        [member_at(peer) for peer in plane_peers()]
        + [{"z": lax.rem(plane + k, 4)} for k in range(1, 4)]
    )
    depart, arrive, turned_back = turn_steps(
        x_ref, held, t_ref, local_sem.at[pl.ds(7, 2)], send_sem, recv_sem, 31
    )
    fetches[2].wait()
    x_ref[...] = grad[...].T.astype(x_ref.dtype)
    finish = []
    for k, (ref, start) in enumerate(((gu_ref, 0), (gu_ref, width), (down_ref, 0))):
        source, target = block_part(start, width), sheet_part(8 * k * width, width)
        copy = mover(send_sem, recv_sem, 7 * k)
        finish.append(exchange_steps(source, target, ref, o_ref, local_sem.at[k], copy))
    for fetch in fetches[:2]:
        fetch.wait()

    @pl.loop(0, part.shape[0] // 256)
    def _(i):
        at = pl.ds(pl.multiple_of(i * 256, 256), 256)
        for j in range(0, part.shape[1], 256):
            product = jnp.dot(
                weight[at, :], hidden[:, j : j + 256], preferred_element_type=jnp.float32
            )
            part[at, j : j + 256] = product.astype(part.dtype)

    cores, chips, relays, ended = scatter_steps(
        member_lanes(y_ref.shape[1]), part, bufs, mover(send_sem, recv_sem, 21)
    )
    cores()
    chips()
    relays()
    depart()
    summed[...] = ended()
    kept = pltpu.make_async_copy(summed, y_ref, local_sem.at[4])
    kept.start()
    arrive()
    for end in finish:
        end()
    kept.wait()
    turned_back()


def feed(gu, down, weight, hidden, grad, after=()):
    rows, length = weight.shape[0], hidden.shape[1]
    width = length // 8
    return kernel_call(
        feed_kernel,
        out_shape=(
            jax.ShapeDtypeStruct((gu.shape[1], 24 * down.shape[-1]), gu.dtype),
            jax.ShapeDtypeStruct((rows, width), jnp.float32),
            jax.ShapeDtypeStruct((width, rows), jnp.bfloat16),
        ),
        in_specs=[IN_HBM] * (5 + len(after)),
        out_specs=(IN_HBM,) * 3,
        scratch_shapes=[
            pltpu.VMEM(weight.shape, weight.dtype),
            pltpu.VMEM(hidden.shape, hidden.dtype),
            pltpu.VMEM((rows, length), jnp.bfloat16),
            pltpu.VMEM((rows, width), jnp.float32),
            pltpu.VMEM((rows, width), jnp.float32),
            pltpu.VMEM((width, rows), jnp.bfloat16),
            pltpu.VMEM((width, rows), jnp.bfloat16),
        ]
        + scatter_bufs(rows, width)
        + [
            pltpu.SemaphoreType.DMA((9,)),
            pltpu.SemaphoreType.DMA((39,)),
            pltpu.SemaphoreType.DMA((39,)),
        ],
        compiler_params=pltpu.CompilerParams(
            collective_id=identity_of("feed", gu, down, weight, *after),
            has_side_effects=True,
            vmem_limit_bytes=28 * 2**20,
        ),
        cost_estimate=BRIEF,
        name="feed",
    )(gu, down, weight, hidden, grad, *after)


def opening_kernel(
    latents_ref,
    cotangent_ref,
    small_ref,
    text_ref,
    sheet_ref,
    t_ref,
    all_ref,
    mine_ref,
    one_ref,
    x_ref,
    held,
    columns,
    one,
    tokens,
    by_feature,
    local_sem,
    send_sem,
    recv_sem,
):
    features = latents_ref.shape[1]
    part, text = D // 8, CTXW // 8
    tail = 6 * D + 3 * FF
    fetches = [
        pltpu.make_async_copy(latents_ref, x_ref.at[:, :features], local_sem.at[5]),
        pltpu.make_async_copy(cotangent_ref, x_ref.at[:, features:], local_sem.at[6]),
        pltpu.make_async_copy(
            sheet_ref.at[:, : 6 * D], columns.at[:, : 6 * D], local_sem.at[7]
        ),
        pltpu.make_async_copy(
            sheet_ref.at[:, tail : tail + 2 * CTXW], columns.at[:, 6 * D :], local_sem.at[8]
        ),
        pltpu.make_async_copy(text_ref, tokens, local_sem.at[10]),
    ]
    for fetch in fetches:
        fetch.start()
    group, core, across, along = near()
    member = group * 2 + core
    plane = lax.axis_index("z")
    step = x_ref.shape[0] // 4
    text_rows = mine_ref.shape[0]
    teacher = jnp.logical_and(group == plane, core == 0)

    def frames(ref, j):
        return ref.at[pl.ds(pl.multiple_of(j * step, 16), step), :]

    peers = plane_peers()
    line = [lax.rem(plane + k, 4) for k in range(1, 4)]
    greet([member_at(peer) for peer in peers] + [{"z": there} for there in line])

    fetches[0].wait()
    fetches[1].wait()

    near_copy = mover(send_sem, recv_sem)
    line_copy = mover(send_sem, recv_sem, 7)
    small_local = pltpu.make_async_copy(small_ref, all_ref.at[plane, member], local_sem.at[0])
    small_local.start()
    first = [
        near_copy(k, small_ref, all_ref.at[plane, member], member_at(peer))
        for k, peer in enumerate(peers)
    ]
    for moving in first:
        moving.start()

    others = [across, along, across + along - group]
    keep = pltpu.make_async_copy(frames(x_ref, group), frames(held, group), local_sem.at[1])
    keep.start()

    def piece(ref, j, a):
        at = pl.ds(pl.multiple_of(j * step, 16), step)
        return ref.at[at, a * features : (a + 1) * features]

    def spread(owner, landing, a):
        return pltpu.make_async_remote_copy(
            src_ref=piece(x_ref, owner, a),
            dst_ref=piece(held, landing, a),
            send_sem=send_sem.at[(10, 36)[a] + owner],
            recv_sem=recv_sem.at[(10, 36)[a] + landing],
            device_id={"dp": owner},
            device_id_type=MESH_ID,
        )

    for a in range(2):
        for owner in others:
            spread(owner, group, a).start()

    def rise(row, a):
        return pltpu.make_async_remote_copy(
            src_ref=piece(held, row, a),
            dst_ref=piece(t_ref, plane, a),
            send_sem=send_sem.at[(28, 32)[a] + row],
            recv_sem=recv_sem.at[(28, 32)[a] + plane],
            device_id={"z": row},
            device_id_type=MESH_ID,
        )

    stay = [
        pltpu.make_async_copy(piece(held, plane, a), piece(t_ref, plane, a), local_sem.at[(4, 9)[a]])
        for a in range(2)
    ]

    def pass_on(row, a):
        pl.when(row == plane)(stay[a].start)
        pl.when(row != plane)(rise(row, a).start)

    keep.wait()
    for a in range(2):
        pass_on(group, a)

    fetches[2].wait()
    fetches[3].wait()

    def move(m, at, start, width):
        one[m, :, at : at + width] = columns[:, start : start + width].astype(one.dtype)

    for m in range(8):
        for k in range(6):
            move(m, (4 * part if k < 3 else -3 * part) + k * part, k * D + m * part, part)
        for k in range(2):
            move(m, 3 * part + k * text, 6 * D + k * CTXW + m * text, text)
    for owner in others:
        spread(owner, owner, 0).wait_recv()
        pass_on(owner, 0)
    weights_done = exchange_steps(
        block, block, one, one_ref, local_sem.at[2], mover(send_sem, recv_sem, 14)
    )

    fetches[4].wait()
    by_feature[...] = wide(tokens).T.astype(by_feature.dtype)

    def text_copy(k, peer):
        return pltpu.make_async_remote_copy(
            src_ref=by_feature.at[pl.ds(pl.multiple_of(peer * text_rows, 16), text_rows), :],
            dst_ref=mine_ref,
            send_sem=send_sem.at[21 + k],
            recv_sem=recv_sem.at[21],
            device_id=member_at(peer),
            device_id_type=MESH_ID,
        )

    own_text = by_feature.at[pl.ds(pl.multiple_of(member * text_rows, 16), text_rows), :]
    text_local = pltpu.make_async_copy(own_text, mine_ref, local_sem.at[3])

    @pl.when(teacher)
    def _():
        text_local.start()
        for k, peer in enumerate(peers):
            text_copy(k, peer).start()

    for owner in others:
        spread(owner, owner, 1).wait_recv()
        pass_on(owner, 1)

    for k in range(7):
        landed = all_ref.at[plane, lax.rem(member + 7 - k, 8)]
        near_copy(k, landed, landed, member_at(peers[k])).wait_recv()
    small_local.wait()
    second = [
        line_copy(k, all_ref.at[plane], all_ref.at[plane], {"z": there})
        for k, there in enumerate(line)
    ]
    for moving in second:
        moving.start()
    for k in range(3):
        landed = all_ref.at[lax.rem(plane + 3 - k, 4)]
        line_copy(k, landed, landed, {"z": line[k]}).wait_recv()

    for a in range(2):
        for there in line:
            landed = piece(t_ref, there, a)
            pltpu.make_async_remote_copy(
                src_ref=landed,
                dst_ref=landed,
                send_sem=send_sem.at[(28, 32)[a] + there],
                recv_sem=recv_sem.at[(28, 32)[a] + there],
                device_id={"z": there},
                device_id_type=MESH_ID,
            ).wait_recv()
        stay[a].wait()
    weights_done()

    @pl.when(teacher)
    def _():
        text_local.wait()
        for k, peer in enumerate(peers):
            text_copy(k, peer).wait_send()

    @pl.when(jnp.logical_not(teacher))
    def _():
        text_copy(0, peers[0]).wait_recv()

    for moving in first + second:
        moving.wait_send()
    for a in range(2):
        for owner in others:
            spread(owner, group, a).wait_send()
        for there in line:
            rise(there, a).wait_send()


def opening(latents, cotangent, small, text, sheet):
    frames, features = latents.shape
    local = (frames, 2 * features)
    one = (8, sheet.shape[0], (6 * D + 2 * CTXW) // 8)
    low = jnp.bfloat16
    return kernel_call(
        opening_kernel,
        out_shape=(
            jax.ShapeDtypeStruct(local, low),
            jax.ShapeDtypeStruct((4, 8) + small.shape, small.dtype),
            jax.ShapeDtypeStruct((text.shape[1] // 8, text.shape[0]), text.dtype),
            jax.ShapeDtypeStruct(one, low),
        ),
        in_specs=[IN_HBM] * 5,
        out_specs=(IN_HBM,) * 4,
        scratch_shapes=[
            pltpu.VMEM(local, low),
            pltpu.VMEM(local, low),
            pltpu.VMEM((sheet.shape[0], 6 * D + 2 * CTXW), jnp.float32),
            pltpu.VMEM(one, low),
            pltpu.VMEM(text.shape, low),
            pltpu.VMEM(text.shape[::-1], low),
            pltpu.SemaphoreType.DMA((11,)),
            pltpu.SemaphoreType.DMA((40,)),
            pltpu.SemaphoreType.DMA((40,)),
        ],
        compiler_params=pltpu.CompilerParams(
            collective_id=identity_of("opening", sheet),
            has_side_effects=True,
            vmem_limit_bytes=16 * 2**20,
        ),
        cost_estimate=BRIEF,
        name="opening",
    )(latents, cotangent, small, text, sheet)


def first_gather_kernel(
    x_ref, y_ref, sheet_ref, ox_ref, oy_ref, gu_ref, down_ref, local_sem, send_sem, recv_sem
):
    place = member_lanes(x_ref.shape[1])
    width = FF // 8
    greet([member_at(peer) for peer in plane_peers()])
    finish = [
        gather_steps(place, x_ref, ox_ref, local_sem.at[0], mover(send_sem, recv_sem)),
        gather_steps(place, y_ref, oy_ref, local_sem.at[1], mover(send_sem, recv_sem, 14)),
    ]
    for k, (ref, start) in enumerate(((gu_ref, 0), (gu_ref, width), (down_ref, 0))):
        source, target = sheet_part(6 * D + k * FF, width), block_part(start, width)
        copy = mover(send_sem, recv_sem, 28 + 7 * k)
        finish.append(exchange_steps(source, target, sheet_ref, ref, local_sem.at[2 + k], copy))
    for end in finish:
        end()


def first_gather(shard, other, sheet):
    rows, width = shard.shape
    whole = jax.ShapeDtypeStruct((rows, 8 * width), shard.dtype)
    return kernel_call(
        first_gather_kernel,
        out_shape=(
            whole,
            whole,
            jax.ShapeDtypeStruct((8, sheet.shape[0], FF // 4), sheet.dtype),
            jax.ShapeDtypeStruct((8, sheet.shape[0], FF // 8), sheet.dtype),
        ),
        in_specs=[IN_HBM] * 3,
        out_specs=(IN_HBM,) * 4,
        scratch_shapes=[
            pltpu.SemaphoreType.DMA((5,)),
            pltpu.SemaphoreType.DMA((49,)),
            pltpu.SemaphoreType.DMA((49,)),
        ],
        compiler_params=pltpu.CompilerParams(
            collective_id=identity_of("first gather", shard, sheet), has_side_effects=True
        ),
        cost_estimate=BRIEF,
        name="first_gather",
    )(shard, other, sheet)


def turn_steps(x_ref, held, t_ref, local_sem, send_sem, recv_sem, first):
    group, core, across, along = near()
    plane = lax.axis_index("z")
    step = x_ref.shape[0] // 4
    groups = [across, along, across + along - group]
    inner = lax.div(plane * (3 - plane), 2)
    two_off, mirrored = lax.rem(plane + 2, 4), 3 - plane
    line = [
        plane + 1 - 2 * lax.rem(plane, 2),
        inner * mirrored + (1 - inner) * two_off,
        inner * two_off + (1 - inner) * mirrored,
    ]

    def frames(ref, j):
        return ref.at[pl.ds(pl.multiple_of(j * step, 16), step), :]

    def copy(source, target, sent, landed, peer):
        return pltpu.make_async_remote_copy(
            src_ref=source,
            dst_ref=target,
            send_sem=send_sem.at[first + sent],
            recv_sem=recv_sem.at[first + landed],
            device_id=peer,
            device_id_type=MESH_ID,
        )

    def along_line(there):
        return copy(frames(x_ref, there), frames(held, plane), there, plane, {"z": there})

    def onward(owner):
        return copy(
            frames(held, owner), frames(t_ref, group), 4 + owner, 4 + group, {"dp": owner}
        )

    own = pltpu.make_async_copy(frames(x_ref, plane), frames(held, plane), local_sem.at[0])
    keep = pltpu.make_async_copy(frames(held, group), frames(t_ref, group), local_sem.at[1])

    def pass_on(owner):
        pl.when(owner == group)(keep.start)
        pl.when(owner != group)(onward(owner).start)

    def start():
        own.start()
        for there in line:
            along_line(there).start()
        own.wait()
        pass_on(plane)

    def arrive():
        for origin in line:
            at = frames(held, origin)
            copy(at, at, origin, origin, {"z": origin}).wait_recv()
            pass_on(origin)

    def finish():
        for origin in groups:
            at = frames(t_ref, origin)
            copy(at, at, 4 + origin, 4 + origin, {"dp": origin}).wait_recv()
        keep.wait()
        for there in line:
            along_line(there).wait_send()
        for owner in groups:
            onward(owner).wait_send()

    return start, arrive, finish


def prepare_kernel(order_ref, y_ref, base_ref, gu_ref, down_ref, two_ref, x_ref, q_ref, y):
    reorder_blocks(y_ref, y, lambda b: order_ref[1, b])
    x_ref[...] = (base_ref[...] + y[...]).T.astype(x_ref.dtype)
    q_ref[...] = jnp.full(q_ref.shape, square_sum((gu_ref, down_ref, two_ref)), jnp.float32)


def prepare(orders, y, base, gu, down, two):
    features, width = base.shape
    return kernel_call(
        prepare_kernel,
        out_shape=(
            jax.ShapeDtypeStruct((width, features), jnp.bfloat16),
            jax.ShapeDtypeStruct((8, 128), jnp.float32),
        ),
        in_specs=[IN_SMEM] + [IN_VMEM] * 5,
        out_specs=(IN_VMEM,) * 2,
        scratch_shapes=[pltpu.VMEM(base.shape, jnp.float32)],
        compiler_params=pltpu.CompilerParams(vmem_limit_bytes=16 * 2**20),
        name="prepare",
    )(orders, y.reshape(orders.shape[1], -1, width), base, gu, down, two)


def square_sum(refs):
    total = jnp.zeros((), jnp.float32)
    for ref in refs:
        line_sum = jnp.zeros((1, ref.shape[2]), jnp.float32)
        for m in range(8):
            line_sum += jnp.sum(jnp.square(wide(ref.at[m])), axis=0, keepdims=True)
        total += jnp.sum(line_sum)
    return total


def closing_kernel(
    x_ref,
    p_ref,
    w_ref,
    g_ref,
    _,
    t_ref,
    o_ref,
    s_ref,
    all_ref,
    held,
    tall,
    q_ref,
    one,
    local_sem,
    send_sem,
    recv_sem,
):
    fetch = pltpu.make_async_copy(w_ref, one, local_sem.at[0])
    fetch.start()
    group, core, _, _ = near()
    member = group * 2 + core
    plane = lax.axis_index("z")
    turned_line = [lax.rem(plane + k, 4) for k in range(1, 4)]
    peers = plane_peers()
    greet([member_at(peer) for peer in peers] + [{"z": there} for there in turned_line])
    start, arrive, finish = turn_steps(
        x_ref, held, t_ref, local_sem.at[pl.ds(1, 2)], send_sem, recv_sem, 0
    )
    gain_line = mover(send_sem, recv_sem, 23)
    gain_plane = mover(send_sem, recv_sem, 26)
    square_plane = mover(send_sem, recv_sem, 33)
    square_line = mover(send_sem, recv_sem, 40)
    back_line = [lax.rem(plane + 3 - k, 4) for k in range(3)]
    gain_local = pltpu.make_async_copy(g_ref, tall.at[plane], local_sem.at[3])
    gain_local.start()
    sent = [
        gain_line(k, g_ref, tall.at[plane], {"z": there}) for k, there in enumerate(turned_line)
    ]
    for moving in sent:
        moving.start()
    start()
    fetch.wait()
    weights_done = exchange_steps(
        block, block, one, o_ref, local_sem.at[5], mover(send_sem, recv_sem, 16)
    )
    q_ref[...] = p_ref[...] + square_sum((one,))
    square_local = pltpu.make_async_copy(q_ref, all_ref.at[plane, member], local_sem.at[6])
    square_local.start()
    shown = [
        square_plane(k, q_ref, all_ref.at[plane, member], member_at(peer))
        for k, peer in enumerate(peers)
    ]
    for moving in shown:
        moving.start()
    gain_local.wait()
    for k, origin in enumerate(back_line):
        gain_line(k, tall.at[origin], tall.at[origin], {"z": origin}).wait_recv()
    tall[4] = tall[0] + tall[1] + tall[2] + tall[3]
    gain_keep = pltpu.make_async_copy(tall.at[4], s_ref.at[member], local_sem.at[7])
    gain_keep.start()
    given = [
        gain_plane(k, tall.at[4], s_ref.at[member], member_at(peer)) for k, peer in enumerate(peers)
    ]
    for moving in given:
        moving.start()
    square_local.wait()
    for k in range(7):
        shown_here = all_ref.at[plane, lax.rem(member + 7 - k, 8)]
        square_plane(k, shown_here, shown_here, member_at(peers[k])).wait_recv()
    for k, there in enumerate(turned_line):
        shown.append(square_line(k, all_ref.at[plane], all_ref.at[plane], {"z": there}))
        shown[-1].start()
    arrive()
    finish()
    weights_done()
    gain_keep.wait()
    for k in range(7):
        given_here = s_ref.at[lax.rem(member + 7 - k, 8)]
        gain_plane(k, given_here, given_here, member_at(peers[k])).wait_recv()
    for k, origin in enumerate(back_line):
        square_line(k, all_ref.at[origin], all_ref.at[origin], {"z": origin}).wait_recv()
    for moving in sent + given + shown:
        moving.wait_send()

def closing(local, squares, one, gains, after):
    return kernel_call(
        closing_kernel,
        out_shape=(
            jax.ShapeDtypeStruct(local.shape, local.dtype),
            jax.ShapeDtypeStruct(one.shape, one.dtype),
            jax.ShapeDtypeStruct((8,) + gains.shape, gains.dtype),
            jax.ShapeDtypeStruct((4, 8) + squares.shape, jnp.float32),
        ),
        in_specs=[IN_VMEM, IN_VMEM] + [IN_HBM] * 3,
        out_specs=(IN_VMEM,) * 4,
        scratch_shapes=[
            pltpu.VMEM(local.shape, local.dtype),
            pltpu.VMEM((5,) + gains.shape, gains.dtype),
            pltpu.VMEM(squares.shape, jnp.float32),
            pltpu.VMEM(one.shape, one.dtype),
            pltpu.SemaphoreType.DMA((8,)),
            pltpu.SemaphoreType.DMA((43,)),
            pltpu.SemaphoreType.DMA((43,)),
        ],
        compiler_params=pltpu.CompilerParams(
            collective_id=identity_of("closing", one),
            has_side_effects=True,
            vmem_limit_bytes=8 * 2**20,
        ),
        cost_estimate=BRIEF,
        name="closing",
    )(local, squares, one, gains, after)


def turned(values, cosine, sine_table):
    half = HEAD // 2
    first_half, second_half = values[:half], values[half:]
    return jnp.concatenate(
        [
            first_half * cosine - second_half * sine_table,
            second_half * cosine + first_half * sine_table,
        ],
        axis=0,
    )


def attend_kernel(
    w_ref,
    h_ref,
    cos_ref,
    sin_ref,
    seg_ref,
    column_ref,
    part_out,
    p_out,
    o_ref,
    weight,
    frames,
    joint_ref,
    part_ref,
    p_ref,
    sems,
):
    heads, length = joint_ref.shape[1], joint_ref.shape[3]
    span = heads * HEAD
    tiles = length // 256
    fetches = [pltpu.make_async_copy(w_ref, weight, sems.at[0])]
    fetches += [
        pltpu.make_async_copy(
            h_ref.at[:, i * 256 : (i + 1) * 256], frames.at[:, i * 256 : (i + 1) * 256], sems.at[1 + i]
        )
        for i in range(tiles)
    ]
    for fetch in fetches:
        fetch.start()
    cosine, sine_table = cos_ref[...], sin_ref[...]
    fetches[0].wait()
    by_row = [weight[:, (4 + k) * span : (5 + k) * span].T for k in range(3)]
    for i in range(tiles):
        fetches[1 + i].wait()
        at = slice(i * 256, (i + 1) * 256)
        for k in range(3):
            part = jnp.dot(by_row[k], frames[:, at], preferred_element_type=jnp.float32)
            for h in range(heads):
                joint_ref[k, h, :, at] = part[h * HEAD : (h + 1) * HEAD]

    kept = []
    for h in range(heads):
        queries = turned(joint_ref[0, h], cosine, sine_table)
        part_ref[0, h] = queries.astype(part_ref.dtype)
        keys = turned(joint_ref[1, h], cosine, sine_table)
        part_ref[1, h] = keys.astype(part_ref.dtype)
        part_ref[2, h] = joint_ref[2, h].astype(part_ref.dtype)
        by_key = keys.T.astype(part_ref.dtype)

        @pl.loop(0, tiles)
        def _(i, h=h, by_key=by_key):
            at = pl.ds(pl.multiple_of(i * 256, 256), 256)
            scores = jnp.dot(
                by_key, part_ref[0, h, :, at], preferred_element_type=jnp.float32
            ) * (HEAD**-0.5)
            scores = jnp.where(column_ref[...] == seg_ref[:, at], scores, MASKED_SCORE)
            exponent = jnp.exp(scores - jnp.max(scores, axis=0, keepdims=True))
            probs = exponent * (1.0 / jnp.sum(exponent, axis=0, keepdims=True))
            p_ref[h, :, at] = probs.astype(p_ref.dtype)
            out = jnp.dot(part_ref[2, h], p_ref[h, :, at], preferred_element_type=jnp.float32)
            o_ref[h * HEAD : (h + 1) * HEAD, at] = out.astype(o_ref.dtype)

        kept.append(pltpu.make_async_copy(p_ref.at[h], p_out.at[h], sems.at[1 + tiles + h]))
        kept[-1].start()
    kept.append(pltpu.make_async_copy(part_ref, part_out, sems.at[1 + tiles + heads]))
    kept[-1].start()
    for keep in kept:
        keep.wait()


def attend(weight, frames, cosine, sine_table, segments):
    heads, length = D // HEAD // 8, frames.shape[1]
    joint = (3, heads, HEAD, length)
    small = jnp.bfloat16
    return kernel_call(
        attend_kernel,
        out_shape=(
            jax.ShapeDtypeStruct(joint, small),
            jax.ShapeDtypeStruct((heads, length, length), small),
            jax.ShapeDtypeStruct((heads * HEAD, length), small),
        ),
        in_specs=[IN_HBM] * 2 + [IN_VMEM] * 4,
        out_specs=(IN_HBM, IN_HBM, IN_VMEM),
        scratch_shapes=[
            pltpu.VMEM(weight.shape, small),
            pltpu.VMEM(frames.shape, small),
            pltpu.VMEM(joint, jnp.float32),
            pltpu.VMEM(joint, small),
            pltpu.VMEM((heads, length, length), small),
            pltpu.SemaphoreType.DMA((2 + length // 256 + heads,)),
        ],
        compiler_params=pltpu.CompilerParams(vmem_limit_bytes=36 * 2**20),
        name="attend",
    )(weight, frames, cosine, sine_table, segments[None, :], segments[:, None])


def cross_kernel(w_ref, h_ref, kv_ref, cq_ref, p_ref, o_ref, weight, frames, sems):
    heads, text, length = p_ref.shape
    span = heads * HEAD
    tiles = length // 256
    fetches = [pltpu.make_async_copy(w_ref.at[:, 128:384], weight, sems.at[0])]
    fetches += [
        pltpu.make_async_copy(
            h_ref.at[:, i * 256 : (i + 1) * 256], frames.at[:, i * 256 : (i + 1) * 256], sems.at[1 + i]
        )
        for i in range(tiles)
    ]
    for fetch in fetches:
        fetch.start()
    keys = [
        wide(kv_ref.at[h * HEAD : (h + 1) * HEAD, :text]).T.astype(cq_ref.dtype)
        for h in range(heads)
    ]
    fetches[0].wait()
    by_row = weight[:, span - 128 : 2 * span - 128].T
    for i in range(tiles):
        fetches[1 + i].wait()
        at = slice(i * 256, (i + 1) * 256)
        cq_ref[:, at] = jnp.dot(
            by_row, frames[:, at], preferred_element_type=jnp.float32
        ).astype(cq_ref.dtype)
        for h in range(heads):
            of = slice(h * HEAD, (h + 1) * HEAD)
            scores = jnp.dot(keys[h], cq_ref[of, at], preferred_element_type=jnp.float32) * (
                HEAD**-0.5
            )
            exponent = jnp.exp(scores - jnp.max(scores, axis=0, keepdims=True))
            probs = exponent * (1.0 / jnp.sum(exponent, axis=0, keepdims=True))
            p_ref[h, :, at] = probs.astype(p_ref.dtype)
            out = jnp.dot(
                kv_ref[of, text:], p_ref[h, :, at], preferred_element_type=jnp.float32
            )
            o_ref[of, at] = out.astype(o_ref.dtype)


def cross(weight, frames, text_kv):
    rows, length = text_kv.shape[0], frames.shape[1]
    text, small = text_kv.shape[1] // 2, jnp.bfloat16
    return kernel_call(
        cross_kernel,
        out_shape=(
            jax.ShapeDtypeStruct((rows, length), small),
            jax.ShapeDtypeStruct((rows // HEAD, text, length), small),
            jax.ShapeDtypeStruct((rows, length), small),
        ),
        in_specs=[IN_HBM, IN_HBM, IN_VMEM],
        out_specs=(IN_VMEM,) * 3,
        scratch_shapes=[
            pltpu.VMEM((weight.shape[0], 256), small),
            pltpu.VMEM(frames.shape, small),
            pltpu.SemaphoreType.DMA((1 + length // 256,)),
        ],
        compiler_params=pltpu.CompilerParams(vmem_limit_bytes=16 * 2**20),
        name="cross",
    )(weight, frames, text_kv)


def cross_back_kernel(cq_ref, p_ref, kv_ref, grad_ref, dq_ref, dkv_ref):
    heads, text, length = p_ref.shape
    scale = HEAD**-0.5
    for h in range(heads):
        of = slice(h * HEAD, (h + 1) * HEAD)
        by_key = wide(kv_ref.at[of, text:]).T.astype(cq_ref.dtype)
        grad_out = grad_ref[of, :]
        grad_probs = jnp.dot(by_key, grad_out, preferred_element_type=jnp.float32)
        probs = wide(p_ref.at[h])
        weighted = jnp.sum(probs * grad_probs, axis=0, keepdims=True)
        grad_scores = (probs * (grad_probs - weighted)).astype(cq_ref.dtype)
        dq_ref[of, :] = (
            jnp.dot(kv_ref[of, :text], grad_scores, preferred_element_type=jnp.float32) * scale
        ).astype(dq_ref.dtype)
        dkv_ref[of, :text] = (contract_last(cq_ref[of, :], grad_scores) * scale).astype(
            dkv_ref.dtype
        )
        dkv_ref[of, text:] = contract_last(grad_out, p_ref[h]).astype(dkv_ref.dtype)


def cross_back(cross_q, probs, text_kv, grad):
    return kernel_call(
        cross_back_kernel,
        out_shape=(
            jax.ShapeDtypeStruct(cross_q.shape, cross_q.dtype),
            jax.ShapeDtypeStruct(text_kv.shape, text_kv.dtype),
        ),
        in_specs=[IN_VMEM] * 4,
        out_specs=(IN_VMEM,) * 2,
        compiler_params=pltpu.CompilerParams(vmem_limit_bytes=16 * 2**20),
        name="cross_back",
    )(cross_q, probs, text_kv, grad)


def attend_back_kernel(
    part_in, p_in, g_in, cos_ref, sin_ref, o_ref, part_ref, p_ref, grad_ref, dq_ref, dk_ref, dv_ref, sems
):
    heads, length = part_ref.shape[1], part_ref.shape[3]
    fetches = [
        pltpu.make_async_copy(part_in, part_ref, sems.at[0]),
        pltpu.make_async_copy(g_in, grad_ref, sems.at[1]),
    ]
    fetches += [
        pltpu.make_async_copy(p_in.at[h], p_ref.at[h], sems.at[2 + h]) for h in range(heads)
    ]
    for fetch in fetches:
        fetch.start()
    cosine, sine_table = cos_ref[...], -sin_ref[...]
    scale = HEAD**-0.5
    fetches[0].wait()
    fetches[1].wait()
    for h in range(heads):
        of = slice(h * HEAD, (h + 1) * HEAD)
        by_key = wide(part_ref.at[2, h]).T.astype(part_ref.dtype)
        dk_ref[...] = jnp.zeros_like(dk_ref)
        dv_ref[...] = jnp.zeros_like(dv_ref)
        fetches[2 + h].wait()

        @pl.loop(0, length // 256)
        def _(i, h=h, of=of, by_key=by_key):
            at = pl.ds(pl.multiple_of(i * 256, 256), 256)
            grad_out = grad_ref[of, at]
            grad_probs = jnp.dot(by_key, grad_out, preferred_element_type=jnp.float32)
            low_probs = p_ref[h, :, at]
            probs = low_probs.astype(jnp.float32)
            weighted = jnp.sum(probs * grad_probs, axis=0, keepdims=True)
            grad_scores = (probs * (grad_probs - weighted)).astype(part_ref.dtype)
            dq_ref[:, at] = jnp.dot(
                part_ref[1, h], grad_scores, preferred_element_type=jnp.float32
            )
            dk_ref[...] += contract_last(part_ref[0, h, :, at], grad_scores)
            dv_ref[...] += contract_last(grad_out, low_probs)

        span = heads * HEAD
        grad_queries = turned(dq_ref[...] * scale, cosine, sine_table)
        grad_keys = turned(dk_ref[...] * scale, cosine, sine_table)
        o_ref[of, :] = grad_queries.astype(o_ref.dtype)
        o_ref[span + of.start : span + of.stop, :] = grad_keys.astype(o_ref.dtype)
        o_ref[2 * span + of.start : 2 * span + of.stop, :] = dv_ref[...].astype(o_ref.dtype)


def attend_back(parts, probs, grad, cosine, sine_table):
    _, heads, _, length = parts.shape
    return kernel_call(
        attend_back_kernel,
        out_shape=jax.ShapeDtypeStruct((3 * heads * HEAD, length), jnp.bfloat16),
        in_specs=[IN_HBM] * 3 + [IN_VMEM] * 2,
        out_specs=IN_VMEM,
        scratch_shapes=[pltpu.VMEM(array.shape, array.dtype) for array in (parts, probs, grad)]
        + [pltpu.VMEM((HEAD, length), jnp.float32)] * 3
        + [pltpu.SemaphoreType.DMA((2 + heads,))],
        compiler_params=pltpu.CompilerParams(vmem_limit_bytes=32 * 2**20),
        name="attend_back",
    )(parts, probs, grad, cosine, sine_table)


def update_kernel(
    block_ref,
    rate_ref,
    one_ref,
    two_ref,
    feed_ref,
    all_ref,
    gain_ref,
    output_ref,
    latent_ref,
    sheet_ref,
    first_ref,
    second_ref,
    grad_out,
    first_out,
    second_out,
    sheet_out,
    copy_out,
    norm_out,
    gain_out,
    output_out,
    latent_out,
    grad,
    gain,
    scale,
):
    step = pl.program_id(0)
    part = D // 8
    text = CTXW // 8

    @pl.when(step == 0)
    def _():
        summed = jnp.sum(gain_ref[...], axis=0)
        rows = grad.shape[0]
        here = lax.broadcasted_iota(jnp.int32, (rows, D), 1) == (
            lax.broadcasted_iota(jnp.int32, (rows, D), 0) + block_ref[0] * rows
        )
        gain[...] = lax.dot_general(
            here.astype(jnp.float32),
            summed,
            (((1,), (1,)), ((), ())),
            precision=HIGHEST,
            preferred_element_type=jnp.float32,
        )
        norm = jnp.sqrt(jnp.sum(all_ref[:, :, 0:1, 0:1]) + jnp.sum(summed * summed))
        norm_out[0] = norm
        scale[0] = 1.0 / jnp.maximum(norm, 1.0)
        gain_out[...] = gain[...] * scale[0]
        output_out[...] = output_ref[...]
        latent_out[...] = wide(latent_ref)

    for k in range(6):

        @pl.when(step == k // 2)
        def _(k=k):
            ref, start = (one_ref, k * part) if k < 3 else (two_ref, (k - 3) * part)
            for m in range(8):
                at = (k % 2) * D + m * part
                grad[:, at : at + part] = wide(ref.at[m, :, start : start + part])

    @pl.when(jnp.logical_and(step >= 3, step < 9))
    def _():
        grad[...] = wide(feed_ref)

    @pl.when(step == 9)
    def _():
        for m in range(8):
            for k in range(2):
                start = 3 * part + k * text
                at = k * CTXW + m * text
                grad[:, at : at + text] = wide(two_ref.at[m, :, start : start + text])
        grad[:, D : D + 8] = gain[...]

    for half in range(2):
        at = slice(half * D, (half + 1) * D)
        clipped = grad[:, at] * scale[0]
        sheet = sheet_ref[:, at]
        first_new = BETA_ONE * first_ref[:, at] + (1.0 - BETA_ONE) * clipped
        second_new = BETA_TWO * second_ref[:, at] + (1.0 - BETA_TWO) * clipped * clipped
        mean_hat = first_new * (1.0 / (1.0 - BETA_ONE**STEP))
        square_hat = second_new * (1.0 / (1.0 - BETA_TWO**STEP))
        sheet_new = sheet - rate_ref[2 * step + half] * (
            mean_hat / (jnp.sqrt(square_hat) + EPS_ADAM) + WEIGHT_DECAY * sheet
        )
        grad_out[:, at] = clipped
        first_out[:, at] = first_new
        second_out[:, at] = second_new
        sheet_out[:, at] = sheet_new
        copy_out[:, at] = sheet_new.astype(copy_out.dtype)


def sheet_update(
    block_index, length, one, two, feed_part, squares, gains, output, latent, sheet, first, second
):
    rows = sheet.shape[0]
    frames = output.shape
    rates = column_spread(length)[jnp.minimum(jnp.arange(20) * D, SHEET - 1)]
    column_block = pl.BlockSpec((rows, 2 * D), lambda i: (0, i))
    like = jax.ShapeDtypeStruct(sheet.shape, sheet.dtype)

    def whole(shape):
        return pl.BlockSpec(shape, lambda i: (0,) * len(shape))

    sheet, first, second, feed_part = (
        pltpu.with_memory_space_constraint(array, pltpu.HBM)
        for array in (sheet, first, second, feed_part)
    )
    return pl.pallas_call(
        update_kernel,
        grid=(10,),
        out_shape=(like, like, like, like, jax.ShapeDtypeStruct(sheet.shape, jnp.bfloat16))
        + (jax.ShapeDtypeStruct((1,), jnp.float32), jax.ShapeDtypeStruct((rows, 8), jnp.float32))
        + (
            jax.ShapeDtypeStruct(frames, jnp.bfloat16),
            jax.ShapeDtypeStruct(frames, jnp.float32),
        ),
        in_specs=[
            IN_SMEM,
            IN_SMEM,
            IN_VMEM,
            IN_VMEM,
            pl.BlockSpec((rows, 2 * D), lambda i: (0, jnp.clip(i - 3, 0, 5))),
            IN_VMEM,
            IN_VMEM,
            IN_VMEM,
            IN_VMEM,
            column_block,
            column_block,
            column_block,
        ],
        out_specs=(column_block,) * 5
        + (IN_SMEM, whole((rows, 8)), whole(frames), whole(frames)),
        scratch_shapes=[
            pltpu.VMEM((rows, 2 * D), jnp.float32),
            pltpu.VMEM((rows, 8), jnp.float32),
            pltpu.SMEM((1,), jnp.float32),
        ],
        compiler_params=pltpu.CompilerParams(vmem_limit_bytes=32 * 2**20),
        name="sheet_update",
    )(
        block_index,
        rates,
        one,
        two,
        feed_part,
        squares,
        gains,
        output,
        latent,
        sheet,
        first,
        second,
    )


def pick_blocks(blocks, order):
    return blocks.at[order].get(mode="promise_in_bounds")


def gather_line(mine, order):
    blocks = lax.all_gather(mine, "z", axis=0, tiled=True)
    return pick_blocks(blocks, order).reshape(-1, mine.shape[-1])


def gather_slots(mine):
    return lax.all_gather(mine, "z", axis=0, tiled=True).reshape(-1, mine.shape[-1])


def sort_blocks(array, order):
    blocks = array.reshape(order.shape[0], -1, array.shape[-1])
    return pick_blocks(blocks, order).reshape(array.shape)


def as_blocks(grad, order):
    return grad.reshape(order.shape[0], -1, grad.shape[-1])


def scatter_line(blocks):
    return lax.psum_scatter(blocks, "z", scatter_dimension=0, tiled=True)


def plane_plan(latents, context, clip_starts, buckets, owners, cotangent, sheet, first, second):
    groups = lax.axis_size("dp")
    planes = lax.axis_size("z")
    cores = lax.axis_size("core")
    members = groups * cores
    frames = latents.shape[1]
    length = frames * members
    rows = sheet.shape[0]
    blocks = owners.shape[0]
    head_count = D // HEAD // members
    span = D // members
    units = FF // members
    score_scale = HEAD ** (-0.5)
    tail_col = 6 * D + 3 * FF
    gain_col = tail_col + 2 * CTXW
    plane = lax.axis_index("z")

    group_ids = jnp.arange(blocks, dtype=jnp.int32)
    inverse = jnp.sum(
        jnp.where(owners[None, :] == group_ids[:, None], group_ids[None, :], 0), axis=1
    )
    slot = group_ids.reshape(groups, planes, cores).swapaxes(0, 1).reshape(-1)
    slot_of = jnp.sum(
        jnp.where(slot[None, :] == group_ids[:, None], group_ids[None, :], 0), axis=1
    )
    to_logical = jnp.take(slot_of, inverse)
    to_slots = jnp.take(owners, slot)

    orders = jnp.stack([to_slots, to_logical])
    small = jnp.concatenate(
        [
            jnp.pad(
                sheet[:, gain_col:].astype(jnp.bfloat16).astype(jnp.float32).T,
                ((0, 0), (0, 64 - rows)),
            ),
            jnp.pad(clip_starts.astype(jnp.float32), ((0, 7), (0, 64 - clip_starts.shape[1]))),
        ],
        axis=1,
    )
    both, small, text_mine, mine_one = opening(
        latents[0], cotangent[0], small, context[0], sheet
    )
    mine_one, later = lax.optimization_barrier((mine_one, sheet))
    low_sheet = later.astype(jnp.bfloat16)
    weight_one = gather_slots(mine_one)
    gains = pick_blocks(small[..., :rows].reshape(blocks, 8, rows), to_logical)
    gains = gains.swapaxes(1, 2).reshape(D, 8)
    starts = lax.dynamic_index_in_dim(
        small[0, :, 0, 64 : 64 + clip_starts.shape[1]], plane * cores, 0, False
    )
    starts = starts.astype(jnp.int32)

    bucket_ids = jnp.arange(NB, dtype=jnp.int32)
    bucket_pick = (bucket_ids == buckets[plane]).astype(jnp.float32)
    counts = jnp.sum((buckets[:, None] == bucket_ids[None, :]).astype(jnp.float32), axis=0)
    row_weight = buckets.shape[0] / (NB * jnp.sum(bucket_pick * counts))
    gain_one = gains[:, 0:1]
    gain_two = gains[:, 1:2]
    gain_three = gains[:, 2:3]
    time_gain = jnp.sum(gains[:, 3:] * bucket_pick[None, :], axis=1, keepdims=True)

    tokens = both[:, :D].astype(jnp.float32).T
    grad_out = both[:, D:].astype(jnp.float32).T * row_weight

    rest = frames // planes
    place = jnp.arange(length, dtype=jnp.int32).reshape(planes, cores, groups, rest)
    positions = place.transpose(2, 1, 0, 3).reshape(-1)
    segments = segment_ids(starts, positions)
    frequency = jnp.exp(
        -math.log(10000.0) * jnp.arange(HEAD // 2, dtype=jnp.float32) / (HEAD // 2)
    )
    angles = frequency[:, None] * positions.astype(jnp.float32)[None, :]
    cosine = jnp.cos(angles)
    sine_table = jnp.sin(angles)

    normed_one, inverse_one = norm_columns(tokens)
    scaled_one = gain_one * time_gain
    h_one, grad_ff, mine_gu, mine_down = first_gather(
        sort_blocks((normed_one * scaled_one).astype(jnp.bfloat16), to_slots),
        sort_blocks(grad_out.astype(jnp.bfloat16), to_slots),
        low_sheet,
    )
    weight_gu = gather_slots(mine_gu)
    line_down = gather_slots(mine_down)

    parts, probs, attn_out = attend(weight_one, h_one, cosine, sine_table, segments)
    attn_out, x_one, normed_two, inverse_two, h_two, text_kv = project(
        "sum",
        0,
        orders,
        attn_out,
        weight_one,
        tokens,
        gain_two,
        text_mine,
    )

    cross_q, cross_probs, cross_out = cross(weight_one, h_two, text_kv)
    cross_out, x_two, normed_three, inverse_three, h_three = project(
        "slots",
        2 * span,
        orders,
        cross_out,
        weight_one,
        x_one,
        gain_three,
    )

    gate_up = contract_rows(weight_gu, h_three)
    gate_pre = gate_up[:units]
    up_part = gate_up[units:]
    sigmoid_gate = jax.nn.sigmoid(gate_pre)
    silu_gate = gate_pre * sigmoid_gate
    hidden = (silu_gate * up_part).astype(jnp.bfloat16)

    grad_blocks_down = as_blocks(contract_last(grad_ff, hidden).astype(jnp.bfloat16), to_slots)
    weight_down, grad_blocks_down = lax.optimization_barrier((line_down, grad_blocks_down))
    sums_down = scatter_line(grad_blocks_down)
    grad_hidden = contract_rows(weight_down, grad_ff)
    grad_gate = grad_hidden * up_part * (sigmoid_gate * (1.0 + gate_pre * (1.0 - sigmoid_gate)))
    grad_up = grad_hidden * silu_gate
    grad_gu = jnp.concatenate([grad_gate, grad_up], axis=0).astype(jnp.bfloat16)
    grad_x_two, grad_weight_gu, sum_three, grad_cross = back(
        orders,
        weight_gu,
        grad_gu,
        h_three,
        (normed_three, inverse_three, gain_three, grad_out),
        send_rows=True,
        in_slots=True,
        after=[grad_blocks_down],
    )
    grad_blocks_gu = as_blocks(grad_weight_gu, to_slots)
    sums_gu = scatter_line(grad_blocks_gu)
    grad_cross_out, grad_weight_co = back(
        orders, weight_one, grad_cross, cross_out, column=2 * span
    )
    grad_cross_q, grad_text = cross_back(cross_q, cross_probs, text_kv, grad_cross_out)
    grad_x_one, grad_weight_cq, sum_two, grad_attn, grad_text = back(
        orders,
        weight_one,
        grad_cross_q,
        h_two,
        (normed_two, inverse_two, gain_two, grad_x_two),
        column=span,
        send_rows=True,
        text=grad_text,
        in_slots=True,
        after=[sums_down],
    )
    grad_attn_out, grad_weight_two = back(
        orders,
        weight_one,
        grad_attn,
        attn_out,
        beside=(grad_weight_cq, grad_weight_co, grad_text, text_mine),
    )
    grad_blocks_two = as_blocks(grad_weight_two, to_slots)
    sums_two = scatter_line(grad_blocks_two)
    grad_qkv = attend_back(parts, probs, grad_attn_out, cosine, sine_table)
    latent_grad, grad_weight_qkv, sum_one = back(
        orders,
        weight_one,
        grad_qkv,
        h_one,
        (normed_one, inverse_one, scaled_one, grad_x_one),
        column=4 * span,
        in_slots=True,
        after=[sums_gu],
    )
    grad_blocks_one = as_blocks(grad_weight_qkv, to_slots)
    sums_one = scatter_line(grad_blocks_one)
    sums_feed, ff_out, latent_grad = feed(
        sums_gu,
        sums_down,
        weight_down,
        hidden,
        latent_grad,
        [grad_blocks_one],
    )
    sum_one = sum_one[0:1]
    grad_gain_one = sum_one * time_gain.T
    grad_time = sum_one * gain_one.T
    gain_grads = jnp.concatenate(
        [
            grad_gain_one,
            sum_two[0:1],
            sum_three[0:1],
            bucket_pick[:, None] * grad_time,
        ],
        axis=0,
    )
    output, squares = prepare(orders, ff_out, x_two, sums_gu, sums_down, sums_two)
    sums_two = exchange_blocks(sums_two, [sums_feed])
    output, sums_one, gain_sums, squares = closing(
        output, squares, sums_one, gain_grads, sums_two
    )
    place = lax.axis_index("dp") * (planes * cores) + plane * cores + lax.axis_index("core")
    (
        clipped,
        first_new,
        second_new,
        sheet_new,
        sheet_copy,
        grad_norm,
        gain_grad,
        output,
        latent_grad,
    ) = sheet_update(
        lax.dynamic_slice_in_dim(owners, place, 1),
        length,
        sums_one,
        sums_two,
        sums_feed,
        squares,
        gain_sums,
        output,
        latent_grad,
        sheet,
        first,
        second,
    )
    return (
        output[None],
        latent_grad[None],
        grad_norm[0],
        clipped,
        gain_grad,
        first_new,
        second_new,
        sheet_new,
        sheet_copy,
    )


def solution(mesh):
    groups, seq_count = mesh.shape["dp"], mesh.shape["seq"]
    by_plane = groups == 4 and seq_count == 8
    if by_plane:
        mesh = Mesh(mesh.devices.reshape(groups, seq_count // 2, 2), ("dp", "z", "core"))
    seq = ("z", "core") if by_plane else "seq"
    both = ("dp", "z", "core") if by_plane else ("dp", "seq")
    in_specs = (
        P("dp", seq, None),
        P("dp", None, None),
        P("dp", None),
        P(),
        P(),
        P("dp", seq, None),
        P(both, None),
        P(both, None),
        P(both, None),
    )
    out_specs = (
        P("dp", seq, None),
        P("dp", seq, None),
        P(),
        P(both, None),
        P(both, None),
        P(both, None),
        P(both, None),
        P(both, None),
        P(both, None),
    )
    return jax.shard_map(
        plane_plan if by_plane else gather_plan,
        mesh=mesh,
        in_specs=in_specs,
        out_specs=out_specs,
        check_vma=False,
    )
```

```python
import functools
import math

import jax
import jax.numpy as jnp
from jax import lax
from jax.experimental import pallas as pl
from jax.experimental.pallas import tpu as pltpu
from jax.sharding import Mesh
from jax.sharding import PartitionSpec as P

D = 1536
FF = 6144
HEAD = 64
CTXW = 768
CTX = 128
NB = 5
STEP = 10
SHEET = 29192


HIGHEST = lax.Precision.HIGHEST
EPS_NORM = 1e-05
EPS_ADAM = 1e-08
MASKED_SCORE = -1e30
BETA_ONE = 0.5
BETA_TWO = 0.5
WEIGHT_DECAY = 0.01


def reorder(values, ordering):
    leading = values.shape[:-1]
    groups = ordering.shape[0]
    blocks = values.reshape(leading + (groups, values.shape[-1] // groups))
    return jnp.take(blocks, ordering, axis=-2).reshape(values.shape)


def norm_parts(values):
    average = jnp.mean(values, axis=-1, keepdims=True)
    centered = values - average
    variance = jnp.mean(centered * centered, axis=-1, keepdims=True)
    inverse_std = lax.rsqrt(variance + EPS_NORM)
    return (centered * inverse_std, inverse_std)


def norm_back(grad_normed, normed, inverse_std):
    return inverse_std * (
        grad_normed
        - jnp.mean(grad_normed, axis=-1, keepdims=True)
        - normed * jnp.mean(grad_normed * normed, axis=-1, keepdims=True)
    )


def softmax_rows(scores):
    row_max = jnp.max(scores, axis=-1, keepdims=True)
    exponent = jnp.exp(scores - row_max)
    return exponent / jnp.sum(exponent, axis=-1, keepdims=True)


def rope_tables(positions, head_dim):
    half_dim = head_dim // 2
    frequency = jnp.exp(-math.log(10000.0) * jnp.arange(half_dim, dtype=jnp.float32) / half_dim)
    angles = positions.astype(jnp.float32)[:, None] * frequency[None, :]
    return (jnp.cos(angles)[:, None, :], jnp.sin(angles)[:, None, :])


def rotate(values, cosine, sine_table):
    half_dim = values.shape[-1] // 2
    first_half = values[..., :half_dim]
    second_half = values[..., half_dim:]
    return jnp.concatenate(
        [
            first_half * cosine - second_half * sine_table,
            second_half * cosine + first_half * sine_table,
        ],
        axis=-1,
    )


def unrotate(grads, cosine, sine_table):
    half_dim = grads.shape[-1] // 2
    first_half = grads[..., :half_dim]
    second_half = grads[..., half_dim:]
    return jnp.concatenate(
        [
            first_half * cosine + second_half * sine_table,
            second_half * cosine - first_half * sine_table,
        ],
        axis=-1,
    )


def segment_ids(starts, positions):
    return jnp.sum((starts[None, :] <= positions[:, None]).astype(jnp.int32), axis=1) - 1


def column_spread(length):
    column = jnp.arange(SHEET, dtype=jnp.int32)
    base_std = D ** (-0.5)
    spread = jnp.full((SHEET,), base_std, jnp.float32)
    spread = jnp.where(
        (column >= 3 * D) & (column < 4 * D), base_std * math.sqrt(length) / 4.0, spread
    )
    spread = jnp.where((column >= 5 * D) & (column < 6 * D), base_std * math.sqrt(CTX), spread)
    spread = jnp.where((column >= 6 * D + 2 * FF) & (column < 6 * D + 3 * FF), FF ** (-0.5), spread)
    spread = jnp.where(
        (column >= 6 * D + 3 * FF) & (column < 6 * D + 3 * FF + 2 * CTXW), CTXW ** (-0.5), spread
    )
    spread = jnp.where(column >= 6 * D + 3 * FF + 2 * CTXW, 0.3, spread)
    return spread


def inner_rows(left, right):
    return lax.dot_general(
        left, right, (((0,), (0,)), ((), ())), preferred_element_type=jnp.float32
    )


def inner_rows_high(left, right):
    return lax.dot_general(
        left, right, (((0,), (0,)), ((), ())), precision=HIGHEST, preferred_element_type=jnp.float32
    )


def gather_plan(latents, context, clip_starts, buckets, owners, cotangent, sheet, first, second):
    frames = latents.shape[1]
    seq_count = lax.axis_size("seq")
    length = frames * seq_count
    head_count = D // HEAD
    score_scale = HEAD ** (-0.5)
    group_ids = jnp.arange(owners.shape[0], dtype=jnp.int32)
    inverse = jnp.sum(
        jnp.where(owners[None, :] == group_ids[:, None], group_ids[None, :], 0), axis=1
    )
    gathered = lax.all_gather(sheet.astype(jnp.bfloat16), ("dp", "seq"), axis=0, tiled=True)
    tail_col = 6 * D + 3 * FF
    gain_col = tail_col + 2 * CTXW
    gain_rows = reorder(gathered[:, gain_col:].astype(jnp.float32).T, inverse)
    row_index = lax.axis_index("dp")
    bucket_ids = jnp.arange(NB, dtype=jnp.int32)
    bucket_pick = (bucket_ids == buckets[row_index]).astype(jnp.float32)
    counts = jnp.sum((buckets[:, None] == bucket_ids[None, :]).astype(jnp.float32), axis=0)
    row_weight = buckets.shape[0] / (NB * jnp.sum(bucket_pick * counts))
    gain_one = gain_rows[0]
    gain_two = gain_rows[1]
    gain_three = gain_rows[2]
    time_gain = jnp.sum(gain_rows[3:] * bucket_pick[:, None], axis=0)
    tokens = latents[0].astype(jnp.float32)
    positions = lax.axis_index("seq") * frames + jnp.arange(frames, dtype=jnp.int32)
    all_positions = jnp.arange(length, dtype=jnp.int32)
    starts = clip_starts[0]
    same_clip = (
        segment_ids(starts, positions)[:, None] == segment_ids(starts, all_positions)[None, :]
    )[None]
    cosine, sine_table = rope_tables(positions, HEAD)
    normed_one, inverse_one = norm_parts(tokens)
    scaled_one = gain_one * time_gain
    h_one_st = reorder((normed_one * scaled_one).astype(jnp.bfloat16), owners)
    joint_qkv = jnp.dot(h_one_st, gathered[:, : 3 * D], preferred_element_type=jnp.float32)
    queries = rotate(joint_qkv[:, :D].reshape(frames, head_count, HEAD), cosine, sine_table).astype(
        jnp.bfloat16
    )
    key_local = rotate(
        joint_qkv[:, D : 2 * D].reshape(frames, head_count, HEAD), cosine, sine_table
    ).astype(jnp.bfloat16)
    value_local = joint_qkv[:, 2 * D :].reshape(frames, head_count, HEAD).astype(jnp.bfloat16)
    key_all, value_all = (
        lax.all_gather(key_local, "seq", axis=0, tiled=True),
        lax.all_gather(value_local, "seq", axis=0, tiled=True),
    )
    scores = (
        jnp.einsum("qhd,khd->hqk", queries, key_all, preferred_element_type=jnp.float32)
        * score_scale
    )
    attn_probs = softmax_rows(jnp.where(same_clip, scores, MASKED_SCORE))
    probs_low = attn_probs.astype(jnp.bfloat16)
    attn_out = (
        jnp.einsum("hqk,khd->qhd", probs_low, value_all, preferred_element_type=jnp.float32)
        .reshape(frames, D)
        .astype(jnp.bfloat16)
    )
    attn_st = reorder(attn_out, owners)
    x_one = tokens + jnp.dot(
        attn_st, gathered[:, 3 * D : 4 * D], preferred_element_type=jnp.float32
    )
    normed_two, inverse_two = norm_parts(x_one)
    h_two_st = reorder((normed_two * gain_two).astype(jnp.bfloat16), owners)
    cross_q = (
        jnp.dot(h_two_st, gathered[:, 4 * D : 5 * D], preferred_element_type=jnp.float32)
        .astype(jnp.bfloat16)
        .reshape(frames, head_count, HEAD)
    )
    text_tokens = context[0]
    text_kv = jnp.einsum(
        "tc,dec->etd",
        text_tokens,
        gathered[:, tail_col:gain_col].reshape(D, 2, CTXW),
        preferred_element_type=jnp.float32,
    )
    text_kv = reorder(text_kv, inverse).astype(jnp.bfloat16).reshape(2, CTX, head_count, HEAD)
    text_keys = text_kv[0]
    text_values = text_kv[1]
    cross_scores = (
        jnp.einsum("qhd,khd->hqk", cross_q, text_keys, preferred_element_type=jnp.float32)
        * score_scale
    )
    cross_probs = softmax_rows(cross_scores)
    cross_low = cross_probs.astype(jnp.bfloat16)
    cross_out = (
        jnp.einsum("hqk,khd->qhd", cross_low, text_values, preferred_element_type=jnp.float32)
        .reshape(frames, D)
        .astype(jnp.bfloat16)
    )
    cross_st = reorder(cross_out, owners)
    x_two = x_one + jnp.dot(
        cross_st, gathered[:, 5 * D : 6 * D], preferred_element_type=jnp.float32
    )
    normed_three, inverse_three = norm_parts(x_two)
    h_three_st = reorder((normed_three * gain_three).astype(jnp.bfloat16), owners)
    grad_out = cotangent[0].astype(jnp.float32) * row_weight
    grad_ff_st = reorder(grad_out.astype(jnp.bfloat16), owners)
    gate_weight = gathered[:, 6 * D : 6 * D + 2 * FF]
    down_weight = gathered[:, 6 * D + 2 * FF : 6 * D + 3 * FF]
    units = down_weight.shape[1]
    gate_up = jnp.dot(h_three_st, gate_weight, preferred_element_type=jnp.float32)
    gate_pre = gate_up[:, :units]
    up_part = gate_up[:, units:]
    sigmoid_gate = jax.nn.sigmoid(gate_pre)
    silu_gate = gate_pre * sigmoid_gate
    hidden = (silu_gate * up_part).astype(jnp.bfloat16)
    ff_out = reorder(
        jnp.einsum("nf,df->nd", hidden, down_weight, preferred_element_type=jnp.float32), inverse
    )
    result = x_two + ff_out
    grad_hidden = jnp.dot(grad_ff_st, down_weight, preferred_element_type=jnp.float32)
    grad_gate = grad_hidden * up_part * (sigmoid_gate * (1.0 + gate_pre * (1.0 - sigmoid_gate)))
    grad_up = grad_hidden * silu_gate
    grad_gu = jnp.concatenate([grad_gate, grad_up], axis=1).astype(jnp.bfloat16)
    grad_h_three = reorder(
        jnp.einsum("nf,df->nd", grad_gu, gate_weight, preferred_element_type=jnp.float32), inverse
    )
    grad_gain_three = jnp.sum(grad_h_three * normed_three, axis=0)
    grad_x_two = grad_out + norm_back(grad_h_three * gain_three, normed_three, inverse_three)
    grad_cross = grad_x_two.astype(jnp.bfloat16)
    grad_cross_out = (
        reorder(
            jnp.einsum(
                "nd,ed->ne",
                grad_cross,
                gathered[:, 5 * D : 6 * D],
                preferred_element_type=jnp.float32,
            ),
            inverse,
        )
        .astype(jnp.bfloat16)
        .reshape(frames, head_count, HEAD)
    )
    grad_cross_probs = jnp.einsum(
        "qhd,khd->hqk", grad_cross_out, text_values, preferred_element_type=jnp.float32
    )
    grad_cross_scores = (
        cross_probs
        * (grad_cross_probs - jnp.sum(cross_probs * grad_cross_probs, axis=-1, keepdims=True))
    ).astype(jnp.bfloat16)
    grad_cross_q = (
        (
            jnp.einsum(
                "hqk,khd->qhd", grad_cross_scores, text_keys, preferred_element_type=jnp.float32
            )
            * score_scale
        )
        .reshape(frames, D)
        .astype(jnp.bfloat16)
    )
    grad_text_keys = (
        jnp.einsum("hqk,qhd->khd", grad_cross_scores, cross_q, preferred_element_type=jnp.float32)
        * score_scale
    )
    grad_text_values = jnp.einsum(
        "hqk,qhd->khd", cross_low, grad_cross_out, preferred_element_type=jnp.float32
    )
    grad_text = reorder(
        jnp.stack([grad_text_keys.reshape(CTX, D), grad_text_values.reshape(CTX, D)]), owners
    )
    grad_h_two = reorder(
        jnp.einsum(
            "ne,de->nd",
            grad_cross_q,
            gathered[:, 4 * D : 5 * D],
            preferred_element_type=jnp.float32,
        ),
        inverse,
    )
    grad_gain_two = jnp.sum(grad_h_two * normed_two, axis=0)
    grad_x_one = grad_x_two + norm_back(grad_h_two * gain_two, normed_two, inverse_two)
    grad_attn = grad_x_one.astype(jnp.bfloat16)
    grad_attn_out = (
        reorder(
            jnp.einsum(
                "nd,ed->ne",
                grad_attn,
                gathered[:, 3 * D : 4 * D],
                preferred_element_type=jnp.float32,
            ),
            inverse,
        )
        .astype(jnp.bfloat16)
        .reshape(frames, head_count, HEAD)
    )
    key_back, value_back = (key_all, value_all)

    def head_grads(head_items):
        head_probs, head_grad_out, head_values = head_items
        grad_probs = jnp.einsum(
            "qd,kd->qk", head_grad_out, head_values, preferred_element_type=jnp.float32
        )
        return (
            head_probs * (grad_probs - jnp.sum(head_probs * grad_probs, axis=-1, keepdims=True))
        ).astype(jnp.bfloat16)

    grad_scores_low = lax.map(
        head_grads, (attn_probs, jnp.swapaxes(grad_attn_out, 0, 1), jnp.swapaxes(value_back, 0, 1))
    )
    grad_queries = (
        jnp.einsum("hqk,khd->qhd", grad_scores_low, key_back, preferred_element_type=jnp.float32)
        * score_scale
    )
    grad_keys = (
        jnp.einsum("hqk,qhd->khd", grad_scores_low, queries, preferred_element_type=jnp.float32)
        * score_scale
    )
    grad_values = jnp.einsum(
        "hqk,qhd->khd", probs_low, grad_attn_out, preferred_element_type=jnp.float32
    )
    key_sums = lax.psum_scatter(
        jnp.concatenate(
            [
                grad_keys.reshape(frames * lax.axis_size("seq"), D),
                grad_values.reshape(frames * lax.axis_size("seq"), D),
            ],
            axis=1,
        ).astype(jnp.bfloat16),
        "seq",
        scatter_dimension=0,
        tiled=True,
    ).astype(jnp.float32)
    grad_q_raw = unrotate(grad_queries, cosine, sine_table).reshape(frames, D)
    grad_k_raw = unrotate(
        key_sums[:, :D].reshape(frames, head_count, HEAD), cosine, sine_table
    ).reshape(frames, D)
    grad_qkv = jnp.concatenate([grad_q_raw, grad_k_raw, key_sums[:, D:]], axis=1).astype(
        jnp.bfloat16
    )
    grad_h_one = reorder(
        jnp.einsum("ne,de->nd", grad_qkv, gathered[:, : 3 * D], preferred_element_type=jnp.float32),
        inverse,
    )
    grad_gain_one = jnp.sum(grad_h_one * normed_one * time_gain, axis=0)
    grad_time = jnp.sum(grad_h_one * normed_one * gain_one, axis=0)
    latent_grad = grad_x_one + norm_back(grad_h_one * scaled_one, normed_one, inverse_one)
    gain_grads = jnp.concatenate(
        [
            jnp.stack([grad_gain_one, grad_gain_two, grad_gain_three]),
            bucket_pick[:, None] * grad_time[None, :],
        ],
        axis=0,
    )
    gain_grads = reorder(gain_grads, owners).T
    text_float = text_tokens.astype(jnp.float32)
    pieces = [
        inner_rows(h_one_st, grad_qkv),
        inner_rows(attn_st, grad_attn),
        inner_rows(h_two_st, grad_cross_q),
        inner_rows(cross_st, grad_cross),
    ]
    pieces = pieces + [inner_rows(h_three_st, grad_gu), inner_rows(grad_ff_st, hidden)]
    pieces = pieces + [
        inner_rows_high(grad_text[0], text_float),
        inner_rows_high(grad_text[1], text_float),
        gain_grads,
    ]
    other_shard = lax.psum_scatter(
        jnp.concatenate(pieces, axis=1), ("dp", "seq"), scatter_dimension=0, tiled=True
    )
    total_squares = lax.psum(jnp.sum(other_shard * other_shard), ("dp", "seq"))
    grad_norm = jnp.sqrt(total_squares)
    clipped = other_shard / jnp.maximum(grad_norm, 1.0)
    gain_grad = clipped[:, 6 * D + 3 * FF + 2 * CTXW :]
    first_new = BETA_ONE * first + (1.0 - BETA_ONE) * clipped
    second_new = BETA_TWO * second + (1.0 - BETA_TWO) * clipped * clipped
    mean_hat = first_new / (1.0 - BETA_ONE**STEP)
    square_hat = second_new / (1.0 - BETA_TWO**STEP)
    rates = column_spread(length)[None, :]
    sheet_new = sheet - rates * (
        mean_hat / (jnp.sqrt(square_hat) + EPS_ADAM) + WEIGHT_DECAY * sheet
    )
    return (
        result.astype(jnp.bfloat16)[None],
        latent_grad[None],
        grad_norm,
        clipped,
        gain_grad,
        first_new,
        second_new,
        sheet_new,
        sheet_new.astype(jnp.bfloat16),
    )


PLANE = ("dp", "core")


def norm_columns(values):
    average = jnp.mean(values, axis=0, keepdims=True)
    centered = values - average
    variance = jnp.mean(centered * centered, axis=0, keepdims=True)
    inverse_std = lax.rsqrt(variance + EPS_NORM)
    return (centered * inverse_std, inverse_std)


def norm_columns_back(grad_normed, normed, inverse_std):
    return inverse_std * (
        grad_normed
        - jnp.mean(grad_normed, axis=0, keepdims=True)
        - normed * jnp.mean(grad_normed * normed, axis=0, keepdims=True)
    )


def contract_rows(left, right):
    return lax.dot_general(
        left, right, (((0,), (0,)), ((), ())), preferred_element_type=jnp.float32
    )


def contract_last(left, right):
    return lax.dot_general(
        left, right, (((1,), (1,)), ((), ())), preferred_element_type=jnp.float32
    )


def matmul(left, right):
    return jnp.dot(left, right, preferred_element_type=jnp.float32)


MESH_ID = pl.DeviceIdType.MESH
IDENTITIES = {}


def identity_of(name, *arrays):
    key = (name,) + tuple((array.shape, str(array.dtype)) for array in arrays)
    return IDENTITIES.setdefault(key, len(IDENTITIES))


IN_HBM = pl.BlockSpec(memory_space=pltpu.HBM)
IN_SMEM = pl.BlockSpec(memory_space=pltpu.SMEM)
IN_VMEM = pl.BlockSpec(memory_space=pltpu.VMEM)
BRIEF = pl.CostEstimate(flops=0, bytes_accessed=1024, transcendentals=0)


def kernel_call(kernel, *, out_shape, in_specs, out_specs, **options):
    single = not isinstance(out_shape, tuple)
    shapes = (out_shape,) if single else out_shape
    places = (out_specs,) if single else out_specs
    shapes = tuple(
        pltpu.HBM(shape.shape, shape.dtype) if place is IN_HBM else shape
        for shape, place in zip(shapes, places)
    )
    call = pl.pallas_call(
        kernel,
        out_shape=shapes[0] if single else shapes,
        in_specs=in_specs,
        out_specs=out_specs,
        **options,
    )

    def run(*operands):
        return call(
            *[
                pltpu.with_memory_space_constraint(operand, pltpu.HBM)
                if place is IN_HBM
                else operand
                for operand, place in zip(operands, in_specs)
            ]
        )

    return run


def reorder_blocks(source, target, order, column=0):
    rows = source.shape[1]
    columns = slice(column, column + target.shape[1])

    @pl.loop(0, source.shape[0])
    def _(b):
        target[pl.ds(pl.multiple_of(b * rows, 16), rows), :] = source[order(b), :, columns]


def wide(ref):
    return ref[...].astype(jnp.float32)


def greet(peers):
    barrier = pltpu.get_barrier_semaphore()
    for peer in peers:
        pl.semaphore_signal(barrier, inc=1, device_id=peer, device_id_type=MESH_ID)
    pl.semaphore_wait(barrier, len(peers))


def near():
    group, core = lax.axis_index("dp"), lax.axis_index("core")
    across = group + 1 - 2 * lax.rem(group, 2)
    along = lax.rem(group + 2, 4)
    return group, core, across, along


def member_rows(width):
    def place(ref, member, start, count):
        first_row = pl.multiple_of(member * width + start, 16)
        return ref.at[pl.ds(first_row, count), :]

    return place


def member_lanes(width):
    def place(ref, member, start, count):
        return ref.at[pl.ds(start, count), pl.ds(pl.multiple_of(member * width, 128), width)]

    return place


def mover(send_sem, recv_sem, first=0):
    def copy(k, source, target, peer):
        return pltpu.make_async_remote_copy(
            src_ref=source,
            dst_ref=target,
            send_sem=send_sem.at[first + k],
            recv_sem=recv_sem.at[first + k],
            device_id=peer,
            device_id_type=MESH_ID,
        )

    return copy


def member_at(member):
    return {"dp": lax.div(member, 2), "core": lax.rem(member, 2)}


def plane_peers():
    group, core, _, _ = near()
    member = group * 2 + core
    return [lax.rem(member + step, 8) for step in range(1, 8)]


def gather_steps(place, x_ref, o_ref, local_sem, copy, arrived_whole=lambda member: None):
    group, core, across, along = near()
    beyond = across + along - group
    other = 1 - core
    sibling, by_x, by_y = {"core": other}, {"dp": across}, {"dp": along}
    half = x_ref.shape[0] // 2

    def part(owner, owner_core, piece):
        return place(o_ref, owner * 2 + owner_core, piece * half, half)

    sent = []

    def send(k, source, target, peer):
        moving = copy(k, source, target, peer)
        moving.start()
        sent.append(moving)

    def own(k, piece, peer):
        send(k, x_ref.at[pl.ds(piece * half, half), :], part(group, core, piece), peer)

    def relay(k, owner, piece, peer):
        send(k, part(owner, core, piece), part(owner, core, piece), peer)

    def arrived(k, owner, owner_core, piece):
        landed = part(owner, owner_core, piece)
        copy(k, landed, landed, sibling).wait_recv()

    local = pltpu.make_async_copy(
        x_ref, place(o_ref, group * 2 + core, 0, 2 * half), local_sem
    )
    local.start()
    own(0, 0, by_x)
    own(1, 1, by_y)
    own(2, 1, by_x)
    own(3, 0, by_y)
    own(4, 0, sibling)
    own(5, 1, sibling)

    def finish():
        local.wait()
        arrived_whole(group * 2 + core)
        arrived(4, group, other, 0)
        arrived(5, group, other, 1)
        arrived_whole(group * 2 + other)
        arrived(0, across, core, 0)
        relay(6, across, 0, by_y)
        relay(7, across, 0, sibling)
        arrived(1, along, core, 1)
        relay(8, along, 1, by_x)
        relay(9, along, 1, sibling)
        arrived(2, across, core, 1)
        relay(10, across, 1, sibling)
        arrived_whole(across * 2 + core)
        arrived(3, along, core, 0)
        relay(11, along, 0, sibling)
        arrived_whole(along * 2 + core)
        arrived(7, across, other, 0)
        arrived(10, across, other, 1)
        arrived_whole(across * 2 + other)
        arrived(6, beyond, core, 0)
        relay(12, beyond, 0, sibling)
        arrived(8, beyond, core, 1)
        relay(13, beyond, 1, sibling)
        arrived_whole(beyond * 2 + core)
        arrived(9, along, other, 1)
        arrived(11, along, other, 0)
        arrived_whole(along * 2 + other)
        arrived(12, beyond, other, 0)
        arrived(13, beyond, other, 1)
        arrived_whole(beyond * 2 + other)
        for moving in sent:
            moving.wait_send()

    return finish


def exchange_steps(source, target, x_ref, o_ref, local_sem, copy):
    group, core, _, _ = near()
    member = group * 2 + core
    local = pltpu.make_async_copy(source(x_ref, member), target(o_ref, member), local_sem)
    local.start()
    sent = []
    for k, peer in enumerate(plane_peers()):
        sent.append(copy(k, source(x_ref, peer), target(o_ref, member), member_at(peer)))
        sent[-1].start()

    def finish():
        for k in range(7):
            sender = lax.rem(member + 7 - k, 8)
            landed = target(o_ref, sender)
            copy(k, landed, landed, member_at(sender)).wait_recv()
        local.wait()
        for moving in sent:
            moving.wait_send()

    return finish


def gather_kernel(place, x_ref, *refs):
    o_ref, local_sem, send_sem, recv_sem = refs[-4:]
    _, core, across, along = near()
    greet([{"dp": across}, {"dp": along}, {"core": 1 - core}])
    gather_steps(place, x_ref, o_ref, local_sem, mover(send_sem, recv_sem))()


def plane_gather_call(shard, shape, place, kind, after):
    return kernel_call(
        functools.partial(gather_kernel, place),
        out_shape=jax.ShapeDtypeStruct(shape, shard.dtype),
        in_specs=[IN_HBM] * (1 + len(after)),
        out_specs=IN_HBM,
        scratch_shapes=[
            pltpu.SemaphoreType.DMA,
            pltpu.SemaphoreType.DMA((14,)),
            pltpu.SemaphoreType.DMA((14,)),
        ],
        compiler_params=pltpu.CompilerParams(
            collective_id=identity_of(kind, shard, *after), has_side_effects=True
        ),
        cost_estimate=BRIEF,
        name="plane_gather",
    )(shard, *after)


def plane_gather(shard, after=()):
    rows, width = shard.shape
    return plane_gather_call(shard, (rows, 8 * width), member_lanes(width), "gather lanes", after)


def plane_gather_rows(shard, after=()):
    rows, width = shard.shape
    return plane_gather_call(shard, (8 * rows, width), member_rows(rows), "gather rows", after)


def scatter_steps(place, p_ref, bufs, copy):
    pair, total, from_x, from_y, relay = bufs
    group, core, across, along = near()
    beyond = across + along - group
    other = 1 - core
    sibling, by_x, by_y = {"core": other}, {"dp": across}, {"dp": along}
    rows = total.shape[1]
    half = rows // 2
    low, high = pl.ds(0, half), pl.ds(half, half)
    sent = []

    def send(k, source, target, peer):
        moving = copy(k, source, target, peer)
        moving.start()
        sent.append(moving)

    def arrived(k, target):
        copy(k, target, target, sibling).wait_recv()

    def both_cores(k, owner):
        arrived(k, pair.at[k])
        summed = wide(place(p_ref, owner * 2 + core, 0, rows)) + wide(pair.at[k])
        total[k] = summed.astype(total.dtype)

    def cores():
        for k, owner in enumerate((beyond, across, along, group)):
            send(k, place(p_ref, owner * 2 + other, 0, rows), pair.at[k], sibling)

    def chips():
        both_cores(0, beyond)
        send(4, total.at[0, low], relay.at[0], by_x)
        send(5, total.at[0, high], relay.at[1], by_y)
        both_cores(1, across)
        send(6, total.at[1, low], from_x.at[low], by_x)
        both_cores(2, along)
        send(7, total.at[2, high], from_y.at[high], by_y)
        both_cores(3, group)

    def relays():
        arrived(5, relay.at[1])
        total[1, high] = (wide(total.at[1, high]) + wide(relay.at[1])).astype(total.dtype)
        send(8, total.at[1, high], from_x.at[high], by_x)
        arrived(4, relay.at[0])
        total[2, low] = (wide(total.at[2, low]) + wide(relay.at[0])).astype(total.dtype)
        send(9, total.at[2, low], from_y.at[low], by_y)

    def finish():
        arrived(6, from_x.at[low])
        arrived(7, from_y.at[high])
        arrived(8, from_x.at[high])
        arrived(9, from_y.at[low])
        summed = wide(total.at[3]) + wide(from_x) + wide(from_y)
        for moving in sent:
            moving.wait_send()
        return summed

    return cores, chips, relays, finish


def scatter_bufs(rows, width):
    slot = pltpu.VMEM((rows, width), jnp.bfloat16)
    four = pltpu.VMEM((4, rows, width), jnp.bfloat16)
    return [four, four, slot, slot, pltpu.VMEM((2, rows // 2, width), jnp.bfloat16)]


def scatter_kernel(place, p_ref, *refs):
    o_ref, *bufs, send_sem, recv_sem = refs[-8:]
    _, core, across, along = near()
    greet([{"dp": across}, {"dp": along}, {"core": 1 - core}])
    cores, chips, relays, finish = scatter_steps(place, p_ref, bufs, mover(send_sem, recv_sem))
    cores()
    chips()
    relays()
    o_ref[...] = finish().astype(o_ref.dtype)


def plane_scatter_call(partial, shape, place, dtype, kind, after):
    rows, width = shape
    return kernel_call(
        functools.partial(scatter_kernel, place),
        out_shape=jax.ShapeDtypeStruct(shape, dtype),
        in_specs=[IN_VMEM] + [IN_HBM] * len(after),
        out_specs=IN_VMEM,
        scratch_shapes=scatter_bufs(rows, width)
        + [
            pltpu.SemaphoreType.DMA((10,)),
            pltpu.SemaphoreType.DMA((10,)),
        ],
        compiler_params=pltpu.CompilerParams(
            collective_id=identity_of(kind, partial, *after),
            has_side_effects=True,
            vmem_limit_bytes=24 * 2**20,
        ),
        cost_estimate=BRIEF,
        name="plane_scatter",
    )(partial, *after)


def plane_scatter_frames(partial, after=()):
    rows, width = partial.shape[0], partial.shape[1] // 8
    place = member_lanes(width)
    return plane_scatter_call(partial, (rows, width), place, jnp.float32, "scatter lanes", after)


def plane_scatter_rows(partial, after=()):
    rows, width = partial.shape[0] // 8, partial.shape[1]
    place = member_rows(rows)
    return plane_scatter_call(partial, (rows, width), place, jnp.bfloat16, "scatter rows", after)


def project_kernel(kind, column, order_ref, s_ref, w_ref, base_ref, gain_ref, *refs):
    if kind == "sum":
        side_ref, full_ref, x_ref, n_ref, i_ref, h_ref, side_out, *refs = refs
    else:
        full_ref, x_ref, n_ref, i_ref, h_ref, *refs = refs
    full, total, part, landed, shard, by_block, base, gain, residual, normed, *refs = refs
    heads, slots, weight, *bufs, local_sem, send_sem, recv_sem = refs
    rows, length = s_ref.shape
    width = base_ref.shape[1]
    fetches = [
        pltpu.make_async_copy(ref, held, local_sem.at[8 + k])
        for k, (ref, held) in enumerate(
            [(s_ref, heads), (w_ref.at[:, :, : slots.shape[2]], slots)]
            + [(base_ref, base), (gain_ref, gain)]
        )
    ]
    for fetch in fetches:
        fetch.start()
    greet([member_at(peer) for peer in plane_peers()])
    total[...] = jnp.zeros_like(total)

    def add(member):
        of = pl.ds(pl.multiple_of(member * rows, 16), rows)

        @pl.loop(0, length // 256)
        def _(i):
            at = pl.ds(pl.multiple_of(i * 256, 256), 256)
            total[:, at] += contract_rows(weight[of, :], full[of, at])

    fetches[0].wait()
    gathered = gather_steps(
        member_rows(rows), heads, full, local_sem.at[0], mover(send_sem, recv_sem), add
    )
    side = mover(send_sem, recv_sem, 35)
    if kind == "sum":
        cores, chips, relays, finish = scatter_steps(
            member_rows(side_out.shape[0]), bufs[-1], bufs[:-2], side
        )
        text_weight = bufs[-2]
        fetches[1].wait()
        reorder_blocks(slots, text_weight, lambda b: order_ref[1, b], 3 * rows)
        tokens = side_ref.shape[1]

        @pl.loop(0, text_weight.shape[0] // 256)
        def _(i):
            at = pl.ds(pl.multiple_of(i * 256, 256), 256)
            for k in range(2):
                half = slice(k * side_ref.shape[0], (k + 1) * side_ref.shape[0])
                bufs[-1][at, k * tokens : (k + 1) * tokens] = jnp.dot(
                    text_weight[at, half], side_ref[...], preferred_element_type=jnp.float32
                ).astype(jnp.bfloat16)

        cores()
    else:
        fetches[1].wait()
    reorder_blocks(slots, weight, lambda b: order_ref[1, b], column)
    if kind == "sum":
        chips()
    gathered()
    kept = pltpu.make_async_copy(full, full_ref, local_sem.at[0])
    kept.start()
    part[...] = total[...].astype(part.dtype)
    exchanged = exchange_steps(
        whole_lanes(rows, width),
        whole_rows(rows),
        part,
        landed,
        local_sem.at[3],
        mover(send_sem, recv_sem, 14),
    )
    if kind == "sum":
        relays()
    exchanged()
    fetches[2].wait()
    fetches[3].wait()
    residual[...] = base[...] + wide(landed)
    standard, inverse_std = norm_columns(residual[...])
    normed[...] = standard
    i_ref[...] = inverse_std
    by_block[...] = (standard * gain[...]).astype(shard.dtype).reshape(by_block.shape)
    reorder_blocks(by_block, shard, lambda b: order_ref[0, b])
    gathered = gather_steps(
        member_lanes(width), shard, h_ref, local_sem.at[4], mover(send_sem, recv_sem, 21)
    )
    x_copy = pltpu.make_async_copy(residual, x_ref, local_sem.at[5])
    x_copy.start()
    n_copy = pltpu.make_async_copy(normed, n_ref, local_sem.at[6])
    n_copy.start()
    if kind == "sum":
        side_out[...] = finish().astype(side_out.dtype)
    gathered()
    kept.wait()
    x_copy.wait()
    n_copy.wait()


def project(kind, column, orders, heads, weight, base, gain, *side):
    rows, length = heads.shape
    features, width = base.shape
    whole = jax.ShapeDtypeStruct((features, length), jnp.bfloat16)
    frames = jax.ShapeDtypeStruct(base.shape, jnp.float32)
    side_outs, bufs = (), []
    if kind == "sum":
        tokens = side[0].shape[1]
        side_outs = (jax.ShapeDtypeStruct((rows, 2 * tokens), jnp.bfloat16),)
        bufs = scatter_bufs(rows, 2 * tokens) + [
            pltpu.VMEM((features, rows), jnp.bfloat16),
            pltpu.VMEM((features, 2 * tokens), jnp.bfloat16),
        ]
    low, high = pltpu.VMEM(base.shape, jnp.bfloat16), pltpu.VMEM(base.shape, jnp.float32)
    return kernel_call(
        functools.partial(project_kernel, kind, column),
        out_shape=(whole, frames, frames, jax.ShapeDtypeStruct((1, width), jnp.float32), whole)
        + side_outs,
        in_specs=[IN_SMEM] + [IN_HBM] * 4 + [IN_VMEM] * len(side),
        out_specs=(IN_HBM, IN_HBM, IN_HBM, IN_VMEM, IN_HBM) + (IN_VMEM,) * len(side),
        scratch_shapes=[
            pltpu.VMEM((features, length), jnp.bfloat16),
            pltpu.VMEM((rows, length), jnp.float32),
            pltpu.VMEM((rows, length), jnp.bfloat16),
            low,
            low,
            pltpu.VMEM((orders.shape[1], features // orders.shape[1], width), jnp.bfloat16),
            high,
            pltpu.VMEM(gain.shape, jnp.float32),
            high,
            high,
            pltpu.VMEM(heads.shape, heads.dtype),
            pltpu.VMEM((orders.shape[1], features // orders.shape[1], 4 * rows), weight.dtype),
            pltpu.VMEM((features, rows), weight.dtype),
        ]
        + bufs
        + [
            pltpu.SemaphoreType.DMA((13,)),
            pltpu.SemaphoreType.DMA((49,)),
            pltpu.SemaphoreType.DMA((49,)),
        ],
        compiler_params=pltpu.CompilerParams(
            collective_id=identity_of("project " + kind, heads),
            has_side_effects=True,
            vmem_limit_bytes=32 * 2**20,
        ),
        cost_estimate=BRIEF,
        name="project_" + kind,
    )(orders, heads, weight.reshape(orders.shape[1], -1, weight.shape[1]), base, gain, *side)


def back_kernel(plan, *refs):
    by_rows, send_rows, text, in_slots, column, beside, after = plan
    refs = list(refs)

    def take(count):
        taken = refs[:count]
        del refs[:count]
        return taken

    order_ref = take(1)[0]
    sources = take(3 if by_rows else 7)
    text_ref = take(1)[0] if text else None
    beside_refs = take(4 if beside else 0)
    take(after)
    o_ref, own_out = take(2)
    sum_ref = None if by_rows else take(1)[0]
    rows_ref = take(1)[0] if send_rows else None
    text_out = take(1)[0] if text else None
    held = take(len(sources))
    w_ref, g_ref, act, *norms = held
    results = take(0 if by_rows else 2)
    mine, theirs, pair, from_x, from_y, relay, shard, slots, own_ref = take(9)
    besides = take(4 if beside else 0)
    by_head = take(1 if by_rows else 0)
    local_sem, send_sem, recv_sem = refs
    if by_rows:
        w_slots, w_ref = w_ref, by_head[0]
    source = sources[0]
    if by_rows:
        sources[0] = source.at[:, :, : w_slots.shape[2]]
    elif w_ref.shape[1] < source.shape[1]:
        sources[0] = source.at[:, : w_ref.shape[1]]
    fetches = [
        pltpu.make_async_copy(ref, here, local_sem.at[4 + k])
        for k, (ref, here) in enumerate(zip(sources + beside_refs, held + besides))
    ]
    for fetch in fetches:
        fetch.start()

    group, core, across, along = near()
    beyond = across + along - group
    sibling, by_x, by_y = {"core": 1 - core}, {"dp": across}, {"dp": along}
    rows, width = mine.shape[1:]
    columns = slice(0, g_ref.shape[0]) if by_rows else slice(column, column + g_ref.shape[0])
    half = rows // 2
    low, high = pl.ds(0, half), pl.ds(half, half)
    copy = mover(send_sem, recv_sem)
    sent = []

    def send(k, source, target, peer):
        moving = copy(k, source, target, peer)
        moving.start()
        sent.append(moving)

    def arrived(k, target):
        copy(k, target, target, sibling).wait_recv()

    def split(k, at_rows, at_lanes, first, second):
        mine[k, at_rows, at_lanes] = jnp.where(core == 0, first, second).astype(mine.dtype)
        theirs[k, at_rows, at_lanes] = jnp.where(core == 0, second, first).astype(mine.dtype)

    def work_out(k, owner):
        if by_rows:

            @pl.loop(0, width // 256)
            def _(i):
                at = pl.ds(pl.multiple_of(i * 256, 256), 256)
                both = jnp.dot(
                    w_ref[pl.ds(pl.multiple_of(owner * 2 * rows, 16), 2 * rows), columns],
                    g_ref[:, at],
                    preferred_element_type=jnp.float32,
                )
                split(k, slice(None), at, both[:rows], both[rows:])

        else:

            @pl.loop(0, rows // 256)
            def _(i):
                at = pl.ds(pl.multiple_of(i * 256, 256), 256)
                both = jnp.dot(
                    w_ref[at, columns],
                    g_ref[:, pl.ds(pl.multiple_of(owner * 2 * width, 256), 2 * width)],
                    preferred_element_type=jnp.float32,
                )
                split(k, at, slice(None), both[:, :width], both[:, width:])

        send(k, theirs.at[k], pair.at[k], sibling)

    def both_cores(k):
        arrived(k, pair.at[k])
        mine[k] = (wide(mine.at[k]) + wide(pair.at[k])).astype(mine.dtype)

    def weight_grads(first, last):
        rows_of = act if in_slots else slots
        tile, count = rows_of.shape[0] // 6, g_ref.shape[0]

        @pl.loop(first, last)
        def _(i):
            at = pl.ds(pl.multiple_of(i * tile, tile), tile)
            for j in range(0, count, 256):
                of = slice(j, min(j + 256, count))
                own_ref[at, of] = contract_last(rows_of[at, :], g_ref[of, :]).astype(
                    own_ref.dtype
                )

    if send_rows or text:
        greet([member_at(peer) for peer in plane_peers()])
    else:
        greet([by_x, by_y, sibling])
    fetches[0].wait()
    if by_rows:
        reorder_blocks(w_slots, w_ref, lambda b: order_ref[1, b], column)
    fetches[1].wait()
    for k, owner in enumerate((beyond, across, along, group)):
        work_out(k, owner)
        if k == 1:
            both_cores(0)
            send(4, mine.at[0, low], relay.at[0], by_x)
            send(5, mine.at[0, high], relay.at[1], by_y)
        if k == 2:
            both_cores(1)
            send(6, mine.at[1, low], from_x.at[low], by_x)
        if k == 3:
            both_cores(2)
            send(7, mine.at[2, high], from_y.at[high], by_y)
    if text:
        text_done = gather_steps(
            member_rows(text_ref.shape[0]),
            text_ref,
            text_out,
            local_sem.at[1],
            mover(send_sem, recv_sem, 17),
        )
    def put_beside():
        cq, co, text_grad, text_mine = besides
        count, rows = g_ref.shape[0], text_grad.shape[1]
        part = text_mine.shape[0]
        tokens = text_mine.shape[1]

        @pl.loop(0, text_grad.shape[0])
        def _(b):
            at = pl.ds(pl.multiple_of(b * rows, 16), rows)
            own_ref[at, count : 2 * count] = cq[at, :]
            own_ref[at, 2 * count : 3 * count] = co[at, :]
            slots[at, : 2 * tokens] = text_grad[order_ref[0, b]]

        @pl.loop(0, 6)
        def _(i):
            at = pl.ds(pl.multiple_of(i * 256, 256), 256)
            for k in range(2):
                grads = contract_last(
                    slots[at, k * tokens : (k + 1) * tokens], text_mine[...]
                )
                start = 3 * count + k * part
                own_ref[at, start : start + part] = grads.astype(own_ref.dtype)

    fetches[2].wait()
    if not in_slots:
        reorder_blocks(act, slots, lambda b: order_ref[0, b])
    weight_grads(0, 2)
    arrived(5, relay.at[1])
    mine[1, high] = (wide(mine.at[1, high]) + wide(relay.at[1])).astype(mine.dtype)
    send(8, mine.at[1, high], from_x.at[high], by_x)
    arrived(4, relay.at[0])
    mine[2, low] = (wide(mine.at[2, low]) + wide(relay.at[0])).astype(mine.dtype)
    send(9, mine.at[2, low], from_y.at[low], by_y)
    both_cores(3)
    weight_grads(2, 6)
    if beside:
        for fetch in fetches[len(sources) :]:
            fetch.wait()
        put_beside()
    if text:
        text_done()
    own_copy = pltpu.make_async_copy(own_ref, own_out, local_sem.at[2])
    own_copy.start()
    arrived(6, from_x.at[low])
    arrived(7, from_y.at[high])
    arrived(8, from_x.at[high])
    arrived(9, from_y.at[low])
    summed = wide(mine.at[3]) + wide(from_x) + wide(from_y)
    if by_rows:
        shard[...] = summed.astype(shard.dtype)
        result_copy = pltpu.make_async_copy(shard, o_ref, local_sem.at[3])
        result_copy.start()
    else:
        for fetch in fetches[3 : len(sources)]:
            fetch.wait()
        normed, inverse_std, gain, base = norms
        result, by_block = results
        if in_slots:
            by_block[...] = summed.reshape(by_block.shape)
            reorder_blocks(by_block, result, lambda b: order_ref[1, b])
            summed = result[...]
        result[...] = base[...] + norm_columns_back(
            summed * gain[...], normed[...], inverse_std[...]
        )
        result_copy = pltpu.make_async_copy(result, o_ref, local_sem.at[3])
        result_copy.start()
        if send_rows:
            shard[...] = result[...].astype(shard.dtype)
            rows_done = exchange_steps(
                whole_rows(rows // 8),
                whole_lanes(rows // 8, width),
                shard,
                rows_ref,
                local_sem.at[0],
                mover(send_sem, recv_sem, 10),
            )
        sum_ref[...] = lax.dot_general(
            jnp.ones((8, width), jnp.float32),
            summed * normed[...],
            (((1,), (1,)), ((), ())),
            precision=HIGHEST,
            preferred_element_type=jnp.float32,
        )
        if send_rows:
            rows_done()
    result_copy.wait()
    own_copy.wait()
    for moving in sent:
        moving.wait_send()


def back(
    orders,
    weight,
    grad,
    act,
    norm=None,
    column=0,
    send_rows=False,
    text=None,
    in_slots=False,
    beside=(),
    after=(),
):
    by_rows = norm is None
    features, length = weight.shape[0], grad.shape[1]
    shape = (features // 8, length) if by_rows else (features, length // 8)
    small = jnp.bfloat16
    own_width = grad.shape[0] * (4 if beside else 1)
    own = jax.ShapeDtypeStruct((features, own_width), small)
    outs = [jax.ShapeDtypeStruct(shape, small if by_rows else jnp.float32), own]
    specs = [IN_HBM, IN_HBM]
    if not by_rows:
        outs.append(jax.ShapeDtypeStruct((8, features), jnp.float32))
        specs.append(IN_VMEM)
    if send_rows:
        outs.append(jax.ShapeDtypeStruct((features // 8, length), small))
        specs.append(IN_HBM)
    count = orders.shape[1]
    if not in_slots:
        act = act.reshape(count, features // count, length)
    few = weight.shape[1] if column + grad.shape[0] > 4 * (features // 8) else 4 * (features // 8)
    if by_rows:
        weight = weight.reshape(count, features // count, weight.shape[1])
        held = jax.ShapeDtypeStruct((count, features // count, few), small)
    else:
        held = jax.ShapeDtypeStruct((features, few), small)
    sources = [weight, grad, act] + list(norm or ())
    operands = [orders] + sources
    if text is not None:
        operands.append(text)
        outs.append(jax.ShapeDtypeStruct((8 * text.shape[0], text.shape[1]), text.dtype))
        specs.append(IN_HBM)
    if beside:
        cq, co, text_grad, text_mine = beside
        beside = (cq, co, text_grad.reshape(count, features // count, -1), text_mine)
        operands += list(beside)
    operands += list(after)
    plan = (by_rows, send_rows, text is not None, in_slots, column, bool(beside), len(after))
    rows, width = shape
    four, slot = pltpu.VMEM((4, rows, width), small), pltpu.VMEM((rows, width), small)
    return kernel_call(
        functools.partial(back_kernel, plan),
        out_shape=tuple(outs),
        in_specs=[IN_SMEM] + [IN_HBM] * (len(operands) - 1),
        out_specs=tuple(specs),
        scratch_shapes=[pltpu.VMEM(array.shape, array.dtype) for array in [held] + sources[1:]]
        + (
            []
            if by_rows
            else [
                pltpu.VMEM(shape, jnp.float32),
                pltpu.VMEM((count, rows // count, width), jnp.float32),
            ]
        )
        + [four, four, four, slot, slot, pltpu.VMEM((2, rows // 2, width), small), slot]
        + [
            pltpu.VMEM((16, 128) if in_slots else (features, length), small),
            pltpu.VMEM(own.shape, small),
        ]
        + [pltpu.VMEM(array.shape, array.dtype) for array in beside]
        + ([pltpu.VMEM((features, grad.shape[0]), small)] if by_rows else [])
        + [
            pltpu.SemaphoreType.DMA((11,)),
            pltpu.SemaphoreType.DMA((31,)),
            pltpu.SemaphoreType.DMA((31,)),
        ],
        compiler_params=pltpu.CompilerParams(
            collective_id=identity_of("back" + str(plan), *operands),
            has_side_effects=True,
            vmem_limit_bytes=44 * 2**20,
        ),
        cost_estimate=BRIEF,
        name="back",
    )(*operands)


def exchange_kernel(source, target, x_ref, *refs):
    o_ref, local_sem, send_sem, recv_sem = refs[-4:]
    greet([member_at(peer) for peer in plane_peers()])
    exchange_steps(source, target, x_ref, o_ref, local_sem, mover(send_sem, recv_sem))()


def exchange(array, shape, source, target, kind, after=()):
    return kernel_call(
        functools.partial(exchange_kernel, source, target),
        out_shape=jax.ShapeDtypeStruct(shape, array.dtype),
        in_specs=[IN_HBM] * (1 + len(after)),
        out_specs=IN_HBM,
        scratch_shapes=[
            pltpu.SemaphoreType.DMA,
            pltpu.SemaphoreType.DMA((7,)),
            pltpu.SemaphoreType.DMA((7,)),
        ],
        compiler_params=pltpu.CompilerParams(
            collective_id=identity_of(kind, array, *after), has_side_effects=True
        ),
        cost_estimate=BRIEF,
        name="plane_exchange",
    )(array, *after)


def whole_rows(rows):
    place = member_rows(rows)
    return lambda ref, member: place(ref, member, 0, rows)


def whole_lanes(rows, width):
    place = member_lanes(width)
    return lambda ref, member: place(ref, member, 0, rows)


def to_frames(part):
    rows, width = part.shape[0], part.shape[1] // 8
    return exchange(part, (8 * rows, width), whole_lanes(rows, width), whole_rows(rows), "to frames")


def to_rows(part):
    rows, width = part.shape[0] // 8, part.shape[1]
    return exchange(part, (rows, 8 * width), whole_rows(rows), whole_lanes(rows, width), "to rows")


def block(ref, member):
    return ref.at[member]


def exchange_blocks(blocks, after=()):
    return exchange(blocks, blocks.shape, block, block, "blocks", after)


def lanes(ref, start, width):
    return ref.at[:, pl.ds(pl.multiple_of(start, 128), width)]


def sheet_part(start, width):
    return lambda ref, member: lanes(ref, start + member * width, width)


def block_part(start, width):
    return lambda ref, member: lanes(ref.at[member], start, width)


def feed_kernel(gu_ref, down_ref, w_ref, h_ref, g_ref, *refs):
    o_ref, y_ref, t_ref, weight, hidden, part, summed, grad, x_ref, held, *refs = refs[-18:]
    *bufs, local_sem, send_sem, recv_sem = refs
    width = down_ref.shape[-1]
    fetches = [
        pltpu.make_async_copy(w_ref, weight, local_sem.at[3]),
        pltpu.make_async_copy(h_ref, hidden, local_sem.at[5]),
        pltpu.make_async_copy(g_ref, grad, local_sem.at[6]),
    ]
    for fetch in fetches:
        fetch.start()
    plane = lax.axis_index("z")
    greet(
        [member_at(peer) for peer in plane_peers()]
        + [{"z": lax.rem(plane + k, 4)} for k in range(1, 4)]
    )
    depart, arrive, turned_back = turn_steps(
        x_ref, held, t_ref, local_sem.at[pl.ds(7, 2)], send_sem, recv_sem, 31
    )
    fetches[2].wait()
    x_ref[...] = grad[...].T.astype(x_ref.dtype)
    finish = []
    for k, (ref, start) in enumerate(((gu_ref, 0), (gu_ref, width), (down_ref, 0))):
        source, target = block_part(start, width), sheet_part(8 * k * width, width)
        copy = mover(send_sem, recv_sem, 7 * k)
        finish.append(exchange_steps(source, target, ref, o_ref, local_sem.at[k], copy))
    for fetch in fetches[:2]:
        fetch.wait()

    @pl.loop(0, part.shape[0] // 256)
    def _(i):
        at = pl.ds(pl.multiple_of(i * 256, 256), 256)
        for j in range(0, part.shape[1], 256):
            product = jnp.dot(
                weight[at, :], hidden[:, j : j + 256], preferred_element_type=jnp.float32
            )
            part[at, j : j + 256] = product.astype(part.dtype)

    cores, chips, relays, ended = scatter_steps(
        member_lanes(y_ref.shape[1]), part, bufs, mover(send_sem, recv_sem, 21)
    )
    cores()
    chips()
    relays()
    depart()
    summed[...] = ended()
    kept = pltpu.make_async_copy(summed, y_ref, local_sem.at[4])
    kept.start()
    arrive()
    for end in finish:
        end()
    kept.wait()
    turned_back()


def feed(gu, down, weight, hidden, grad, after=()):
    rows, length = weight.shape[0], hidden.shape[1]
    width = length // 8
    return kernel_call(
        feed_kernel,
        out_shape=(
            jax.ShapeDtypeStruct((gu.shape[1], 24 * down.shape[-1]), gu.dtype),
            jax.ShapeDtypeStruct((rows, width), jnp.float32),
            jax.ShapeDtypeStruct((width, rows), jnp.bfloat16),
        ),
        in_specs=[IN_HBM] * (5 + len(after)),
        out_specs=(IN_HBM,) * 3,
        scratch_shapes=[
            pltpu.VMEM(weight.shape, weight.dtype),
            pltpu.VMEM(hidden.shape, hidden.dtype),
            pltpu.VMEM((rows, length), jnp.bfloat16),
            pltpu.VMEM((rows, width), jnp.float32),
            pltpu.VMEM((rows, width), jnp.float32),
            pltpu.VMEM((width, rows), jnp.bfloat16),
            pltpu.VMEM((width, rows), jnp.bfloat16),
        ]
        + scatter_bufs(rows, width)
        + [
            pltpu.SemaphoreType.DMA((9,)),
            pltpu.SemaphoreType.DMA((39,)),
            pltpu.SemaphoreType.DMA((39,)),
        ],
        compiler_params=pltpu.CompilerParams(
            collective_id=identity_of("feed", gu, down, weight, *after),
            has_side_effects=True,
            vmem_limit_bytes=28 * 2**20,
        ),
        cost_estimate=BRIEF,
        name="feed",
    )(gu, down, weight, hidden, grad, *after)


def opening_kernel(
    latents_ref,
    cotangent_ref,
    small_ref,
    text_ref,
    sheet_ref,
    t_ref,
    all_ref,
    mine_ref,
    one_ref,
    x_ref,
    held,
    columns,
    one,
    tokens,
    by_feature,
    local_sem,
    send_sem,
    recv_sem,
):
    features = latents_ref.shape[1]
    part, text = D // 8, CTXW // 8
    tail = 6 * D + 3 * FF
    fetches = [
        pltpu.make_async_copy(latents_ref, x_ref.at[:, :features], local_sem.at[5]),
        pltpu.make_async_copy(cotangent_ref, x_ref.at[:, features:], local_sem.at[6]),
        pltpu.make_async_copy(
            sheet_ref.at[:, : 6 * D], columns.at[:, : 6 * D], local_sem.at[7]
        ),
        pltpu.make_async_copy(
            sheet_ref.at[:, tail : tail + 2 * CTXW], columns.at[:, 6 * D :], local_sem.at[8]
        ),
        pltpu.make_async_copy(text_ref, tokens, local_sem.at[10]),
    ]
    for fetch in fetches:
        fetch.start()
    group, core, across, along = near()
    member = group * 2 + core
    plane = lax.axis_index("z")
    step = x_ref.shape[0] // 4
    text_rows = mine_ref.shape[0]
    teacher = jnp.logical_and(group == plane, core == 0)

    def frames(ref, j):
        return ref.at[pl.ds(pl.multiple_of(j * step, 16), step), :]

    peers = plane_peers()
    line = [lax.rem(plane + k, 4) for k in range(1, 4)]
    greet([member_at(peer) for peer in peers] + [{"z": there} for there in line])

    fetches[0].wait()
    fetches[1].wait()

    near_copy = mover(send_sem, recv_sem)
    line_copy = mover(send_sem, recv_sem, 7)
    small_local = pltpu.make_async_copy(small_ref, all_ref.at[plane, member], local_sem.at[0])
    small_local.start()
    first = [
        near_copy(k, small_ref, all_ref.at[plane, member], member_at(peer))
        for k, peer in enumerate(peers)
    ]
    for moving in first:
        moving.start()

    others = [across, along, across + along - group]
    keep = pltpu.make_async_copy(frames(x_ref, group), frames(held, group), local_sem.at[1])
    keep.start()

    def piece(ref, j, a):
        at = pl.ds(pl.multiple_of(j * step, 16), step)
        return ref.at[at, a * features : (a + 1) * features]

    def spread(owner, landing, a):
        return pltpu.make_async_remote_copy(
            src_ref=piece(x_ref, owner, a),
            dst_ref=piece(held, landing, a),
            send_sem=send_sem.at[(10, 36)[a] + owner],
            recv_sem=recv_sem.at[(10, 36)[a] + landing],
            device_id={"dp": owner},
            device_id_type=MESH_ID,
        )

    for a in range(2):
        for owner in others:
            spread(owner, group, a).start()

    def rise(row, a):
        return pltpu.make_async_remote_copy(
            src_ref=piece(held, row, a),
            dst_ref=piece(t_ref, plane, a),
            send_sem=send_sem.at[(28, 32)[a] + row],
            recv_sem=recv_sem.at[(28, 32)[a] + plane],
            device_id={"z": row},
            device_id_type=MESH_ID,
        )

    stay = [
        pltpu.make_async_copy(piece(held, plane, a), piece(t_ref, plane, a), local_sem.at[(4, 9)[a]])
        for a in range(2)
    ]

    def pass_on(row, a):
        pl.when(row == plane)(stay[a].start)
        pl.when(row != plane)(rise(row, a).start)

    keep.wait()
    for a in range(2):
        pass_on(group, a)

    fetches[2].wait()
    fetches[3].wait()

    def move(m, at, start, width):
        one[m, :, at : at + width] = columns[:, start : start + width].astype(one.dtype)

    for m in range(8):
        for k in range(6):
            move(m, (4 * part if k < 3 else -3 * part) + k * part, k * D + m * part, part)
        for k in range(2):
            move(m, 3 * part + k * text, 6 * D + k * CTXW + m * text, text)
    for owner in others:
        spread(owner, owner, 0).wait_recv()
        pass_on(owner, 0)
    weights_done = exchange_steps(
        block, block, one, one_ref, local_sem.at[2], mover(send_sem, recv_sem, 14)
    )

    fetches[4].wait()
    by_feature[...] = wide(tokens).T.astype(by_feature.dtype)

    def text_copy(k, peer):
        return pltpu.make_async_remote_copy(
            src_ref=by_feature.at[pl.ds(pl.multiple_of(peer * text_rows, 16), text_rows), :],
            dst_ref=mine_ref,
            send_sem=send_sem.at[21 + k],
            recv_sem=recv_sem.at[21],
            device_id=member_at(peer),
            device_id_type=MESH_ID,
        )

    own_text = by_feature.at[pl.ds(pl.multiple_of(member * text_rows, 16), text_rows), :]
    text_local = pltpu.make_async_copy(own_text, mine_ref, local_sem.at[3])

    @pl.when(teacher)
    def _():
        text_local.start()
        for k, peer in enumerate(peers):
            text_copy(k, peer).start()

    for owner in others:
        spread(owner, owner, 1).wait_recv()
        pass_on(owner, 1)

    for k in range(7):
        landed = all_ref.at[plane, lax.rem(member + 7 - k, 8)]
        near_copy(k, landed, landed, member_at(peers[k])).wait_recv()
    small_local.wait()
    second = [
        line_copy(k, all_ref.at[plane], all_ref.at[plane], {"z": there})
        for k, there in enumerate(line)
    ]
    for moving in second:
        moving.start()
    for k in range(3):
        landed = all_ref.at[lax.rem(plane + 3 - k, 4)]
        line_copy(k, landed, landed, {"z": line[k]}).wait_recv()

    for a in range(2):
        for there in line:
            landed = piece(t_ref, there, a)
            pltpu.make_async_remote_copy(
                src_ref=landed,
                dst_ref=landed,
                send_sem=send_sem.at[(28, 32)[a] + there],
                recv_sem=recv_sem.at[(28, 32)[a] + there],
                device_id={"z": there},
                device_id_type=MESH_ID,
            ).wait_recv()
        stay[a].wait()
    weights_done()

    @pl.when(teacher)
    def _():
        text_local.wait()
        for k, peer in enumerate(peers):
            text_copy(k, peer).wait_send()

    @pl.when(jnp.logical_not(teacher))
    def _():
        text_copy(0, peers[0]).wait_recv()

    for moving in first + second:
        moving.wait_send()
    for a in range(2):
        for owner in others:
            spread(owner, group, a).wait_send()
        for there in line:
            rise(there, a).wait_send()


def opening(latents, cotangent, small, text, sheet):
    frames, features = latents.shape
    local = (frames, 2 * features)
    one = (8, sheet.shape[0], (6 * D + 2 * CTXW) // 8)
    low = jnp.bfloat16
    return kernel_call(
        opening_kernel,
        out_shape=(
            jax.ShapeDtypeStruct(local, low),
            jax.ShapeDtypeStruct((4, 8) + small.shape, small.dtype),
            jax.ShapeDtypeStruct((text.shape[1] // 8, text.shape[0]), text.dtype),
            jax.ShapeDtypeStruct(one, low),
        ),
        in_specs=[IN_HBM] * 5,
        out_specs=(IN_HBM,) * 4,
        scratch_shapes=[
            pltpu.VMEM(local, low),
            pltpu.VMEM(local, low),
            pltpu.VMEM((sheet.shape[0], 6 * D + 2 * CTXW), jnp.float32),
            pltpu.VMEM(one, low),
            pltpu.VMEM(text.shape, low),
            pltpu.VMEM(text.shape[::-1], low),
            pltpu.SemaphoreType.DMA((11,)),
            pltpu.SemaphoreType.DMA((40,)),
            pltpu.SemaphoreType.DMA((40,)),
        ],
        compiler_params=pltpu.CompilerParams(
            collective_id=identity_of("opening", sheet),
            has_side_effects=True,
            vmem_limit_bytes=16 * 2**20,
        ),
        cost_estimate=BRIEF,
        name="opening",
    )(latents, cotangent, small, text, sheet)


def first_gather_kernel(
    x_ref, y_ref, sheet_ref, ox_ref, oy_ref, gu_ref, down_ref, local_sem, send_sem, recv_sem
):
    place = member_lanes(x_ref.shape[1])
    width = FF // 8
    greet([member_at(peer) for peer in plane_peers()])
    finish = [
        gather_steps(place, x_ref, ox_ref, local_sem.at[0], mover(send_sem, recv_sem)),
        gather_steps(place, y_ref, oy_ref, local_sem.at[1], mover(send_sem, recv_sem, 14)),
    ]
    for k, (ref, start) in enumerate(((gu_ref, 0), (gu_ref, width), (down_ref, 0))):
        source, target = sheet_part(6 * D + k * FF, width), block_part(start, width)
        copy = mover(send_sem, recv_sem, 28 + 7 * k)
        finish.append(exchange_steps(source, target, sheet_ref, ref, local_sem.at[2 + k], copy))
    for end in finish:
        end()


def first_gather(shard, other, sheet):
    rows, width = shard.shape
    whole = jax.ShapeDtypeStruct((rows, 8 * width), shard.dtype)
    return kernel_call(
        first_gather_kernel,
        out_shape=(
            whole,
            whole,
            jax.ShapeDtypeStruct((8, sheet.shape[0], FF // 4), sheet.dtype),
            jax.ShapeDtypeStruct((8, sheet.shape[0], FF // 8), sheet.dtype),
        ),
        in_specs=[IN_HBM] * 3,
        out_specs=(IN_HBM,) * 4,
        scratch_shapes=[
            pltpu.SemaphoreType.DMA((5,)),
            pltpu.SemaphoreType.DMA((49,)),
            pltpu.SemaphoreType.DMA((49,)),
        ],
        compiler_params=pltpu.CompilerParams(
            collective_id=identity_of("first gather", shard, sheet), has_side_effects=True
        ),
        cost_estimate=BRIEF,
        name="first_gather",
    )(shard, other, sheet)


def turn_steps(x_ref, held, t_ref, local_sem, send_sem, recv_sem, first):
    group, core, across, along = near()
    plane = lax.axis_index("z")
    step = x_ref.shape[0] // 4
    groups = [across, along, across + along - group]
    inner = lax.div(plane * (3 - plane), 2)
    two_off, mirrored = lax.rem(plane + 2, 4), 3 - plane
    line = [
        plane + 1 - 2 * lax.rem(plane, 2),
        inner * mirrored + (1 - inner) * two_off,
        inner * two_off + (1 - inner) * mirrored,
    ]

    def frames(ref, j):
        return ref.at[pl.ds(pl.multiple_of(j * step, 16), step), :]

    def copy(source, target, sent, landed, peer):
        return pltpu.make_async_remote_copy(
            src_ref=source,
            dst_ref=target,
            send_sem=send_sem.at[first + sent],
            recv_sem=recv_sem.at[first + landed],
            device_id=peer,
            device_id_type=MESH_ID,
        )

    def along_line(there):
        return copy(frames(x_ref, there), frames(held, plane), there, plane, {"z": there})

    def onward(owner):
        return copy(
            frames(held, owner), frames(t_ref, group), 4 + owner, 4 + group, {"dp": owner}
        )

    own = pltpu.make_async_copy(frames(x_ref, plane), frames(held, plane), local_sem.at[0])
    keep = pltpu.make_async_copy(frames(held, group), frames(t_ref, group), local_sem.at[1])

    def pass_on(owner):
        pl.when(owner == group)(keep.start)
        pl.when(owner != group)(onward(owner).start)

    def start():
        own.start()
        for there in line:
            along_line(there).start()
        own.wait()
        pass_on(plane)

    def arrive():
        for origin in line:
            at = frames(held, origin)
            copy(at, at, origin, origin, {"z": origin}).wait_recv()
            pass_on(origin)

    def finish():
        for origin in groups:
            at = frames(t_ref, origin)
            copy(at, at, 4 + origin, 4 + origin, {"dp": origin}).wait_recv()
        keep.wait()
        for there in line:
            along_line(there).wait_send()
        for owner in groups:
            onward(owner).wait_send()

    return start, arrive, finish


def prepare_kernel(order_ref, y_ref, base_ref, gu_ref, down_ref, two_ref, x_ref, q_ref, y):
    reorder_blocks(y_ref, y, lambda b: order_ref[1, b])
    x_ref[...] = (base_ref[...] + y[...]).T.astype(x_ref.dtype)
    q_ref[...] = jnp.full(q_ref.shape, square_sum((gu_ref, down_ref, two_ref)), jnp.float32)


def prepare(orders, y, base, gu, down, two):
    features, width = base.shape
    return kernel_call(
        prepare_kernel,
        out_shape=(
            jax.ShapeDtypeStruct((width, features), jnp.bfloat16),
            jax.ShapeDtypeStruct((8, 128), jnp.float32),
        ),
        in_specs=[IN_SMEM] + [IN_VMEM] * 5,
        out_specs=(IN_VMEM,) * 2,
        scratch_shapes=[pltpu.VMEM(base.shape, jnp.float32)],
        compiler_params=pltpu.CompilerParams(vmem_limit_bytes=16 * 2**20),
        name="prepare",
    )(orders, y.reshape(orders.shape[1], -1, width), base, gu, down, two)


def square_sum(refs):
    total = jnp.zeros((), jnp.float32)
    for ref in refs:
        line_sum = jnp.zeros((1, ref.shape[2]), jnp.float32)
        for m in range(8):
            line_sum += jnp.sum(jnp.square(wide(ref.at[m])), axis=0, keepdims=True)
        total += jnp.sum(line_sum)
    return total


def closing_kernel(
    x_ref,
    p_ref,
    w_ref,
    g_ref,
    _,
    t_ref,
    o_ref,
    s_ref,
    all_ref,
    held,
    tall,
    q_ref,
    one,
    local_sem,
    send_sem,
    recv_sem,
):
    fetch = pltpu.make_async_copy(w_ref, one, local_sem.at[0])
    fetch.start()
    group, core, _, _ = near()
    member = group * 2 + core
    plane = lax.axis_index("z")
    turned_line = [lax.rem(plane + k, 4) for k in range(1, 4)]
    peers = plane_peers()
    greet([member_at(peer) for peer in peers] + [{"z": there} for there in turned_line])
    start, arrive, finish = turn_steps(
        x_ref, held, t_ref, local_sem.at[pl.ds(1, 2)], send_sem, recv_sem, 0
    )
    gain_line = mover(send_sem, recv_sem, 23)
    gain_plane = mover(send_sem, recv_sem, 26)
    square_plane = mover(send_sem, recv_sem, 33)
    square_line = mover(send_sem, recv_sem, 40)
    back_line = [lax.rem(plane + 3 - k, 4) for k in range(3)]
    gain_local = pltpu.make_async_copy(g_ref, tall.at[plane], local_sem.at[3])
    gain_local.start()
    sent = [
        gain_line(k, g_ref, tall.at[plane], {"z": there}) for k, there in enumerate(turned_line)
    ]
    for moving in sent:
        moving.start()
    start()
    fetch.wait()
    weights_done = exchange_steps(
        block, block, one, o_ref, local_sem.at[5], mover(send_sem, recv_sem, 16)
    )
    q_ref[...] = p_ref[...] + square_sum((one,))
    square_local = pltpu.make_async_copy(q_ref, all_ref.at[plane, member], local_sem.at[6])
    square_local.start()
    shown = [
        square_plane(k, q_ref, all_ref.at[plane, member], member_at(peer))
        for k, peer in enumerate(peers)
    ]
    for moving in shown:
        moving.start()
    gain_local.wait()
    for k, origin in enumerate(back_line):
        gain_line(k, tall.at[origin], tall.at[origin], {"z": origin}).wait_recv()
    tall[4] = tall[0] + tall[1] + tall[2] + tall[3]
    gain_keep = pltpu.make_async_copy(tall.at[4], s_ref.at[member], local_sem.at[7])
    gain_keep.start()
    given = [
        gain_plane(k, tall.at[4], s_ref.at[member], member_at(peer)) for k, peer in enumerate(peers)
    ]
    for moving in given:
        moving.start()
    square_local.wait()
    for k in range(7):
        shown_here = all_ref.at[plane, lax.rem(member + 7 - k, 8)]
        square_plane(k, shown_here, shown_here, member_at(peers[k])).wait_recv()
    for k, there in enumerate(turned_line):
        shown.append(square_line(k, all_ref.at[plane], all_ref.at[plane], {"z": there}))
        shown[-1].start()
    arrive()
    finish()
    weights_done()
    gain_keep.wait()
    for k in range(7):
        given_here = s_ref.at[lax.rem(member + 7 - k, 8)]
        gain_plane(k, given_here, given_here, member_at(peers[k])).wait_recv()
    for k, origin in enumerate(back_line):
        square_line(k, all_ref.at[origin], all_ref.at[origin], {"z": origin}).wait_recv()
    for moving in sent + given + shown:
        moving.wait_send()

def closing(local, squares, one, gains, after):
    return kernel_call(
        closing_kernel,
        out_shape=(
            jax.ShapeDtypeStruct(local.shape, local.dtype),
            jax.ShapeDtypeStruct(one.shape, one.dtype),
            jax.ShapeDtypeStruct((8,) + gains.shape, gains.dtype),
            jax.ShapeDtypeStruct((4, 8) + squares.shape, jnp.float32),
        ),
        in_specs=[IN_VMEM, IN_VMEM] + [IN_HBM] * 3,
        out_specs=(IN_VMEM,) * 4,
        scratch_shapes=[
            pltpu.VMEM(local.shape, local.dtype),
            pltpu.VMEM((5,) + gains.shape, gains.dtype),
            pltpu.VMEM(squares.shape, jnp.float32),
            pltpu.VMEM(one.shape, one.dtype),
            pltpu.SemaphoreType.DMA((8,)),
            pltpu.SemaphoreType.DMA((43,)),
            pltpu.SemaphoreType.DMA((43,)),
        ],
        compiler_params=pltpu.CompilerParams(
            collective_id=identity_of("closing", one),
            has_side_effects=True,
            vmem_limit_bytes=8 * 2**20,
        ),
        cost_estimate=BRIEF,
        name="closing",
    )(local, squares, one, gains, after)


def turned(values, cosine, sine_table):
    half = HEAD // 2
    first_half, second_half = values[:half], values[half:]
    return jnp.concatenate(
        [
            first_half * cosine - second_half * sine_table,
            second_half * cosine + first_half * sine_table,
        ],
        axis=0,
    )


def attend_kernel(
    w_ref,
    h_ref,
    cos_ref,
    sin_ref,
    seg_ref,
    column_ref,
    part_out,
    p_out,
    o_ref,
    weight,
    frames,
    joint_ref,
    part_ref,
    p_ref,
    sems,
):
    heads, length = joint_ref.shape[1], joint_ref.shape[3]
    span = heads * HEAD
    tiles = length // 256
    fetches = [pltpu.make_async_copy(w_ref, weight, sems.at[0])]
    fetches += [
        pltpu.make_async_copy(
            h_ref.at[:, i * 256 : (i + 1) * 256], frames.at[:, i * 256 : (i + 1) * 256], sems.at[1 + i]
        )
        for i in range(tiles)
    ]
    for fetch in fetches:
        fetch.start()
    cosine, sine_table = cos_ref[...], sin_ref[...]
    fetches[0].wait()
    by_row = [weight[:, (4 + k) * span : (5 + k) * span].T for k in range(3)]
    for i in range(tiles):
        fetches[1 + i].wait()
        at = slice(i * 256, (i + 1) * 256)
        for k in range(3):
            part = jnp.dot(by_row[k], frames[:, at], preferred_element_type=jnp.float32)
            for h in range(heads):
                joint_ref[k, h, :, at] = part[h * HEAD : (h + 1) * HEAD]

    kept = []
    for h in range(heads):
        queries = turned(joint_ref[0, h], cosine, sine_table)
        part_ref[0, h] = queries.astype(part_ref.dtype)
        keys = turned(joint_ref[1, h], cosine, sine_table)
        part_ref[1, h] = keys.astype(part_ref.dtype)
        part_ref[2, h] = joint_ref[2, h].astype(part_ref.dtype)
        by_key = (part_ref[1, h].astype(jnp.float32) * (HEAD**-0.5)).T.astype(part_ref.dtype)

        @pl.loop(0, tiles)
        def _(i, h=h, by_key=by_key):
            at = pl.ds(pl.multiple_of(i * 256, 256), 256)
            scores = jnp.dot(
                by_key, part_ref[0, h, :, at], preferred_element_type=jnp.float32
            )
            scores = jnp.where(column_ref[...] == seg_ref[:, at], scores, MASKED_SCORE)
            exponent = jnp.exp(scores - jnp.max(scores, axis=0, keepdims=True))
            probs = exponent * (1.0 / jnp.sum(exponent, axis=0, keepdims=True))
            p_ref[h, :, at] = probs.astype(p_ref.dtype)
            out = jnp.dot(part_ref[2, h], p_ref[h, :, at], preferred_element_type=jnp.float32)
            o_ref[h * HEAD : (h + 1) * HEAD, at] = out.astype(o_ref.dtype)

        kept.append(pltpu.make_async_copy(p_ref.at[h], p_out.at[h], sems.at[1 + tiles + h]))
        kept[-1].start()
    kept.append(pltpu.make_async_copy(part_ref, part_out, sems.at[1 + tiles + heads]))
    kept[-1].start()
    for keep in kept:
        keep.wait()


def attend(weight, frames, cosine, sine_table, segments):
    heads, length = D // HEAD // 8, frames.shape[1]
    joint = (3, heads, HEAD, length)
    small = jnp.bfloat16
    return kernel_call(
        attend_kernel,
        out_shape=(
            jax.ShapeDtypeStruct(joint, small),
            jax.ShapeDtypeStruct((heads, length, length), small),
            jax.ShapeDtypeStruct((heads * HEAD, length), small),
        ),
        in_specs=[IN_HBM] * 2 + [IN_VMEM] * 4,
        out_specs=(IN_HBM, IN_HBM, IN_VMEM),
        scratch_shapes=[
            pltpu.VMEM(weight.shape, small),
            pltpu.VMEM(frames.shape, small),
            pltpu.VMEM(joint, jnp.float32),
            pltpu.VMEM(joint, small),
            pltpu.VMEM((heads, length, length), small),
            pltpu.SemaphoreType.DMA((2 + length // 256 + heads,)),
        ],
        compiler_params=pltpu.CompilerParams(vmem_limit_bytes=36 * 2**20),
        name="attend",
    )(weight, frames, cosine, sine_table, segments[None, :], segments[:, None])


def cross_kernel(w_ref, h_ref, kv_ref, cq_ref, p_ref, o_ref, weight, frames, sems):
    heads, text, length = p_ref.shape
    span = heads * HEAD
    tiles = length // 256
    fetches = [pltpu.make_async_copy(w_ref.at[:, 128:384], weight, sems.at[0])]
    fetches += [
        pltpu.make_async_copy(
            h_ref.at[:, i * 256 : (i + 1) * 256], frames.at[:, i * 256 : (i + 1) * 256], sems.at[1 + i]
        )
        for i in range(tiles)
    ]
    for fetch in fetches:
        fetch.start()
    keys = [
        wide(kv_ref.at[h * HEAD : (h + 1) * HEAD, :text]).T.astype(cq_ref.dtype)
        for h in range(heads)
    ]
    fetches[0].wait()
    by_row = weight[:, span - 128 : 2 * span - 128].T
    for i in range(tiles):
        fetches[1 + i].wait()
        at = slice(i * 256, (i + 1) * 256)
        cq_ref[:, at] = jnp.dot(
            by_row, frames[:, at], preferred_element_type=jnp.float32
        ).astype(cq_ref.dtype)
        for h in range(heads):
            of = slice(h * HEAD, (h + 1) * HEAD)
            scores = jnp.dot(keys[h], cq_ref[of, at], preferred_element_type=jnp.float32) * (
                HEAD**-0.5
            )
            exponent = jnp.exp(scores - jnp.max(scores, axis=0, keepdims=True))
            probs = exponent * (1.0 / jnp.sum(exponent, axis=0, keepdims=True))
            p_ref[h, :, at] = probs.astype(p_ref.dtype)
            out = jnp.dot(
                kv_ref[of, text:], p_ref[h, :, at], preferred_element_type=jnp.float32
            )
            o_ref[of, at] = out.astype(o_ref.dtype)


def cross(weight, frames, text_kv):
    rows, length = text_kv.shape[0], frames.shape[1]
    text, small = text_kv.shape[1] // 2, jnp.bfloat16
    return kernel_call(
        cross_kernel,
        out_shape=(
            jax.ShapeDtypeStruct((rows, length), small),
            jax.ShapeDtypeStruct((rows // HEAD, text, length), small),
            jax.ShapeDtypeStruct((rows, length), small),
        ),
        in_specs=[IN_HBM, IN_HBM, IN_VMEM],
        out_specs=(IN_VMEM,) * 3,
        scratch_shapes=[
            pltpu.VMEM((weight.shape[0], 256), small),
            pltpu.VMEM(frames.shape, small),
            pltpu.SemaphoreType.DMA((1 + length // 256,)),
        ],
        compiler_params=pltpu.CompilerParams(vmem_limit_bytes=16 * 2**20),
        name="cross",
    )(weight, frames, text_kv)


def cross_back_kernel(cq_ref, p_ref, kv_ref, grad_ref, dq_ref, dkv_ref):
    heads, text, length = p_ref.shape
    scale = HEAD**-0.5
    for h in range(heads):
        of = slice(h * HEAD, (h + 1) * HEAD)
        by_key = wide(kv_ref.at[of, text:]).T.astype(cq_ref.dtype)
        grad_out = grad_ref[of, :]
        grad_probs = jnp.dot(by_key, grad_out, preferred_element_type=jnp.float32)
        probs = wide(p_ref.at[h])
        weighted = jnp.sum(probs * grad_probs, axis=0, keepdims=True)
        grad_scores = (probs * (grad_probs - weighted)).astype(cq_ref.dtype)
        dq_ref[of, :] = (
            jnp.dot(kv_ref[of, :text], grad_scores, preferred_element_type=jnp.float32) * scale
        ).astype(dq_ref.dtype)
        dkv_ref[of, :text] = (contract_last(cq_ref[of, :], grad_scores) * scale).astype(
            dkv_ref.dtype
        )
        dkv_ref[of, text:] = contract_last(grad_out, p_ref[h]).astype(dkv_ref.dtype)


def cross_back(cross_q, probs, text_kv, grad):
    return kernel_call(
        cross_back_kernel,
        out_shape=(
            jax.ShapeDtypeStruct(cross_q.shape, cross_q.dtype),
            jax.ShapeDtypeStruct(text_kv.shape, text_kv.dtype),
        ),
        in_specs=[IN_VMEM] * 4,
        out_specs=(IN_VMEM,) * 2,
        compiler_params=pltpu.CompilerParams(vmem_limit_bytes=16 * 2**20),
        name="cross_back",
    )(cross_q, probs, text_kv, grad)


def attend_back_kernel(
    part_in, p_in, g_in, cos_ref, sin_ref, o_ref, part_ref, p_ref, grad_ref, dq_ref, dk_ref, dv_ref, sems
):
    heads, length = part_ref.shape[1], part_ref.shape[3]
    fetches = [
        pltpu.make_async_copy(part_in, part_ref, sems.at[0]),
        pltpu.make_async_copy(g_in, grad_ref, sems.at[1]),
    ]
    fetches += [
        pltpu.make_async_copy(p_in.at[h], p_ref.at[h], sems.at[2 + h]) for h in range(heads)
    ]
    for fetch in fetches:
        fetch.start()
    cosine, sine_table = cos_ref[...], -sin_ref[...]
    scale = HEAD**-0.5
    fetches[0].wait()
    fetches[1].wait()
    for h in range(heads):
        of = slice(h * HEAD, (h + 1) * HEAD)
        by_key = wide(part_ref.at[2, h]).T.astype(part_ref.dtype)
        dk_ref[...] = jnp.zeros_like(dk_ref)
        dv_ref[...] = jnp.zeros_like(dv_ref)
        fetches[2 + h].wait()

        @pl.loop(0, length // 256)
        def _(i, h=h, of=of, by_key=by_key):
            at = pl.ds(pl.multiple_of(i * 256, 256), 256)
            grad_out = grad_ref[of, at]
            grad_probs = jnp.dot(by_key, grad_out, preferred_element_type=jnp.float32)
            low_probs = p_ref[h, :, at]
            probs = low_probs.astype(jnp.float32)
            weighted = jnp.sum(probs * grad_probs, axis=0, keepdims=True)
            grad_scores = (probs * (grad_probs - weighted)).astype(part_ref.dtype)
            dq_ref[:, at] = jnp.dot(
                part_ref[1, h], grad_scores, preferred_element_type=jnp.float32
            )
            dk_ref[...] += contract_last(part_ref[0, h, :, at], grad_scores)
            dv_ref[...] += contract_last(grad_out, low_probs)

        span = heads * HEAD
        grad_queries = turned(dq_ref[...] * scale, cosine, sine_table)
        grad_keys = turned(dk_ref[...] * scale, cosine, sine_table)
        o_ref[of, :] = grad_queries.astype(o_ref.dtype)
        o_ref[span + of.start : span + of.stop, :] = grad_keys.astype(o_ref.dtype)
        o_ref[2 * span + of.start : 2 * span + of.stop, :] = dv_ref[...].astype(o_ref.dtype)


def attend_back(parts, probs, grad, cosine, sine_table):
    _, heads, _, length = parts.shape
    return kernel_call(
        attend_back_kernel,
        out_shape=jax.ShapeDtypeStruct((3 * heads * HEAD, length), jnp.bfloat16),
        in_specs=[IN_HBM] * 3 + [IN_VMEM] * 2,
        out_specs=IN_VMEM,
        scratch_shapes=[pltpu.VMEM(array.shape, array.dtype) for array in (parts, probs, grad)]
        + [pltpu.VMEM((HEAD, length), jnp.float32)] * 3
        + [pltpu.SemaphoreType.DMA((2 + heads,))],
        compiler_params=pltpu.CompilerParams(vmem_limit_bytes=32 * 2**20),
        name="attend_back",
    )(parts, probs, grad, cosine, sine_table)


def update_kernel(
    block_ref,
    rate_ref,
    one_ref,
    two_ref,
    feed_ref,
    all_ref,
    gain_ref,
    output_ref,
    latent_ref,
    sheet_ref,
    first_ref,
    second_ref,
    grad_out,
    first_out,
    second_out,
    sheet_out,
    copy_out,
    norm_out,
    gain_out,
    output_out,
    latent_out,
    grad,
    gain,
    scale,
):
    step = pl.program_id(0)
    part = D // 8
    text = CTXW // 8

    @pl.when(step == 0)
    def _():
        summed = jnp.sum(gain_ref[...], axis=0)
        rows = grad.shape[0]
        here = lax.broadcasted_iota(jnp.int32, (rows, D), 1) == (
            lax.broadcasted_iota(jnp.int32, (rows, D), 0) + block_ref[0] * rows
        )
        gain[...] = lax.dot_general(
            here.astype(jnp.float32),
            summed,
            (((1,), (1,)), ((), ())),
            precision=HIGHEST,
            preferred_element_type=jnp.float32,
        )
        norm = jnp.sqrt(jnp.sum(all_ref[:, :, 0:1, 0:1]) + jnp.sum(summed * summed))
        norm_out[0] = norm
        scale[0] = 1.0 / jnp.maximum(norm, 1.0)
        gain_out[...] = gain[...] * scale[0]
        output_out[...] = output_ref[...]
        latent_out[...] = wide(latent_ref)

    for k in range(6):

        @pl.when(step == k // 2)
        def _(k=k):
            ref, start = (one_ref, k * part) if k < 3 else (two_ref, (k - 3) * part)
            for m in range(8):
                at = (k % 2) * D + m * part
                grad[:, at : at + part] = wide(ref.at[m, :, start : start + part])

    @pl.when(jnp.logical_and(step >= 3, step < 9))
    def _():
        grad[...] = wide(feed_ref)

    @pl.when(step == 9)
    def _():
        for m in range(8):
            for k in range(2):
                start = 3 * part + k * text
                at = k * CTXW + m * text
                grad[:, at : at + text] = wide(two_ref.at[m, :, start : start + text])
        grad[:, D : D + 8] = gain[...]

    for half in range(2):
        at = slice(half * D, (half + 1) * D)
        clipped = grad[:, at] * scale[0]
        sheet = sheet_ref[:, at]
        first_new = BETA_ONE * first_ref[:, at] + (1.0 - BETA_ONE) * clipped
        second_new = BETA_TWO * second_ref[:, at] + (1.0 - BETA_TWO) * clipped * clipped
        mean_hat = first_new * (1.0 / (1.0 - BETA_ONE**STEP))
        square_hat = second_new * (1.0 / (1.0 - BETA_TWO**STEP))
        sheet_new = sheet - rate_ref[2 * step + half] * (
            mean_hat / (jnp.sqrt(square_hat) + EPS_ADAM) + WEIGHT_DECAY * sheet
        )
        grad_out[:, at] = clipped
        first_out[:, at] = first_new
        second_out[:, at] = second_new
        sheet_out[:, at] = sheet_new
        copy_out[:, at] = sheet_new.astype(copy_out.dtype)


def sheet_update(
    block_index, length, one, two, feed_part, squares, gains, output, latent, sheet, first, second
):
    rows = sheet.shape[0]
    frames = output.shape
    rates = column_spread(length)[jnp.minimum(jnp.arange(20) * D, SHEET - 1)]
    column_block = pl.BlockSpec((rows, 2 * D), lambda i: (0, i))
    like = jax.ShapeDtypeStruct(sheet.shape, sheet.dtype)

    def whole(shape):
        return pl.BlockSpec(shape, lambda i: (0,) * len(shape))

    sheet, first, second, feed_part = (
        pltpu.with_memory_space_constraint(array, pltpu.HBM)
        for array in (sheet, first, second, feed_part)
    )
    return pl.pallas_call(
        update_kernel,
        grid=(10,),
        out_shape=(like, like, like, like, jax.ShapeDtypeStruct(sheet.shape, jnp.bfloat16))
        + (jax.ShapeDtypeStruct((1,), jnp.float32), jax.ShapeDtypeStruct((rows, 8), jnp.float32))
        + (
            jax.ShapeDtypeStruct(frames, jnp.bfloat16),
            jax.ShapeDtypeStruct(frames, jnp.float32),
        ),
        in_specs=[
            IN_SMEM,
            IN_SMEM,
            IN_VMEM,
            IN_VMEM,
            pl.BlockSpec((rows, 2 * D), lambda i: (0, jnp.clip(i - 3, 0, 5))),
            IN_VMEM,
            IN_VMEM,
            IN_VMEM,
            IN_VMEM,
            column_block,
            column_block,
            column_block,
        ],
        out_specs=(column_block,) * 5
        + (IN_SMEM, whole((rows, 8)), whole(frames), whole(frames)),
        scratch_shapes=[
            pltpu.VMEM((rows, 2 * D), jnp.float32),
            pltpu.VMEM((rows, 8), jnp.float32),
            pltpu.SMEM((1,), jnp.float32),
        ],
        compiler_params=pltpu.CompilerParams(vmem_limit_bytes=32 * 2**20),
        name="sheet_update",
    )(
        block_index,
        rates,
        one,
        two,
        feed_part,
        squares,
        gains,
        output,
        latent,
        sheet,
        first,
        second,
    )


def pick_blocks(blocks, order):
    return blocks.at[order].get(mode="promise_in_bounds")


def gather_line(mine, order):
    blocks = lax.all_gather(mine, "z", axis=0, tiled=True)
    return pick_blocks(blocks, order).reshape(-1, mine.shape[-1])


def gather_slots(mine):
    return lax.all_gather(mine, "z", axis=0, tiled=True).reshape(-1, mine.shape[-1])


def sort_blocks(array, order):
    blocks = array.reshape(order.shape[0], -1, array.shape[-1])
    return pick_blocks(blocks, order).reshape(array.shape)


def as_blocks(grad, order):
    return grad.reshape(order.shape[0], -1, grad.shape[-1])


def scatter_line(blocks):
    return lax.psum_scatter(blocks, "z", scatter_dimension=0, tiled=True)


def plane_plan(latents, context, clip_starts, buckets, owners, cotangent, sheet, first, second):
    groups = lax.axis_size("dp")
    planes = lax.axis_size("z")
    cores = lax.axis_size("core")
    members = groups * cores
    frames = latents.shape[1]
    length = frames * members
    rows = sheet.shape[0]
    blocks = owners.shape[0]
    head_count = D // HEAD // members
    span = D // members
    units = FF // members
    score_scale = HEAD ** (-0.5)
    tail_col = 6 * D + 3 * FF
    gain_col = tail_col + 2 * CTXW
    plane = lax.axis_index("z")

    group_ids = jnp.arange(blocks, dtype=jnp.int32)
    inverse = jnp.sum(
        jnp.where(owners[None, :] == group_ids[:, None], group_ids[None, :], 0), axis=1
    )
    slot = group_ids.reshape(groups, planes, cores).swapaxes(0, 1).reshape(-1)
    slot_of = jnp.sum(
        jnp.where(slot[None, :] == group_ids[:, None], group_ids[None, :], 0), axis=1
    )
    to_logical = jnp.take(slot_of, inverse)
    to_slots = jnp.take(owners, slot)

    orders = jnp.stack([to_slots, to_logical])
    small = jnp.concatenate(
        [
            jnp.pad(
                sheet[:, gain_col:].astype(jnp.bfloat16).astype(jnp.float32).T,
                ((0, 0), (0, 64 - rows)),
            ),
            jnp.pad(clip_starts.astype(jnp.float32), ((0, 7), (0, 64 - clip_starts.shape[1]))),
        ],
        axis=1,
    )
    both, small, text_mine, mine_one = opening(
        latents[0], cotangent[0], small, context[0], sheet
    )
    mine_one, later = lax.optimization_barrier((mine_one, sheet))
    low_sheet = later.astype(jnp.bfloat16)
    weight_one = gather_slots(mine_one)
    gains = pick_blocks(small[..., :rows].reshape(blocks, 8, rows), to_logical)
    gains = gains.swapaxes(1, 2).reshape(D, 8)
    starts = lax.dynamic_index_in_dim(
        small[0, :, 0, 64 : 64 + clip_starts.shape[1]], plane * cores, 0, False
    )
    starts = starts.astype(jnp.int32)

    bucket_ids = jnp.arange(NB, dtype=jnp.int32)
    bucket_pick = (bucket_ids == buckets[plane]).astype(jnp.float32)
    counts = jnp.sum((buckets[:, None] == bucket_ids[None, :]).astype(jnp.float32), axis=0)
    row_weight = buckets.shape[0] / (NB * jnp.sum(bucket_pick * counts))
    gain_one = gains[:, 0:1]
    gain_two = gains[:, 1:2]
    gain_three = gains[:, 2:3]
    time_gain = jnp.sum(gains[:, 3:] * bucket_pick[None, :], axis=1, keepdims=True)

    tokens = both[:, :D].astype(jnp.float32).T
    grad_out = both[:, D:].astype(jnp.float32).T * row_weight

    rest = frames // planes
    place = jnp.arange(length, dtype=jnp.int32).reshape(planes, cores, groups, rest)
    positions = place.transpose(2, 1, 0, 3).reshape(-1)
    segments = segment_ids(starts, positions)
    frequency = jnp.exp(
        -math.log(10000.0) * jnp.arange(HEAD // 2, dtype=jnp.float32) / (HEAD // 2)
    )
    angles = frequency[:, None] * positions.astype(jnp.float32)[None, :]
    cosine = jnp.cos(angles)
    sine_table = jnp.sin(angles)

    normed_one, inverse_one = norm_columns(tokens)
    scaled_one = gain_one * time_gain
    h_one, grad_ff, mine_gu, mine_down = first_gather(
        sort_blocks((normed_one * scaled_one).astype(jnp.bfloat16), to_slots),
        sort_blocks(grad_out.astype(jnp.bfloat16), to_slots),
        low_sheet,
    )
    weight_gu = gather_slots(mine_gu)
    line_down = gather_slots(mine_down)

    parts, probs, attn_out = attend(weight_one, h_one, cosine, sine_table, segments)
    attn_out, x_one, normed_two, inverse_two, h_two, text_kv = project(
        "sum",
        0,
        orders,
        attn_out,
        weight_one,
        tokens,
        gain_two,
        text_mine,
    )

    cross_q, cross_probs, cross_out = cross(weight_one, h_two, text_kv)
    cross_out, x_two, normed_three, inverse_three, h_three = project(
        "slots",
        2 * span,
        orders,
        cross_out,
        weight_one,
        x_one,
        gain_three,
    )

    gate_up = contract_rows(weight_gu, h_three)
    gate_pre = gate_up[:units]
    up_part = gate_up[units:]
    sigmoid_gate = jax.nn.sigmoid(gate_pre)
    silu_gate = gate_pre * sigmoid_gate
    hidden = (silu_gate * up_part).astype(jnp.bfloat16)

    grad_blocks_down = as_blocks(contract_last(grad_ff, hidden).astype(jnp.bfloat16), to_slots)
    weight_down, grad_blocks_down = lax.optimization_barrier((line_down, grad_blocks_down))
    sums_down = scatter_line(grad_blocks_down)
    grad_hidden = contract_rows(weight_down, grad_ff)
    grad_gate = grad_hidden * up_part * (sigmoid_gate * (1.0 + gate_pre * (1.0 - sigmoid_gate)))
    grad_up = grad_hidden * silu_gate
    grad_gu = jnp.concatenate([grad_gate, grad_up], axis=0).astype(jnp.bfloat16)
    grad_x_two, grad_weight_gu, sum_three, grad_cross = back(
        orders,
        weight_gu,
        grad_gu,
        h_three,
        (normed_three, inverse_three, gain_three, grad_out),
        send_rows=True,
        in_slots=True,
        after=[grad_blocks_down],
    )
    grad_blocks_gu = as_blocks(grad_weight_gu, to_slots)
    sums_gu = scatter_line(grad_blocks_gu)
    grad_cross_out, grad_weight_co = back(
        orders, weight_one, grad_cross, cross_out, column=2 * span
    )
    grad_cross_q, grad_text = cross_back(cross_q, cross_probs, text_kv, grad_cross_out)
    grad_x_one, grad_weight_cq, sum_two, grad_attn, grad_text = back(
        orders,
        weight_one,
        grad_cross_q,
        h_two,
        (normed_two, inverse_two, gain_two, grad_x_two),
        column=span,
        send_rows=True,
        text=grad_text,
        in_slots=True,
        after=[sums_down],
    )
    grad_attn_out, grad_weight_two = back(
        orders,
        weight_one,
        grad_attn,
        attn_out,
        beside=(grad_weight_cq, grad_weight_co, grad_text, text_mine),
    )
    grad_blocks_two = as_blocks(grad_weight_two, to_slots)
    sums_two = scatter_line(grad_blocks_two)
    grad_qkv = attend_back(parts, probs, grad_attn_out, cosine, sine_table)
    latent_grad, grad_weight_qkv, sum_one = back(
        orders,
        weight_one,
        grad_qkv,
        h_one,
        (normed_one, inverse_one, scaled_one, grad_x_one),
        column=4 * span,
        in_slots=True,
        after=[sums_gu],
    )
    grad_blocks_one = as_blocks(grad_weight_qkv, to_slots)
    sums_one = scatter_line(grad_blocks_one)
    sums_feed, ff_out, latent_grad = feed(
        sums_gu,
        sums_down,
        weight_down,
        hidden,
        latent_grad,
        [grad_blocks_one],
    )
    sum_one = sum_one[0:1]
    grad_gain_one = sum_one * time_gain.T
    grad_time = sum_one * gain_one.T
    gain_grads = jnp.concatenate(
        [
            grad_gain_one,
            sum_two[0:1],
            sum_three[0:1],
            bucket_pick[:, None] * grad_time,
        ],
        axis=0,
    )
    output, squares = prepare(orders, ff_out, x_two, sums_gu, sums_down, sums_two)
    sums_two = exchange_blocks(sums_two, [sums_feed])
    output, sums_one, gain_sums, squares = closing(
        output, squares, sums_one, gain_grads, sums_two
    )
    place = lax.axis_index("dp") * (planes * cores) + plane * cores + lax.axis_index("core")
    (
        clipped,
        first_new,
        second_new,
        sheet_new,
        sheet_copy,
        grad_norm,
        gain_grad,
        output,
        latent_grad,
    ) = sheet_update(
        lax.dynamic_slice_in_dim(owners, place, 1),
        length,
        sums_one,
        sums_two,
        sums_feed,
        squares,
        gain_sums,
        output,
        latent_grad,
        sheet,
        first,
        second,
    )
    return (
        output[None],
        latent_grad[None],
        grad_norm[0],
        clipped,
        gain_grad,
        first_new,
        second_new,
        sheet_new,
        sheet_copy,
    )


def solution(mesh):
    groups, seq_count = mesh.shape["dp"], mesh.shape["seq"]
    by_plane = groups == 4 and seq_count == 8
    if by_plane:
        mesh = Mesh(mesh.devices.reshape(groups, seq_count // 2, 2), ("dp", "z", "core"))
    seq = ("z", "core") if by_plane else "seq"
    both = ("dp", "z", "core") if by_plane else ("dp", "seq")
    in_specs = (
        P("dp", seq, None),
        P("dp", None, None),
        P("dp", None),
        P(),
        P(),
        P("dp", seq, None),
        P(both, None),
        P(both, None),
        P(both, None),
    )
    out_specs = (
        P("dp", seq, None),
        P("dp", seq, None),
        P(),
        P(both, None),
        P(both, None),
        P(both, None),
        P(both, None),
        P(both, None),
        P(both, None),
    )
    return jax.shard_map(
        plane_plan if by_plane else gather_plan,
        mesh=mesh,
        in_specs=in_specs,
        out_specs=out_specs,
        check_vma=False,
    )
```
